32 devices in a mesh: rep: 4 (over z), shard: 8 (over y, x, core).
Axes of the slice: x: 2, y: 2, z: 4, core: 2. Of those that a mesh axis runs over, the one named last changes fastest.
Arguments:
- block_input: bfloat16 [32, 1024, 1024], P(('rep', 'shard')), may hold values from -6 to 6
- document_numbers: int32 [32, 1024], P(('rep', 'shard')), may hold values from 0 to 3, as said below
- attn_gain: bfloat16 [1024], P('shard'), may hold values from 0.099609375 to 1.8984375
- w_query: bfloat16 [1024, 1024], P('shard'), may hold values from -0.1875 to 0.1875
- key_weight: bfloat16 [1024, 512], P('shard'), may hold values from -0.1875 to 0.1875
- value_weight: bfloat16 [1024, 512], P('shard'), may hold values from -0.1875 to 0.1875
- query_gain: bfloat16 [64], P('shard'), may hold values from 0.796875 to 1.796875
- key_gain: bfloat16 [64], P('shard'), may hold values from 0.796875 to 1.796875
- w_output: bfloat16 [1024, 1024], P('shard'), may hold values from -0.75 to 0.75
- ffn_gain: bfloat16 [1024], P('shard'), may hold values from 0.099609375 to 1.8984375
- w_gate: bfloat16 [1024, 4608], P('shard'), may hold values from -0.1875 to 0.1875
- w_up: bfloat16 [1024, 4608], P('shard'), may hold values from -0.1875 to 0.1875
- w_down: bfloat16 [4608, 1024], P('shard'), may hold values from -0.09375 to 0.09375
- cotangent: bfloat16 [32, 1024, 1024], P(('rep', 'shard')), may hold values from -6 to 6
Outputs:
- block_output: bfloat16 [32, 1024, 1024], P(('rep', 'shard'))
- input_grad: float32 [32, 1024, 1024], P(('rep', 'shard'))
- grad_attn_gain: float32 [1024], P('shard')
- grad_w_query: float32 [1024, 1024], P('shard')
- grad_w_key: float32 [1024, 512], P('shard')
- grad_w_value: float32 [1024, 512], P('shard')
- grad_query_gain: float32 [64], P('shard')
- grad_key_gain: float32 [64], P('shard')
- grad_w_output: float32 [1024, 1024], P('shard')
- grad_ffn_gain: float32 [1024], P('shard')
- grad_w_gate: float32 [1024, 4608], P('shard')
- grad_w_up: float32 [1024, 4608], P('shard')
- grad_w_down: float32 [4608, 1024], P('shard')
The draws below stay inside these ranges and needn't reach their ends.
Inputs may be any that keep to these rules, and one draw needn't show every extreme that they name: `document_numbers`: within each sequence the ids start at 0 on its first token, never fall, and reach 3 on its last token; a document is a run of equal ids, and an id may skip values.
All inputs are finite; a program needn't handle non-finite values.
Results may differ from the reference program's by a relative error of at most 0.02.
Values may be sent and summed in bfloat16 or wider, within the bound.
No kernel may reach another device: no remote copies, remote signals or barrier semaphores. Data moves between devices by JAX's collectives and lax.ppermute only.
A program may use at most 256 MiB of HBM per device.

```python
import math
import jax
import jax.numpy as jnp
from jax import lax

MODEL_WIDTH = 1024
QUERY_HEADS = 16
KEY_VALUE_HEADS = 8
HEAD_SIZE = 64
FF = 4608
SEQ_LEN = 1024
CUTS = 3
SEQS = 32


def draw_document_numbers(key, part):
    key = jax.random.fold_in(key, 7)
    boundaries = jax.random.randint(key, (SEQS, CUTS), 1, SEQ_LEN, dtype=jnp.int32)
    positions = jnp.arange(SEQ_LEN, dtype=jnp.int32)
    passed = (boundaries[:, :, None] <= positions[None, None, :]).astype(jnp.int32)
    return jnp.sum(passed, axis=1).astype(jnp.int32)


def steps_of(stream_key, extent, cuts, smallest, high):
    level, own = 1.0, jax.random.fold_in(stream_key, 6)
    for axis_at, shards_of in cuts:
        draws = jnp.exp(jax.random.uniform(jax.random.fold_in(own, axis_at), (shards_of,), jnp.float32, smallest / len(cuts), high / len(cuts)))
        level = level * jnp.repeat(draws, extent[axis_at] // shards_of).reshape([-1 if axis == axis_at else 1 for axis in range(len(extent))])
    return level


def noise(stream_key, extent, spread, limit, shards=(), kind=jnp.bfloat16):
    array = spread * jax.random.normal(stream_key, extent, jnp.float32)
    if shards:
        array = array * steps_of(stream_key, extent, shards, -0.22, 0.18)
    return jnp.clip(array, -limit, limit).astype(kind)


def setup_inputs(seed: int = 0) -> dict:
    splits = jax.random.split(jax.random.key(seed), 15)
    block_input = noise(splits[0], (SEQS, SEQ_LEN, MODEL_WIDTH), 1.0, 6.0, ((0, 32),))
    document_numbers = draw_document_numbers(jax.random.fold_in(splits[14], 71), 0)
    attn_gain = jnp.clip(1.0 + 0.18 * jax.random.normal(splits[2], (MODEL_WIDTH,), jnp.float32), 0.099609375, 1.8984375).astype(jnp.bfloat16)
    w_query = noise(splits[3], (MODEL_WIDTH, QUERY_HEADS * HEAD_SIZE), MODEL_WIDTH ** -0.5, 0.1875, ((0, 8),))
    key_weight = noise(splits[4], (MODEL_WIDTH, KEY_VALUE_HEADS * HEAD_SIZE), MODEL_WIDTH ** -0.5, 0.1875, ((0, 8),))
    value_weight = noise(splits[5], (MODEL_WIDTH, KEY_VALUE_HEADS * HEAD_SIZE), MODEL_WIDTH ** -0.5, 0.1875, ((0, 8),))
    query_gain = jnp.clip(0.796875 + 1.0 * jax.random.uniform(splits[6], (HEAD_SIZE,), jnp.float32) ** steps_of(splits[6], (HEAD_SIZE,), ((0, 8),), -0.2, 0.2), 0.796875, 1.796875).astype(jnp.bfloat16)
    key_gain = jnp.clip(0.796875 + 1.0 * jax.random.uniform(splits[7], (HEAD_SIZE,), jnp.float32) ** steps_of(splits[7], (HEAD_SIZE,), ((0, 8),), -0.2, 0.2), 0.796875, 1.796875).astype(jnp.bfloat16)
    w_output = noise(splits[8], (QUERY_HEADS * HEAD_SIZE, MODEL_WIDTH), (QUERY_HEADS * HEAD_SIZE // 16) ** -0.5, 0.75, ((0, 8),))
    ffn_gain = jnp.clip(1.0 + 0.18 * jax.random.normal(splits[9], (MODEL_WIDTH,), jnp.float32), 0.099609375, 1.8984375).astype(jnp.bfloat16)
    w_gate = noise(splits[10], (MODEL_WIDTH, FF), MODEL_WIDTH ** -0.5, 0.1875, ((0, 8),))
    w_up = noise(splits[11], (MODEL_WIDTH, FF), MODEL_WIDTH ** -0.5, 0.1875, ((0, 8),))
    w_down = noise(splits[12], (FF, MODEL_WIDTH), FF ** -0.5, 0.09375, ((0, 8),))
    cotangent = noise(splits[13], (SEQS, SEQ_LEN, MODEL_WIDTH), 1.0, 6.0, ((0, 32),))
    return {"block_input": block_input, "document_numbers": document_numbers, "attn_gain": attn_gain, "w_query": w_query, "key_weight": key_weight, "value_weight": value_weight, "query_gain": query_gain, "key_gain": key_gain, "w_output": w_output, "ffn_gain": ffn_gain, "w_gate": w_gate, "w_up": w_up, "w_down": w_down, "cotangent": cotangent}


EPS = 1e-05
rope_base = 1000000.0
precise = lax.Precision.HIGHEST

@jax.custom_vjp
def reduced_input(v):
    return lax.optimization_barrier(v.astype(jnp.bfloat16)).astype(jnp.float32)

@jax.custom_vjp
def reduced_gradient(v):
    return v

def low_keep(v):
    return (reduced_input(v), None)

def low_pass(kept, grad):
    return (grad,)

def back_keep(v):
    return (v, None)

def back_low(kept, grad):
    return (reduced_input(grad),)
reduced_input.defvjp(low_keep, low_pass)
reduced_gradient.defvjp(back_keep, back_low)

def matrix_product(left, right):
    return jnp.dot(left, right, precision=precise, preferred_element_type=jnp.float32)

def rms_norm(value_rows, gain):
    return value_rows * lax.rsqrt(lax.optimization_barrier(jnp.mean(value_rows * value_rows, axis=-1, keepdims=True)) + EPS) * gain

def rope_tables(seg_group):
    query_groups, token_length = seg_group.shape
    indices = jnp.arange(token_length, dtype=jnp.int32)
    starts = jnp.concatenate([jnp.ones((query_groups, 1), dtype=bool), seg_group[:, 1:] != seg_group[:, :-1]], axis=1)
    begins = lax.cummax(jnp.where(starts, indices[None, :], jnp.zeros_like(seg_group)), axis=1)
    offsets = (indices[None, :] - begins).astype(jnp.float32)[:, :, None, None]
    frequency = rope_base ** (-jnp.arange(0, HEAD_SIZE, 2).astype(jnp.float32) / HEAD_SIZE)
    angles = offsets * frequency
    angles = jnp.concatenate([angles, angles], axis=-1)
    return (jnp.cos(angles), jnp.sin(angles))

def rotate(value_rows, cosine, sine):
    half_dim = value_rows.shape[-1] // 2
    turned = jnp.concatenate([-value_rows[..., half_dim:], value_rows[..., :half_dim]], axis=-1)
    return value_rows * cosine + turned * sine

def attend(pieces):
    query_rows, key_rows, value_rows, seg_row = pieces
    token_length = query_rows.shape[0]
    head_grouped = query_rows.reshape(token_length, KEY_VALUE_HEADS, QUERY_HEADS // KEY_VALUE_HEADS, HEAD_SIZE)
    scores = jnp.einsum('qkgd,pkd->kgqp', head_grouped, key_rows, precision=precise) * HEAD_SIZE ** (-0.5)
    indices = jnp.arange(token_length)
    allowed = (indices[:, None] >= indices[None, :]) & (seg_row[:, None] == seg_row[None, :])
    scores = reduced_gradient(jnp.where(allowed[None, None], scores, -1e+30))
    probabilities = reduced_input(jax.nn.softmax(scores, axis=-1))
    attended = jnp.einsum('kgqp,pkd->qkgd', probabilities, value_rows, precision=precise)
    return attended.reshape(token_length, QUERY_HEADS, HEAD_SIZE)

def block(inputs, seg_group, attn_gain, w_query, key_weight, value_weight, query_gain, key_gain, w_output, ffn_gain, w_gate, w_up, w_down):
    query_groups, token_length, features = inputs.shape
    rows_all = query_groups * token_length
    flat = inputs.reshape(rows_all, features)
    first_normed = reduced_input(rms_norm(flat, attn_gain))
    query_rows = reduced_gradient(matrix_product(first_normed, w_query)).reshape(query_groups, token_length, QUERY_HEADS, HEAD_SIZE)
    key_rows = reduced_gradient(matrix_product(first_normed, key_weight)).reshape(query_groups, token_length, KEY_VALUE_HEADS, HEAD_SIZE)
    value_rows = reduced_input(reduced_gradient(matrix_product(first_normed, value_weight))).reshape(query_groups, token_length, KEY_VALUE_HEADS, HEAD_SIZE)
    cosine, sine = rope_tables(seg_group)
    query_rows = reduced_input(rotate(rms_norm(query_rows, query_gain), cosine, sine))
    key_rows = reduced_input(rotate(rms_norm(key_rows, key_gain), cosine, sine))
    attended = lax.map(jax.checkpoint(attend), (query_rows, key_rows, value_rows, seg_group))
    attended = reduced_input(reduced_gradient(attended.reshape(rows_all, QUERY_HEADS * HEAD_SIZE)))
    first_sum = flat + reduced_gradient(matrix_product(attended, w_output))
    normed_two = reduced_input(rms_norm(first_sum, ffn_gain))
    gate_value = reduced_gradient(matrix_product(normed_two, w_gate))
    up_value = reduced_gradient(matrix_product(normed_two, w_up))
    hidden = reduced_input(jax.nn.silu(gate_value) * up_value)
    return (first_sum + reduced_gradient(matrix_product(hidden, w_down))).reshape(query_groups, token_length, features)

def reference(block_input, document_numbers, attn_gain, w_query, key_weight, value_weight, query_gain, key_gain, w_output, ffn_gain, w_gate, w_up, w_down, cotangent):
    params = tuple((matrix.astype(jnp.float32) for matrix in (attn_gain, w_query, key_weight, value_weight, query_gain, key_gain, w_output, ffn_gain, w_gate, w_up, w_down)))
    seq_total, token_length, features = block_input.shape
    per_group = math.gcd(seq_total, max(1, 4096 // token_length))
    turns = seq_total // per_group
    inputs = block_input.astype(jnp.float32).reshape(turns, per_group, token_length, features)
    seg_groups = document_numbers.reshape(turns, per_group, token_length)
    cot_groups = cotangent.astype(jnp.float32).reshape(turns, per_group, token_length, features)

    def step_fn(totals, pieces):
        input_group, seg_group, cot_group = pieces

        def forward(input_part, *weights):
            return block(input_part, seg_group, *weights)
        outputs, pull = jax.vjp(forward, input_group, *params)
        grads = pull(cot_group)
        return (tuple((total_part + grad_part for total_part, grad_part in zip(totals, grads[1:]))), (outputs, grads[0]))
    zeros_all = tuple((jnp.zeros(matrix.shape, jnp.float32) for matrix in params))
    totals, (outputs, input_grads) = lax.scan(step_fn, zeros_all, (inputs, seg_groups, cot_groups))
    block_output = outputs.reshape(seq_total, token_length, features).astype(jnp.bfloat16)
    input_grad = input_grads.reshape(seq_total, token_length, features)
    return (block_output, input_grad, totals[0], totals[1], totals[2], totals[3], totals[4], totals[5], totals[6], totals[7], totals[8], totals[9], totals[10])
```

```python
import jax
import jax.numpy as jnp
from jax import lax
from jax.experimental import pallas as pl
from jax.experimental.pallas import tpu as pltpu
from jax.sharding import PartitionSpec as P

QUERY_HEADS = 16
KEY_VALUE_HEADS = 8
HEAD_SIZE = 64
FF = 4608
EPS = 1e-05
ROPE_BASE = 1000000.0
FAR = 32768.0
TILE = 256
VMEM_LIMIT = 56 * 1024 * 1024
NT = ((1,), (1,))
NN = ((1,), (0,))


def dot(left, right, dims=NN):
    return lax.dot_general(left, right, (dims, ((), ())), preferred_element_type=jnp.float32)


def einsum_result(form, left, right):
    return jnp.einsum(form, left, right, preferred_element_type=jnp.float32)


def unit_rows(rows):
    inverse = lax.rsqrt(jnp.mean(rows * rows, axis=-1, keepdims=True) + EPS)
    return rows * inverse, inverse


def unit_back(grad_out, unit_part, inverse, gain):
    scaled = grad_out * gain
    return inverse * (scaled - unit_part * jnp.mean(scaled * unit_part, axis=-1, keepdims=True))


def split3(value):
    high = value.astype(jnp.bfloat16).astype(jnp.float32)
    rest = value - high
    middle = rest.astype(jnp.bfloat16).astype(jnp.float32)
    return high, middle, rest - middle


def causal(query_axis):
    first = lax.broadcasted_iota(jnp.int32, (TILE, TILE), 0)
    second = lax.broadcasted_iota(jnp.int32, (TILE, TILE), 1)
    return (first >= second) if query_axis == 0 else (second >= first)


def attend_kernel(q_ref, k_ref, v_ref, o_ref, qb_ref):
    tiles = q_ref.shape[1] // TILE
    keep = causal(0)
    lane = lax.broadcasted_iota(jnp.int32, (TILE, 128), 1)
    for i in range(tiles):
        rows = slice(i * TILE, (i + 1) * TILE)
        halves = []
        for h in range(2):
            q = q_ref[h, rows, :]
            out = None
            for j in range(i + 1):
                cols = slice(j * TILE, (j + 1) * TILE)
                weights = jnp.exp(dot(q, k_ref[0, cols, :], NT))
                if j == i:
                    weights = jnp.where(keep, weights, 0.0)
                part = dot(weights.astype(jnp.bfloat16), v_ref[0, cols, :])
                out = part if out is None else out + part
            total = out[:, 64:65]
            halves.append(out / total)
            high, middle, low = split3(-jnp.log(total))
            extra = jnp.where(
                lane == 68, high, jnp.where(lane == 69, middle, jnp.where(lane == 70, low, 0.0))
            )
            qb_ref[h, rows, :] = (q.astype(jnp.float32) + extra).astype(jnp.bfloat16)
        both = jnp.where(lane < 64, halves[0], pltpu.roll(halves[1], 64, 1))
        o_ref[rows, :] = both.astype(jnp.bfloat16)


def attend(q_aug, k_aug, v_aug):
    heads, length, _ = q_aug.shape
    groups = k_aug.shape[0]
    return pl.pallas_call(
        attend_kernel,
        grid=(groups,),
        in_specs=[
            pl.BlockSpec((2, length, 128), lambda g: (g, 0, 0)),
            pl.BlockSpec((1, length, 128), lambda g: (g, 0, 0)),
            pl.BlockSpec((1, length, 128), lambda g: (g, 0, 0)),
        ],
        out_specs=[
            pl.BlockSpec((length, 128), lambda g: (0, g)),
            pl.BlockSpec((2, length, 128), lambda g: (g, 0, 0)),
        ],
        out_shape=[
            jax.ShapeDtypeStruct((length, groups * 128), jnp.bfloat16),
            jax.ShapeDtypeStruct((heads, length, 128), jnp.bfloat16),
        ],
        compiler_params=pltpu.CompilerParams(vmem_limit_bytes=VMEM_LIMIT),
        cost_estimate=pl.CostEstimate(
            flops=20 * 10**9, bytes_accessed=16 * 2**20, transcendentals=10 * 2**20
        ),
        name="attend",
    )(q_aug, k_aug, v_aug)


def attend_back_kernel(q_ref, k_ref, v_ref, o_ref, do_ref, dq_ref, dkv_ref, do_aug, k_t, dq_t):
    length = q_ref.shape[1]
    tiles = length // TILE
    keep = causal(1)
    lane = lax.broadcasted_iota(jnp.int32, (length, 128), 1)
    back = do_ref[...].astype(jnp.float32)
    product = back * o_ref[...].astype(jnp.float32)
    for h in range(2):
        own = (lane < 64) if h == 0 else (lane >= 64)
        centre = jnp.sum(jnp.where(own, product, 0.0), axis=1, keepdims=True)
        moved = back if h == 0 else pltpu.roll(back, 64, 1)
        high, middle, low = split3(-centre)
        extra = jnp.where(
            lane == 64, high, jnp.where(lane == 65, middle, jnp.where(lane == 66, low, 0.0))
        )
        do_aug[h] = jnp.where(lane < 64, moved, extra).astype(jnp.bfloat16)
    k_t[...] = k_ref[0].astype(jnp.float32).T[:64, :].astype(jnp.bfloat16)
    low_half = lax.broadcasted_iota(jnp.int32, (TILE, 128), 1) < 64
    for j in range(tiles):
        cols = slice(j * TILE, (j + 1) * TILE)
        k = k_ref[0, cols, :]
        v = v_ref[0, cols, :]
        dk = None
        dv = None
        for i in range(j, tiles):
            rows = slice(i * TILE, (i + 1) * TILE)
            for h in range(2):
                q = q_ref[h, rows, :]
                do = do_aug[h, rows, :]
                probs = jnp.exp(dot(k, q, NT))
                if i == j:
                    probs = jnp.where(keep, probs, 0.0)
                scores = (probs * dot(v, do, NT)).astype(jnp.bfloat16)
                to_v = dot(probs.astype(jnp.bfloat16), do)
                to_k = dot(scores, q)
                dv = to_v if dv is None else dv + to_v
                dk = to_k if dk is None else dk + to_k
                to_q = dot(k_t[:, cols], scores)
                if j == 0:
                    dq_t[h * 64 : (h + 1) * 64, rows] = to_q
                else:
                    dq_t[h * 64 : (h + 1) * 64, rows] += to_q
        dkv_ref[cols, :] = jnp.where(low_half, dk, pltpu.roll(dv, 64, 1))
    dq_ref[...] = dq_t[...].T


def attend_back(q_back, k_aug, v_aug, attended, back_attended):
    _, length, _ = q_back.shape
    groups = k_aug.shape[0]
    by_group = pl.BlockSpec((length, 128), lambda g: (0, g))
    return pl.pallas_call(
        attend_back_kernel,
        grid=(groups,),
        in_specs=[
            pl.BlockSpec((2, length, 128), lambda g: (g, 0, 0)),
            pl.BlockSpec((1, length, 128), lambda g: (g, 0, 0)),
            pl.BlockSpec((1, length, 128), lambda g: (g, 0, 0)),
            by_group,
            by_group,
        ],
        out_specs=[by_group, by_group],
        out_shape=[jax.ShapeDtypeStruct((length, groups * 128), jnp.float32)] * 2,
        scratch_shapes=[
            pltpu.VMEM((2, length, 128), jnp.bfloat16),
            pltpu.VMEM((64, length), jnp.bfloat16),
            pltpu.VMEM((128, length), jnp.float32),
        ],
        compiler_params=pltpu.CompilerParams(vmem_limit_bytes=VMEM_LIMIT),
        cost_estimate=pl.CostEstimate(
            flops=38 * 10**9, bytes_accessed=24 * 2**20, transcendentals=10 * 2**20
        ),
        name="attend_back",
    )(q_back, k_aug, v_aug, attended, back_attended)


def rope_tables(numbers):
    length = numbers.shape[0]
    indices = jnp.arange(length, dtype=jnp.int32)
    starts = jnp.concatenate([jnp.ones((1,), dtype=bool), numbers[1:] != numbers[:-1]])
    begins = lax.cummax(jnp.where(starts, indices, jnp.zeros_like(numbers)), axis=0)
    offsets = (indices - begins).astype(jnp.float32).reshape(length, 1)
    frequency = ROPE_BASE ** (-jnp.arange(0, HEAD_SIZE, 2).astype(jnp.float32) / HEAD_SIZE)
    angles = offsets * frequency
    cosine = jnp.cos(angles)
    sine = jnp.sin(angles)
    return (
        jnp.concatenate([cosine, cosine], axis=-1)[:, None, :],
        jnp.concatenate([sine, sine], axis=-1)[:, None, :],
    )


def rotate(rows, cosine, sine):
    half = rows.shape[-1] // 2
    turned = jnp.concatenate([-rows[..., half:], rows[..., :half]], axis=-1)
    return rows * cosine + turned * sine


def rotate_back(grads, cosine, sine):
    half = grads.shape[-1] // 2
    moved = grads * sine
    return grads * cosine + jnp.concatenate([moved[..., half:], -moved[..., :half]], axis=-1)


def augment(q, k, v, numbers):
    length = numbers.shape[0]
    same = (numbers[:, None] == jnp.arange(4)[None]).astype(jnp.float32)
    q_more = jnp.concatenate([-FAR * same, jnp.zeros((length, 60))], 1)
    k_more = jnp.concatenate([1 - same, jnp.ones((length, 3)), jnp.zeros((length, 57))], 1)
    v_more = jnp.concatenate([jnp.ones((length, 3)), jnp.zeros((length, 61))], 1)

    def join(rows, more):
        rows = rows.transpose(1, 0, 2)
        more = jnp.broadcast_to(more.astype(jnp.bfloat16), rows.shape)
        return jnp.concatenate([rows, more], 2)

    return (
        join(q * jnp.bfloat16(HEAD_SIZE**-0.5), q_more),
        join(k, k_more),
        join(v, v_more),
    )


def gather(array):
    return lax.all_gather(array, "shard", axis=0, tiled=True)


def scatter(array):
    return lax.psum_scatter(array, "shard", scatter_dimension=0, tiled=True)


def block_step(
    inputs,
    numbers,
    gain_attn,
    gain_query,
    gain_key,
    gain_ffn,
    attn_pack,
    pair,
    down,
    cotangent,
):
    rows = inputs.shape[0]
    w_query = attn_pack[:, :1024]
    w_key = attn_pack[:, 1024:1536]
    w_value = attn_pack[:, 1536:2048]
    w_output = attn_pack[:, 2048:]
    unit_one, inverse_one = unit_rows(inputs)
    normed_one = (unit_one * gain_attn).astype(jnp.bfloat16)
    raw = einsum_result("vp,pl->vl", normed_one, attn_pack[:, :2048])
    query_raw = raw[:, :1024].reshape(rows, QUERY_HEADS, HEAD_SIZE)
    key_raw = raw[:, 1024:1536].reshape(rows, KEY_VALUE_HEADS, HEAD_SIZE)
    values = raw[:, 1536:].astype(jnp.bfloat16).reshape(rows, KEY_VALUE_HEADS, HEAD_SIZE)
    cosine, sine = rope_tables(numbers)
    query_unit, query_inverse = unit_rows(query_raw)
    key_unit, key_inverse = unit_rows(key_raw)
    queries = rotate(query_unit * gain_query, cosine, sine).astype(jnp.bfloat16)
    keys = rotate(key_unit * gain_key, cosine, sine).astype(jnp.bfloat16)
    q_aug, k_aug, v_aug = augment(queries, keys, values, numbers)
    attended, q_back = attend(q_aug, k_aug, v_aug)
    first_sum = inputs + einsum_result("nh,hd->nd", attended, w_output)
    unit_two, inverse_two = unit_rows(first_sum)
    normed_two = (unit_two * gain_ffn).astype(jnp.bfloat16)
    gate_value = einsum_result("nc,cf->nf", normed_two, pair[:, :FF])
    up_value = einsum_result("nc,cf->nf", normed_two, pair[:, FF:])
    sigmoid_gate = jax.nn.sigmoid(gate_value)
    swish_gate = gate_value * sigmoid_gate
    hidden = (swish_gate * up_value).astype(jnp.bfloat16)
    grad_down = scatter(einsum_result("nf,nd->fd", hidden, cotangent).astype(jnp.bfloat16))
    back_hidden = einsum_result("nd,fd->nf", cotangent, down)
    back_up = (back_hidden * swish_gate).astype(jnp.bfloat16)
    back_gate = (
        back_hidden * up_value * sigmoid_gate * (1.0 + gate_value * (1.0 - sigmoid_gate))
    ).astype(jnp.bfloat16)
    grad_gate = scatter(einsum_result("nc,nf->cf", normed_two, back_gate).astype(jnp.bfloat16))
    grad_up = scatter(einsum_result("nc,nf->cf", normed_two, back_up).astype(jnp.bfloat16))
    back_two = einsum_result("nf,cf->nc", back_gate, pair[:, :FF]) + einsum_result(
        "nf,cf->nc", back_up, pair[:, FF:]
    )
    grad_gain_ffn = jnp.sum(back_two * unit_two, axis=0)
    back_first = cotangent.astype(jnp.float32) + unit_back(
        back_two, unit_two, inverse_two, gain_ffn
    )
    back_attn = back_first.astype(jnp.bfloat16)
    back_attended = einsum_result("nd,hd->nh", back_attn, w_output).astype(jnp.bfloat16)
    grad_out = einsum_result("nh,nd->hd", attended, back_attn).astype(jnp.bfloat16)
    dq, dkv = attend_back(q_back, k_aug, v_aug, attended, back_attended)
    dkv = dkv.reshape(rows, KEY_VALUE_HEADS, 2 * HEAD_SIZE)
    scaling = HEAD_SIZE**-0.5
    back_queries = dq.reshape(rows, QUERY_HEADS, HEAD_SIZE) * scaling
    back_keys = dkv[:, :, :HEAD_SIZE]
    back_values = dkv[:, :, HEAD_SIZE:].astype(jnp.bfloat16).reshape(rows, 512)
    query_turned = rotate_back(back_queries, cosine, sine)
    key_turned = rotate_back(back_keys, cosine, sine)
    grad_gain_query = jnp.sum(query_turned * query_unit, axis=(0, 1))
    grad_gain_key = jnp.sum(key_turned * key_unit, axis=(0, 1))
    back_query_raw = unit_back(query_turned, query_unit, query_inverse, gain_query)
    back_key_raw = unit_back(key_turned, key_unit, key_inverse, gain_key)
    back_raw = jnp.concatenate(
        [
            back_query_raw.astype(jnp.bfloat16).reshape(rows, 1024),
            back_key_raw.astype(jnp.bfloat16).reshape(rows, 512),
            back_values,
        ],
        axis=1,
    )
    back_one = einsum_result("nh,ch->nc", back_raw, attn_pack[:, :2048])
    grad_gain_attn = jnp.sum(back_one * unit_one, axis=0)
    input_grad = back_first + unit_back(back_one, unit_one, inverse_one, gain_attn)
    grad_attn = scatter(
        jnp.concatenate(
            [einsum_result("nc,nh->ch", normed_one, back_raw).astype(jnp.bfloat16), grad_out],
            axis=1,
        )
    )
    ffn_out = einsum_result("nf,fd->nd", hidden, down)
    block_output = (first_sum + ffn_out).astype(jnp.bfloat16)
    gains = [grad_gain_attn, grad_gain_query, grad_gain_key, grad_gain_ffn]
    return block_output, input_grad, grad_down, grad_gate, grad_up, grad_attn, gains


def on_device(
    block_input,
    document_numbers,
    attn_gain,
    w_query,
    key_weight,
    value_weight,
    query_gain,
    key_gain,
    w_output,
    ffn_gain,
    w_gate,
    w_up,
    w_down,
    cotangent,
):
    _, length, features = block_input.shape
    parts = features // attn_gain.shape[0]
    widths = [attn_gain.shape[0], query_gain.shape[0], key_gain.shape[0], ffn_gain.shape[0]]
    gains = lax.all_gather(
        jnp.concatenate([attn_gain, query_gain, key_gain, ffn_gain]), "shard", axis=0, tiled=False
    ).astype(jnp.float32)
    offsets = [sum(widths[:i]) for i in range(5)]
    gain_attn, gain_query, gain_key, gain_ffn = [
        gains[:, offsets[i] : offsets[i + 1]].reshape(-1) for i in range(4)
    ]
    attn_pack = gather(jnp.concatenate([w_query, key_weight, value_weight, w_output], axis=1))
    pair = gather(jnp.concatenate([w_gate, w_up], axis=1))
    down = gather(w_down)
    inputs = block_input.reshape(length, features).astype(jnp.float32)
    back_ffn = cotangent.reshape(length, features)
    (block_output, input_grad, grad_down, grad_gate, grad_up, grad_attn, gain_grads) = block_step(
        inputs,
        document_numbers.reshape(length),
        gain_attn,
        gain_query,
        gain_key,
        gain_ffn,
        attn_pack,
        pair,
        down,
        back_ffn,
    )

    def over(array):
        return lax.psum(array, "rep")

    sum_down = over(grad_down)
    grad_gate, sum_down = lax.optimization_barrier((grad_gate, sum_down))
    sum_gate = over(grad_gate)
    grad_up, sum_gate = lax.optimization_barrier((grad_up, sum_gate))
    sum_up = over(grad_up)
    grad_attn, sum_up = lax.optimization_barrier((grad_attn, sum_up))
    sum_attn = over(grad_attn).astype(jnp.float32)
    gain_grads = jnp.concatenate([part.reshape(parts, -1) for part in gain_grads], axis=1)
    sums = lax.psum(
        lax.psum_scatter(gain_grads, "shard", scatter_dimension=0, tiled=True), "rep"
    ).reshape(-1)
    return (
        block_output[None],
        input_grad[None],
        sums[offsets[0] : offsets[1]],
        sum_attn[:, :1024],
        sum_attn[:, 1024:1536],
        sum_attn[:, 1536:2048],
        sums[offsets[1] : offsets[2]],
        sums[offsets[2] : offsets[3]],
        sum_attn[:, 2048:],
        sums[offsets[3] : offsets[4]],
        sum_gate.astype(jnp.float32),
        sum_up.astype(jnp.float32),
        sum_down.astype(jnp.float32),
    )


def solution(mesh):
    in_specs = (
        P(("rep", "shard"), None, None),
        P(("rep", "shard"), None),
        P("shard"),
        P("shard", None),
        P("shard", None),
        P("shard", None),
        P("shard"),
        P("shard"),
        P("shard", None),
        P("shard"),
        P("shard", None),
        P("shard", None),
        P("shard", None),
        P(("rep", "shard"), None, None),
    )
    out_specs = (
        P(("rep", "shard"), None, None),
        P(("rep", "shard"), None, None),
        P("shard"),
        P("shard", None),
        P("shard", None),
        P("shard", None),
        P("shard"),
        P("shard"),
        P("shard", None),
        P("shard"),
        P("shard", None),
        P("shard", None),
        P("shard", None),
    )
    return jax.shard_map(
        on_device, mesh=mesh, in_specs=in_specs, out_specs=out_specs, check_vma=False
    )
```

```python
import jax
import jax.numpy as jnp
from jax import lax
from jax.experimental import pallas as pl
from jax.experimental.pallas import tpu as pltpu
from jax.sharding import PartitionSpec as P

QUERY_HEADS = 16
KEY_VALUE_HEADS = 8
HEAD_SIZE = 64
EPS = 1e-05
ROPE_BASE = 1000000.0
FAR = 32768.0
TILE = 256
SLAB = 512
VMEM_LIMIT = 60 * 1024 * 1024
NT = ((1,), (1,))
NN = ((1,), (0,))
TN = ((0,), (0,))
BF16 = jnp.bfloat16
F32 = jnp.float32
SMALL = pl.BlockSpec(memory_space=pltpu.SMEM)


def dot(left, right, dims=NN):
    return lax.dot_general(left, right, (dims, ((), ())), preferred_element_type=F32)


def params():
    return pltpu.CompilerParams(vmem_limit_bytes=VMEM_LIMIT)


def cost(giga_flops, mega_bytes, exps=0):
    return pl.CostEstimate(
        flops=int(giga_flops * 10**6),
        bytes_accessed=int(mega_bytes * 10**3),
        transcendentals=exps // 1000,
    )


def fixed(shape, where=None):
    index = (0,) * len(shape) if where is None else where
    return pl.BlockSpec(shape, lambda *_: index, pipeline_mode=pl.Buffered(1))


def by_rows(width, rows=TILE):
    return pl.BlockSpec((rows, width), lambda i: (i, 0))


class Pieces:
    def __init__(self, groups=None, stacked=None):
        self.stacked = stacked
        self.count = len(groups) if stacked is None else stacked.shape[0]
        self.groups = groups if stacked is None else [[stacked]] * self.count
        self.arrays = [array for group in self.groups for array in group]
        self.layout = [len(group) for group in self.groups]

    def specs(self, rows, start):
        once = pl.Buffered(1) if start(0) == start(1) else None
        found = []
        for k, group in enumerate(self.groups):
            for array in group:
                shape = (pl.Element(rows), pl.Element(array.shape[-1]))
                if self.stacked is None:
                    found.append(
                        pl.BlockSpec(shape, lambda i: (start(i), 0), pipeline_mode=once)
                    )
                else:
                    found.append(
                        pl.BlockSpec(
                            (pl.Squeezed(),) + shape,
                            lambda i, k=k: (k, start(i), 0),
                            pipeline_mode=once,
                        )
                    )
        return found


def grouped(refs, layout):
    groups, at = [], 0
    for size in layout:
        groups.append(refs[at : at + size])
        at += size
    return groups


def fill(target, at, group, rows):
    left = 0
    for ref in group:
        right = left + ref.shape[1]
        target[at, left:right] = ref[rows, :]
        left = right


def split3(value):
    high = value.astype(BF16).astype(F32)
    rest = value - high
    middle = rest.astype(BF16).astype(F32)
    return high, middle, rest - middle


def aligned(index, rows):
    return pl.ds(pl.multiple_of(index * rows, rows), rows)


def unit_of(rows):
    inverse = lax.rsqrt(jnp.mean(rows * rows, axis=-1, keepdims=True) + EPS)
    return rows * inverse, inverse


def head_blocks():
    first = lax.broadcasted_iota(jnp.int32, (128, 128), 0) // HEAD_SIZE
    second = lax.broadcasted_iota(jnp.int32, (128, 128), 1) // HEAD_SIZE
    return (first == second).astype(BF16)


def head_mean(rows, blocks):
    return dot(rows.astype(BF16), blocks) * (1.0 / HEAD_SIZE)


def swap_halves(rows, first):
    return jnp.where(first, pltpu.roll(rows, 96, 1), pltpu.roll(rows, 32, 1))


def lanes(rows=TILE):
    return lax.broadcasted_iota(jnp.int32, (rows, 128), 1)


def load_pairs(parts, me_ref, refs, w_all):
    rows = w_all.shape[0] // parts

    @pl.when(pl.program_id(0) == 0)
    def _():
        for k in range(parts):
            at = aligned(me_ref[0] ^ k, rows)
            w_all[at, :1024] = refs[2 * k][...]
            w_all[at, 1024:] = refs[2 * k + 1][...]


def pair_specs(pieces, rows):
    arrays, specs = [], []
    for piece in pieces:
        left, right, at = piece
        arrays += [left, right]
        specs += [fixed((rows, 1024)), fixed((rows, 1024), (at, 0))]
    return arrays, specs


def project_kernel(parts, me_ref, x_ref, cos_ref, sin_ref, qx_ref, kx_ref, *refs):
    gain_refs = refs[2 * parts : 3 * parts]
    n_ref, unit_ref, scale_ref, q_ref, k_ref, v_ref, gain_ref, w_all = refs[3 * parts :]
    load_pairs(parts, me_ref, refs, w_all)

    @pl.when(pl.program_id(0) == 0)
    def _():
        total = gain_refs[0][...].astype(F32)
        for ref in gain_refs[1:]:
            total = total + ref[...].astype(F32)
        gain_ref[...] = total

    unit, _ = unit_of(x_ref[...].astype(F32))
    normed = (unit * gain_ref[0:1, :]).astype(BF16)
    n_ref[...] = normed
    raw = dot(normed, w_all[...])
    blocks = head_blocks()
    lane = lanes()
    first = (lane % HEAD_SIZE) < HEAD_SIZE // 2
    low = lane < HEAD_SIZE
    cosine, sine = cos_ref[...], sin_ref[...]
    for p in range(12):
        at = slice(p * 128, (p + 1) * 128)
        rows_in = raw[:, at]
        inverse = lax.rsqrt(head_mean(rows_in * rows_in, blocks) + EPS)
        unit = rows_in * inverse
        unit_ref[:, at] = unit.astype(BF16)
        scale_ref[:, at] = inverse.astype(BF16)
        scaled = unit * gain_ref[1 + p // 8 : 2 + p // 8, :128]
        turned = scaled * cosine + swap_halves(scaled, first) * sine
        if p < 8:
            turned = turned * HEAD_SIZE**-0.5
            out, more, at = q_ref, qx_ref[...], 2 * p
        else:
            out, more, at = k_ref, kx_ref[...], 2 * (p - 8)
        out[at] = jnp.where(low, turned, more).astype(BF16)
        out[at + 1] = jnp.where(low, pltpu.roll(turned, 64, 1), more).astype(BF16)
    more = ((lane >= 64) & (lane < 67)).astype(F32)
    for p in range(4):
        rows_in = raw[:, 1536 + p * 128 : 1664 + p * 128]
        v_ref[2 * p] = jnp.where(low, rows_in, more).astype(BF16)
        v_ref[2 * p + 1] = jnp.where(low, pltpu.roll(rows_in, 64, 1), more).astype(BF16)


def project(pieces, me, x, tables):
    length, width = x.shape
    parts = len(pieces)
    rows = width // parts
    arrays, specs = pair_specs(pieces, rows)
    gains = [(piece[1], (piece[2] + 1) * rows // 16) for piece in pieces]

    def heads(count):
        return pl.BlockSpec((count, TILE, 128), lambda i: (0, i, 0))

    return pl.pallas_call(
        lambda *refs: project_kernel(parts, *refs),
        grid=(length // TILE,),
        in_specs=[SMALL, by_rows(width)]
        + [by_rows(128)] * 4
        + specs
        + [fixed((16, 1024), (at, 0)) for _, at in gains],
        out_specs=[by_rows(width), by_rows(1536), by_rows(1536), heads(16), heads(8), heads(8)]
        + [fixed((16, 1024))],
        out_shape=[
            jax.ShapeDtypeStruct((length, width), BF16),
            jax.ShapeDtypeStruct((length, 1536), BF16),
            jax.ShapeDtypeStruct((length, 1536), BF16),
            jax.ShapeDtypeStruct((16, length, 128), BF16),
            jax.ShapeDtypeStruct((8, length, 128), BF16),
            jax.ShapeDtypeStruct((8, length, 128), BF16),
            jax.ShapeDtypeStruct((16, 1024), F32),
        ],
        scratch_shapes=[pltpu.VMEM((width, 2048), BF16)],
        compiler_params=params(),
        cost_estimate=cost(8, 25),
        name="project",
    )(me, x, *tables, *arrays, *[array for array, _ in gains])


def causal(query_axis):
    first = lax.broadcasted_iota(jnp.int32, (TILE, TILE), 0)
    second = lax.broadcasted_iota(jnp.int32, (TILE, TILE), 1)
    return (first >= second) if query_axis == 0 else (second >= first)


def attend_kernel(q_ref, k_ref, v_ref, o_ref, qb_ref):
    tiles = q_ref.shape[1] // TILE
    keep = causal(0)
    lane = lax.broadcasted_iota(jnp.int32, (TILE, 128), 1)
    for i in range(tiles):
        rows = slice(i * TILE, (i + 1) * TILE)
        halves = []
        for h in range(2):
            q = q_ref[h, rows, :]
            out = None
            for j in range(i + 1):
                cols = slice(j * TILE, (j + 1) * TILE)
                weights = jnp.exp(dot(q, k_ref[0, cols, :], NT))
                if j == i:
                    weights = jnp.where(keep, weights, 0.0)
                part = dot(weights.astype(BF16), v_ref[0, cols, :])
                out = part if out is None else out + part
            total = out[:, 64:65]
            halves.append(out / total)
            high, middle, low = split3(-jnp.log(total))
            extra = jnp.where(
                lane == 68, high, jnp.where(lane == 69, middle, jnp.where(lane == 70, low, 0.0))
            )
            qb_ref[h, rows, :] = (q.astype(F32) + extra).astype(BF16)
        both = jnp.where(lane < 64, halves[0], pltpu.roll(halves[1], 64, 1))
        o_ref[rows, :] = both.astype(BF16)


def attend(q_aug, k_aug, v_aug, begin, groups):
    _, length, _ = q_aug.shape
    return pl.pallas_call(
        attend_kernel,
        grid=(groups,),
        in_specs=[
            pl.BlockSpec((2, length, 128), lambda g: (g + begin, 0, 0)),
            pl.BlockSpec((1, length, 128), lambda g: (g + begin, 0, 0)),
            pl.BlockSpec((1, length, 128), lambda g: (g + begin, 0, 0)),
        ],
        out_specs=[
            pl.BlockSpec((length, 128), lambda g: (0, g)),
            pl.BlockSpec((2, length, 128), lambda g: (g, 0, 0)),
        ],
        out_shape=[
            jax.ShapeDtypeStruct((length, groups * 128), BF16),
            jax.ShapeDtypeStruct((2 * groups, length, 128), BF16),
        ],
        compiler_params=params(),
        cost_estimate=cost(2.5 * groups, 2 * groups, groups * 2**20),
        name="attend",
    )(q_aug, k_aug, v_aug)


def attend_back_kernel(q_ref, k_ref, v_ref, o_ref, do_ref, dq_ref, dkv_ref, do_aug, k_t, dq_t):
    length = q_ref.shape[1]
    tiles = length // TILE
    keep = causal(1)
    lane = lax.broadcasted_iota(jnp.int32, (length, 128), 1)
    back = do_ref[...].astype(F32)
    product = back * o_ref[...].astype(F32)
    for h in range(2):
        own = (lane < 64) if h == 0 else (lane >= 64)
        centre = jnp.sum(jnp.where(own, product, 0.0), axis=1, keepdims=True)
        moved = back if h == 0 else pltpu.roll(back, 64, 1)
        high, middle, low = split3(-centre)
        extra = jnp.where(
            lane == 64, high, jnp.where(lane == 65, middle, jnp.where(lane == 66, low, 0.0))
        )
        do_aug[h] = jnp.where(lane < 64, moved, extra).astype(BF16)
    k_t[...] = k_ref[0].astype(F32).T[:64, :].astype(BF16)
    low_half = lax.broadcasted_iota(jnp.int32, (TILE, 128), 1) < 64
    for j in range(tiles):
        cols = slice(j * TILE, (j + 1) * TILE)
        k = k_ref[0, cols, :]
        v = v_ref[0, cols, :]
        dk = None
        dv = None
        for i in range(j, tiles):
            rows = slice(i * TILE, (i + 1) * TILE)
            for h in range(2):
                q = q_ref[h, rows, :]
                do = do_aug[h, rows, :]
                probs = jnp.exp(dot(k, q, NT))
                if i == j:
                    probs = jnp.where(keep, probs, 0.0)
                scores = (probs * dot(v, do, NT)).astype(BF16)
                to_v = dot(probs.astype(BF16), do)
                to_k = dot(scores, q)
                dv = to_v if dv is None else dv + to_v
                dk = to_k if dk is None else dk + to_k
                to_q = dot(k_t[:, cols], scores)
                if j == 0:
                    dq_t[h * 64 : (h + 1) * 64, rows] = to_q
                else:
                    dq_t[h * 64 : (h + 1) * 64, rows] += to_q
        dkv_ref[cols, :] = jnp.where(low_half, dk, pltpu.roll(dv, 64, 1))
    dq_ref[...] = dq_t[...].T


def attend_back(q_back, k_aug, v_aug, attended, back_attended, begin, groups):
    _, length, _ = q_back.shape
    by_group = pl.BlockSpec((length, 128), lambda g: (0, g + begin))
    out_group = pl.BlockSpec((length, 128), lambda g: (0, g))
    return pl.pallas_call(
        attend_back_kernel,
        grid=(groups,),
        in_specs=[
            pl.BlockSpec((2, length, 128), lambda g: (g, 0, 0)),
            pl.BlockSpec((1, length, 128), lambda g: (g + begin, 0, 0)),
            pl.BlockSpec((1, length, 128), lambda g: (g + begin, 0, 0)),
            out_group,
            by_group,
        ],
        out_specs=[out_group, out_group],
        out_shape=[jax.ShapeDtypeStruct((length, groups * 128), F32)] * 2,
        scratch_shapes=[
            pltpu.VMEM((2, length, 128), BF16),
            pltpu.VMEM((64, length), BF16),
            pltpu.VMEM((128, length), F32),
        ],
        compiler_params=params(),
        cost_estimate=cost(5 * groups, 3 * groups, groups * 2**20),
        name="attend_back",
    )(q_back, k_aug, v_aug, attended, back_attended)


def output_kernel(layout, me_ref, o0_ref, o1_ref, x_ref, gain_ref, *refs):
    sum_ref, n_ref, nt_ref, w_all = refs[-4:]
    rows = w_all.shape[0] // len(layout)

    @pl.when(pl.program_id(0) == 0)
    def _():
        for k, group in enumerate(grouped(refs, layout)):
            fill(w_all, aligned(me_ref[0] ^ k, rows), group, slice(None))

    total = x_ref[...].astype(F32) + dot(o0_ref[...], w_all[:512, :])
    total = total + dot(o1_ref[...], w_all[512:, :])
    sum_ref[...] = total
    unit, _ = unit_of(total)
    normed = unit * gain_ref[3:4, :]
    n_ref[...] = normed.astype(BF16)
    nt_ref[...] = normed.T.astype(BF16)


def output_rows(pieces, me, attended, x, gain):
    length, width = x.shape
    parts = pieces.count
    rows = width // parts
    return pl.pallas_call(
        lambda *refs: output_kernel(pieces.layout, *refs),
        grid=(length // TILE,),
        in_specs=[SMALL, by_rows(512), by_rows(512), by_rows(width), fixed((16, 1024))]
        + pieces.specs(rows, lambda i: 0),
        out_specs=[by_rows(width), by_rows(width), pl.BlockSpec((width, TILE), lambda i: (0, i))],
        out_shape=[
            jax.ShapeDtypeStruct((length, width), F32),
            jax.ShapeDtypeStruct((length, width), BF16),
            jax.ShapeDtypeStruct((width, length), BF16),
        ],
        scratch_shapes=[pltpu.VMEM((1024, width), BF16)],
        compiler_params=params(),
        cost_estimate=cost(5, 15),
        name="output_rows",
    )(me, *attended, x, gain, *pieces.arrays)


def scatter_rows(me, parts, value, rows, own_ref, sib_ref, at):
    half = me >> 1
    core = me & 1
    for q in range(parts // 2):
        for s, ref in enumerate((own_ref, sib_ref)):
            source = 2 * q + (core ^ s)
            ref[q ^ half, at : at + rows, :] = value[aligned(source, rows), :]


def feed_kernel(layout, paired, me_ref, n_ref, nt_ref, c_ref, *refs):
    parts = len(layout)
    f_ref, b_ref, *grad_refs = refs[sum(layout) : -7]
    w_all, d_all, back, w_grad, d_grad, f_sum, b_sum = refs[-7:]
    me = me_ref[0]
    rows = w_all.shape[0] // parts
    seg = SLAB // parts
    for k, group in enumerate(grouped(refs, layout)):
        fill(w_all, aligned(me ^ k, rows), group, slice(0, rows))
        fill(d_all, aligned(me ^ k, seg), group, slice(rows, rows + seg))
    both = dot(n_ref[...], w_all[...])
    gate = both[:, :SLAB]
    up = both[:, SLAB:]
    sig = 1.0 / (1.0 + jnp.exp(-gate))
    swish = gate * sig
    hidden = (swish * up).astype(BF16)
    back_hidden = dot(c_ref[...], d_all[...], NT)
    back[:, SLAB:] = (back_hidden * swish).astype(BF16)
    back[:, :SLAB] = (back_hidden * up * sig * (1.0 + gate * (1.0 - sig))).astype(BF16)
    out = dot(hidden, d_all[...])
    w_grad[...] = dot(nt_ref[...], back[...]).astype(BF16)
    d_grad[...] = dot(hidden, c_ref[...], TN).astype(BF16)
    back_in = dot(back[...], w_all[...], NT)

    step = pl.program_id(0)

    @pl.when(step == 0)
    def _():
        f_sum[...] = out
        b_sum[...] = back_in

    @pl.when(step > 0)
    def _():
        f_sum[...] += out
        b_sum[...] += back_in

    @pl.when(step == pl.num_programs(0) - 1)
    def _():
        f_ref[...] = f_sum[...].astype(BF16)
        b_ref[...] = b_sum[...].astype(BF16)

    if paired:
        own_ref, sib_ref = grad_refs
        scatter_rows(me, parts, w_grad, rows, own_ref, sib_ref, 0)
        scatter_rows(me, parts, d_grad, seg, own_ref, sib_ref, rows)
    else:
        for d in range(parts):
            grad_refs[0][d, :rows, :] = w_grad[d * rows : (d + 1) * rows, :]
            grad_refs[0][d, rows:, :] = d_grad[d * seg : (d + 1) * seg, :]


def feed(pieces, me, begin, slabs, normed, normed_t, cotangent, paired):
    length, width = normed.shape
    parts = pieces.count
    rows = width // parts + SLAB // parts
    depth = parts // 2 if paired else parts
    count = 2 if paired else 1
    grads = pl.BlockSpec((depth, rows, 2 * SLAB), lambda i: (0, i, 0))
    return pl.pallas_call(
        lambda *refs: feed_kernel(pieces.layout, paired, *refs),
        grid=(slabs,),
        in_specs=[SMALL, fixed((length, width)), fixed((width, length)), fixed((length, width))]
        + pieces.specs(rows, lambda i: (begin // 16 + i * (rows // 16)) * 16),
        out_specs=[fixed((length, width)), fixed((length, width))] + [grads] * count,
        out_shape=[
            jax.ShapeDtypeStruct((length, width), BF16),
            jax.ShapeDtypeStruct((length, width), BF16),
        ]
        + [jax.ShapeDtypeStruct((depth, slabs * rows, 2 * SLAB), BF16)] * count,
        scratch_shapes=[
            pltpu.VMEM((width, 2 * SLAB), BF16),
            pltpu.VMEM((SLAB, width), BF16),
            pltpu.VMEM((length, 2 * SLAB), BF16),
            pltpu.VMEM((width, 2 * SLAB), BF16),
            pltpu.VMEM((SLAB, width), BF16),
            pltpu.VMEM((length, width), F32),
            pltpu.VMEM((length, width), F32),
        ],
        compiler_params=params(),
        cost_estimate=cost(12.5 * slabs, 20 + 6 * slabs),
        name="feed",
    )(me, normed, normed_t, cotangent, *pieces.arrays)


def middle_kernel(layout, sums, me_ref, s_ref, c_ref, o0_ref, o1_ref, gain_ref, *refs):
    b_refs = refs[:sums]
    f_ref, a_ref, g_ref, w_all, total = refs[-5:]
    rows = w_all.shape[0] // len(layout)
    step = pl.program_id(0)

    @pl.when(step == 0)
    def _():
        for k, group in enumerate(grouped(refs[sums:], layout)):
            fill(w_all, aligned(me_ref[0] ^ k, rows), group, slice(None))

    back = b_refs[0][...].astype(F32)
    for ref in b_refs[1:]:
        back = back + ref[...].astype(F32)
    unit, inverse = unit_of(s_ref[...])
    scaled = back * gain_ref[3:4, :]
    first = c_ref[...].astype(F32) + inverse * (
        scaled - unit * jnp.mean(scaled * unit, axis=-1, keepdims=True)
    )
    f_ref[...] = first
    short = first.astype(BF16)
    a_ref[...] = dot(short, w_all[...], NT).astype(BF16)
    grads = [dot(ref[...], short, TN) for ref in (o0_ref, o1_ref)]

    @pl.when(step == 0)
    def _():
        total[:512, :] = grads[0]
        total[512:, :] = grads[1]

    @pl.when(step > 0)
    def _():
        total[:512, :] += grads[0]
        total[512:, :] += grads[1]

    @pl.when(step == pl.num_programs(0) - 1)
    def _():
        g_ref[...] = total[...].astype(BF16)


def middle(pieces, me, first_sum, cotangent, attended, gain, backs):
    length, width = first_sum.shape
    parts = pieces.count
    rows = width // parts
    return pl.pallas_call(
        lambda *refs: middle_kernel(pieces.layout, len(backs), *refs),
        grid=(length // TILE,),
        in_specs=[SMALL, by_rows(width), by_rows(width), by_rows(512), by_rows(512), fixed((16, 1024))]
        + [by_rows(width)] * len(backs)
        + pieces.specs(rows, lambda i: 0),
        out_specs=[by_rows(width), by_rows(1024), fixed((1024, width))],
        out_shape=[
            jax.ShapeDtypeStruct((length, width), F32),
            jax.ShapeDtypeStruct((length, 1024), BF16),
            jax.ShapeDtypeStruct((1024, width), BF16),
        ],
        scratch_shapes=[pltpu.VMEM((1024, width), BF16), pltpu.VMEM((1024, width), F32)],
        compiler_params=params(),
        cost_estimate=cost(9, 32),
        name="middle",
    )(me, first_sum, cotangent, *attended, gain, *backs, *pieces.arrays)


def raw_back_kernel(
    parts, me_ref, dq0_ref, dq1_ref, dkv0_ref, dkv1_ref, unit_ref, scale_ref, n_ref, cos_ref, sin_ref, gain_ref, wo_ref,
    b_ref, own_ref, sib_ref, total, gains,
):
    step = pl.program_id(0)
    rows = total.shape[0] // parts
    blocks = head_blocks()
    lane = lanes()
    first = (lane % HEAD_SIZE) < HEAD_SIZE // 2
    low = lane < HEAD_SIZE
    cosine, sine = cos_ref[...], sin_ref[...]
    sums = [None, None]
    for p in range(12):
        at = slice(p * 128, (p + 1) * 128)
        if p < 8:
            dq_ref = dq0_ref if p < 4 else dq1_ref
            grads = dq_ref[:, (p % 4) * 128 : (p % 4 + 1) * 128] * HEAD_SIZE**-0.5
        else:
            dkv_ref = dkv0_ref if p < 10 else dkv1_ref
            left = dkv_ref[:, (p % 2) * 256 : (p % 2) * 256 + 128]
            right = dkv_ref[:, (p % 2) * 256 + 128 : (p % 2) * 256 + 256]
            grads = jnp.where(low, left, pltpu.roll(right, 64, 1))
            values = jnp.where(low, pltpu.roll(left, 64, 1), right)
            b_ref[:, 512 + p * 128 : 640 + p * 128] = values.astype(BF16)
        turned = grads * cosine + swap_halves(grads * sine, first)
        unit = unit_ref[:, at].astype(F32)
        inverse = scale_ref[:, at].astype(F32)
        kind = 0 if p < 8 else 1
        part = jnp.sum(turned * unit, axis=0, keepdims=True)
        sums[kind] = part if sums[kind] is None else sums[kind] + part
        scaled = turned * gain_ref[1 + kind : 2 + kind, :128]
        b_ref[:, at] = (inverse * (scaled - unit * head_mean(scaled * unit, blocks))).astype(BF16)
    grad = dot(n_ref[...], b_ref[...], TN)

    @pl.when(step == 0)
    def _():
        total[...] = grad
        gains[...] = jnp.zeros_like(gains)

    @pl.when(step > 0)
    def _():
        total[...] += grad

    gains[0:1, :] += sums[0]
    gains[1:2, :] += sums[1]

    @pl.when(step == pl.num_programs(0) - 1)
    def _():
        me = me_ref[0]
        half = me >> 1
        core = me & 1
        more = gains[...].astype(BF16)
        for q in range(parts // 2):
            for s, ref in enumerate((own_ref, sib_ref)):
                source = aligned(2 * q + (core ^ s), rows)
                block = total[source, :].astype(BF16)
                ref[q ^ half, :rows, :] = block[:, :1024]
                ref[q ^ half, rows : 2 * rows, :] = block[:, 1024:]
                ref[q ^ half, 2 * rows : 3 * rows, :] = wo_ref[source, :]
                ref[q ^ half, 3 * rows :, :] = jnp.zeros((16, 1024), BF16)
                ref[q ^ half, 3 * rows :, :128] = more


def raw_back(parts, me, halves, units, normed, cosine, sine, gains, grad_out):
    length, width = normed.shape
    rows = 3 * (width // parts) + 16
    grads = fixed((parts // 2, rows, 1024))
    return pl.pallas_call(
        lambda *refs: raw_back_kernel(parts, *refs),
        grid=(length // TILE,),
        in_specs=[SMALL] + [by_rows(512)] * 4 + [by_rows(1536)] * 2 + [by_rows(width)]
        + [by_rows(128)] * 2
        + [fixed((16, 1024)), fixed((1024, width))],
        out_specs=[by_rows(2048), grads, grads],
        out_shape=[jax.ShapeDtypeStruct((length, 2048), BF16)]
        + [jax.ShapeDtypeStruct((parts // 2, rows, 1024), BF16)] * 2,
        scratch_shapes=[pltpu.VMEM((width, 2048), F32), pltpu.VMEM((16, 128), F32)],
        compiler_params=params(),
        cost_estimate=cost(10, 30),
        name="raw_back",
    )(me, *halves, *units, normed, cosine, sine, gains, grad_out)


def input_kernel(parts, me_ref, b_ref, x_ref, f_ref, gain_ref, *refs):
    out_ref, w_all = refs[2 * parts :]
    load_pairs(parts, me_ref, refs, w_all)
    unit, inverse = unit_of(x_ref[...].astype(F32))
    scaled = dot(b_ref[...], w_all[...], NT) * gain_ref[0:1, :]
    out_ref[...] = f_ref[...] + inverse * (
        scaled - unit * jnp.mean(scaled * unit, axis=-1, keepdims=True)
    )


def input_back(pieces, me, back_raw, x, back_first, gain):
    length, width = x.shape
    parts = len(pieces)
    arrays, specs = pair_specs(pieces, width // parts)
    return pl.pallas_call(
        lambda *refs: input_kernel(parts, *refs),
        grid=(length // TILE,),
        in_specs=[SMALL, by_rows(2048), by_rows(width), by_rows(width), fixed((16, 1024))] + specs,
        out_specs=by_rows(width),
        out_shape=jax.ShapeDtypeStruct((length, width), F32),
        scratch_shapes=[pltpu.VMEM((width, 2048), BF16)],
        compiler_params=params(),
        cost_estimate=cost(6, 18),
        name="input_back",
    )(me, back_raw, x, back_first, gain, *arrays)


def tables_of(numbers):
    length = numbers.shape[0]
    indices = jnp.arange(length, dtype=jnp.int32)
    starts = jnp.concatenate([jnp.ones((1,), dtype=bool), numbers[1:] != numbers[:-1]])
    begins = lax.cummax(jnp.where(starts, indices, jnp.zeros_like(numbers)), axis=0)
    offsets = (indices - begins).astype(F32).reshape(length, 1)
    frequency = ROPE_BASE ** (-jnp.arange(0, HEAD_SIZE, 2).astype(F32) / HEAD_SIZE)
    angles = offsets * frequency
    cosine = jnp.cos(angles)
    sine = jnp.sin(angles)
    same = (numbers[:, None] == jnp.arange(4)[None]).astype(F32)
    empty = jnp.zeros((length, 64), F32)
    return (
        jnp.concatenate([cosine] * 4, axis=1),
        jnp.concatenate([-sine, sine, -sine, sine], axis=1),
        jnp.concatenate([empty, -FAR * same, empty[:, :60]], axis=1),
        jnp.concatenate([empty, 1 - same, jnp.ones((length, 3)), empty[:, :57]], axis=1),
    )


def pack_kernel(chunks, o_ref, gate_ref, up_ref, down_ref, *out_refs):
    low = lanes(128) < 64
    out_refs[0][:128, :] = o_ref[...]
    places = [(c, i) for c, n in enumerate(chunks) for i in range(n)]
    for t, (c, i) in enumerate(places):
        row = i * 192 + (0 if c else 128)
        for side, ref in enumerate((gate_ref, up_ref)):
            for e in range(4):
                left, right = (18 * e + t) // 2, (18 * e + 9 + t) // 2
                a = ref[:, left * 128 : left * 128 + 128].astype(F32)
                b = ref[:, right * 128 : right * 128 + 128].astype(F32)
                both = pltpu.roll(jnp.where(low, b, a), 64, 1) if t % 2 else jnp.where(low, a, b)
                at = side * SLAB + e * 128
                out_refs[c][row : row + 128, at : at + 128] = both.astype(BF16)
        out_refs[c][row + 128 : row + 192, :] = down_ref[t * 64 : t * 64 + 64, :]


def pack_rows(chunks, w_output, w_gate, w_up, w_down):
    return pl.pallas_call(
        lambda *refs: pack_kernel(chunks, *refs),
        out_shape=[
            jax.ShapeDtypeStruct((n * 192 + (0 if c else 128), 1024), BF16)
            for c, n in enumerate(chunks)
        ],
        compiler_params=params(),
        cost_estimate=cost(0, 7),
        name="pack_rows",
    )(w_output, w_gate, w_up, w_down)


def unpack_kernel(*refs):
    *in_refs, gate_ref, up_ref, down_ref = refs
    low = lanes(128) < 64

    def rows_of(at, size, columns):
        for ref in in_refs:
            if at < ref.shape[0]:
                return ref[at : at + size, columns].astype(F32)
            at -= ref.shape[0]

    def segment(side, s, half):
        d = s // 9
        at = side * SLAB + (d // 2) * 128
        tile = rows_of((s % 9) * 192, 128, slice(at, at + 128))
        return tile if d % 2 == half else pltpu.roll(tile, 64, 1)

    for side, out in enumerate((gate_ref, up_ref)):
        for m in range(36):
            out[:, m * 128 : m * 128 + 128] = jnp.where(
                low, segment(side, 2 * m, 0), segment(side, 2 * m + 1, 1)
            )
    for t in range(9):
        down_ref[t * 64 : t * 64 + 64, :] = rows_of(t * 192 + 128, 64, slice(None))


def unpack_rows(*totals):
    return pl.pallas_call(
        unpack_kernel,
        out_shape=[
            jax.ShapeDtypeStruct((128, 4608), F32),
            jax.ShapeDtypeStruct((128, 4608), F32),
            jax.ShapeDtypeStruct((576, 1024), F32),
        ],
        compiler_params=params(),
        cost_estimate=cost(0, 14),
        name="unpack_rows",
    )(*totals)


def tie(*values):
    return lax.optimization_barrier(values)


def after(value, *tokens):
    return tie(value, *tokens)[0]


def hop(array, bit):
    return lax.ppermute(array, "shard", [(i, i ^ bit) for i in range(8)])


def gather_all(pack):
    return lax.all_gather(pack, "shard", axis=0, tiled=False)


def scatter_all(every):
    return lax.psum_scatter(every, "shard", scatter_dimension=0, tiled=True)[0]


def weave(near, far):
    groups = []
    for one, two in zip(near, far):
        groups += [list(one), list(two)]
    return Pieces(groups)


def add_parts(k, own, other, *more):
    total = own[k].astype(F32) + other[k].astype(F32)
    for term in more:
        total = total + term.astype(F32)
    return total


def rep_hop(array, pairs):
    return lax.ppermute(array.astype(BF16), "rep", pairs)


INWARD = [(0, 1), (3, 2)]
ACROSS = [(1, 2), (2, 1)]
OUTWARD = [(1, 0), (2, 3)]


def at_end(inner, outer):
    place = lax.axis_index("rep")
    return jnp.where((place == 0) | (place == 3), outer.astype(F32), inner)


def on_device(sizes, *arrays):
    (
        block_input, document_numbers, attn_gain, w_query, key_weight, value_weight, query_gain,
        key_gain, w_output, ffn_gain, w_gate, w_up, w_down, cotangent,
    ) = arrays
    reps, parts = sizes
    _, length, width = block_input.shape
    ff = w_gate.shape[1]
    paired = parts == 8 and reps == 4
    me = lax.axis_index("shard").astype(jnp.int32)
    place = me.reshape(1) if paired else jnp.zeros((1,), jnp.int32)
    x = block_input.reshape(length, width)
    back_out = cotangent.reshape(length, width)
    numbers = document_numbers.reshape(length)
    rows = width // parts
    seg = SLAB // parts
    slabs = ff // SLAB
    few = query_gain.shape[0]

    lane = jnp.arange(width)

    def spot(gain, times, size):
        share = gain.shape[0]
        wide = jnp.tile(gain, width // share)
        return jnp.where((lane < size * times) & ((lane % size) // share == me), wide, 0)

    empty = jnp.zeros((width,), BF16)
    gain_rows = [
        spot(attn_gain, 1, width),
        spot(query_gain, 2, HEAD_SIZE),
        spot(key_gain, 2, HEAD_SIZE),
        spot(ffn_gain, 1, width),
    ]
    first_pack = jnp.concatenate(
        [
            w_query,
            jnp.concatenate([key_weight, value_weight], axis=1),
            jnp.stack(gain_rows + [empty] * 12),
        ]
    )
    tables = tables_of(numbers)
    run = block_paired if paired else block_simple
    args = (me, place, x, back_out, tables, first_pack, w_output, w_gate, w_up, w_down)
    block_output, input_grad, attn_grad, feed_grads = run(*args)
    grad_gate, grad_up, grad_down = feed_grads
    grad_query = attn_grad[:rows]
    grad_key = attn_grad[rows : 2 * rows, :512]
    grad_value = attn_grad[rows : 2 * rows, 512:]

    def diagonal(*pairs):
        total = 0.0
        for weight, grad in pairs:
            total = total + jnp.sum(weight.astype(F32) * grad, axis=1)
        return total

    grad_gain_attn = diagonal(
        (w_query, grad_query), (key_weight, grad_key), (value_weight, grad_value)
    ) / attn_gain.astype(F32)
    grad_gain_ffn = diagonal((w_gate, grad_gate), (w_up, grad_up)) / ffn_gain.astype(F32)

    def small(row):
        both = attn_grad[3 * rows + row, :64] + attn_grad[3 * rows + row, 64:128]
        return lax.dynamic_slice(both, (me * few,), (few,))

    return (
        block_output[None],
        input_grad[None],
        grad_gain_attn,
        grad_query,
        grad_key,
        grad_value,
        small(0),
        small(1),
        attn_grad[2 * rows : 3 * rows],
        grad_gain_ffn,
        grad_gate,
        grad_up,
        grad_down,
    )


def block_simple(me, place, x, back_out, tables, first_pack, w_output, w_gate, w_up, w_down):
    rows, ff = w_gate.shape
    parts = x.shape[1] // rows
    seg = SLAB // parts
    slabs = ff // SLAB
    tall = rows + seg

    def columns(weight):
        cut = weight.reshape(rows, parts, slabs, seg).transpose(2, 0, 1, 3)
        return cut.reshape(slabs, rows, SLAB)

    pack = jnp.concatenate(
        [
            jnp.concatenate([columns(w_gate), columns(w_up)], axis=2),
            w_down.reshape(slabs, seg, x.shape[1]),
        ],
        axis=1,
    ).reshape(slabs * tall, 2 * SLAB)
    every = gather_all(first_pack)
    pairs = [(every[k], every[k], 1) for k in range(parts)]
    pieces = Pieces(stacked=gather_all(jnp.concatenate([w_output, pack])))
    normed_one, *units, q_aug, k_aug, v_aug, gains = project(pairs, place, x, tables)
    attended_0, q_back_0 = attend(q_aug, k_aug, v_aug, 0, 4)
    attended_1, q_back_1 = attend(q_aug, k_aug, v_aug, 4, 4)
    attended = (attended_0, attended_1)
    first_sum, normed_two, normed_two_t = output_rows(pieces, place, attended, x, gains)
    out, back, grads = feed(
        pieces, place, rows, slabs, normed_two, normed_two_t, back_out, False
    )
    total = lax.psum(scatter_all(grads), "rep").astype(F32).reshape(slabs, tall, 2 * SLAB)
    back_first, back_attended, grad_out = middle(
        pieces, place, first_sum, back_out, attended, gains, [back]
    )
    halves_0 = attend_back(q_back_0, k_aug, v_aug, attended_0, back_attended, 0, 4)
    halves_1 = attend_back(q_back_1, k_aug, v_aug, attended_1, back_attended, 4, 4)
    back_raw, own, sib = raw_back(
        parts, place, (halves_0[0], halves_1[0], halves_0[1], halves_1[1]), units, normed_one,
        tables[0], tables[1], gains, grad_out,
    )
    every = jnp.stack([own, sib], axis=1).reshape((parts,) + own.shape[1:])
    attn_grad = lax.psum(scatter_all(every), "rep").astype(F32)
    input_grad = input_back(pairs, place, back_raw, x, back_first, gains)

    def uncut(block):
        return block.reshape(slabs, rows, parts, seg).transpose(1, 2, 0, 3).reshape(rows, ff)

    feed_grads = (
        uncut(total[:, :rows, :SLAB]),
        uncut(total[:, :rows, SLAB:]),
        total[:, rows:, :].reshape(slabs * seg, x.shape[1]),
    )
    return (first_sum + out).astype(BF16), input_grad, attn_grad, feed_grads


def fence(outputs, *hops):
    found = tie(*outputs, *hops)
    return found[: len(outputs)], list(found[len(outputs) :])


def block_paired(me, place, x, back_out, tables, first_pack, w_output, w_gate, w_up, w_down):
    rows = w_gate.shape[0]
    chunks = (4, 3, 2)

    first = hop(first_pack, 2)
    second = hop(first_pack, 4)
    twin = hop(first_pack, 1)
    made, (first, second, twin) = fence(
        [*pack_rows(chunks, w_output, w_gate, w_up, w_down), *tables], first, second, twin
    )
    packs, tables = list(made[:3]), made[3:]
    corner_a = hop(second[:rows], 2)
    corner_b = hop(first[rows:], 4)
    far = [twin] + [hop(piece, 1) for piece in (first, second, corner_a, corner_b)]
    near = [first_pack, first, second, corner_a, corner_b]
    pairs = []
    for k in range(3):
        pairs += [(near[k], near[k], 1), (far[k], far[k], 1)]
    pairs += [(near[3], near[4], 0), (far[3], far[4], 0)]

    pack = after(packs[0], corner_a, corner_b)
    first, second, twin = hop(pack, 2), hop(pack, 4), hop(pack, 1)
    normed_one, *units, q_aug, k_aug, v_aug, gains = project(pairs, place, x, tables)
    (attended_0, q_back_0, k_aug), (first, second, twin) = fence(
        [*attend(q_aug, k_aug, v_aug, 0, 4), k_aug], first, second, twin
    )
    corner_a, corner_b = hop(second[:, :512], 2), hop(first[:, 512:], 4)
    far = [hop(first, 1), hop(second, 1)]
    packs[1] = after(packs[1], first, second)
    waiting = [hop(packs[1], bit) for bit in (1, 2, 4, 6)]
    (attended_1, q_back_1), (corner_a, corner_b, *far) = fence(
        attend(q_aug, k_aug, v_aug, 4, 4), corner_a, corner_b, *far
    )
    attended = (attended_0, attended_1)
    early = weave(
        [[pack], [first], [second], [corner_a, corner_b]],
        [[twin], [far[0]], [far[1]], [hop(corner_a, 1), hop(corner_b, 1)]],
    )
    first_sum, normed_two, normed_two_t = output_rows(early, place, attended, x, gains)

    def finish(pack, twin, first, second, corner):
        near = (first, second, corner)
        far = [hop(piece, 1) for piece in near]
        return weave([[pack]] + [[a] for a in near], [[twin]] + [[a] for a in far])

    def feed_step(pieces, begin, n, paired):
        return feed(pieces, place, begin, n, normed_two, normed_two_t, back_out, paired)

    (out_0, back_0, own_0, sib_0, normed_two), waiting = fence(
        [*feed_step(early, rows, chunks[0], True), normed_two], *waiting
    )
    later = finish(packs[1], *waiting)
    waiting = [hop(packs[2], bit) for bit in (1, 2, 4, 6)]
    other_0 = hop(after(sib_0, *later.arrays), 1)
    (out_1, back_1, stack_1, normed_two), (other_0, *waiting) = fence(
        [*feed_step(later, 0, chunks[1], False), normed_two], other_0, *waiting
    )
    grads_1 = scatter_all(stack_1)
    last = finish(packs[2], *waiting)
    moved_0 = hop(add_parts(3, own_0, other_0).astype(BF16), 2)
    (out_2, back_2, own_2, sib_2), (moved_0,) = fence(
        feed_step(last, 0, chunks[2], True), moved_0
    )
    other_2 = hop(sib_2, 1)
    first_0 = hop(add_parts(1, own_0, other_0).astype(BF16), 2)
    second_0 = hop(add_parts(2, own_0, other_0, moved_0).astype(BF16), 4)
    middles = middle(
        early, place, first_sum, back_out, attended, gains, [back_0, back_1, back_2]
    )
    (back_first, back_attended, grad_out), (other_2,) = fence(middles, other_2)
    moved_2 = hop(add_parts(3, own_2, other_2).astype(BF16), 4)
    halves = attend_back(q_back_0, k_aug, v_aug, attended_0, back_attended, 0, 4)
    (dq_0, dkv_0, back_attended), (first_0, second_0, grads_1) = fence(
        [*halves, back_attended], first_0, second_0, grads_1
    )
    total_1 = lax.psum(grads_1, "rep")
    grads_0 = add_parts(0, own_0, other_0, first_0, second_0)
    grads_0, back_attended = tie(grads_0, back_attended)
    inward_0 = rep_hop(grads_0, INWARD)
    halves = attend_back(q_back_1, k_aug, v_aug, attended_1, back_attended, 4, 4)
    (dq_1, dkv_1), (moved_2,) = fence(halves, moved_2)
    first_2 = hop(add_parts(1, own_2, other_2, moved_2).astype(BF16), 2)
    second_2 = hop(add_parts(2, own_2, other_2).astype(BF16), 4)
    result = raw_back(
        8, place, (dq_0, dq_1, dkv_0, dkv_1), units, normed_one, tables[0], tables[1], gains,
        grad_out,
    )
    (back_raw, own, sib), (first_2, second_2, inward_0, total_1) = fence(
        result, first_2, second_2, inward_0, total_1
    )
    other = hop(sib, 1)
    half_0 = grads_0 + inward_0.astype(F32)
    grads_2 = add_parts(0, own_2, other_2, first_2, second_2)
    back_raw, other, half_0, grads_2 = tie(back_raw, other, half_0, grads_2)
    terms = [add_parts(k, own, other).astype(BF16) for k in (1, 2, 3)]
    back_raw, *terms = tie(back_raw, *terms)
    steps = [hop(term, 2 * k) for k, term in zip((1, 2, 3), terms)]
    across_0 = rep_hop(half_0, ACROSS)
    inward_2 = rep_hop(grads_2, INWARD)
    input_grad = input_back(pairs, place, back_raw, x, back_first, gains)
    (input_grad,), (inward_2, across_0, *steps) = fence([input_grad], inward_2, across_0, *steps)
    attn_grad = add_parts(0, own, other, *steps)
    attn_grad, inward_2, across_0, first_sum = tie(attn_grad, inward_2, across_0, first_sum)
    inward = rep_hop(attn_grad, INWARD)
    total_0 = half_0 + across_0.astype(F32)
    outward_0 = rep_hop(total_0, OUTWARD)
    half_2 = grads_2 + inward_2.astype(F32)
    across_2 = rep_hop(half_2, ACROSS)
    outs = out_0.astype(F32) + out_1.astype(F32) + out_2.astype(F32)
    block_output = (first_sum + outs).astype(BF16)
    (block_output,), (inward, across_2) = fence([block_output], inward, across_2)
    half = attn_grad + inward.astype(F32)
    half, across_2 = tie(half, across_2)
    across = rep_hop(half, ACROSS)
    total_2 = half_2 + across_2.astype(F32)
    outward_2 = rep_hop(total_2, OUTWARD)
    total_2, across = tie(total_2, across)
    total = half + across.astype(F32)
    total, outward_2, outward_0 = tie(total, outward_2, outward_0)
    outward = rep_hop(total, OUTWARD)
    feed_grads = unpack_rows(at_end(total_0, outward_0), total_1, at_end(total_2, outward_2))
    (*feed_grads,), (outward,) = fence(feed_grads, outward)
    return block_output, input_grad, at_end(total, outward), feed_grads


def solution(mesh):
    sizes = (mesh.shape["rep"], mesh.shape["shard"])
    whole = P(("rep", "shard"), None, None)
    matrix = P("shard", None)
    vector = P("shard")
    in_specs = (
        whole, P(("rep", "shard"), None), vector, matrix, matrix, matrix, vector, vector, matrix,
        vector, matrix, matrix, matrix, whole,
    )
    out_specs = (
        whole, whole, vector, matrix, matrix, matrix, vector, vector, matrix, vector, matrix,
        matrix, matrix,
    )
    return jax.shard_map(
        lambda *arrays: on_device(sizes, *arrays),
        mesh=mesh,
        in_specs=in_specs,
        out_specs=out_specs,
        check_vma=False,
    )
```

```python
import jax
import jax.numpy as jnp
from jax import lax
from jax.experimental import pallas as pl
from jax.experimental.pallas import tpu as pltpu
from jax.sharding import PartitionSpec as P

QUERY_HEADS = 16
KEY_VALUE_HEADS = 8
HEAD_SIZE = 64
EPS = 1e-05
ROPE_BASE = 1000000.0
FAR = 32768.0
TILE = 256
SLAB = 512
VMEM_LIMIT = 60 * 1024 * 1024
NT = ((1,), (1,))
NN = ((1,), (0,))
TN = ((0,), (0,))
BF16 = jnp.bfloat16
F32 = jnp.float32
SMALL = pl.BlockSpec(memory_space=pltpu.SMEM)


def dot(left, right, dims=NN):
    return lax.dot_general(left, right, (dims, ((), ())), preferred_element_type=F32)


def params():
    return pltpu.CompilerParams(vmem_limit_bytes=VMEM_LIMIT)


def cost(giga_flops, mega_bytes, exps=0):
    return pl.CostEstimate(
        flops=int(giga_flops * 10**6),
        bytes_accessed=int(mega_bytes * 10**3),
        transcendentals=exps // 1000,
    )


def fixed(shape, where=None):
    index = (0,) * len(shape) if where is None else where
    return pl.BlockSpec(shape, lambda *_: index, pipeline_mode=pl.Buffered(1))


def by_rows(width, rows=TILE):
    return pl.BlockSpec((rows, width), lambda i: (i, 0))


class Pieces:
    def __init__(self, groups=None, stacked=None):
        self.stacked = stacked
        self.count = len(groups) if stacked is None else stacked.shape[0]
        self.groups = groups if stacked is None else [[stacked]] * self.count
        self.arrays = [array for group in self.groups for array in group]
        self.layout = [len(group) for group in self.groups]

    def specs(self, rows, start):
        once = pl.Buffered(1) if start(0) == start(1) else None
        found = []
        for k, group in enumerate(self.groups):
            for array in group:
                shape = (pl.Element(rows), pl.Element(array.shape[-1]))
                if self.stacked is None:
                    found.append(
                        pl.BlockSpec(shape, lambda i: (start(i), 0), pipeline_mode=once)
                    )
                else:
                    found.append(
                        pl.BlockSpec(
                            (pl.Squeezed(),) + shape,
                            lambda i, k=k: (k, start(i), 0),
                            pipeline_mode=once,
                        )
                    )
        return found


def grouped(refs, layout):
    groups, at = [], 0
    for size in layout:
        groups.append(refs[at : at + size])
        at += size
    return groups


def fill(target, at, group, rows):
    left = 0
    for ref in group:
        right = left + ref.shape[1]
        target[at, left:right] = ref[rows, :]
        left = right


def split3(value):
    high = value.astype(BF16).astype(F32)
    rest = value - high
    middle = rest.astype(BF16).astype(F32)
    return high, middle, rest - middle


def aligned(index, rows):
    return pl.ds(pl.multiple_of(index * rows, rows), rows)


def unit_of(rows):
    inverse = lax.rsqrt(jnp.mean(rows * rows, axis=-1, keepdims=True) + EPS)
    return rows * inverse, inverse


def head_blocks():
    first = lax.broadcasted_iota(jnp.int32, (128, 128), 0) // HEAD_SIZE
    second = lax.broadcasted_iota(jnp.int32, (128, 128), 1) // HEAD_SIZE
    return (first == second).astype(BF16)


def head_mean(rows, blocks):
    return dot(rows.astype(BF16), blocks) * (1.0 / HEAD_SIZE)


def swap_halves(rows, first):
    return jnp.where(first, pltpu.roll(rows, 96, 1), pltpu.roll(rows, 32, 1))


def lanes(rows=TILE):
    return lax.broadcasted_iota(jnp.int32, (rows, 128), 1)


def load_pairs(parts, me_ref, refs, w_all):
    rows = w_all.shape[0] // parts

    @pl.when(pl.program_id(0) == 0)
    def _():
        for k in range(parts):
            at = aligned(me_ref[0] ^ k, rows)
            w_all[at, :1024] = refs[2 * k][...]
            w_all[at, 1024:] = refs[2 * k + 1][...]


def pair_specs(pieces, rows):
    arrays, specs = [], []
    for piece in pieces:
        left, right, at = piece
        arrays += [left, right]
        specs += [fixed((rows, 1024)), fixed((rows, 1024), (at, 0))]
    return arrays, specs


def project_kernel(parts, me_ref, x_ref, cos_ref, sin_ref, qx_ref, kx_ref, *refs):
    gain_refs = refs[2 * parts : 3 * parts]
    n_ref, unit_ref, scale_ref, q_ref, k_ref, v_ref, gain_ref, w_all = refs[3 * parts :]
    load_pairs(parts, me_ref, refs, w_all)

    @pl.when(pl.program_id(0) == 0)
    def _():
        total = gain_refs[0][...].astype(F32)
        for ref in gain_refs[1:]:
            total = total + ref[...].astype(F32)
        gain_ref[...] = total

    unit, _ = unit_of(x_ref[...].astype(F32))
    normed = (unit * gain_ref[0:1, :]).astype(BF16)
    n_ref[...] = normed
    raw = dot(normed, w_all[...])
    blocks = head_blocks()
    lane = lanes()
    first = (lane % HEAD_SIZE) < HEAD_SIZE // 2
    low = lane < HEAD_SIZE
    cosine, sine = cos_ref[...], sin_ref[...]
    for p in range(12):
        at = slice(p * 128, (p + 1) * 128)
        rows_in = raw[:, at]
        inverse = lax.rsqrt(head_mean(rows_in * rows_in, blocks) + EPS)
        unit = rows_in * inverse
        unit_ref[:, at] = unit.astype(BF16)
        scale_ref[:, at] = inverse.astype(BF16)
        scaled = unit * gain_ref[1 + p // 8 : 2 + p // 8, :128]
        turned = scaled * cosine + swap_halves(scaled, first) * sine
        if p < 8:
            turned = turned * HEAD_SIZE**-0.5
            out, more, at = q_ref, qx_ref[...], 2 * p
        else:
            out, more, at = k_ref, kx_ref[...], 2 * (p - 8)
        out[at] = jnp.where(low, turned, more).astype(BF16)
        out[at + 1] = jnp.where(low, pltpu.roll(turned, 64, 1), more).astype(BF16)
    more = ((lane >= 64) & (lane < 67)).astype(F32)
    for p in range(4):
        rows_in = raw[:, 1536 + p * 128 : 1664 + p * 128]
        v_ref[2 * p] = jnp.where(low, rows_in, more).astype(BF16)
        v_ref[2 * p + 1] = jnp.where(low, pltpu.roll(rows_in, 64, 1), more).astype(BF16)


def project(pieces, me, x, tables):
    length, width = x.shape
    parts = len(pieces)
    rows = width // parts
    arrays, specs = pair_specs(pieces, rows)
    gains = [(piece[1], (piece[2] + 1) * rows // 16) for piece in pieces]

    def heads(count):
        return pl.BlockSpec((count, TILE, 128), lambda i: (0, i, 0))

    return pl.pallas_call(
        lambda *refs: project_kernel(parts, *refs),
        grid=(length // TILE,),
        in_specs=[SMALL, by_rows(width)]
        + [by_rows(128)] * 4
        + specs
        + [fixed((16, 1024), (at, 0)) for _, at in gains],
        out_specs=[by_rows(width), by_rows(1536), by_rows(1536), heads(16), heads(8), heads(8)]
        + [fixed((16, 1024))],
        out_shape=[
            jax.ShapeDtypeStruct((length, width), BF16),
            jax.ShapeDtypeStruct((length, 1536), BF16),
            jax.ShapeDtypeStruct((length, 1536), BF16),
            jax.ShapeDtypeStruct((16, length, 128), BF16),
            jax.ShapeDtypeStruct((8, length, 128), BF16),
            jax.ShapeDtypeStruct((8, length, 128), BF16),
            jax.ShapeDtypeStruct((16, 1024), F32),
        ],
        scratch_shapes=[pltpu.VMEM((width, 2048), BF16)],
        compiler_params=params(),
        cost_estimate=cost(8, 25),
        name="project",
    )(me, x, *tables, *arrays, *[array for array, _ in gains])


def causal(query_axis):
    first = lax.broadcasted_iota(jnp.int32, (TILE, TILE), 0)
    second = lax.broadcasted_iota(jnp.int32, (TILE, TILE), 1)
    return (first >= second) if query_axis == 0 else (second >= first)


def attend_kernel(q_ref, k_ref, v_ref, o_ref, qb_ref):
    tiles = q_ref.shape[1] // TILE
    keep = causal(0)
    lane = lax.broadcasted_iota(jnp.int32, (TILE, 128), 1)
    for i in range(tiles):
        rows = slice(i * TILE, (i + 1) * TILE)
        halves = []
        for h in range(2):
            q = q_ref[h, rows, :]
            out = None
            for j in range(i + 1):
                cols = slice(j * TILE, (j + 1) * TILE)
                weights = jnp.exp(dot(q, k_ref[0, cols, :], NT))
                if j == i:
                    weights = jnp.where(keep, weights, 0.0)
                part = dot(weights.astype(BF16), v_ref[0, cols, :])
                out = part if out is None else out + part
            total = out[:, 64:65]
            halves.append(out / total)
            high, middle, low = split3(-jnp.log(total))
            extra = jnp.where(
                lane == 68, high, jnp.where(lane == 69, middle, jnp.where(lane == 70, low, 0.0))
            )
            qb_ref[h, rows, :] = (q.astype(F32) + extra).astype(BF16)
        both = jnp.where(lane < 64, halves[0], pltpu.roll(halves[1], 64, 1))
        o_ref[rows, :] = both.astype(BF16)


def attend(q_aug, k_aug, v_aug, begin, groups):
    _, length, _ = q_aug.shape
    return pl.pallas_call(
        attend_kernel,
        grid=(groups,),
        in_specs=[
            pl.BlockSpec((2, length, 128), lambda g: (g + begin, 0, 0)),
            pl.BlockSpec((1, length, 128), lambda g: (g + begin, 0, 0)),
            pl.BlockSpec((1, length, 128), lambda g: (g + begin, 0, 0)),
        ],
        out_specs=[
            pl.BlockSpec((length, 128), lambda g: (0, g)),
            pl.BlockSpec((2, length, 128), lambda g: (g, 0, 0)),
        ],
        out_shape=[
            jax.ShapeDtypeStruct((length, groups * 128), BF16),
            jax.ShapeDtypeStruct((2 * groups, length, 128), BF16),
        ],
        compiler_params=params(),
        cost_estimate=cost(2.5 * groups, 2 * groups, groups * 2**20),
        name="attend",
    )(q_aug, k_aug, v_aug)


def attend_back_kernel(q_ref, k_ref, v_ref, o_ref, do_ref, dq_ref, dkv_ref, do_aug, k_t, dq_t):
    length = q_ref.shape[1]
    tiles = length // TILE
    keep = causal(1)
    lane = lax.broadcasted_iota(jnp.int32, (length, 128), 1)
    back = do_ref[...].astype(F32)
    product = back * o_ref[...].astype(F32)
    for h in range(2):
        own = (lane < 64) if h == 0 else (lane >= 64)
        centre = jnp.sum(jnp.where(own, product, 0.0), axis=1, keepdims=True)
        moved = back if h == 0 else pltpu.roll(back, 64, 1)
        high, middle, low = split3(-centre)
        extra = jnp.where(
            lane == 64, high, jnp.where(lane == 65, middle, jnp.where(lane == 66, low, 0.0))
        )
        do_aug[h] = jnp.where(lane < 64, moved, extra).astype(BF16)
    k_t[...] = k_ref[0].astype(F32).T[:64, :].astype(BF16)
    low_half = lax.broadcasted_iota(jnp.int32, (TILE, 128), 1) < 64
    for j in range(tiles):
        cols = slice(j * TILE, (j + 1) * TILE)
        k = k_ref[0, cols, :]
        v = v_ref[0, cols, :]
        dk = None
        dv = None
        for i in range(j, tiles):
            rows = slice(i * TILE, (i + 1) * TILE)
            for h in range(2):
                q = q_ref[h, rows, :]
                do = do_aug[h, rows, :]
                probs = jnp.exp(dot(k, q, NT))
                if i == j:
                    probs = jnp.where(keep, probs, 0.0)
                scores = (probs * dot(v, do, NT)).astype(BF16)
                to_v = dot(probs.astype(BF16), do)
                to_k = dot(scores, q)
                dv = to_v if dv is None else dv + to_v
                dk = to_k if dk is None else dk + to_k
                to_q = dot(k_t[:, cols], scores)
                if j == 0:
                    dq_t[h * 64 : (h + 1) * 64, rows] = to_q
                else:
                    dq_t[h * 64 : (h + 1) * 64, rows] += to_q
        dkv_ref[cols, :] = jnp.where(low_half, dk, pltpu.roll(dv, 64, 1))
    dq_ref[...] = dq_t[...].T


def attend_back(q_back, k_aug, v_aug, attended, back_attended, begin, groups):
    _, length, _ = q_back.shape
    by_group = pl.BlockSpec((length, 128), lambda g: (0, g + begin))
    out_group = pl.BlockSpec((length, 128), lambda g: (0, g))
    return pl.pallas_call(
        attend_back_kernel,
        grid=(groups,),
        in_specs=[
            pl.BlockSpec((2, length, 128), lambda g: (g, 0, 0)),
            pl.BlockSpec((1, length, 128), lambda g: (g + begin, 0, 0)),
            pl.BlockSpec((1, length, 128), lambda g: (g + begin, 0, 0)),
            out_group,
            by_group,
        ],
        out_specs=[out_group, out_group],
        out_shape=[jax.ShapeDtypeStruct((length, groups * 128), F32)] * 2,
        scratch_shapes=[
            pltpu.VMEM((2, length, 128), BF16),
            pltpu.VMEM((64, length), BF16),
            pltpu.VMEM((128, length), F32),
        ],
        compiler_params=params(),
        cost_estimate=cost(5 * groups, 3 * groups, groups * 2**20),
        name="attend_back",
    )(q_back, k_aug, v_aug, attended, back_attended)


def output_kernel(layout, me_ref, o0_ref, o1_ref, x_ref, gain_ref, *refs):
    sum_ref, n_ref, nt_ref, w_all = refs[-4:]
    rows = w_all.shape[0] // len(layout)

    @pl.when(pl.program_id(0) == 0)
    def _():
        for k, group in enumerate(grouped(refs, layout)):
            fill(w_all, aligned(me_ref[0] ^ k, rows), group, slice(None))

    total = x_ref[...].astype(F32) + dot(o0_ref[...], w_all[:512, :])
    total = total + dot(o1_ref[...], w_all[512:, :])
    sum_ref[...] = total
    unit, _ = unit_of(total)
    normed = unit * gain_ref[3:4, :]
    n_ref[...] = normed.astype(BF16)
    nt_ref[...] = normed.T.astype(BF16)


def output_rows(pieces, me, attended, x, gain):
    length, width = x.shape
    parts = pieces.count
    rows = width // parts
    return pl.pallas_call(
        lambda *refs: output_kernel(pieces.layout, *refs),
        grid=(length // TILE,),
        in_specs=[SMALL, by_rows(512), by_rows(512), by_rows(width), fixed((16, 1024))]
        + pieces.specs(rows, lambda i: 0),
        out_specs=[by_rows(width), by_rows(width), pl.BlockSpec((width, TILE), lambda i: (0, i))],
        out_shape=[
            jax.ShapeDtypeStruct((length, width), F32),
            jax.ShapeDtypeStruct((length, width), BF16),
            jax.ShapeDtypeStruct((width, length), BF16),
        ],
        scratch_shapes=[pltpu.VMEM((1024, width), BF16)],
        compiler_params=params(),
        cost_estimate=cost(5, 15),
        name="output_rows",
    )(me, *attended, x, gain, *pieces.arrays)


def scatter_rows(me, parts, value, rows, own_ref, sib_ref, at):
    half = me >> 1
    core = me & 1
    for q in range(parts // 2):
        for s, ref in enumerate((own_ref, sib_ref)):
            source = 2 * q + (core ^ s)
            ref[q ^ half, at : at + rows, :] = value[aligned(source, rows), :]


def feed_kernel(layout, paired, me_ref, n_ref, nt_ref, c_ref, *refs):
    parts = len(layout)
    f_ref, b_ref, *grad_refs = refs[sum(layout) : -7]
    w_all, d_all, back, w_grad, d_grad, f_sum, b_sum = refs[-7:]
    me = me_ref[0]
    rows = w_all.shape[0] // parts
    seg = SLAB // parts
    for k, group in enumerate(grouped(refs, layout)):
        fill(w_all, aligned(me ^ k, rows), group, slice(0, rows))
        fill(d_all, aligned(me ^ k, seg), group, slice(rows, rows + seg))
    both = dot(n_ref[...], w_all[...])
    gate = both[:, :SLAB]
    up = both[:, SLAB:]
    sig = 1.0 / (1.0 + jnp.exp(-gate))
    swish = gate * sig
    hidden = (swish * up).astype(BF16)
    back_hidden = dot(c_ref[...], d_all[...], NT)
    back[:, SLAB:] = (back_hidden * swish).astype(BF16)
    back[:, :SLAB] = (back_hidden * up * sig * (1.0 + gate * (1.0 - sig))).astype(BF16)
    out = dot(hidden, d_all[...])
    w_grad[...] = dot(nt_ref[...], back[...]).astype(BF16)
    d_grad[...] = dot(hidden, c_ref[...], TN).astype(BF16)
    back_in = dot(back[...], w_all[...], NT)

    step = pl.program_id(0)

    @pl.when(step == 0)
    def _():
        f_sum[...] = out
        b_sum[...] = back_in

    @pl.when(step > 0)
    def _():
        f_sum[...] += out
        b_sum[...] += back_in

    @pl.when(step == pl.num_programs(0) - 1)
    def _():
        f_ref[...] = f_sum[...].astype(BF16)
        b_ref[...] = b_sum[...].astype(BF16)

    if paired:
        own_ref, sib_ref = grad_refs
        scatter_rows(me, parts, w_grad, rows, own_ref, sib_ref, 0)
        scatter_rows(me, parts, d_grad, seg, own_ref, sib_ref, rows)
    else:
        for d in range(parts):
            grad_refs[0][d, :rows, :] = w_grad[d * rows : (d + 1) * rows, :]
            grad_refs[0][d, rows:, :] = d_grad[d * seg : (d + 1) * seg, :]


def feed(pieces, me, begin, slabs, normed, normed_t, cotangent, paired):
    length, width = normed.shape
    parts = pieces.count
    rows = width // parts + SLAB // parts
    depth = parts // 2 if paired else parts
    count = 2 if paired else 1
    grads = pl.BlockSpec((depth, rows, 2 * SLAB), lambda i: (0, i, 0))
    return pl.pallas_call(
        lambda *refs: feed_kernel(pieces.layout, paired, *refs),
        grid=(slabs,),
        in_specs=[SMALL, fixed((length, width)), fixed((width, length)), fixed((length, width))]
        + pieces.specs(rows, lambda i: (begin // 16 + i * (rows // 16)) * 16),
        out_specs=[fixed((length, width)), fixed((length, width))] + [grads] * count,
        out_shape=[
            jax.ShapeDtypeStruct((length, width), BF16),
            jax.ShapeDtypeStruct((length, width), BF16),
        ]
        + [jax.ShapeDtypeStruct((depth, slabs * rows, 2 * SLAB), BF16)] * count,
        scratch_shapes=[
            pltpu.VMEM((width, 2 * SLAB), BF16),
            pltpu.VMEM((SLAB, width), BF16),
            pltpu.VMEM((length, 2 * SLAB), BF16),
            pltpu.VMEM((width, 2 * SLAB), BF16),
            pltpu.VMEM((SLAB, width), BF16),
            pltpu.VMEM((length, width), F32),
            pltpu.VMEM((length, width), F32),
        ],
        compiler_params=params(),
        cost_estimate=cost(12.5 * slabs, 20 + 6 * slabs),
        name="feed",
    )(me, normed, normed_t, cotangent, *pieces.arrays)


def middle_kernel(layout, sums, me_ref, s_ref, c_ref, o0_ref, o1_ref, gain_ref, *refs):
    b_refs = refs[:sums]
    f_ref, a_ref, g_ref, w_all, total = refs[-5:]
    rows = w_all.shape[0] // len(layout)
    step = pl.program_id(0)

    @pl.when(step == 0)
    def _():
        for k, group in enumerate(grouped(refs[sums:], layout)):
            fill(w_all, aligned(me_ref[0] ^ k, rows), group, slice(None))

    back = b_refs[0][...].astype(F32)
    for ref in b_refs[1:]:
        back = back + ref[...].astype(F32)
    unit, inverse = unit_of(s_ref[...])
    scaled = back * gain_ref[3:4, :]
    first = c_ref[...].astype(F32) + inverse * (
        scaled - unit * jnp.mean(scaled * unit, axis=-1, keepdims=True)
    )
    f_ref[...] = first
    short = first.astype(BF16)
    a_ref[...] = dot(short, w_all[...], NT).astype(BF16)
    grads = [dot(ref[...], short, TN) for ref in (o0_ref, o1_ref)]

    @pl.when(step == 0)
    def _():
        total[:512, :] = grads[0]
        total[512:, :] = grads[1]

    @pl.when(step > 0)
    def _():
        total[:512, :] += grads[0]
        total[512:, :] += grads[1]

    @pl.when(step == pl.num_programs(0) - 1)
    def _():
        g_ref[...] = total[...].astype(BF16)


def middle(pieces, me, first_sum, cotangent, attended, gain, backs):
    length, width = first_sum.shape
    parts = pieces.count
    rows = width // parts
    return pl.pallas_call(
        lambda *refs: middle_kernel(pieces.layout, len(backs), *refs),
        grid=(length // TILE,),
        in_specs=[SMALL, by_rows(width), by_rows(width), by_rows(512), by_rows(512), fixed((16, 1024))]
        + [by_rows(width)] * len(backs)
        + pieces.specs(rows, lambda i: 0),
        out_specs=[by_rows(width), by_rows(1024), fixed((1024, width))],
        out_shape=[
            jax.ShapeDtypeStruct((length, width), F32),
            jax.ShapeDtypeStruct((length, 1024), BF16),
            jax.ShapeDtypeStruct((1024, width), BF16),
        ],
        scratch_shapes=[pltpu.VMEM((1024, width), BF16), pltpu.VMEM((1024, width), F32)],
        compiler_params=params(),
        cost_estimate=cost(9, 32),
        name="middle",
    )(me, first_sum, cotangent, *attended, gain, *backs, *pieces.arrays)


def raw_back_kernel(
    parts, me_ref, dq0_ref, dq1_ref, dkv0_ref, dkv1_ref, unit_ref, scale_ref, n_ref, cos_ref, sin_ref, gain_ref, wo_ref,
    b_ref, own_ref, sib_ref, total, gains,
):
    step = pl.program_id(0)
    rows = total.shape[0] // parts
    blocks = head_blocks()
    lane = lanes()
    first = (lane % HEAD_SIZE) < HEAD_SIZE // 2
    low = lane < HEAD_SIZE
    cosine, sine = cos_ref[...], sin_ref[...]
    sums = [None, None]
    for p in range(12):
        at = slice(p * 128, (p + 1) * 128)
        if p < 8:
            dq_ref = dq0_ref if p < 4 else dq1_ref
            grads = dq_ref[:, (p % 4) * 128 : (p % 4 + 1) * 128] * HEAD_SIZE**-0.5
        else:
            dkv_ref = dkv0_ref if p < 10 else dkv1_ref
            left = dkv_ref[:, (p % 2) * 256 : (p % 2) * 256 + 128]
            right = dkv_ref[:, (p % 2) * 256 + 128 : (p % 2) * 256 + 256]
            grads = jnp.where(low, left, pltpu.roll(right, 64, 1))
            values = jnp.where(low, pltpu.roll(left, 64, 1), right)
            b_ref[:, 512 + p * 128 : 640 + p * 128] = values.astype(BF16)
        turned = grads * cosine + swap_halves(grads * sine, first)
        unit = unit_ref[:, at].astype(F32)
        inverse = scale_ref[:, at].astype(F32)
        kind = 0 if p < 8 else 1
        part = jnp.sum(turned * unit, axis=0, keepdims=True)
        sums[kind] = part if sums[kind] is None else sums[kind] + part
        scaled = turned * gain_ref[1 + kind : 2 + kind, :128]
        b_ref[:, at] = (inverse * (scaled - unit * head_mean(scaled * unit, blocks))).astype(BF16)
    grad = dot(n_ref[...], b_ref[...], TN)

    @pl.when(step == 0)
    def _():
        total[...] = grad
        gains[...] = jnp.zeros_like(gains)

    @pl.when(step > 0)
    def _():
        total[...] += grad

    gains[0:1, :] += sums[0]
    gains[1:2, :] += sums[1]

    @pl.when(step == pl.num_programs(0) - 1)
    def _():
        me = me_ref[0]
        half = me >> 1
        core = me & 1
        more = gains[...].astype(BF16)
        for q in range(parts // 2):
            for s, ref in enumerate((own_ref, sib_ref)):
                source = aligned(2 * q + (core ^ s), rows)
                block = total[source, :].astype(BF16)
                ref[q ^ half, :rows, :] = block[:, :1024]
                ref[q ^ half, rows : 2 * rows, :] = block[:, 1024:]
                ref[q ^ half, 2 * rows : 3 * rows, :] = wo_ref[source, :]
                ref[q ^ half, 3 * rows :, :] = jnp.zeros((16, 1024), BF16)
                ref[q ^ half, 3 * rows :, :128] = more


def raw_back(parts, me, halves, units, normed, cosine, sine, gains, grad_out):
    length, width = normed.shape
    rows = 3 * (width // parts) + 16
    grads = fixed((parts // 2, rows, 1024))
    return pl.pallas_call(
        lambda *refs: raw_back_kernel(parts, *refs),
        grid=(length // TILE,),
        in_specs=[SMALL] + [by_rows(512)] * 4 + [by_rows(1536)] * 2 + [by_rows(width)]
        + [by_rows(128)] * 2
        + [fixed((16, 1024)), fixed((1024, width))],
        out_specs=[by_rows(2048), grads, grads],
        out_shape=[jax.ShapeDtypeStruct((length, 2048), BF16)]
        + [jax.ShapeDtypeStruct((parts // 2, rows, 1024), BF16)] * 2,
        scratch_shapes=[pltpu.VMEM((width, 2048), F32), pltpu.VMEM((16, 128), F32)],
        compiler_params=params(),
        cost_estimate=cost(10, 30),
        name="raw_back",
    )(me, *halves, *units, normed, cosine, sine, gains, grad_out)


def input_kernel(parts, me_ref, b_ref, x_ref, f_ref, gain_ref, *refs):
    out_ref, w_all = refs[2 * parts :]
    load_pairs(parts, me_ref, refs, w_all)
    unit, inverse = unit_of(x_ref[...].astype(F32))
    scaled = dot(b_ref[...], w_all[...], NT) * gain_ref[0:1, :]
    out_ref[...] = f_ref[...] + inverse * (
        scaled - unit * jnp.mean(scaled * unit, axis=-1, keepdims=True)
    )


def input_back(pieces, me, back_raw, x, back_first, gain):
    length, width = x.shape
    parts = len(pieces)
    arrays, specs = pair_specs(pieces, width // parts)
    return pl.pallas_call(
        lambda *refs: input_kernel(parts, *refs),
        grid=(length // TILE,),
        in_specs=[SMALL, by_rows(2048), by_rows(width), by_rows(width), fixed((16, 1024))] + specs,
        out_specs=by_rows(width),
        out_shape=jax.ShapeDtypeStruct((length, width), F32),
        scratch_shapes=[pltpu.VMEM((width, 2048), BF16)],
        compiler_params=params(),
        cost_estimate=cost(6, 18),
        name="input_back",
    )(me, back_raw, x, back_first, gain, *arrays)


def tables_of(numbers):
    length = numbers.shape[0]
    indices = jnp.arange(length, dtype=jnp.int32)
    starts = jnp.concatenate([jnp.ones((1,), dtype=bool), numbers[1:] != numbers[:-1]])
    begins = lax.cummax(jnp.where(starts, indices, jnp.zeros_like(numbers)), axis=0)
    offsets = (indices - begins).astype(F32).reshape(length, 1)
    frequency = ROPE_BASE ** (-jnp.arange(0, HEAD_SIZE, 2).astype(F32) / HEAD_SIZE)
    angles = offsets * frequency
    cosine = jnp.cos(angles)
    sine = jnp.sin(angles)
    same = (numbers[:, None] == jnp.arange(4)[None]).astype(F32)
    empty = jnp.zeros((length, 64), F32)
    return (
        jnp.concatenate([cosine] * 4, axis=1),
        jnp.concatenate([-sine, sine, -sine, sine], axis=1),
        jnp.concatenate([empty, -FAR * same, empty[:, :60]], axis=1),
        jnp.concatenate([empty, 1 - same, jnp.ones((length, 3)), empty[:, :57]], axis=1),
    )


def pack_kernel(chunks, o_ref, gate_ref, up_ref, down_ref, *out_refs):
    low = lanes(128) < 64
    out_refs[0][:128, :] = o_ref[...]
    places = [(c, i) for c, n in enumerate(chunks) for i in range(n)]
    for t, (c, i) in enumerate(places):
        row = i * 192 + (0 if c else 128)
        for side, ref in enumerate((gate_ref, up_ref)):
            for e in range(4):
                left, right = (18 * e + t) // 2, (18 * e + 9 + t) // 2
                a = ref[:, left * 128 : left * 128 + 128].astype(F32)
                b = ref[:, right * 128 : right * 128 + 128].astype(F32)
                both = pltpu.roll(jnp.where(low, b, a), 64, 1) if t % 2 else jnp.where(low, a, b)
                at = side * SLAB + e * 128
                out_refs[c][row : row + 128, at : at + 128] = both.astype(BF16)
        out_refs[c][row + 128 : row + 192, :] = down_ref[t * 64 : t * 64 + 64, :]


def pack_rows(chunks, w_output, w_gate, w_up, w_down):
    return pl.pallas_call(
        lambda *refs: pack_kernel(chunks, *refs),
        out_shape=[
            jax.ShapeDtypeStruct((n * 192 + (0 if c else 128), 1024), BF16)
            for c, n in enumerate(chunks)
        ],
        compiler_params=params(),
        cost_estimate=cost(0, 7),
        name="pack_rows",
    )(w_output, w_gate, w_up, w_down)


def unpack_kernel(*refs):
    *in_refs, gate_ref, up_ref, down_ref = refs
    low = lanes(128) < 64

    def rows_of(at, size, columns):
        for ref in in_refs:
            if at < ref.shape[0]:
                return ref[at : at + size, columns].astype(F32)
            at -= ref.shape[0]

    def segment(side, s, half):
        d = s // 9
        at = side * SLAB + (d // 2) * 128
        tile = rows_of((s % 9) * 192, 128, slice(at, at + 128))
        return tile if d % 2 == half else pltpu.roll(tile, 64, 1)

    for side, out in enumerate((gate_ref, up_ref)):
        for m in range(36):
            out[:, m * 128 : m * 128 + 128] = jnp.where(
                low, segment(side, 2 * m, 0), segment(side, 2 * m + 1, 1)
            )
    for t in range(9):
        down_ref[t * 64 : t * 64 + 64, :] = rows_of(t * 192 + 128, 64, slice(None))


def unpack_rows(*totals):
    return pl.pallas_call(
        unpack_kernel,
        out_shape=[
            jax.ShapeDtypeStruct((128, 4608), F32),
            jax.ShapeDtypeStruct((128, 4608), F32),
            jax.ShapeDtypeStruct((576, 1024), F32),
        ],
        compiler_params=params(),
        cost_estimate=cost(0, 14),
        name="unpack_rows",
    )(*totals)


def tie(*values):
    return lax.optimization_barrier(values)


def after(value, *tokens):
    return tie(value, *tokens)[0]


def hop(array, bit):
    return lax.ppermute(array, "shard", [(i, i ^ bit) for i in range(8)])


def gather_all(pack):
    return lax.all_gather(pack, "shard", axis=0, tiled=False)


def scatter_all(every):
    return lax.psum_scatter(every, "shard", scatter_dimension=0, tiled=True)[0]


def weave(near, far):
    groups = []
    for one, two in zip(near, far):
        groups += [list(one), list(two)]
    return Pieces(groups)


def add_parts(k, own, other, *more):
    total = own[k].astype(F32) + other[k].astype(F32)
    for term in more:
        total = total + term.astype(F32)
    return total


def rep_hop(array, pairs):
    return lax.ppermute(array.astype(BF16), "rep", pairs)


INWARD = [(0, 1), (3, 2)]
ACROSS = [(1, 2), (2, 1)]
OUTWARD = [(1, 0), (2, 3)]


def at_end(inner, outer):
    place = lax.axis_index("rep")
    return jnp.where((place == 0) | (place == 3), outer.astype(F32), inner)


def on_device(sizes, *arrays):
    (
        block_input, document_numbers, attn_gain, w_query, key_weight, value_weight, query_gain,
        key_gain, w_output, ffn_gain, w_gate, w_up, w_down, cotangent,
    ) = arrays
    reps, parts = sizes
    _, length, width = block_input.shape
    ff = w_gate.shape[1]
    paired = parts == 8 and reps == 4
    me = lax.axis_index("shard").astype(jnp.int32)
    place = me.reshape(1) if paired else jnp.zeros((1,), jnp.int32)
    x = block_input.reshape(length, width)
    back_out = cotangent.reshape(length, width)
    numbers = document_numbers.reshape(length)
    rows = width // parts
    seg = SLAB // parts
    slabs = ff // SLAB
    few = query_gain.shape[0]

    lane = jnp.arange(width)

    def spot(gain, times, size):
        share = gain.shape[0]
        wide = jnp.tile(gain, width // share)
        return jnp.where((lane < size * times) & ((lane % size) // share == me), wide, 0)

    empty = jnp.zeros((width,), BF16)
    gain_rows = [
        spot(attn_gain, 1, width),
        spot(query_gain, 2, HEAD_SIZE),
        spot(key_gain, 2, HEAD_SIZE),
        spot(ffn_gain, 1, width),
    ]
    first_pack = jnp.concatenate(
        [
            w_query,
            jnp.concatenate([key_weight, value_weight], axis=1),
            jnp.stack(gain_rows + [empty] * 12),
        ]
    )
    tables = tables_of(numbers)
    run = block_paired if paired else block_simple
    args = (me, place, x, back_out, tables, first_pack, w_output, w_gate, w_up, w_down)
    block_output, input_grad, attn_grad, feed_grads = run(*args)
    grad_gate, grad_up, grad_down = feed_grads
    grad_query = attn_grad[:rows]
    grad_key = attn_grad[rows : 2 * rows, :512]
    grad_value = attn_grad[rows : 2 * rows, 512:]

    def diagonal(*pairs):
        total = 0.0
        for weight, grad in pairs:
            total = total + jnp.sum(weight.astype(F32) * grad, axis=1)
        return total

    grad_gain_attn = diagonal(
        (w_query, grad_query), (key_weight, grad_key), (value_weight, grad_value)
    ) / attn_gain.astype(F32)
    grad_gain_ffn = diagonal((w_gate, grad_gate), (w_up, grad_up)) / ffn_gain.astype(F32)

    def small(row):
        both = attn_grad[3 * rows + row, :64] + attn_grad[3 * rows + row, 64:128]
        return lax.dynamic_slice(both, (me * few,), (few,))

    return (
        block_output[None],
        input_grad[None],
        grad_gain_attn,
        grad_query,
        grad_key,
        grad_value,
        small(0),
        small(1),
        attn_grad[2 * rows : 3 * rows],
        grad_gain_ffn,
        grad_gate,
        grad_up,
        grad_down,
    )


def block_simple(me, place, x, back_out, tables, first_pack, w_output, w_gate, w_up, w_down):
    rows, ff = w_gate.shape
    parts = x.shape[1] // rows
    seg = SLAB // parts
    slabs = ff // SLAB
    tall = rows + seg

    def columns(weight):
        cut = weight.reshape(rows, parts, slabs, seg).transpose(2, 0, 1, 3)
        return cut.reshape(slabs, rows, SLAB)

    pack = jnp.concatenate(
        [
            jnp.concatenate([columns(w_gate), columns(w_up)], axis=2),
            w_down.reshape(slabs, seg, x.shape[1]),
        ],
        axis=1,
    ).reshape(slabs * tall, 2 * SLAB)
    every = gather_all(first_pack)
    pairs = [(every[k], every[k], 1) for k in range(parts)]
    pieces = Pieces(stacked=gather_all(jnp.concatenate([w_output, pack])))
    normed_one, *units, q_aug, k_aug, v_aug, gains = project(pairs, place, x, tables)
    attended_0, q_back_0 = attend(q_aug, k_aug, v_aug, 0, 4)
    attended_1, q_back_1 = attend(q_aug, k_aug, v_aug, 4, 4)
    attended = (attended_0, attended_1)
    first_sum, normed_two, normed_two_t = output_rows(pieces, place, attended, x, gains)
    out, back, grads = feed(
        pieces, place, rows, slabs, normed_two, normed_two_t, back_out, False
    )
    total = lax.psum(scatter_all(grads), "rep").astype(F32).reshape(slabs, tall, 2 * SLAB)
    back_first, back_attended, grad_out = middle(
        pieces, place, first_sum, back_out, attended, gains, [back]
    )
    halves_0 = attend_back(q_back_0, k_aug, v_aug, attended_0, back_attended, 0, 4)
    halves_1 = attend_back(q_back_1, k_aug, v_aug, attended_1, back_attended, 4, 4)
    back_raw, own, sib = raw_back(
        parts, place, (halves_0[0], halves_1[0], halves_0[1], halves_1[1]), units, normed_one,
        tables[0], tables[1], gains, grad_out,
    )
    every = jnp.stack([own, sib], axis=1).reshape((parts,) + own.shape[1:])
    attn_grad = lax.psum(scatter_all(every), "rep").astype(F32)
    input_grad = input_back(pairs, place, back_raw, x, back_first, gains)

    def uncut(block):
        return block.reshape(slabs, rows, parts, seg).transpose(1, 2, 0, 3).reshape(rows, ff)

    feed_grads = (
        uncut(total[:, :rows, :SLAB]),
        uncut(total[:, :rows, SLAB:]),
        total[:, rows:, :].reshape(slabs * seg, x.shape[1]),
    )
    return (first_sum + out).astype(BF16), input_grad, attn_grad, feed_grads


def fence(outputs, *hops):
    found = tie(*outputs, *hops)
    return found[: len(outputs)], list(found[len(outputs) :])


def block_paired(me, place, x, back_out, tables, first_pack, w_output, w_gate, w_up, w_down):
    rows = w_gate.shape[0]
    chunks = (3, 3, 3)

    first = hop(first_pack, 2)
    second = hop(first_pack, 4)
    twin = hop(first_pack, 1)
    made, (first, second, twin) = fence(
        [*pack_rows(chunks, w_output, w_gate, w_up, w_down), *tables], first, second, twin
    )
    packs, tables = list(made[:3]), made[3:]
    corner_a = hop(second[:rows], 2)
    corner_b = hop(first[rows:], 4)
    far = [twin] + [hop(piece, 1) for piece in (first, second, corner_a, corner_b)]
    near = [first_pack, first, second, corner_a, corner_b]
    pairs = []
    for k in range(3):
        pairs += [(near[k], near[k], 1), (far[k], far[k], 1)]
    pairs += [(near[3], near[4], 0), (far[3], far[4], 0)]

    pack = after(packs[0], corner_a, corner_b)
    first, second, twin = hop(pack, 2), hop(pack, 4), hop(pack, 1)
    normed_one, *units, q_aug, k_aug, v_aug, gains = project(pairs, place, x, tables)
    (attended_0, q_back_0, k_aug), (first, second, twin) = fence(
        [*attend(q_aug, k_aug, v_aug, 0, 4), k_aug], first, second, twin
    )
    corner_a, corner_b = hop(second[:, :512], 2), hop(first[:, 512:], 4)
    far = [hop(first, 1), hop(second, 1)]
    packs[1] = after(packs[1], first, second)
    waiting = [hop(packs[1], bit) for bit in (1, 2, 4, 6)]
    (attended_1, q_back_1), (corner_a, corner_b, *far) = fence(
        attend(q_aug, k_aug, v_aug, 4, 4), corner_a, corner_b, *far
    )
    attended = (attended_0, attended_1)
    early = weave(
        [[pack], [first], [second], [corner_a, corner_b]],
        [[twin], [far[0]], [far[1]], [hop(corner_a, 1), hop(corner_b, 1)]],
    )
    first_sum, normed_two, normed_two_t = output_rows(early, place, attended, x, gains)

    def finish(pack, twin, first, second, corner):
        near = (first, second, corner)
        far = [hop(piece, 1) for piece in near]
        return weave([[pack]] + [[a] for a in near], [[twin]] + [[a] for a in far])

    def feed_step(pieces, begin, n, paired):
        return feed(pieces, place, begin, n, normed_two, normed_two_t, back_out, paired)

    (out_0, back_0, stack_0, normed_two), waiting = fence(
        [*feed_step(early, rows, chunks[0], False), normed_two], *waiting
    )
    grads_0 = scatter_all(stack_0)
    later = finish(packs[1], *waiting)
    waiting = [hop(packs[2], bit) for bit in (1, 2, 4, 6)]
    (out_1, back_1, stack_1, normed_two), waiting = fence(
        [*feed_step(later, 0, chunks[1], False), normed_two], *waiting
    )
    last = finish(packs[2], *waiting)
    (out_2, back_2, own_2, sib_2), (grads_0,) = fence(
        feed_step(last, 0, chunks[2], True), grads_0
    )
    grads_1 = scatter_all(after(stack_1, grads_0))
    other_2 = hop(sib_2, 1)
    middles = middle(
        early, place, first_sum, back_out, attended, gains, [back_0, back_1, back_2]
    )
    (back_first, back_attended, grad_out), (other_2,) = fence(middles, other_2)
    moved_2 = hop(add_parts(3, own_2, other_2).astype(BF16), 4)
    halves = attend_back(q_back_0, k_aug, v_aug, attended_0, back_attended, 0, 4)
    (dq_0, dkv_0, back_attended), (moved_2,) = fence([*halves, back_attended], moved_2)
    first_2 = hop(add_parts(1, own_2, other_2, moved_2).astype(BF16), 2)
    second_2 = hop(add_parts(2, own_2, other_2).astype(BF16), 4)
    halves = attend_back(q_back_1, k_aug, v_aug, attended_1, back_attended, 4, 4)
    (dq_1, dkv_1), (first_2, second_2) = fence(halves, first_2, second_2)
    grads_2 = add_parts(0, own_2, other_2, first_2, second_2)
    inward_2 = rep_hop(grads_2, INWARD)
    result = raw_back(
        8, place, (dq_0, dq_1, dkv_0, dkv_1), units, normed_one, tables[0], tables[1], gains,
        grad_out,
    )
    (back_raw, own, sib), (inward_2, grads_1) = fence(result, inward_2, grads_1)
    other = hop(sib, 1)
    both = jnp.concatenate([grads_0, grads_1])
    back_raw, both = tie(back_raw, both)
    total_01 = lax.psum(both, "rep")
    half_2 = grads_2 + inward_2.astype(F32)
    back_raw, other, half_2 = tie(back_raw, other, half_2)
    terms = [add_parts(k, own, other).astype(BF16) for k in (1, 2, 3)]
    back_raw, *terms = tie(back_raw, *terms)
    steps = [hop(term, 2 * k) for k, term in zip((1, 2, 3), terms)]
    across_2 = rep_hop(half_2, ACROSS)
    input_grad = input_back(pairs, place, back_raw, x, back_first, gains)
    (input_grad,), (across_2, *steps) = fence([input_grad], across_2, *steps)
    grads = add_parts(0, own, other, *steps)
    grads, across_2, first_sum = tie(grads, across_2, first_sum)
    inward = rep_hop(grads, INWARD)
    total_2 = half_2 + across_2.astype(F32)
    outward_2 = rep_hop(total_2, OUTWARD)
    outs = out_0.astype(F32) + out_1.astype(F32) + out_2.astype(F32)
    block_output = (first_sum + outs).astype(BF16)
    (block_output,), (inward,) = fence([block_output], inward)
    half = grads + inward.astype(F32)
    across = rep_hop(half, ACROSS)
    total = half + across.astype(F32)
    total, total_01 = tie(total, total_01)
    outward = rep_hop(total, OUTWARD)
    feed_grads = unpack_rows(total_01, at_end(total_2, outward_2))
    (*feed_grads,), (outward,) = fence(feed_grads, outward)
    return block_output, input_grad, at_end(total, outward), feed_grads


def solution(mesh):
    sizes = (mesh.shape["rep"], mesh.shape["shard"])
    whole = P(("rep", "shard"), None, None)
    matrix = P("shard", None)
    vector = P("shard")
    in_specs = (
        whole, P(("rep", "shard"), None), vector, matrix, matrix, matrix, vector, vector, matrix,
        vector, matrix, matrix, matrix, whole,
    )
    out_specs = (
        whole, whole, vector, matrix, matrix, matrix, vector, vector, matrix, vector, matrix,
        matrix, matrix,
    )
    return jax.shard_map(
        lambda *arrays: on_device(sizes, *arrays),
        mesh=mesh,
        in_specs=in_specs,
        out_specs=out_specs,
        check_vma=False,
    )
```

```python
import jax
import jax.numpy as jnp
from jax import lax
from jax.experimental import pallas as pl
from jax.experimental.pallas import tpu as pltpu
from jax.sharding import PartitionSpec as P

QUERY_HEADS = 16
KEY_VALUE_HEADS = 8
HEAD_SIZE = 64
EPS = 1e-05
ROPE_BASE = 1000000.0
FAR = 32768.0
TILE = 256
SLAB = 512
VMEM_LIMIT = 60 * 1024 * 1024
NT = ((1,), (1,))
NN = ((1,), (0,))
TN = ((0,), (0,))
BF16 = jnp.bfloat16
F32 = jnp.float32
SMALL = pl.BlockSpec(memory_space=pltpu.SMEM)


def dot(left, right, dims=NN):
    return lax.dot_general(left, right, (dims, ((), ())), preferred_element_type=F32)


def params():
    return pltpu.CompilerParams(vmem_limit_bytes=VMEM_LIMIT)


def cost(giga_flops, mega_bytes, exps=0):
    return pl.CostEstimate(
        flops=int(giga_flops * 10**6),
        bytes_accessed=int(mega_bytes * 10**3),
        transcendentals=exps // 1000,
    )


def fixed(shape, where=None):
    index = (0,) * len(shape) if where is None else where
    return pl.BlockSpec(shape, lambda *_: index, pipeline_mode=pl.Buffered(1))


def by_rows(width, rows=TILE):
    return pl.BlockSpec((rows, width), lambda i: (i, 0))


class Pieces:
    def __init__(self, groups=None, stacked=None):
        self.stacked = stacked
        self.count = len(groups) if stacked is None else stacked.shape[0]
        self.groups = groups if stacked is None else [[stacked]] * self.count
        self.arrays = [array for group in self.groups for array in group]
        self.layout = [len(group) for group in self.groups]

    def specs(self, rows, start):
        once = pl.Buffered(1) if start(0) == start(1) else None
        found = []
        for k, group in enumerate(self.groups):
            for array in group:
                shape = (pl.Element(rows), pl.Element(array.shape[-1]))
                if self.stacked is None:
                    found.append(
                        pl.BlockSpec(shape, lambda i: (start(i), 0), pipeline_mode=once)
                    )
                else:
                    found.append(
                        pl.BlockSpec(
                            (pl.Squeezed(),) + shape,
                            lambda i, k=k: (k, start(i), 0),
                            pipeline_mode=once,
                        )
                    )
        return found


def grouped(refs, layout):
    groups, at = [], 0
    for size in layout:
        groups.append(refs[at : at + size])
        at += size
    return groups


def fill(target, at, group, rows):
    left = 0
    for ref in group:
        right = left + ref.shape[1]
        target[at, left:right] = ref[rows, :]
        left = right


def split3(value):
    high = value.astype(BF16).astype(F32)
    rest = value - high
    middle = rest.astype(BF16).astype(F32)
    return high, middle, rest - middle


def aligned(index, rows):
    return pl.ds(pl.multiple_of(index * rows, rows), rows)


def unit_of(rows):
    inverse = lax.rsqrt(jnp.mean(rows * rows, axis=-1, keepdims=True) + EPS)
    return rows * inverse, inverse


def head_blocks():
    first = lax.broadcasted_iota(jnp.int32, (128, 128), 0) // HEAD_SIZE
    second = lax.broadcasted_iota(jnp.int32, (128, 128), 1) // HEAD_SIZE
    return (first == second).astype(BF16)


def head_mean(rows, blocks):
    return dot(rows.astype(BF16), blocks) * (1.0 / HEAD_SIZE)


def swap_halves(rows, first):
    return jnp.where(first, pltpu.roll(rows, 96, 1), pltpu.roll(rows, 32, 1))


def lanes(rows=TILE):
    return lax.broadcasted_iota(jnp.int32, (rows, 128), 1)


def load_pairs(parts, me_ref, refs, w_all):
    rows = w_all.shape[0] // parts

    @pl.when(pl.program_id(0) == 0)
    def _():
        for k in range(parts):
            at = aligned(me_ref[0] ^ k, rows)
            w_all[at, :1024] = refs[2 * k][...]
            w_all[at, 1024:] = refs[2 * k + 1][...]


def pair_specs(pieces, rows):
    arrays, specs = [], []
    for piece in pieces:
        left, right, at = piece
        arrays += [left, right]
        specs += [fixed((rows, 1024)), fixed((rows, 1024), (at, 0))]
    return arrays, specs


def project_kernel(parts, me_ref, x_ref, cos_ref, sin_ref, qx_ref, kx_ref, *refs):
    gain_refs = refs[2 * parts : 3 * parts]
    n_ref, unit_ref, scale_ref, q_ref, k_ref, v_ref, gain_ref, w_all = refs[3 * parts :]
    load_pairs(parts, me_ref, refs, w_all)

    @pl.when(pl.program_id(0) == 0)
    def _():
        total = gain_refs[0][...].astype(F32)
        for ref in gain_refs[1:]:
            total = total + ref[...].astype(F32)
        gain_ref[...] = total

    unit, _ = unit_of(x_ref[...].astype(F32))
    normed = (unit * gain_ref[0:1, :]).astype(BF16)
    n_ref[...] = normed
    raw = dot(normed, w_all[...])
    blocks = head_blocks()
    lane = lanes()
    first = (lane % HEAD_SIZE) < HEAD_SIZE // 2
    low = lane < HEAD_SIZE
    cosine, sine = cos_ref[...], sin_ref[...]
    for p in range(12):
        at = slice(p * 128, (p + 1) * 128)
        rows_in = raw[:, at]
        inverse = lax.rsqrt(head_mean(rows_in * rows_in, blocks) + EPS)
        unit = rows_in * inverse
        unit_ref[:, at] = unit.astype(BF16)
        scale_ref[:, at] = inverse.astype(BF16)
        scaled = unit * gain_ref[1 + p // 8 : 2 + p // 8, :128]
        turned = scaled * cosine + swap_halves(scaled, first) * sine
        if p < 8:
            turned = turned * HEAD_SIZE**-0.5
            out, more, at = q_ref, qx_ref[...], 2 * p
        else:
            out, more, at = k_ref, kx_ref[...], 2 * (p - 8)
        out[at] = jnp.where(low, turned, more).astype(BF16)
        out[at + 1] = jnp.where(low, pltpu.roll(turned, 64, 1), more).astype(BF16)
    more = ((lane >= 64) & (lane < 67)).astype(F32)
    for p in range(4):
        rows_in = raw[:, 1536 + p * 128 : 1664 + p * 128]
        v_ref[2 * p] = jnp.where(low, rows_in, more).astype(BF16)
        v_ref[2 * p + 1] = jnp.where(low, pltpu.roll(rows_in, 64, 1), more).astype(BF16)


def project(pieces, me, x, tables):
    length, width = x.shape
    parts = len(pieces)
    rows = width // parts
    arrays, specs = pair_specs(pieces, rows)
    gains = [(piece[1], (piece[2] + 1) * rows // 16) for piece in pieces]

    def heads(count):
        return pl.BlockSpec((count, TILE, 128), lambda i: (0, i, 0))

    return pl.pallas_call(
        lambda *refs: project_kernel(parts, *refs),
        grid=(length // TILE,),
        in_specs=[SMALL, by_rows(width)]
        + [by_rows(128)] * 4
        + specs
        + [fixed((16, 1024), (at, 0)) for _, at in gains],
        out_specs=[by_rows(width), by_rows(1536), by_rows(1536), heads(16), heads(8), heads(8)]
        + [fixed((16, 1024))],
        out_shape=[
            jax.ShapeDtypeStruct((length, width), BF16),
            jax.ShapeDtypeStruct((length, 1536), BF16),
            jax.ShapeDtypeStruct((length, 1536), BF16),
            jax.ShapeDtypeStruct((16, length, 128), BF16),
            jax.ShapeDtypeStruct((8, length, 128), BF16),
            jax.ShapeDtypeStruct((8, length, 128), BF16),
            jax.ShapeDtypeStruct((16, 1024), F32),
        ],
        scratch_shapes=[pltpu.VMEM((width, 2048), BF16)],
        compiler_params=params(),
        cost_estimate=cost(8, 25),
        name="project",
    )(me, x, *tables, *arrays, *[array for array, _ in gains])


def causal(query_axis):
    first = lax.broadcasted_iota(jnp.int32, (TILE, TILE), 0)
    second = lax.broadcasted_iota(jnp.int32, (TILE, TILE), 1)
    return (first >= second) if query_axis == 0 else (second >= first)


def attend_kernel(q_ref, k_ref, v_ref, o_ref, qb_ref):
    tiles = q_ref.shape[1] // TILE
    keep = causal(0)
    lane = lax.broadcasted_iota(jnp.int32, (TILE, 128), 1)
    for i in range(tiles):
        rows = slice(i * TILE, (i + 1) * TILE)
        halves = []
        for h in range(2):
            q = q_ref[h, rows, :]
            out = None
            for j in range(i + 1):
                cols = slice(j * TILE, (j + 1) * TILE)
                weights = jnp.exp(dot(q, k_ref[0, cols, :], NT))
                if j == i:
                    weights = jnp.where(keep, weights, 0.0)
                part = dot(weights.astype(BF16), v_ref[0, cols, :])
                out = part if out is None else out + part
            total = out[:, 64:65]
            halves.append(out / total)
            high, middle, low = split3(-jnp.log(total))
            extra = jnp.where(
                lane == 68, high, jnp.where(lane == 69, middle, jnp.where(lane == 70, low, 0.0))
            )
            qb_ref[h, rows, :] = (q.astype(F32) + extra).astype(BF16)
        both = jnp.where(lane < 64, halves[0], pltpu.roll(halves[1], 64, 1))
        o_ref[rows, :] = both.astype(BF16)


def attend(q_aug, k_aug, v_aug, begin, groups):
    _, length, _ = q_aug.shape
    return pl.pallas_call(
        attend_kernel,
        grid=(groups,),
        in_specs=[
            pl.BlockSpec((2, length, 128), lambda g: (g + begin, 0, 0)),
            pl.BlockSpec((1, length, 128), lambda g: (g + begin, 0, 0)),
            pl.BlockSpec((1, length, 128), lambda g: (g + begin, 0, 0)),
        ],
        out_specs=[
            pl.BlockSpec((length, 128), lambda g: (0, g)),
            pl.BlockSpec((2, length, 128), lambda g: (g, 0, 0)),
        ],
        out_shape=[
            jax.ShapeDtypeStruct((length, groups * 128), BF16),
            jax.ShapeDtypeStruct((2 * groups, length, 128), BF16),
        ],
        compiler_params=params(),
        cost_estimate=cost(2.5 * groups, 2 * groups, groups * 2**20),
        name="attend",
    )(q_aug, k_aug, v_aug)


def attend_back_kernel(q_ref, k_ref, v_ref, o_ref, do_ref, dq_ref, dkv_ref, do_aug, k_t, dq_t):
    length = q_ref.shape[1]
    tiles = length // TILE
    keep = causal(1)
    lane = lax.broadcasted_iota(jnp.int32, (length, 128), 1)
    back = do_ref[...].astype(F32)
    product = back * o_ref[...].astype(F32)
    for h in range(2):
        own = (lane < 64) if h == 0 else (lane >= 64)
        centre = jnp.sum(jnp.where(own, product, 0.0), axis=1, keepdims=True)
        moved = back if h == 0 else pltpu.roll(back, 64, 1)
        high, middle, low = split3(-centre)
        extra = jnp.where(
            lane == 64, high, jnp.where(lane == 65, middle, jnp.where(lane == 66, low, 0.0))
        )
        do_aug[h] = jnp.where(lane < 64, moved, extra).astype(BF16)
    k_t[...] = k_ref[0].astype(F32).T[:64, :].astype(BF16)
    low_half = lax.broadcasted_iota(jnp.int32, (TILE, 128), 1) < 64
    for j in range(tiles):
        cols = slice(j * TILE, (j + 1) * TILE)
        k = k_ref[0, cols, :]
        v = v_ref[0, cols, :]
        dk = None
        dv = None
        for i in range(j, tiles):
            rows = slice(i * TILE, (i + 1) * TILE)
            for h in range(2):
                q = q_ref[h, rows, :]
                do = do_aug[h, rows, :]
                probs = jnp.exp(dot(k, q, NT))
                if i == j:
                    probs = jnp.where(keep, probs, 0.0)
                scores = (probs * dot(v, do, NT)).astype(BF16)
                to_v = dot(probs.astype(BF16), do)
                to_k = dot(scores, q)
                dv = to_v if dv is None else dv + to_v
                dk = to_k if dk is None else dk + to_k
                to_q = dot(k_t[:, cols], scores)
                if j == 0:
                    dq_t[h * 64 : (h + 1) * 64, rows] = to_q
                else:
                    dq_t[h * 64 : (h + 1) * 64, rows] += to_q
        dkv_ref[cols, :] = jnp.where(low_half, dk, pltpu.roll(dv, 64, 1))
    dq_ref[...] = dq_t[...].T


def attend_back(q_back, k_aug, v_aug, attended, back_attended, begin, groups):
    _, length, _ = q_back.shape
    by_group = pl.BlockSpec((length, 128), lambda g: (0, g + begin))
    out_group = pl.BlockSpec((length, 128), lambda g: (0, g))
    return pl.pallas_call(
        attend_back_kernel,
        grid=(groups,),
        in_specs=[
            pl.BlockSpec((2, length, 128), lambda g: (g, 0, 0)),
            pl.BlockSpec((1, length, 128), lambda g: (g + begin, 0, 0)),
            pl.BlockSpec((1, length, 128), lambda g: (g + begin, 0, 0)),
            out_group,
            by_group,
        ],
        out_specs=[out_group, out_group],
        out_shape=[jax.ShapeDtypeStruct((length, groups * 128), F32)] * 2,
        scratch_shapes=[
            pltpu.VMEM((2, length, 128), BF16),
            pltpu.VMEM((64, length), BF16),
            pltpu.VMEM((128, length), F32),
        ],
        compiler_params=params(),
        cost_estimate=cost(5 * groups, 3 * groups, groups * 2**20),
        name="attend_back",
    )(q_back, k_aug, v_aug, attended, back_attended)


def output_kernel(layout, me_ref, o0_ref, o1_ref, x_ref, gain_ref, *refs):
    sum_ref, n_ref, nt_ref, w_all = refs[-4:]
    rows = w_all.shape[0] // len(layout)

    @pl.when(pl.program_id(0) == 0)
    def _():
        for k, group in enumerate(grouped(refs, layout)):
            fill(w_all, aligned(me_ref[0] ^ k, rows), group, slice(None))

    total = x_ref[...].astype(F32) + dot(o0_ref[...], w_all[:512, :])
    total = total + dot(o1_ref[...], w_all[512:, :])
    sum_ref[...] = total
    unit, _ = unit_of(total)
    normed = unit * gain_ref[3:4, :]
    n_ref[...] = normed.astype(BF16)
    nt_ref[...] = normed.T.astype(BF16)


def output_rows(pieces, me, attended, x, gain):
    length, width = x.shape
    parts = pieces.count
    rows = width // parts
    return pl.pallas_call(
        lambda *refs: output_kernel(pieces.layout, *refs),
        grid=(length // TILE,),
        in_specs=[SMALL, by_rows(512), by_rows(512), by_rows(width), fixed((16, 1024))]
        + pieces.specs(rows, lambda i: 0),
        out_specs=[by_rows(width), by_rows(width), pl.BlockSpec((width, TILE), lambda i: (0, i))],
        out_shape=[
            jax.ShapeDtypeStruct((length, width), F32),
            jax.ShapeDtypeStruct((length, width), BF16),
            jax.ShapeDtypeStruct((width, length), BF16),
        ],
        scratch_shapes=[pltpu.VMEM((1024, width), BF16)],
        compiler_params=params(),
        cost_estimate=cost(5, 15),
        name="output_rows",
    )(me, *attended, x, gain, *pieces.arrays)


def scatter_rows(me, parts, value, rows, own_ref, sib_ref, at):
    half = me >> 1
    core = me & 1
    for q in range(parts // 2):
        for s, ref in enumerate((own_ref, sib_ref)):
            source = 2 * q + (core ^ s)
            ref[q ^ half, at : at + rows, :] = value[aligned(source, rows), :]


def feed_kernel(layout, paired, me_ref, n_ref, nt_ref, c_ref, *refs):
    parts = len(layout)
    f_ref, b_ref, *grad_refs = refs[sum(layout) : -7]
    w_all, d_all, back, w_grad, d_grad, f_sum, b_sum = refs[-7:]
    me = me_ref[0]
    rows = w_all.shape[0] // parts
    seg = SLAB // parts
    for k, group in enumerate(grouped(refs, layout)):
        fill(w_all, aligned(me ^ k, rows), group, slice(0, rows))
        fill(d_all, aligned(me ^ k, seg), group, slice(rows, rows + seg))
    both = dot(n_ref[...], w_all[...])
    gate = both[:, :SLAB]
    up = both[:, SLAB:]
    sig = 1.0 / (1.0 + jnp.exp(-gate))
    swish = gate * sig
    hidden = (swish * up).astype(BF16)
    back_hidden = dot(c_ref[...], d_all[...], NT)
    back[:, SLAB:] = (back_hidden * swish).astype(BF16)
    back[:, :SLAB] = (back_hidden * up * sig * (1.0 + gate * (1.0 - sig))).astype(BF16)
    out = dot(hidden, d_all[...])
    w_grad[...] = dot(nt_ref[...], back[...]).astype(BF16)
    d_grad[...] = dot(hidden, c_ref[...], TN).astype(BF16)
    back_in = dot(back[...], w_all[...], NT)

    step = pl.program_id(0)

    @pl.when(step == 0)
    def _():
        f_sum[...] = out
        b_sum[...] = back_in

    @pl.when(step > 0)
    def _():
        f_sum[...] += out
        b_sum[...] += back_in

    @pl.when(step == pl.num_programs(0) - 1)
    def _():
        f_ref[...] = f_sum[...].astype(BF16)
        b_ref[...] = b_sum[...].astype(BF16)

    if paired:
        own_ref, sib_ref = grad_refs
        scatter_rows(me, parts, w_grad, rows, own_ref, sib_ref, 0)
        scatter_rows(me, parts, d_grad, seg, own_ref, sib_ref, rows)
    else:
        for d in range(parts):
            grad_refs[0][d, :rows, :] = w_grad[d * rows : (d + 1) * rows, :]
            grad_refs[0][d, rows:, :] = d_grad[d * seg : (d + 1) * seg, :]


def feed(pieces, me, begin, slabs, normed, normed_t, cotangent, paired):
    length, width = normed.shape
    parts = pieces.count
    rows = width // parts + SLAB // parts
    depth = parts // 2 if paired else parts
    count = 2 if paired else 1
    grads = pl.BlockSpec((depth, rows, 2 * SLAB), lambda i: (0, i, 0))
    return pl.pallas_call(
        lambda *refs: feed_kernel(pieces.layout, paired, *refs),
        grid=(slabs,),
        in_specs=[SMALL, fixed((length, width)), fixed((width, length)), fixed((length, width))]
        + pieces.specs(rows, lambda i: (begin // 16 + i * (rows // 16)) * 16),
        out_specs=[fixed((length, width)), fixed((length, width))] + [grads] * count,
        out_shape=[
            jax.ShapeDtypeStruct((length, width), BF16),
            jax.ShapeDtypeStruct((length, width), BF16),
        ]
        + [jax.ShapeDtypeStruct((depth, slabs * rows, 2 * SLAB), BF16)] * count,
        scratch_shapes=[
            pltpu.VMEM((width, 2 * SLAB), BF16),
            pltpu.VMEM((SLAB, width), BF16),
            pltpu.VMEM((length, 2 * SLAB), BF16),
            pltpu.VMEM((width, 2 * SLAB), BF16),
            pltpu.VMEM((SLAB, width), BF16),
            pltpu.VMEM((length, width), F32),
            pltpu.VMEM((length, width), F32),
        ],
        compiler_params=params(),
        cost_estimate=cost(12.5 * slabs, 20 + 6 * slabs),
        name="feed",
    )(me, normed, normed_t, cotangent, *pieces.arrays)


def middle_kernel(layout, sums, me_ref, s_ref, c_ref, o0_ref, o1_ref, gain_ref, *refs):
    b_refs = refs[:sums]
    f_ref, a_ref, g_ref, w_all, total = refs[-5:]
    rows = w_all.shape[0] // len(layout)
    step = pl.program_id(0)

    @pl.when(step == 0)
    def _():
        for k, group in enumerate(grouped(refs[sums:], layout)):
            fill(w_all, aligned(me_ref[0] ^ k, rows), group, slice(None))

    back = b_refs[0][...].astype(F32)
    for ref in b_refs[1:]:
        back = back + ref[...].astype(F32)
    unit, inverse = unit_of(s_ref[...])
    scaled = back * gain_ref[3:4, :]
    first = c_ref[...].astype(F32) + inverse * (
        scaled - unit * jnp.mean(scaled * unit, axis=-1, keepdims=True)
    )
    f_ref[...] = first
    short = first.astype(BF16)
    a_ref[...] = dot(short, w_all[...], NT).astype(BF16)
    grads = [dot(ref[...], short, TN) for ref in (o0_ref, o1_ref)]

    @pl.when(step == 0)
    def _():
        total[:512, :] = grads[0]
        total[512:, :] = grads[1]

    @pl.when(step > 0)
    def _():
        total[:512, :] += grads[0]
        total[512:, :] += grads[1]

    @pl.when(step == pl.num_programs(0) - 1)
    def _():
        g_ref[...] = total[...].astype(BF16)


def middle(pieces, me, first_sum, cotangent, attended, gain, backs):
    length, width = first_sum.shape
    parts = pieces.count
    rows = width // parts
    return pl.pallas_call(
        lambda *refs: middle_kernel(pieces.layout, len(backs), *refs),
        grid=(length // TILE,),
        in_specs=[SMALL, by_rows(width), by_rows(width), by_rows(512), by_rows(512), fixed((16, 1024))]
        + [by_rows(width)] * len(backs)
        + pieces.specs(rows, lambda i: 0),
        out_specs=[by_rows(width), by_rows(1024), fixed((1024, width))],
        out_shape=[
            jax.ShapeDtypeStruct((length, width), F32),
            jax.ShapeDtypeStruct((length, 1024), BF16),
            jax.ShapeDtypeStruct((1024, width), BF16),
        ],
        scratch_shapes=[pltpu.VMEM((1024, width), BF16), pltpu.VMEM((1024, width), F32)],
        compiler_params=params(),
        cost_estimate=cost(9, 32),
        name="middle",
    )(me, first_sum, cotangent, *attended, gain, *backs, *pieces.arrays)


def raw_back_kernel(
    parts, me_ref, dq0_ref, dq1_ref, dkv0_ref, dkv1_ref, unit_ref, scale_ref, n_ref, cos_ref, sin_ref, gain_ref, wo_ref,
    b_ref, own_ref, sib_ref, total, gains,
):
    step = pl.program_id(0)
    rows = total.shape[0] // parts
    blocks = head_blocks()
    lane = lanes()
    first = (lane % HEAD_SIZE) < HEAD_SIZE // 2
    low = lane < HEAD_SIZE
    cosine, sine = cos_ref[...], sin_ref[...]
    sums = [None, None]
    for p in range(12):
        at = slice(p * 128, (p + 1) * 128)
        if p < 8:
            dq_ref = dq0_ref if p < 4 else dq1_ref
            grads = dq_ref[:, (p % 4) * 128 : (p % 4 + 1) * 128] * HEAD_SIZE**-0.5
        else:
            dkv_ref = dkv0_ref if p < 10 else dkv1_ref
            left = dkv_ref[:, (p % 2) * 256 : (p % 2) * 256 + 128]
            right = dkv_ref[:, (p % 2) * 256 + 128 : (p % 2) * 256 + 256]
            grads = jnp.where(low, left, pltpu.roll(right, 64, 1))
            values = jnp.where(low, pltpu.roll(left, 64, 1), right)
            b_ref[:, 512 + p * 128 : 640 + p * 128] = values.astype(BF16)
        turned = grads * cosine + swap_halves(grads * sine, first)
        unit = unit_ref[:, at].astype(F32)
        inverse = scale_ref[:, at].astype(F32)
        kind = 0 if p < 8 else 1
        part = jnp.sum(turned * unit, axis=0, keepdims=True)
        sums[kind] = part if sums[kind] is None else sums[kind] + part
        scaled = turned * gain_ref[1 + kind : 2 + kind, :128]
        b_ref[:, at] = (inverse * (scaled - unit * head_mean(scaled * unit, blocks))).astype(BF16)
    grad = dot(n_ref[...], b_ref[...], TN)

    @pl.when(step == 0)
    def _():
        total[...] = grad
        gains[...] = jnp.zeros_like(gains)

    @pl.when(step > 0)
    def _():
        total[...] += grad

    gains[0:1, :] += sums[0]
    gains[1:2, :] += sums[1]

    @pl.when(step == pl.num_programs(0) - 1)
    def _():
        me = me_ref[0]
        half = me >> 1
        core = me & 1
        more = gains[...].astype(BF16)
        for q in range(parts // 2):
            for s, ref in enumerate((own_ref, sib_ref)):
                source = aligned(2 * q + (core ^ s), rows)
                block = total[source, :].astype(BF16)
                ref[q ^ half, :rows, :] = block[:, :1024]
                ref[q ^ half, rows : 2 * rows, :] = block[:, 1024:]
                ref[q ^ half, 2 * rows : 3 * rows, :] = wo_ref[source, :]
                ref[q ^ half, 3 * rows :, :] = jnp.zeros((16, 1024), BF16)
                ref[q ^ half, 3 * rows :, :128] = more


def raw_back(parts, me, halves, units, normed, cosine, sine, gains, grad_out):
    length, width = normed.shape
    rows = 3 * (width // parts) + 16
    grads = fixed((parts // 2, rows, 1024))
    return pl.pallas_call(
        lambda *refs: raw_back_kernel(parts, *refs),
        grid=(length // TILE,),
        in_specs=[SMALL] + [by_rows(512)] * 4 + [by_rows(1536)] * 2 + [by_rows(width)]
        + [by_rows(128)] * 2
        + [fixed((16, 1024)), fixed((1024, width))],
        out_specs=[by_rows(2048), grads, grads],
        out_shape=[jax.ShapeDtypeStruct((length, 2048), BF16)]
        + [jax.ShapeDtypeStruct((parts // 2, rows, 1024), BF16)] * 2,
        scratch_shapes=[pltpu.VMEM((width, 2048), F32), pltpu.VMEM((16, 128), F32)],
        compiler_params=params(),
        cost_estimate=cost(10, 30),
        name="raw_back",
    )(me, *halves, *units, normed, cosine, sine, gains, grad_out)


def input_kernel(parts, me_ref, b_ref, x_ref, f_ref, gain_ref, *refs):
    out_ref, w_all = refs[2 * parts :]
    load_pairs(parts, me_ref, refs, w_all)
    unit, inverse = unit_of(x_ref[...].astype(F32))
    scaled = dot(b_ref[...], w_all[...], NT) * gain_ref[0:1, :]
    out_ref[...] = f_ref[...] + inverse * (
        scaled - unit * jnp.mean(scaled * unit, axis=-1, keepdims=True)
    )


def input_back(pieces, me, back_raw, x, back_first, gain):
    length, width = x.shape
    parts = len(pieces)
    arrays, specs = pair_specs(pieces, width // parts)
    return pl.pallas_call(
        lambda *refs: input_kernel(parts, *refs),
        grid=(length // TILE,),
        in_specs=[SMALL, by_rows(2048), by_rows(width), by_rows(width), fixed((16, 1024))] + specs,
        out_specs=by_rows(width),
        out_shape=jax.ShapeDtypeStruct((length, width), F32),
        scratch_shapes=[pltpu.VMEM((width, 2048), BF16)],
        compiler_params=params(),
        cost_estimate=cost(6, 18),
        name="input_back",
    )(me, back_raw, x, back_first, gain, *arrays)


def tables_of(numbers):
    length = numbers.shape[0]
    indices = jnp.arange(length, dtype=jnp.int32)
    starts = jnp.concatenate([jnp.ones((1,), dtype=bool), numbers[1:] != numbers[:-1]])
    begins = lax.cummax(jnp.where(starts, indices, jnp.zeros_like(numbers)), axis=0)
    offsets = (indices - begins).astype(F32).reshape(length, 1)
    frequency = ROPE_BASE ** (-jnp.arange(0, HEAD_SIZE, 2).astype(F32) / HEAD_SIZE)
    angles = offsets * frequency
    cosine = jnp.cos(angles)
    sine = jnp.sin(angles)
    same = (numbers[:, None] == jnp.arange(4)[None]).astype(F32)
    empty = jnp.zeros((length, 64), F32)
    return (
        jnp.concatenate([cosine] * 4, axis=1),
        jnp.concatenate([-sine, sine, -sine, sine], axis=1),
        jnp.concatenate([empty, -FAR * same, empty[:, :60]], axis=1),
        jnp.concatenate([empty, 1 - same, jnp.ones((length, 3)), empty[:, :57]], axis=1),
    )


def pack_kernel(chunks, o_ref, gate_ref, up_ref, down_ref, *out_refs):
    low = lanes(128) < 64
    out_refs[0][:128, :] = o_ref[...]
    places = [(c, i) for c, n in enumerate(chunks) for i in range(n)]
    for t, (c, i) in enumerate(places):
        row = i * 192 + (0 if c else 128)
        for side, ref in enumerate((gate_ref, up_ref)):
            for e in range(4):
                left, right = (18 * e + t) // 2, (18 * e + 9 + t) // 2
                a = ref[:, left * 128 : left * 128 + 128].astype(F32)
                b = ref[:, right * 128 : right * 128 + 128].astype(F32)
                both = pltpu.roll(jnp.where(low, b, a), 64, 1) if t % 2 else jnp.where(low, a, b)
                at = side * SLAB + e * 128
                out_refs[c][row : row + 128, at : at + 128] = both.astype(BF16)
        out_refs[c][row + 128 : row + 192, :] = down_ref[t * 64 : t * 64 + 64, :]


def pack_rows(chunks, w_output, w_gate, w_up, w_down):
    return pl.pallas_call(
        lambda *refs: pack_kernel(chunks, *refs),
        out_shape=[
            jax.ShapeDtypeStruct((n * 192 + (0 if c else 128), 1024), BF16)
            for c, n in enumerate(chunks)
        ],
        compiler_params=params(),
        cost_estimate=cost(0, 7),
        name="pack_rows",
    )(w_output, w_gate, w_up, w_down)


def unpack_kernel(flag_ref, *refs):
    *in_refs, gate_ref, up_ref, down_ref = refs
    low = lanes(128) < 64
    outer = flag_ref[0] > 0

    def rows_of(at, size, columns):
        for inside, outside in zip(in_refs[::2], in_refs[1::2]):
            if at < inside.shape[0]:
                one = inside[at : at + size, columns].astype(F32)
                return jnp.where(outer, outside[at : at + size, columns].astype(F32), one)
            at -= inside.shape[0]

    def segment(side, s, half):
        d = s // 9
        at = side * SLAB + (d // 2) * 128
        tile = rows_of((s % 9) * 192, 128, slice(at, at + 128))
        return tile if d % 2 == half else pltpu.roll(tile, 64, 1)

    for side, out in enumerate((gate_ref, up_ref)):
        for m in range(36):
            out[:, m * 128 : m * 128 + 128] = jnp.where(
                low, segment(side, 2 * m, 0), segment(side, 2 * m + 1, 1)
            )
    for t in range(9):
        down_ref[t * 64 : t * 64 + 64, :] = rows_of(t * 192 + 128, 64, slice(None))


def unpack_rows(flag, *totals):
    whole = pl.BlockSpec(memory_space=pltpu.VMEM)
    return pl.pallas_call(
        unpack_kernel,
        in_specs=[SMALL] + [whole] * len(totals),
        out_shape=[
            jax.ShapeDtypeStruct((128, 4608), F32),
            jax.ShapeDtypeStruct((128, 4608), F32),
            jax.ShapeDtypeStruct((576, 1024), F32),
        ],
        compiler_params=params(),
        cost_estimate=cost(0, 14),
        name="unpack_rows",
    )(flag, *totals)


def tie(*values):
    return lax.optimization_barrier(values)


def after(value, *tokens):
    return tie(value, *tokens)[0]


def hop(array, bit):
    return lax.ppermute(array, "shard", [(i, i ^ bit) for i in range(8)])


def gather_all(pack):
    return lax.all_gather(pack, "shard", axis=0, tiled=False)


def scatter_all(every):
    return lax.psum_scatter(every, "shard", scatter_dimension=0, tiled=True)[0]


def weave(near, far):
    groups = []
    for one, two in zip(near, far):
        groups += [list(one), list(two)]
    return Pieces(groups)


def combine(*outputs, half=None):
    terms = [term if isinstance(term, tuple) else (term, None) for out in outputs for term in out]
    rows, width = terms[0][0].shape[-2:]
    wide = width if half is None else width // 2
    step = rows // (5 if rows % 64 else 4)

    def spec(array, k):
        column = half if half is not None and array.shape[-1] == width else 0
        if k is None:
            return pl.BlockSpec((step, wide), lambda i: (i, column))
        return pl.BlockSpec((pl.Squeezed(), step, wide), lambda i: (k, i, column))

    def kernel(*refs):
        at = 0
        for out, out_ref in zip(outputs, refs[len(terms) :]):
            total = refs[at][...].astype(F32)
            for ref in refs[at + 1 : at + len(out)]:
                total = total + ref[...].astype(F32)
            at += len(out)
            out_ref[...] = total.astype(BF16)

    found = pl.pallas_call(
        kernel,
        grid=(rows // step,),
        in_specs=[spec(*term) for term in terms],
        out_specs=[pl.BlockSpec((step, wide), lambda i: (i, 0))] * len(outputs),
        out_shape=[jax.ShapeDtypeStruct((rows, wide), BF16)] * len(outputs),
        compiler_params=params(),
        cost_estimate=cost(0, 4),
        name="combine",
    )(*[array for array, _ in terms])
    return found[0] if len(outputs) == 1 else found


def rep_hop(array, pairs):
    return lax.ppermute(array.astype(BF16), "rep", pairs)


INWARD = [(0, 1), (3, 2)]
ACROSS = [(1, 2), (2, 1)]
OUTWARD = [(1, 0), (2, 3)]


def at_end(inner, outer):
    place = lax.axis_index("rep")
    return jnp.where((place == 0) | (place == 3), outer.astype(F32), inner)


def on_device(sizes, *arrays):
    (
        block_input, document_numbers, attn_gain, w_query, key_weight, value_weight, query_gain,
        key_gain, w_output, ffn_gain, w_gate, w_up, w_down, cotangent,
    ) = arrays
    reps, parts = sizes
    _, length, width = block_input.shape
    ff = w_gate.shape[1]
    paired = parts == 8 and reps == 4
    me = lax.axis_index("shard").astype(jnp.int32)
    place = me.reshape(1) if paired else jnp.zeros((1,), jnp.int32)
    x = block_input.reshape(length, width)
    back_out = cotangent.reshape(length, width)
    numbers = document_numbers.reshape(length)
    rows = width // parts
    seg = SLAB // parts
    slabs = ff // SLAB
    few = query_gain.shape[0]

    lane = jnp.arange(width)

    def spot(gain, times, size):
        share = gain.shape[0]
        wide = jnp.tile(gain, width // share)
        return jnp.where((lane < size * times) & ((lane % size) // share == me), wide, 0)

    empty = jnp.zeros((width,), BF16)
    gain_rows = [
        spot(attn_gain, 1, width),
        spot(query_gain, 2, HEAD_SIZE),
        spot(key_gain, 2, HEAD_SIZE),
        spot(ffn_gain, 1, width),
    ]
    first_pack = jnp.concatenate(
        [
            w_query,
            jnp.concatenate([key_weight, value_weight], axis=1),
            jnp.stack(gain_rows + [empty] * 12),
        ]
    )
    tables = tables_of(numbers)
    run = block_paired if paired else block_simple
    args = (me, place, x, back_out, tables, first_pack, w_output, w_gate, w_up, w_down)
    block_output, input_grad, attn_grad, feed_grads = run(*args)
    grad_gate, grad_up, grad_down = feed_grads
    grad_query = attn_grad[:rows]
    grad_key = attn_grad[rows : 2 * rows, :512]
    grad_value = attn_grad[rows : 2 * rows, 512:]

    def diagonal(*pairs):
        total = 0.0
        for weight, grad in pairs:
            total = total + jnp.sum(weight.astype(F32) * grad, axis=1)
        return total

    grad_gain_attn = diagonal(
        (w_query, grad_query), (key_weight, grad_key), (value_weight, grad_value)
    ) / attn_gain.astype(F32)
    grad_gain_ffn = diagonal((w_gate, grad_gate), (w_up, grad_up)) / ffn_gain.astype(F32)

    def small(row):
        both = attn_grad[3 * rows + row, :64] + attn_grad[3 * rows + row, 64:128]
        return lax.dynamic_slice(both, (me * few,), (few,))

    return (
        block_output[None],
        input_grad[None],
        grad_gain_attn,
        grad_query,
        grad_key,
        grad_value,
        small(0),
        small(1),
        attn_grad[2 * rows : 3 * rows],
        grad_gain_ffn,
        grad_gate,
        grad_up,
        grad_down,
    )


def block_simple(me, place, x, back_out, tables, first_pack, w_output, w_gate, w_up, w_down):
    rows, ff = w_gate.shape
    parts = x.shape[1] // rows
    seg = SLAB // parts
    slabs = ff // SLAB
    tall = rows + seg

    def columns(weight):
        cut = weight.reshape(rows, parts, slabs, seg).transpose(2, 0, 1, 3)
        return cut.reshape(slabs, rows, SLAB)

    pack = jnp.concatenate(
        [
            jnp.concatenate([columns(w_gate), columns(w_up)], axis=2),
            w_down.reshape(slabs, seg, x.shape[1]),
        ],
        axis=1,
    ).reshape(slabs * tall, 2 * SLAB)
    every = gather_all(first_pack)
    pairs = [(every[k], every[k], 1) for k in range(parts)]
    pieces = Pieces(stacked=gather_all(jnp.concatenate([w_output, pack])))
    normed_one, *units, q_aug, k_aug, v_aug, gains = project(pairs, place, x, tables)
    attended_0, q_back_0 = attend(q_aug, k_aug, v_aug, 0, 4)
    attended_1, q_back_1 = attend(q_aug, k_aug, v_aug, 4, 4)
    attended = (attended_0, attended_1)
    first_sum, normed_two, normed_two_t = output_rows(pieces, place, attended, x, gains)
    out, back, grads = feed(
        pieces, place, rows, slabs, normed_two, normed_two_t, back_out, False
    )
    total = lax.psum(scatter_all(grads), "rep").astype(F32).reshape(slabs, tall, 2 * SLAB)
    back_first, back_attended, grad_out = middle(
        pieces, place, first_sum, back_out, attended, gains, [back]
    )
    halves_0 = attend_back(q_back_0, k_aug, v_aug, attended_0, back_attended, 0, 4)
    halves_1 = attend_back(q_back_1, k_aug, v_aug, attended_1, back_attended, 4, 4)
    back_raw, own, sib = raw_back(
        parts, place, (halves_0[0], halves_1[0], halves_0[1], halves_1[1]), units, normed_one,
        tables[0], tables[1], gains, grad_out,
    )
    every = jnp.stack([own, sib], axis=1).reshape((parts,) + own.shape[1:])
    attn_grad = lax.psum(scatter_all(every), "rep").astype(F32)
    input_grad = input_back(pairs, place, back_raw, x, back_first, gains)

    def uncut(block):
        return block.reshape(slabs, rows, parts, seg).transpose(1, 2, 0, 3).reshape(rows, ff)

    feed_grads = (
        uncut(total[:, :rows, :SLAB]),
        uncut(total[:, :rows, SLAB:]),
        total[:, rows:, :].reshape(slabs * seg, x.shape[1]),
    )
    return (first_sum + out).astype(BF16), input_grad, attn_grad, feed_grads


def fence(outputs, *hops):
    found = tie(*outputs, *hops)
    return found[: len(outputs)], list(found[len(outputs) :])


def block_paired(me, place, x, back_out, tables, first_pack, w_output, w_gate, w_up, w_down):
    rows = w_gate.shape[0]
    chunks = (3, 3, 3)

    first = hop(first_pack, 2)
    second = hop(first_pack, 4)
    twin = hop(first_pack, 1)
    made, (first, second, twin) = fence(
        [*pack_rows(chunks, w_output, w_gate, w_up, w_down), *tables], first, second, twin
    )
    packs, tables = list(made[:3]), made[3:]
    corner_a = hop(second[:rows], 2)
    corner_b = hop(first[rows:], 4)
    far = [twin] + [hop(piece, 1) for piece in (first, second, corner_a, corner_b)]
    near = [first_pack, first, second, corner_a, corner_b]
    pairs = []
    for k in range(3):
        pairs += [(near[k], near[k], 1), (far[k], far[k], 1)]
    pairs += [(near[3], near[4], 0), (far[3], far[4], 0)]

    pack = after(packs[0], corner_a, corner_b)
    first, second, twin = hop(pack, 2), hop(pack, 4), hop(pack, 1)
    normed_one, *units, q_aug, k_aug, v_aug, gains = project(pairs, place, x, tables)
    (attended_0, q_back_0, k_aug), (first, second, twin) = fence(
        [*attend(q_aug, k_aug, v_aug, 0, 4), k_aug], first, second, twin
    )
    corner_a, corner_b = hop(second[:, :512], 2), hop(first[:, 512:], 4)
    far = [hop(first, 1), hop(second, 1)]
    packs[1] = after(packs[1], first, second)
    waiting = [hop(packs[1], bit) for bit in (1, 2, 4, 6)]
    (attended_1, q_back_1), (corner_a, corner_b, *far) = fence(
        attend(q_aug, k_aug, v_aug, 4, 4), corner_a, corner_b, *far
    )
    attended = (attended_0, attended_1)
    early = weave(
        [[pack], [first], [second], [corner_a, corner_b]],
        [[twin], [far[0]], [far[1]], [hop(corner_a, 1), hop(corner_b, 1)]],
    )
    first_sum, normed_two, normed_two_t = output_rows(early, place, attended, x, gains)

    def finish(pack, twin, first, second, corner):
        near = (first, second, corner)
        far = [hop(piece, 1) for piece in near]
        return weave([[pack]] + [[a] for a in near], [[twin]] + [[a] for a in far])

    def feed_step(pieces, begin, n, paired):
        return feed(pieces, place, begin, n, normed_two, normed_two_t, back_out, paired)

    (out_0, back_0, own_0, sib_0, normed_two), waiting = fence(
        [*feed_step(early, rows, chunks[0], True), normed_two], *waiting
    )
    later = finish(packs[1], *waiting)
    waiting = [hop(packs[2], bit) for bit in (1, 2, 4, 6)]
    other_0 = hop(after(sib_0, *later.arrays), 1)
    (out_1, back_1, own_1, sib_1, normed_two), (other_0, *waiting) = fence(
        [*feed_step(later, 0, chunks[1], True), normed_two], other_0, *waiting
    )
    last = finish(packs[2], *waiting)
    other_1 = hop(sib_1, 1)
    moved_0 = hop(combine([(own_0, 3), (other_0, 3)]), 2)
    normed_two, other_1 = tie(normed_two, other_1)
    term = combine([(own_1, 3), (other_1, 3)])
    normed_two, term = tie(normed_two, term)
    moved_1 = hop(term, 4)
    (out_2, back_2, own_2, sib_2), (moved_0, moved_1) = fence(
        feed_step(last, 0, chunks[2], True), moved_0, moved_1
    )
    other_2 = hop(sib_2, 1)
    one, two = combine([(own_0, 1), (other_0, 1)], [(own_0, 2), (other_0, 2), moved_0])
    first_0, second_0 = hop(one, 2), hop(two, 4)
    three, four = combine([(own_1, 1), (other_1, 1), moved_1], [(own_1, 2), (other_1, 2)])
    back_2, one, two, three, four = tie(back_2, one, two, three, four)
    first_1, second_1 = hop(after(three, one), 2), hop(after(four, two), 4)
    middles = middle(
        early, place, first_sum, back_out, attended, gains, [back_0, back_1, back_2]
    )
    (back_first, back_attended, grad_out), (other_2,) = fence(middles, other_2)
    term = combine([(own_2, 3), (other_2, 3)])
    back_attended, term = tie(back_attended, term)
    moved_2 = hop(term, 2)
    halves = attend_back(q_back_0, k_aug, v_aug, attended_0, back_attended, 0, 4)
    (dq_0, dkv_0, back_attended), (first_0, second_0, first_1, second_1) = fence(
        [*halves, back_attended], first_0, second_0, first_1, second_1
    )
    grads_0, grads_1 = combine(
        [(own_0, 0), (other_0, 0), first_0, second_0], [(own_1, 0), (other_1, 0), first_1, second_1]
    )
    back_attended, grads_0, grads_1 = tie(back_attended, grads_0, grads_1)
    inward_0 = rep_hop(grads_0, INWARD)
    inward_1 = rep_hop(grads_1, INWARD)
    halves = attend_back(q_back_1, k_aug, v_aug, attended_1, back_attended, 4, 4)
    (dq_1, dkv_1), (moved_2, inward_0) = fence(halves, moved_2, inward_0)
    one, two = combine([(own_2, 1), (other_2, 1)], [(own_2, 2), (other_2, 2), moved_2])
    half_0 = combine([grads_0, inward_0])
    dq_1, one, two, half_0 = tie(dq_1, one, two, half_0)
    first_2, second_2 = hop(one, 2), hop(two, 4)
    across_0 = rep_hop(half_0, ACROSS)
    result = raw_back(
        8, place, (dq_0, dq_1, dkv_0, dkv_1), units, normed_one, tables[0], tables[1], gains,
        grad_out,
    )
    (back_raw, own, sib), (first_2, second_2, inward_1, across_0) = fence(
        result, first_2, second_2, inward_1, across_0
    )
    other = hop(sib, 1)
    half_1, total_0 = combine([grads_1, inward_1], [half_0, across_0])
    grads_2 = combine([(own_2, 0), (other_2, 0), first_2, second_2])
    back_raw, other, half_1, total_0, grads_2 = tie(back_raw, other, half_1, total_0, grads_2)
    terms = [
        combine(*[[(own, k), (other, k)] for k in (1, 2, 3)], half=side) for side in (0, 1)
    ]
    back_raw, *flat = tie(back_raw, *terms[0], *terms[1])
    steps = [hop(term, 2 * k) for k, term in zip((1, 2, 3), flat[:3])]
    inward_2 = rep_hop(grads_2, INWARD)
    outward_0 = rep_hop(total_0, OUTWARD)
    input_grad = input_back(pairs, place, back_raw, x, back_first, gains)
    (input_grad, half_1, *flat), (outward_0, *steps) = fence(
        [input_grad, half_1, *flat[3:]], outward_0, *steps
    )
    across_1 = rep_hop(half_1, ACROSS)
    more = [hop(term, 2 * k) for k, term in zip((1, 2, 3), flat)]
    part_a = combine([(own, 0), (other, 0), *steps], half=0)
    inward_a = rep_hop(part_a, INWARD)
    first_sum, _ = tie(first_sum, part_a)
    outs = out_0.astype(F32) + out_1.astype(F32) + out_2.astype(F32)
    block_output = (first_sum + outs).astype(BF16)
    (block_output,), (inward_2,) = fence([block_output], inward_2)
    half_2 = combine([grads_2, inward_2])
    across_2 = rep_hop(half_2, ACROSS)
    *more, _ = tie(*more, half_2)
    part_b = combine([(own, 0), (other, 0), *more], half=1)
    inward_b = rep_hop(part_b, INWARD)
    across_1, _ = tie(across_1, part_b)
    total_1 = combine([half_1, across_1])
    outward_1 = rep_hop(total_1, OUTWARD)
    inward_a, _ = tie(inward_a, total_1)
    half_a = combine([part_a, inward_a])
    across_a = rep_hop(half_a, ACROSS)
    inward_b, _ = tie(inward_b, half_a)
    half_b = combine([part_b, inward_b])
    across_b = rep_hop(half_b, ACROSS)
    across_2, _ = tie(across_2, half_b)
    total_2 = combine([half_2, across_2])
    outward_2 = rep_hop(total_2, OUTWARD)
    across_a, outward_1, _ = tie(across_a, outward_1, total_2)
    total_a = combine([half_a, across_a])
    outward_a = rep_hop(total_a, OUTWARD)
    across_b, _ = tie(across_b, total_a)
    total_b = combine([half_b, across_b])
    outward_b = rep_hop(total_b, OUTWARD)
    spot = lax.axis_index("rep")
    flag = ((spot == 0) | (spot == 3)).astype(jnp.int32).reshape(1)
    outward_2, _ = tie(outward_2, total_b)
    feed_grads = unpack_rows(flag, total_0, outward_0, total_1, outward_1, total_2, outward_2)
    (*feed_grads,), (outward_a, outward_b) = fence(feed_grads, outward_a, outward_b)
    attn_grad = jnp.concatenate(
        [at_end(total_a.astype(F32), outward_a), at_end(total_b.astype(F32), outward_b)], axis=1
    )
    return block_output, input_grad, attn_grad, feed_grads


def solution(mesh):
    sizes = (mesh.shape["rep"], mesh.shape["shard"])
    whole = P(("rep", "shard"), None, None)
    matrix = P("shard", None)
    vector = P("shard")
    in_specs = (
        whole, P(("rep", "shard"), None), vector, matrix, matrix, matrix, vector, vector, matrix,
        vector, matrix, matrix, matrix, whole,
    )
    out_specs = (
        whole, whole, vector, matrix, matrix, matrix, vector, vector, matrix, vector, matrix,
        matrix, matrix,
    )
    return jax.shard_map(
        lambda *arrays: on_device(sizes, *arrays),
        mesh=mesh,
        in_specs=in_specs,
        out_specs=out_specs,
        check_vma=False,
    )
```

```python
import jax
import jax.numpy as jnp
from jax import lax
from jax.experimental import pallas as pl
from jax.experimental.pallas import tpu as pltpu
from jax.sharding import PartitionSpec as P

QUERY_HEADS = 16
KEY_VALUE_HEADS = 8
HEAD_SIZE = 64
EPS = 1e-05
ROPE_BASE = 1000000.0
FAR = 32768.0
TILE = 256
SLAB = 512
VMEM_LIMIT = 60 * 1024 * 1024
NT = ((1,), (1,))
NN = ((1,), (0,))
TN = ((0,), (0,))
BF16 = jnp.bfloat16
F32 = jnp.float32
SMALL = pl.BlockSpec(memory_space=pltpu.SMEM)


def dot(left, right, dims=NN):
    return lax.dot_general(left, right, (dims, ((), ())), preferred_element_type=F32)


def params():
    return pltpu.CompilerParams(vmem_limit_bytes=VMEM_LIMIT)


def cost(giga_flops, mega_bytes, exps=0):
    return pl.CostEstimate(
        flops=int(giga_flops * 10**6),
        bytes_accessed=int(mega_bytes * 10**3),
        transcendentals=exps // 1000,
    )


def fixed(shape, where=None):
    index = (0,) * len(shape) if where is None else where
    return pl.BlockSpec(shape, lambda *_: index, pipeline_mode=pl.Buffered(1))


def by_rows(width, rows=TILE):
    return pl.BlockSpec((rows, width), lambda i: (i, 0))


class Pieces:
    def __init__(self, groups=None, stacked=None):
        self.stacked = stacked
        self.count = len(groups) if stacked is None else stacked.shape[0]
        self.groups = groups if stacked is None else [[stacked]] * self.count
        self.arrays = [array for group in self.groups for array in group]
        self.layout = [len(group) for group in self.groups]

    def specs(self, rows, start):
        once = pl.Buffered(1) if start(0) == start(1) else None
        found = []
        for k, group in enumerate(self.groups):
            for array in group:
                shape = (pl.Element(rows), pl.Element(array.shape[-1]))
                if self.stacked is None:
                    found.append(
                        pl.BlockSpec(shape, lambda i: (start(i), 0), pipeline_mode=once)
                    )
                else:
                    found.append(
                        pl.BlockSpec(
                            (pl.Squeezed(),) + shape,
                            lambda i, k=k: (k, start(i), 0),
                            pipeline_mode=once,
                        )
                    )
        return found


def grouped(refs, layout):
    groups, at = [], 0
    for size in layout:
        groups.append(refs[at : at + size])
        at += size
    return groups


def fill(target, at, group, rows):
    left = 0
    for ref in group:
        right = left + ref.shape[1]
        target[at, left:right] = ref[rows, :]
        left = right


def split3(value):
    high = value.astype(BF16).astype(F32)
    rest = value - high
    middle = rest.astype(BF16).astype(F32)
    return high, middle, rest - middle


def aligned(index, rows):
    return pl.ds(pl.multiple_of(index * rows, rows), rows)


def unit_of(rows):
    inverse = lax.rsqrt(jnp.mean(rows * rows, axis=-1, keepdims=True) + EPS)
    return rows * inverse, inverse


def head_blocks():
    first = lax.broadcasted_iota(jnp.int32, (128, 128), 0) // HEAD_SIZE
    second = lax.broadcasted_iota(jnp.int32, (128, 128), 1) // HEAD_SIZE
    return (first == second).astype(BF16)


def head_mean(rows, blocks):
    return dot(rows.astype(BF16), blocks) * (1.0 / HEAD_SIZE)


def swap_halves(rows, first):
    return jnp.where(first, pltpu.roll(rows, 96, 1), pltpu.roll(rows, 32, 1))


def lanes(rows=TILE):
    return lax.broadcasted_iota(jnp.int32, (rows, 128), 1)


def load_pairs(parts, me_ref, refs, w_all):
    rows = w_all.shape[0] // parts

    @pl.when(pl.program_id(0) == 0)
    def _():
        for k in range(parts):
            at = aligned(me_ref[0] ^ k, rows)
            w_all[at, :1024] = refs[2 * k][...]
            w_all[at, 1024:] = refs[2 * k + 1][...]


def pair_specs(pieces, rows):
    arrays, specs = [], []
    for piece in pieces:
        left, right, at = piece
        arrays += [left, right]
        specs += [fixed((rows, 1024)), fixed((rows, 1024), (at, 0))]
    return arrays, specs


def project_kernel(parts, me_ref, x_ref, cos_ref, sin_ref, qx_ref, kx_ref, *refs):
    gain_refs = refs[2 * parts : 3 * parts]
    n_ref, unit_ref, scale_ref, q_ref, k_ref, v_ref, gain_ref, w_all = refs[3 * parts :]
    load_pairs(parts, me_ref, refs, w_all)

    @pl.when(pl.program_id(0) == 0)
    def _():
        total = gain_refs[0][...].astype(F32)
        for ref in gain_refs[1:]:
            total = total + ref[...].astype(F32)
        gain_ref[...] = total

    unit, _ = unit_of(x_ref[...].astype(F32))
    normed = (unit * gain_ref[0:1, :]).astype(BF16)
    n_ref[...] = normed
    raw = dot(normed, w_all[...])
    blocks = head_blocks()
    lane = lanes()
    first = (lane % HEAD_SIZE) < HEAD_SIZE // 2
    low = lane < HEAD_SIZE
    cosine, sine = cos_ref[...], sin_ref[...]
    for p in range(12):
        at = slice(p * 128, (p + 1) * 128)
        rows_in = raw[:, at]
        inverse = lax.rsqrt(head_mean(rows_in * rows_in, blocks) + EPS)
        unit = rows_in * inverse
        unit_ref[:, at] = unit.astype(BF16)
        scale_ref[:, at] = inverse.astype(BF16)
        scaled = unit * gain_ref[1 + p // 8 : 2 + p // 8, :128]
        turned = scaled * cosine + swap_halves(scaled, first) * sine
        if p < 8:
            turned = turned * HEAD_SIZE**-0.5
            out, more, at = q_ref, qx_ref[...], 2 * p
        else:
            out, more, at = k_ref, kx_ref[...], 2 * (p - 8)
        out[at] = jnp.where(low, turned, more).astype(BF16)
        out[at + 1] = jnp.where(low, pltpu.roll(turned, 64, 1), more).astype(BF16)
    more = ((lane >= 64) & (lane < 67)).astype(F32)
    for p in range(4):
        rows_in = raw[:, 1536 + p * 128 : 1664 + p * 128]
        v_ref[2 * p] = jnp.where(low, rows_in, more).astype(BF16)
        v_ref[2 * p + 1] = jnp.where(low, pltpu.roll(rows_in, 64, 1), more).astype(BF16)


def project(pieces, me, x, tables):
    length, width = x.shape
    parts = len(pieces)
    rows = width // parts
    arrays, specs = pair_specs(pieces, rows)
    gains = [(piece[1], (piece[2] + 1) * rows // 16) for piece in pieces]

    def heads(count):
        return pl.BlockSpec((count, TILE, 128), lambda i: (0, i, 0))

    return pl.pallas_call(
        lambda *refs: project_kernel(parts, *refs),
        grid=(length // TILE,),
        in_specs=[SMALL, by_rows(width)]
        + [by_rows(128)] * 4
        + specs
        + [fixed((16, 1024), (at, 0)) for _, at in gains],
        out_specs=[by_rows(width), by_rows(1536), by_rows(1536), heads(16), heads(8), heads(8)]
        + [fixed((16, 1024))],
        out_shape=[
            jax.ShapeDtypeStruct((length, width), BF16),
            jax.ShapeDtypeStruct((length, 1536), BF16),
            jax.ShapeDtypeStruct((length, 1536), BF16),
            jax.ShapeDtypeStruct((16, length, 128), BF16),
            jax.ShapeDtypeStruct((8, length, 128), BF16),
            jax.ShapeDtypeStruct((8, length, 128), BF16),
            jax.ShapeDtypeStruct((16, 1024), F32),
        ],
        scratch_shapes=[pltpu.VMEM((width, 2048), BF16)],
        compiler_params=params(),
        cost_estimate=cost(8, 25),
        name="project",
    )(me, x, *tables, *arrays, *[array for array, _ in gains])


def causal(query_axis):
    first = lax.broadcasted_iota(jnp.int32, (TILE, TILE), 0)
    second = lax.broadcasted_iota(jnp.int32, (TILE, TILE), 1)
    return (first >= second) if query_axis == 0 else (second >= first)


def attend_kernel(q_ref, k_ref, v_ref, o_ref, qb_ref):
    tiles = q_ref.shape[1] // TILE
    keep = causal(0)
    lane = lax.broadcasted_iota(jnp.int32, (TILE, 128), 1)
    for i in range(tiles):
        rows = slice(i * TILE, (i + 1) * TILE)
        halves = []
        for h in range(2):
            q = q_ref[h, rows, :]
            out = None
            for j in range(i + 1):
                cols = slice(j * TILE, (j + 1) * TILE)
                weights = jnp.exp(dot(q, k_ref[0, cols, :], NT))
                if j == i:
                    weights = jnp.where(keep, weights, 0.0)
                part = dot(weights.astype(BF16), v_ref[0, cols, :])
                out = part if out is None else out + part
            total = out[:, 64:65]
            halves.append(out / total)
            high, middle, low = split3(-jnp.log(total))
            extra = jnp.where(
                lane == 68, high, jnp.where(lane == 69, middle, jnp.where(lane == 70, low, 0.0))
            )
            qb_ref[h, rows, :] = (q.astype(F32) + extra).astype(BF16)
        both = jnp.where(lane < 64, halves[0], pltpu.roll(halves[1], 64, 1))
        o_ref[rows, :] = both.astype(BF16)


def attend(q_aug, k_aug, v_aug, begin, groups):
    _, length, _ = q_aug.shape
    return pl.pallas_call(
        attend_kernel,
        grid=(groups,),
        in_specs=[
            pl.BlockSpec((2, length, 128), lambda g: (g + begin, 0, 0)),
            pl.BlockSpec((1, length, 128), lambda g: (g + begin, 0, 0)),
            pl.BlockSpec((1, length, 128), lambda g: (g + begin, 0, 0)),
        ],
        out_specs=[
            pl.BlockSpec((length, 128), lambda g: (0, g)),
            pl.BlockSpec((2, length, 128), lambda g: (g, 0, 0)),
        ],
        out_shape=[
            jax.ShapeDtypeStruct((length, groups * 128), BF16),
            jax.ShapeDtypeStruct((2 * groups, length, 128), BF16),
        ],
        compiler_params=params(),
        cost_estimate=cost(2.5 * groups, 2 * groups, groups * 2**20),
        name="attend",
    )(q_aug, k_aug, v_aug)


def attend_back_kernel(q_ref, k_ref, v_ref, o_ref, do_ref, dq_ref, dkv_ref, do_aug, k_t, dq_t):
    length = q_ref.shape[1]
    tiles = length // TILE
    keep = causal(1)
    lane = lax.broadcasted_iota(jnp.int32, (length, 128), 1)
    back = do_ref[...].astype(F32)
    product = back * o_ref[...].astype(F32)
    for h in range(2):
        own = (lane < 64) if h == 0 else (lane >= 64)
        centre = jnp.sum(jnp.where(own, product, 0.0), axis=1, keepdims=True)
        moved = back if h == 0 else pltpu.roll(back, 64, 1)
        high, middle, low = split3(-centre)
        extra = jnp.where(
            lane == 64, high, jnp.where(lane == 65, middle, jnp.where(lane == 66, low, 0.0))
        )
        do_aug[h] = jnp.where(lane < 64, moved, extra).astype(BF16)
    k_t[...] = k_ref[0].astype(F32).T[:64, :].astype(BF16)
    low_half = lax.broadcasted_iota(jnp.int32, (TILE, 128), 1) < 64
    for j in range(tiles):
        cols = slice(j * TILE, (j + 1) * TILE)
        k = k_ref[0, cols, :]
        v = v_ref[0, cols, :]
        dk = None
        dv = None
        for i in range(j, tiles):
            rows = slice(i * TILE, (i + 1) * TILE)
            for h in range(2):
                q = q_ref[h, rows, :]
                do = do_aug[h, rows, :]
                probs = jnp.exp(dot(k, q, NT))
                if i == j:
                    probs = jnp.where(keep, probs, 0.0)
                scores = (probs * dot(v, do, NT)).astype(BF16)
                to_v = dot(probs.astype(BF16), do)
                to_k = dot(scores, q)
                dv = to_v if dv is None else dv + to_v
                dk = to_k if dk is None else dk + to_k
                to_q = dot(k_t[:, cols], scores)
                if j == 0:
                    dq_t[h * 64 : (h + 1) * 64, rows] = to_q
                else:
                    dq_t[h * 64 : (h + 1) * 64, rows] += to_q
        dkv_ref[cols, :] = jnp.where(low_half, dk, pltpu.roll(dv, 64, 1))
    dq_ref[...] = dq_t[...].T


def attend_back(q_back, k_aug, v_aug, attended, back_attended, begin, groups):
    _, length, _ = q_back.shape
    by_group = pl.BlockSpec((length, 128), lambda g: (0, g + begin))
    out_group = pl.BlockSpec((length, 128), lambda g: (0, g))
    return pl.pallas_call(
        attend_back_kernel,
        grid=(groups,),
        in_specs=[
            pl.BlockSpec((2, length, 128), lambda g: (g, 0, 0)),
            pl.BlockSpec((1, length, 128), lambda g: (g + begin, 0, 0)),
            pl.BlockSpec((1, length, 128), lambda g: (g + begin, 0, 0)),
            out_group,
            by_group,
        ],
        out_specs=[out_group, out_group],
        out_shape=[jax.ShapeDtypeStruct((length, groups * 128), F32)] * 2,
        scratch_shapes=[
            pltpu.VMEM((2, length, 128), BF16),
            pltpu.VMEM((64, length), BF16),
            pltpu.VMEM((128, length), F32),
        ],
        compiler_params=params(),
        cost_estimate=cost(5 * groups, 3 * groups, groups * 2**20),
        name="attend_back",
    )(q_back, k_aug, v_aug, attended, back_attended)


def output_kernel(layout, me_ref, o0_ref, o1_ref, x_ref, gain_ref, *refs):
    sum_ref, n_ref, nt_ref, w_all = refs[-4:]
    rows = w_all.shape[0] // len(layout)

    @pl.when(pl.program_id(0) == 0)
    def _():
        for k, group in enumerate(grouped(refs, layout)):
            fill(w_all, aligned(me_ref[0] ^ k, rows), group, slice(None))

    total = x_ref[...].astype(F32) + dot(o0_ref[...], w_all[:512, :])
    total = total + dot(o1_ref[...], w_all[512:, :])
    sum_ref[...] = total
    unit, _ = unit_of(total)
    normed = unit * gain_ref[3:4, :]
    n_ref[...] = normed.astype(BF16)
    nt_ref[...] = normed.T.astype(BF16)


def output_rows(pieces, me, attended, x, gain):
    length, width = x.shape
    parts = pieces.count
    rows = width // parts
    return pl.pallas_call(
        lambda *refs: output_kernel(pieces.layout, *refs),
        grid=(length // TILE,),
        in_specs=[SMALL, by_rows(512), by_rows(512), by_rows(width), fixed((16, 1024))]
        + pieces.specs(rows, lambda i: 0),
        out_specs=[by_rows(width), by_rows(width), pl.BlockSpec((width, TILE), lambda i: (0, i))],
        out_shape=[
            jax.ShapeDtypeStruct((length, width), F32),
            jax.ShapeDtypeStruct((length, width), BF16),
            jax.ShapeDtypeStruct((width, length), BF16),
        ],
        scratch_shapes=[pltpu.VMEM((1024, width), BF16)],
        compiler_params=params(),
        cost_estimate=cost(5, 15),
        name="output_rows",
    )(me, *attended, x, gain, *pieces.arrays)


def scatter_rows(me, parts, value, rows, own_ref, sib_ref, at):
    half = me >> 1
    core = me & 1
    for q in range(parts // 2):
        for s, ref in enumerate((own_ref, sib_ref)):
            source = 2 * q + (core ^ s)
            ref[q ^ half, at : at + rows, :] = value[aligned(source, rows), :]


def feed_kernel(layout, paired, me_ref, n_ref, nt_ref, c_ref, *refs):
    parts = len(layout)
    f_ref, b_ref, *grad_refs = refs[sum(layout) : -7]
    w_all, d_all, back, w_grad, d_grad, f_sum, b_sum = refs[-7:]
    me = me_ref[0]
    rows = w_all.shape[0] // parts
    seg = SLAB // parts
    for k, group in enumerate(grouped(refs, layout)):
        fill(w_all, aligned(me ^ k, rows), group, slice(0, rows))
        fill(d_all, aligned(me ^ k, seg), group, slice(rows, rows + seg))
    both = dot(n_ref[...], w_all[...])
    gate = both[:, :SLAB]
    up = both[:, SLAB:]
    sig = 1.0 / (1.0 + jnp.exp(-gate))
    swish = gate * sig
    hidden = (swish * up).astype(BF16)
    back_hidden = dot(c_ref[...], d_all[...], NT)
    back[:, SLAB:] = (back_hidden * swish).astype(BF16)
    back[:, :SLAB] = (back_hidden * up * sig * (1.0 + gate * (1.0 - sig))).astype(BF16)
    out = dot(hidden, d_all[...])
    w_grad[...] = dot(nt_ref[...], back[...]).astype(BF16)
    d_grad[...] = dot(hidden, c_ref[...], TN).astype(BF16)
    back_in = dot(back[...], w_all[...], NT)

    step = pl.program_id(0)

    @pl.when(step == 0)
    def _():
        f_sum[...] = out
        b_sum[...] = back_in

    @pl.when(step > 0)
    def _():
        f_sum[...] += out
        b_sum[...] += back_in

    @pl.when(step == pl.num_programs(0) - 1)
    def _():
        f_ref[...] = f_sum[...].astype(BF16)
        b_ref[...] = b_sum[...].astype(BF16)

    if paired:
        own_ref, sib_ref = grad_refs
        scatter_rows(me, parts, w_grad, rows, own_ref, sib_ref, 0)
        scatter_rows(me, parts, d_grad, seg, own_ref, sib_ref, rows)
    else:
        for d in range(parts):
            grad_refs[0][d, :rows, :] = w_grad[d * rows : (d + 1) * rows, :]
            grad_refs[0][d, rows:, :] = d_grad[d * seg : (d + 1) * seg, :]


def feed(pieces, me, begin, slabs, normed, normed_t, cotangent, paired):
    length, width = normed.shape
    parts = pieces.count
    rows = width // parts + SLAB // parts
    depth = parts // 2 if paired else parts
    count = 2 if paired else 1
    grads = pl.BlockSpec((depth, rows, 2 * SLAB), lambda i: (0, i, 0))
    return pl.pallas_call(
        lambda *refs: feed_kernel(pieces.layout, paired, *refs),
        grid=(slabs,),
        in_specs=[SMALL, fixed((length, width)), fixed((width, length)), fixed((length, width))]
        + pieces.specs(rows, lambda i: (begin // 16 + i * (rows // 16)) * 16),
        out_specs=[fixed((length, width)), fixed((length, width))] + [grads] * count,
        out_shape=[
            jax.ShapeDtypeStruct((length, width), BF16),
            jax.ShapeDtypeStruct((length, width), BF16),
        ]
        + [jax.ShapeDtypeStruct((depth, slabs * rows, 2 * SLAB), BF16)] * count,
        scratch_shapes=[
            pltpu.VMEM((width, 2 * SLAB), BF16),
            pltpu.VMEM((SLAB, width), BF16),
            pltpu.VMEM((length, 2 * SLAB), BF16),
            pltpu.VMEM((width, 2 * SLAB), BF16),
            pltpu.VMEM((SLAB, width), BF16),
            pltpu.VMEM((length, width), F32),
            pltpu.VMEM((length, width), F32),
        ],
        compiler_params=params(),
        cost_estimate=cost(12.5 * slabs, 20 + 6 * slabs),
        name="feed",
    )(me, normed, normed_t, cotangent, *pieces.arrays)


def middle_kernel(layout, sums, me_ref, s_ref, c_ref, o0_ref, o1_ref, gain_ref, *refs):
    b_refs = refs[:sums]
    f_ref, a_ref, g_ref, w_all, total = refs[-5:]
    rows = w_all.shape[0] // len(layout)
    step = pl.program_id(0)

    @pl.when(step == 0)
    def _():
        for k, group in enumerate(grouped(refs[sums:], layout)):
            fill(w_all, aligned(me_ref[0] ^ k, rows), group, slice(None))

    back = b_refs[0][...].astype(F32)
    for ref in b_refs[1:]:
        back = back + ref[...].astype(F32)
    unit, inverse = unit_of(s_ref[...])
    scaled = back * gain_ref[3:4, :]
    first = c_ref[...].astype(F32) + inverse * (
        scaled - unit * jnp.mean(scaled * unit, axis=-1, keepdims=True)
    )
    f_ref[...] = first
    short = first.astype(BF16)
    a_ref[...] = dot(short, w_all[...], NT).astype(BF16)
    grads = [dot(ref[...], short, TN) for ref in (o0_ref, o1_ref)]

    @pl.when(step == 0)
    def _():
        total[:512, :] = grads[0]
        total[512:, :] = grads[1]

    @pl.when(step > 0)
    def _():
        total[:512, :] += grads[0]
        total[512:, :] += grads[1]

    @pl.when(step == pl.num_programs(0) - 1)
    def _():
        g_ref[...] = total[...].astype(BF16)


def middle(pieces, me, first_sum, cotangent, attended, gain, backs):
    length, width = first_sum.shape
    parts = pieces.count
    rows = width // parts
    return pl.pallas_call(
        lambda *refs: middle_kernel(pieces.layout, len(backs), *refs),
        grid=(length // TILE,),
        in_specs=[SMALL, by_rows(width), by_rows(width), by_rows(512), by_rows(512), fixed((16, 1024))]
        + [by_rows(width)] * len(backs)
        + pieces.specs(rows, lambda i: 0),
        out_specs=[by_rows(width), by_rows(1024), fixed((1024, width))],
        out_shape=[
            jax.ShapeDtypeStruct((length, width), F32),
            jax.ShapeDtypeStruct((length, 1024), BF16),
            jax.ShapeDtypeStruct((1024, width), BF16),
        ],
        scratch_shapes=[pltpu.VMEM((1024, width), BF16), pltpu.VMEM((1024, width), F32)],
        compiler_params=params(),
        cost_estimate=cost(9, 32),
        name="middle",
    )(me, first_sum, cotangent, *attended, gain, *backs, *pieces.arrays)


def raw_back_kernel(
    parts, me_ref, dq0_ref, dq1_ref, dkv0_ref, dkv1_ref, unit_ref, scale_ref, n_ref, cos_ref, sin_ref, gain_ref, wo_ref,
    b_ref, own_ref, sib_ref, total, gains,
):
    step = pl.program_id(0)
    rows = total.shape[0] // parts
    blocks = head_blocks()
    lane = lanes()
    first = (lane % HEAD_SIZE) < HEAD_SIZE // 2
    low = lane < HEAD_SIZE
    cosine, sine = cos_ref[...], sin_ref[...]
    sums = [None, None]
    for p in range(12):
        at = slice(p * 128, (p + 1) * 128)
        if p < 8:
            dq_ref = dq0_ref if p < 4 else dq1_ref
            grads = dq_ref[:, (p % 4) * 128 : (p % 4 + 1) * 128] * HEAD_SIZE**-0.5
        else:
            dkv_ref = dkv0_ref if p < 10 else dkv1_ref
            left = dkv_ref[:, (p % 2) * 256 : (p % 2) * 256 + 128]
            right = dkv_ref[:, (p % 2) * 256 + 128 : (p % 2) * 256 + 256]
            grads = jnp.where(low, left, pltpu.roll(right, 64, 1))
            values = jnp.where(low, pltpu.roll(left, 64, 1), right)
            b_ref[:, 512 + p * 128 : 640 + p * 128] = values.astype(BF16)
        turned = grads * cosine + swap_halves(grads * sine, first)
        unit = unit_ref[:, at].astype(F32)
        inverse = scale_ref[:, at].astype(F32)
        kind = 0 if p < 8 else 1
        part = jnp.sum(turned * unit, axis=0, keepdims=True)
        sums[kind] = part if sums[kind] is None else sums[kind] + part
        scaled = turned * gain_ref[1 + kind : 2 + kind, :128]
        b_ref[:, at] = (inverse * (scaled - unit * head_mean(scaled * unit, blocks))).astype(BF16)
    grad = dot(n_ref[...], b_ref[...], TN)

    @pl.when(step == 0)
    def _():
        total[...] = grad
        gains[...] = jnp.zeros_like(gains)

    @pl.when(step > 0)
    def _():
        total[...] += grad

    gains[0:1, :] += sums[0]
    gains[1:2, :] += sums[1]

    @pl.when(step == pl.num_programs(0) - 1)
    def _():
        me = me_ref[0]
        half = me >> 1
        core = me & 1
        more = gains[...].astype(BF16)
        for q in range(parts // 2):
            for s, ref in enumerate((own_ref, sib_ref)):
                source = aligned(2 * q + (core ^ s), rows)
                block = total[source, :].astype(BF16)
                ref[q ^ half, :rows, :] = block[:, :1024]
                ref[q ^ half, rows : 2 * rows, :] = block[:, 1024:]
                ref[q ^ half, 2 * rows : 3 * rows, :] = wo_ref[source, :]
                ref[q ^ half, 3 * rows :, :] = jnp.zeros((32, 1024), BF16)
                ref[q ^ half, 3 * rows :, :128] = more


def raw_back(parts, me, halves, units, normed, cosine, sine, gains, grad_out):
    length, width = normed.shape
    rows = 3 * (width // parts) + 32
    grads = fixed((parts // 2, rows, 1024))
    return pl.pallas_call(
        lambda *refs: raw_back_kernel(parts, *refs),
        grid=(length // TILE,),
        in_specs=[SMALL] + [by_rows(512)] * 4 + [by_rows(1536)] * 2 + [by_rows(width)]
        + [by_rows(128)] * 2
        + [fixed((16, 1024)), fixed((1024, width))],
        out_specs=[by_rows(2048), grads, grads],
        out_shape=[jax.ShapeDtypeStruct((length, 2048), BF16)]
        + [jax.ShapeDtypeStruct((parts // 2, rows, 1024), BF16)] * 2,
        scratch_shapes=[pltpu.VMEM((width, 2048), F32), pltpu.VMEM((32, 128), F32)],
        compiler_params=params(),
        cost_estimate=cost(10, 30),
        name="raw_back",
    )(me, *halves, *units, normed, cosine, sine, gains, grad_out)


def input_kernel(parts, me_ref, b_ref, x_ref, f_ref, gain_ref, *refs):
    out_ref, w_all = refs[2 * parts :]
    load_pairs(parts, me_ref, refs, w_all)
    unit, inverse = unit_of(x_ref[...].astype(F32))
    scaled = dot(b_ref[...], w_all[...], NT) * gain_ref[0:1, :]
    out_ref[...] = f_ref[...] + inverse * (
        scaled - unit * jnp.mean(scaled * unit, axis=-1, keepdims=True)
    )


def input_back(pieces, me, back_raw, x, back_first, gain):
    length, width = x.shape
    parts = len(pieces)
    arrays, specs = pair_specs(pieces, width // parts)
    return pl.pallas_call(
        lambda *refs: input_kernel(parts, *refs),
        grid=(length // TILE,),
        in_specs=[SMALL, by_rows(2048), by_rows(width), by_rows(width), fixed((16, 1024))] + specs,
        out_specs=by_rows(width),
        out_shape=jax.ShapeDtypeStruct((length, width), F32),
        scratch_shapes=[pltpu.VMEM((width, 2048), BF16)],
        compiler_params=params(),
        cost_estimate=cost(6, 18),
        name="input_back",
    )(me, back_raw, x, back_first, gain, *arrays)


def tables_of(numbers):
    length = numbers.shape[0]
    indices = jnp.arange(length, dtype=jnp.int32)
    starts = jnp.concatenate([jnp.ones((1,), dtype=bool), numbers[1:] != numbers[:-1]])
    begins = lax.cummax(jnp.where(starts, indices, jnp.zeros_like(numbers)), axis=0)
    offsets = (indices - begins).astype(F32).reshape(length, 1)
    frequency = ROPE_BASE ** (-jnp.arange(0, HEAD_SIZE, 2).astype(F32) / HEAD_SIZE)
    angles = offsets * frequency
    cosine = jnp.cos(angles)
    sine = jnp.sin(angles)
    same = (numbers[:, None] == jnp.arange(4)[None]).astype(F32)
    empty = jnp.zeros((length, 64), F32)
    return (
        jnp.concatenate([cosine] * 4, axis=1),
        jnp.concatenate([-sine, sine, -sine, sine], axis=1),
        jnp.concatenate([empty, -FAR * same, empty[:, :60]], axis=1),
        jnp.concatenate([empty, 1 - same, jnp.ones((length, 3)), empty[:, :57]], axis=1),
    )


def pack_kernel(chunks, o_ref, gate_ref, up_ref, down_ref, *out_refs):
    low = lanes(128) < 64
    out_refs[0][:128, :] = o_ref[...]
    places = [(c, i) for c, n in enumerate(chunks) for i in range(n)]
    for t, (c, i) in enumerate(places):
        row = i * 192 + (0 if c else 128)
        for side, ref in enumerate((gate_ref, up_ref)):
            for e in range(4):
                left, right = (18 * e + t) // 2, (18 * e + 9 + t) // 2
                a = ref[:, left * 128 : left * 128 + 128].astype(F32)
                b = ref[:, right * 128 : right * 128 + 128].astype(F32)
                both = pltpu.roll(jnp.where(low, b, a), 64, 1) if t % 2 else jnp.where(low, a, b)
                at = side * SLAB + e * 128
                out_refs[c][row : row + 128, at : at + 128] = both.astype(BF16)
        out_refs[c][row + 128 : row + 192, :] = down_ref[t * 64 : t * 64 + 64, :]


def pack_rows(chunks, w_output, w_gate, w_up, w_down):
    return pl.pallas_call(
        lambda *refs: pack_kernel(chunks, *refs),
        out_shape=[
            jax.ShapeDtypeStruct((n * 192 + (0 if c else 128), 1024), BF16)
            for c, n in enumerate(chunks)
        ],
        compiler_params=params(),
        cost_estimate=cost(0, 7),
        name="pack_rows",
    )(w_output, w_gate, w_up, w_down)


def unpack_kernel(flag_ref, *refs):
    *in_refs, gate_ref, up_ref, down_ref = refs
    low = lanes(128) < 64
    outer = flag_ref[0] > 0

    def rows_of(at, size, columns):
        for inside, outside in zip(in_refs[::2], in_refs[1::2]):
            if at < inside.shape[0]:
                one = inside[at : at + size, columns].astype(F32)
                return jnp.where(outer, outside[at : at + size, columns].astype(F32), one)
            at -= inside.shape[0]

    def segment(side, s, half):
        d = s // 9
        at = side * SLAB + (d // 2) * 128
        tile = rows_of((s % 9) * 192, 128, slice(at, at + 128))
        return tile if d % 2 == half else pltpu.roll(tile, 64, 1)

    for side, out in enumerate((gate_ref, up_ref)):
        for m in range(36):
            out[:, m * 128 : m * 128 + 128] = jnp.where(
                low, segment(side, 2 * m, 0), segment(side, 2 * m + 1, 1)
            )
    for t in range(9):
        down_ref[t * 64 : t * 64 + 64, :] = rows_of(t * 192 + 128, 64, slice(None))


def unpack_rows(flag, *totals):
    whole = pl.BlockSpec(memory_space=pltpu.VMEM)
    return pl.pallas_call(
        unpack_kernel,
        in_specs=[SMALL] + [whole] * len(totals),
        out_shape=[
            jax.ShapeDtypeStruct((128, 4608), F32),
            jax.ShapeDtypeStruct((128, 4608), F32),
            jax.ShapeDtypeStruct((576, 1024), F32),
        ],
        compiler_params=params(),
        cost_estimate=cost(0, 14),
        name="unpack_rows",
    )(flag, *totals)


def tie(*values):
    return lax.optimization_barrier(values)


def after(value, *tokens):
    return tie(value, *tokens)[0]


def hop(array, bit):
    return lax.ppermute(array, "shard", [(i, i ^ bit) for i in range(8)])


def gather_all(pack):
    return lax.all_gather(pack, "shard", axis=0, tiled=False)


def scatter_all(every):
    return lax.psum_scatter(every, "shard", scatter_dimension=0, tiled=True)[0]


def weave(near, far):
    groups = []
    for one, two in zip(near, far):
        groups += [list(one), list(two)]
    return Pieces(groups)


def combine(*outputs):
    terms = [term if isinstance(term, tuple) else (term, None) for out in outputs for term in out]
    rows, width = terms[0][0].shape[-2:]
    step = rows // 2

    def spec(k):
        if k is None:
            return pl.BlockSpec((step, width), lambda i: (i, 0))
        return pl.BlockSpec((pl.Squeezed(), step, width), lambda i: (k, i, 0))

    def kernel(*refs):
        at = 0
        for out, out_ref in zip(outputs, refs[len(terms) :]):
            total = refs[at][...].astype(F32)
            for ref in refs[at + 1 : at + len(out)]:
                total = total + ref[...].astype(F32)
            at += len(out)
            out_ref[...] = total.astype(BF16)

    found = pl.pallas_call(
        kernel,
        grid=(rows // step,),
        in_specs=[spec(k) for _, k in terms],
        out_specs=[pl.BlockSpec((step, width), lambda i: (i, 0))] * len(outputs),
        out_shape=[jax.ShapeDtypeStruct((rows, width), BF16)] * len(outputs),
        compiler_params=params(),
        cost_estimate=cost(0, 4),
        name="combine",
    )(*[array for array, _ in terms])
    return found[0] if len(outputs) == 1 else found


def rep_hop(array, pairs):
    return lax.ppermute(array.astype(BF16), "rep", pairs)


INWARD = [(0, 1), (3, 2)]
ACROSS = [(1, 2), (2, 1)]
OUTWARD = [(1, 0), (2, 3)]


def at_end(inner, outer):
    place = lax.axis_index("rep")
    return jnp.where((place == 0) | (place == 3), outer.astype(F32), inner)


def on_device(sizes, *arrays):
    (
        block_input, document_numbers, attn_gain, w_query, key_weight, value_weight, query_gain,
        key_gain, w_output, ffn_gain, w_gate, w_up, w_down, cotangent,
    ) = arrays
    reps, parts = sizes
    _, length, width = block_input.shape
    ff = w_gate.shape[1]
    paired = parts == 8 and reps == 4
    me = lax.axis_index("shard").astype(jnp.int32)
    place = me.reshape(1) if paired else jnp.zeros((1,), jnp.int32)
    x = block_input.reshape(length, width)
    back_out = cotangent.reshape(length, width)
    numbers = document_numbers.reshape(length)
    rows = width // parts
    seg = SLAB // parts
    slabs = ff // SLAB
    few = query_gain.shape[0]

    lane = jnp.arange(width)

    def spot(gain, times, size):
        share = gain.shape[0]
        wide = jnp.tile(gain, width // share)
        return jnp.where((lane < size * times) & ((lane % size) // share == me), wide, 0)

    empty = jnp.zeros((width,), BF16)
    gain_rows = [
        spot(attn_gain, 1, width),
        spot(query_gain, 2, HEAD_SIZE),
        spot(key_gain, 2, HEAD_SIZE),
        spot(ffn_gain, 1, width),
    ]
    first_pack = jnp.concatenate(
        [
            w_query,
            jnp.concatenate([key_weight, value_weight], axis=1),
            jnp.stack(gain_rows + [empty] * 12),
        ]
    )
    tables = tables_of(numbers)
    run = block_paired if paired else block_simple
    args = (me, place, x, back_out, tables, first_pack, w_output, w_gate, w_up, w_down)
    block_output, input_grad, attn_grad, feed_grads = run(*args)
    grad_gate, grad_up, grad_down = feed_grads
    grad_query = attn_grad[:rows]
    grad_key = attn_grad[rows : 2 * rows, :512]
    grad_value = attn_grad[rows : 2 * rows, 512:]

    def diagonal(*pairs):
        total = 0.0
        for weight, grad in pairs:
            total = total + jnp.sum(weight.astype(F32) * grad, axis=1)
        return total

    grad_gain_attn = diagonal(
        (w_query, grad_query), (key_weight, grad_key), (value_weight, grad_value)
    ) / attn_gain.astype(F32)
    grad_gain_ffn = diagonal((w_gate, grad_gate), (w_up, grad_up)) / ffn_gain.astype(F32)

    def small(row):
        both = attn_grad[3 * rows + row, :64] + attn_grad[3 * rows + row, 64:128]
        return lax.dynamic_slice(both, (me * few,), (few,))

    return (
        block_output[None],
        input_grad[None],
        grad_gain_attn,
        grad_query,
        grad_key,
        grad_value,
        small(0),
        small(1),
        attn_grad[2 * rows : 3 * rows],
        grad_gain_ffn,
        grad_gate,
        grad_up,
        grad_down,
    )


def block_simple(me, place, x, back_out, tables, first_pack, w_output, w_gate, w_up, w_down):
    rows, ff = w_gate.shape
    parts = x.shape[1] // rows
    seg = SLAB // parts
    slabs = ff // SLAB
    tall = rows + seg

    def columns(weight):
        cut = weight.reshape(rows, parts, slabs, seg).transpose(2, 0, 1, 3)
        return cut.reshape(slabs, rows, SLAB)

    pack = jnp.concatenate(
        [
            jnp.concatenate([columns(w_gate), columns(w_up)], axis=2),
            w_down.reshape(slabs, seg, x.shape[1]),
        ],
        axis=1,
    ).reshape(slabs * tall, 2 * SLAB)
    every = gather_all(first_pack)
    pairs = [(every[k], every[k], 1) for k in range(parts)]
    pieces = Pieces(stacked=gather_all(jnp.concatenate([w_output, pack])))
    normed_one, *units, q_aug, k_aug, v_aug, gains = project(pairs, place, x, tables)
    attended_0, q_back_0 = attend(q_aug, k_aug, v_aug, 0, 4)
    attended_1, q_back_1 = attend(q_aug, k_aug, v_aug, 4, 4)
    attended = (attended_0, attended_1)
    first_sum, normed_two, normed_two_t = output_rows(pieces, place, attended, x, gains)
    out, back, grads = feed(
        pieces, place, rows, slabs, normed_two, normed_two_t, back_out, False
    )
    total = lax.psum(scatter_all(grads), "rep").astype(F32).reshape(slabs, tall, 2 * SLAB)
    back_first, back_attended, grad_out = middle(
        pieces, place, first_sum, back_out, attended, gains, [back]
    )
    halves_0 = attend_back(q_back_0, k_aug, v_aug, attended_0, back_attended, 0, 4)
    halves_1 = attend_back(q_back_1, k_aug, v_aug, attended_1, back_attended, 4, 4)
    back_raw, own, sib = raw_back(
        parts, place, (halves_0[0], halves_1[0], halves_0[1], halves_1[1]), units, normed_one,
        tables[0], tables[1], gains, grad_out,
    )
    every = jnp.stack([own, sib], axis=1).reshape((parts,) + own.shape[1:])
    attn_grad = lax.psum(scatter_all(every), "rep").astype(F32)
    input_grad = input_back(pairs, place, back_raw, x, back_first, gains)

    def uncut(block):
        return block.reshape(slabs, rows, parts, seg).transpose(1, 2, 0, 3).reshape(rows, ff)

    feed_grads = (
        uncut(total[:, :rows, :SLAB]),
        uncut(total[:, :rows, SLAB:]),
        total[:, rows:, :].reshape(slabs * seg, x.shape[1]),
    )
    return (first_sum + out).astype(BF16), input_grad, attn_grad, feed_grads


def fence(outputs, *hops):
    found = tie(*outputs, *hops)
    return found[: len(outputs)], list(found[len(outputs) :])


def block_paired(me, place, x, back_out, tables, first_pack, w_output, w_gate, w_up, w_down):
    rows = w_gate.shape[0]
    chunks = (3, 3, 3)

    first = hop(first_pack, 2)
    second = hop(first_pack, 4)
    twin = hop(first_pack, 1)
    made, (first, second, twin) = fence(
        [*pack_rows(chunks, w_output, w_gate, w_up, w_down), *tables], first, second, twin
    )
    packs, tables = list(made[:3]), made[3:]
    corner_a = hop(second[:rows], 2)
    corner_b = hop(first[rows:], 4)
    far = [twin] + [hop(piece, 1) for piece in (first, second, corner_a, corner_b)]
    near = [first_pack, first, second, corner_a, corner_b]
    pairs = []
    for k in range(3):
        pairs += [(near[k], near[k], 1), (far[k], far[k], 1)]
    pairs += [(near[3], near[4], 0), (far[3], far[4], 0)]

    pack = after(packs[0], corner_a, corner_b)
    first, second, twin = hop(pack, 2), hop(pack, 4), hop(pack, 1)
    normed_one, *units, q_aug, k_aug, v_aug, gains = project(pairs, place, x, tables)
    (attended_0, q_back_0, k_aug), (first, second, twin) = fence(
        [*attend(q_aug, k_aug, v_aug, 0, 4), k_aug], first, second, twin
    )
    corner_a, corner_b = hop(second[:, :512], 2), hop(first[:, 512:], 4)
    far = [hop(first, 1), hop(second, 1)]
    packs[1] = after(packs[1], first, second)
    waiting = [hop(packs[1], bit) for bit in (1, 2, 4, 6)]
    (attended_1, q_back_1), (corner_a, corner_b, *far) = fence(
        attend(q_aug, k_aug, v_aug, 4, 4), corner_a, corner_b, *far
    )
    attended = (attended_0, attended_1)
    early = weave(
        [[pack], [first], [second], [corner_a, corner_b]],
        [[twin], [far[0]], [far[1]], [hop(corner_a, 1), hop(corner_b, 1)]],
    )
    first_sum, normed_two, normed_two_t = output_rows(early, place, attended, x, gains)

    def finish(pack, twin, first, second, corner):
        near = (first, second, corner)
        far = [hop(piece, 1) for piece in near]
        return weave([[pack]] + [[a] for a in near], [[twin]] + [[a] for a in far])

    def feed_step(pieces, begin, n, paired):
        return feed(pieces, place, begin, n, normed_two, normed_two_t, back_out, paired)

    (out_0, back_0, own_0, sib_0, normed_two), waiting = fence(
        [*feed_step(early, rows, chunks[0], True), normed_two], *waiting
    )
    later = finish(packs[1], *waiting)
    waiting = [hop(packs[2], bit) for bit in (1, 2, 4, 6)]
    other_0 = hop(after(sib_0, *later.arrays), 1)
    (out_1, back_1, own_1, sib_1, normed_two), (other_0, *waiting) = fence(
        [*feed_step(later, 0, chunks[1], True), normed_two], other_0, *waiting
    )
    last = finish(packs[2], *waiting)
    other_1 = hop(sib_1, 1)
    moved_0 = hop(combine([(own_0, 3), (other_0, 3)]), 2)
    normed_two, other_1 = tie(normed_two, other_1)
    term = combine([(own_1, 3), (other_1, 3)])
    normed_two, term = tie(normed_two, term)
    moved_1 = hop(term, 4)
    (out_2, back_2, own_2, sib_2), (moved_0, moved_1) = fence(
        feed_step(last, 0, chunks[2], True), moved_0, moved_1
    )
    other_2 = hop(sib_2, 1)
    one, two, three, four = combine(
        [(own_0, 1), (other_0, 1)],
        [(own_0, 2), (other_0, 2), moved_0],
        [(own_1, 1), (other_1, 1), moved_1],
        [(own_1, 2), (other_1, 2)],
    )
    back_2, one, two, three, four = tie(back_2, one, two, three, four)
    first_0, second_0 = hop(one, 2), hop(two, 4)
    first_1, second_1 = hop(three, 2), hop(four, 4)
    middles = middle(
        early, place, first_sum, back_out, attended, gains, [back_0, back_1, back_2]
    )
    (back_first, back_attended, grad_out), (other_2,) = fence(middles, other_2)
    term = combine([(own_2, 3), (other_2, 3)])
    back_attended, term = tie(back_attended, term)
    moved_2 = hop(term, 2)
    halves = attend_back(q_back_0, k_aug, v_aug, attended_0, back_attended, 0, 4)
    (dq_0, dkv_0, back_attended), (first_0, second_0) = fence(
        [*halves, back_attended], first_0, second_0
    )
    grads_0 = combine([(own_0, 0), (other_0, 0), first_0, second_0])
    back_attended, grads_0 = tie(back_attended, grads_0)
    inward_0 = rep_hop(grads_0, INWARD)
    halves = attend_back(q_back_1, k_aug, v_aug, attended_1, back_attended, 4, 4)
    (dq_1, dkv_1), (moved_2, inward_0, first_1, second_1) = fence(
        halves, moved_2, inward_0, first_1, second_1
    )
    one, two, grads_1, half_0 = combine(
        [(own_2, 1), (other_2, 1)],
        [(own_2, 2), (other_2, 2), moved_2],
        [(own_1, 0), (other_1, 0), first_1, second_1],
        [grads_0, inward_0],
    )
    dq_1, one, two, grads_1, half_0 = tie(dq_1, one, two, grads_1, half_0)
    first_2, second_2 = hop(one, 2), hop(two, 4)
    inward_1 = rep_hop(grads_1, INWARD)
    across_0 = rep_hop(half_0, ACROSS)
    result = raw_back(
        8, place, (dq_0, dq_1, dkv_0, dkv_1), units, normed_one, tables[0], tables[1], gains,
        grad_out,
    )
    (back_raw, own, sib), (first_2, second_2, inward_1, across_0) = fence(
        result, first_2, second_2, inward_1, across_0
    )
    other = hop(sib, 1)
    half_1, total_0, grads_2 = combine(
        [grads_1, inward_1], [half_0, across_0], [(own_2, 0), (other_2, 0), first_2, second_2]
    )
    back_raw, other, half_1, total_0, grads_2 = tie(back_raw, other, half_1, total_0, grads_2)
    term = combine([(own, 3), (other, 3)])
    back_raw, term = tie(back_raw, term)
    moved = hop(term, 4)
    outward_0 = rep_hop(total_0, OUTWARD)
    across_1 = rep_hop(half_1, ACROSS)
    inward_2 = rep_hop(grads_2, INWARD)
    input_grad = input_back(pairs, place, back_raw, x, back_first, gains)
    (input_grad,), (moved,) = fence([input_grad], moved)
    one, two = combine([(own, 1), (other, 1), moved], [(own, 2), (other, 2)])
    one, two, across_1, inward_2, first_sum = tie(one, two, across_1, inward_2, first_sum)
    first, second = hop(one, 2), hop(two, 4)
    total_1, half_2 = combine([half_1, across_1], [grads_2, inward_2])
    first_sum, total_1, half_2, outward_0 = tie(first_sum, total_1, half_2, outward_0)
    outward_1 = rep_hop(total_1, OUTWARD)
    across_2 = rep_hop(half_2, ACROSS)
    outs = out_0.astype(F32) + out_1.astype(F32) + out_2.astype(F32)
    block_output = (first_sum + outs).astype(BF16)
    (block_output,), (first, second) = fence([block_output], first, second)
    grads = combine([(own, 0), (other, 0), first, second])
    inward = rep_hop(grads, INWARD)
    across_2, _ = tie(across_2, grads)
    total_2 = combine([half_2, across_2])
    outward_2 = rep_hop(total_2, OUTWARD)
    inward, outward_1, _ = tie(inward, outward_1, total_2)
    half = combine([grads, inward])
    across = rep_hop(half, ACROSS)
    outward_2, across, _ = tie(outward_2, across, half)
    total = combine([half, across])
    outward = rep_hop(total, OUTWARD)
    total, outward_2 = tie(total, outward_2)
    spot = lax.axis_index("rep")
    flag = ((spot == 0) | (spot == 3)).astype(jnp.int32).reshape(1)
    feed_grads = unpack_rows(flag, total_0, outward_0, total_1, outward_1, total_2, outward_2)
    (*feed_grads,), (outward,) = fence(feed_grads, outward)
    return block_output, input_grad, at_end(total.astype(F32), outward), feed_grads


def solution(mesh):
    sizes = (mesh.shape["rep"], mesh.shape["shard"])
    whole = P(("rep", "shard"), None, None)
    matrix = P("shard", None)
    vector = P("shard")
    in_specs = (
        whole, P(("rep", "shard"), None), vector, matrix, matrix, matrix, vector, vector, matrix,
        vector, matrix, matrix, matrix, whole,
    )
    out_specs = (
        whole, whole, vector, matrix, matrix, matrix, vector, vector, matrix, vector, matrix,
        matrix, matrix,
    )
    return jax.shard_map(
        lambda *arrays: on_device(sizes, *arrays),
        mesh=mesh,
        in_specs=in_specs,
        out_specs=out_specs,
        check_vma=False,
    )
```

```python
import jax
import jax.numpy as jnp
from jax import lax
from jax.experimental import pallas as pl
from jax.experimental.pallas import tpu as pltpu
from jax.sharding import PartitionSpec as P

QUERY_HEADS = 16
KEY_VALUE_HEADS = 8
HEAD_SIZE = 64
EPS = 1e-05
ROPE_BASE = 1000000.0
FAR = 32768.0
TILE = 256
SLAB = 512
VMEM_LIMIT = 60 * 1024 * 1024
NT = ((1,), (1,))
NN = ((1,), (0,))
TN = ((0,), (0,))
BF16 = jnp.bfloat16
F32 = jnp.float32
SMALL = pl.BlockSpec(memory_space=pltpu.SMEM)


def dot(left, right, dims=NN):
    return lax.dot_general(left, right, (dims, ((), ())), preferred_element_type=F32)


def params():
    return pltpu.CompilerParams(vmem_limit_bytes=VMEM_LIMIT)


def cost(giga_flops, mega_bytes, exps=0):
    return pl.CostEstimate(
        flops=int(giga_flops * 10**6),
        bytes_accessed=int(mega_bytes * 10**3),
        transcendentals=exps // 1000,
    )


def fixed(shape, where=None):
    index = (0,) * len(shape) if where is None else where
    return pl.BlockSpec(shape, lambda *_: index, pipeline_mode=pl.Buffered(1))


def by_rows(width, rows=TILE):
    return pl.BlockSpec((rows, width), lambda i: (i, 0))


class Pieces:
    def __init__(self, groups=None, stacked=None):
        self.stacked = stacked
        self.count = len(groups) if stacked is None else stacked.shape[0]
        self.groups = groups if stacked is None else [[stacked]] * self.count
        self.arrays = [array for group in self.groups for array in group]
        self.layout = [len(group) for group in self.groups]

    def specs(self, rows, start):
        once = pl.Buffered(1) if start(0) == start(1) else None
        found = []
        for k, group in enumerate(self.groups):
            for array in group:
                shape = (pl.Element(rows), pl.Element(array.shape[-1]))
                if self.stacked is None:
                    found.append(
                        pl.BlockSpec(shape, lambda i: (start(i), 0), pipeline_mode=once)
                    )
                else:
                    found.append(
                        pl.BlockSpec(
                            (pl.Squeezed(),) + shape,
                            lambda i, k=k: (k, start(i), 0),
                            pipeline_mode=once,
                        )
                    )
        return found


def grouped(refs, layout):
    groups, at = [], 0
    for size in layout:
        groups.append(refs[at : at + size])
        at += size
    return groups


def fill(target, at, group, rows):
    left = 0
    for ref in group:
        right = left + ref.shape[1]
        target[at, left:right] = ref[rows, :]
        left = right


def split3(value):
    high = value.astype(BF16).astype(F32)
    rest = value - high
    middle = rest.astype(BF16).astype(F32)
    return high, middle, rest - middle


def aligned(index, rows):
    return pl.ds(pl.multiple_of(index * rows, rows), rows)


def unit_of(rows):
    inverse = lax.rsqrt(jnp.mean(rows * rows, axis=-1, keepdims=True) + EPS)
    return rows * inverse, inverse


def head_blocks():
    first = lax.broadcasted_iota(jnp.int32, (128, 128), 0) // HEAD_SIZE
    second = lax.broadcasted_iota(jnp.int32, (128, 128), 1) // HEAD_SIZE
    return (first == second).astype(BF16)


def head_mean(rows, blocks):
    return dot(rows.astype(BF16), blocks) * (1.0 / HEAD_SIZE)


def swap_halves(rows, first):
    return jnp.where(first, pltpu.roll(rows, 96, 1), pltpu.roll(rows, 32, 1))


def lanes(rows=TILE):
    return lax.broadcasted_iota(jnp.int32, (rows, 128), 1)


def load_pairs(parts, me_ref, refs, w_all):
    rows = w_all.shape[0] // parts

    @pl.when(pl.program_id(0) == 0)
    def _():
        for k in range(parts):
            at = aligned(me_ref[0] ^ k, rows)
            w_all[at, :1024] = refs[2 * k][...]
            w_all[at, 1024:] = refs[2 * k + 1][...]


def pair_specs(pieces, rows):
    arrays, specs = [], []
    for piece in pieces:
        left, right, at = piece
        arrays += [left, right]
        specs += [fixed((rows, 1024)), fixed((rows, 1024), (at, 0))]
    return arrays, specs


def project_kernel(parts, me_ref, x_ref, cos_ref, sin_ref, qx_ref, kx_ref, *refs):
    gain_refs = refs[2 * parts : 3 * parts]
    n_ref, unit_ref, scale_ref, q_ref, k_ref, v_ref, gain_ref, w_all = refs[3 * parts :]
    load_pairs(parts, me_ref, refs, w_all)

    @pl.when(pl.program_id(0) == 0)
    def _():
        total = gain_refs[0][...].astype(F32)
        for ref in gain_refs[1:]:
            total = total + ref[...].astype(F32)
        gain_ref[...] = total

    unit, _ = unit_of(x_ref[...].astype(F32))
    normed = (unit * gain_ref[0:1, :]).astype(BF16)
    n_ref[...] = normed
    raw = dot(normed, w_all[...])
    blocks = head_blocks()
    lane = lanes()
    first = (lane % HEAD_SIZE) < HEAD_SIZE // 2
    low = lane < HEAD_SIZE
    cosine, sine = cos_ref[...], sin_ref[...]
    for p in range(12):
        at = slice(p * 128, (p + 1) * 128)
        rows_in = raw[:, at]
        inverse = lax.rsqrt(head_mean(rows_in * rows_in, blocks) + EPS)
        unit = rows_in * inverse
        unit_ref[:, at] = unit.astype(BF16)
        scale_ref[:, at] = inverse.astype(BF16)
        scaled = unit * gain_ref[1 + p // 8 : 2 + p // 8, :128]
        turned = scaled * cosine + swap_halves(scaled, first) * sine
        if p < 8:
            turned = turned * HEAD_SIZE**-0.5
            out, more, at = q_ref, qx_ref[...], 2 * p
        else:
            out, more, at = k_ref, kx_ref[...], 2 * (p - 8)
        out[at] = jnp.where(low, turned, more).astype(BF16)
        out[at + 1] = jnp.where(low, pltpu.roll(turned, 64, 1), more).astype(BF16)
    more = ((lane >= 64) & (lane < 67)).astype(F32)
    for p in range(4):
        rows_in = raw[:, 1536 + p * 128 : 1664 + p * 128]
        v_ref[2 * p] = jnp.where(low, rows_in, more).astype(BF16)
        v_ref[2 * p + 1] = jnp.where(low, pltpu.roll(rows_in, 64, 1), more).astype(BF16)


def project(pieces, me, x, tables):
    length, width = x.shape
    parts = len(pieces)
    rows = width // parts
    arrays, specs = pair_specs(pieces, rows)
    gains = [(piece[1], (piece[2] + 1) * rows // 16) for piece in pieces]

    def heads(count):
        return pl.BlockSpec((count, TILE, 128), lambda i: (0, i, 0))

    return pl.pallas_call(
        lambda *refs: project_kernel(parts, *refs),
        grid=(length // TILE,),
        in_specs=[SMALL, by_rows(width)]
        + [by_rows(128)] * 4
        + specs
        + [fixed((16, 1024), (at, 0)) for _, at in gains],
        out_specs=[by_rows(width), by_rows(1536), by_rows(1536), heads(16), heads(8), heads(8)]
        + [fixed((16, 1024))],
        out_shape=[
            jax.ShapeDtypeStruct((length, width), BF16),
            jax.ShapeDtypeStruct((length, 1536), BF16),
            jax.ShapeDtypeStruct((length, 1536), BF16),
            jax.ShapeDtypeStruct((16, length, 128), BF16),
            jax.ShapeDtypeStruct((8, length, 128), BF16),
            jax.ShapeDtypeStruct((8, length, 128), BF16),
            jax.ShapeDtypeStruct((16, 1024), F32),
        ],
        scratch_shapes=[pltpu.VMEM((width, 2048), BF16)],
        compiler_params=params(),
        cost_estimate=cost(8, 25),
        name="project",
    )(me, x, *tables, *arrays, *[array for array, _ in gains])


def causal(query_axis):
    first = lax.broadcasted_iota(jnp.int32, (TILE, TILE), 0)
    second = lax.broadcasted_iota(jnp.int32, (TILE, TILE), 1)
    return (first >= second) if query_axis == 0 else (second >= first)


def attend_kernel(q_ref, k_ref, v_ref, o_ref, qb_ref):
    tiles = q_ref.shape[1] // TILE
    keep = causal(0)
    lane = lax.broadcasted_iota(jnp.int32, (TILE, 128), 1)
    for i in range(tiles):
        rows = slice(i * TILE, (i + 1) * TILE)
        before = slice(0, i * TILE)
        halves = []
        for h in range(2):
            q = q_ref[h, rows, :]
            weights = jnp.where(keep, jnp.exp(dot(q, k_ref[0, rows, :], NT)), 0.0)
            out = dot(weights.astype(BF16), v_ref[0, rows, :])
            if i:
                weights = jnp.exp(dot(q, k_ref[0, before, :], NT)).astype(BF16)
                out = out + dot(weights, v_ref[0, before, :])
            total = out[:, 64:65]
            halves.append(out / total)
            high, middle, low = split3(-jnp.log(total))
            extra = jnp.where(
                lane == 68, high, jnp.where(lane == 69, middle, jnp.where(lane == 70, low, 0.0))
            )
            qb_ref[h, rows, :] = (q.astype(F32) + extra).astype(BF16)
        both = jnp.where(lane < 64, halves[0], pltpu.roll(halves[1], 64, 1))
        o_ref[rows, :] = both.astype(BF16)


def attend(q_aug, k_aug, v_aug, begin, groups):
    _, length, _ = q_aug.shape
    return pl.pallas_call(
        attend_kernel,
        grid=(groups,),
        in_specs=[
            pl.BlockSpec((2, length, 128), lambda g: (g + begin, 0, 0)),
            pl.BlockSpec((1, length, 128), lambda g: (g + begin, 0, 0)),
            pl.BlockSpec((1, length, 128), lambda g: (g + begin, 0, 0)),
        ],
        out_specs=[
            pl.BlockSpec((length, 128), lambda g: (0, g)),
            pl.BlockSpec((2, length, 128), lambda g: (g, 0, 0)),
        ],
        out_shape=[
            jax.ShapeDtypeStruct((length, groups * 128), BF16),
            jax.ShapeDtypeStruct((2 * groups, length, 128), BF16),
        ],
        compiler_params=params(),
        cost_estimate=cost(2.5 * groups, 2 * groups, groups * 2**20),
        name="attend",
    )(q_aug, k_aug, v_aug)


def attend_back_kernel(q_ref, k_ref, v_ref, o_ref, do_ref, dq_ref, dkv_ref, do_aug, k_t, dq_t):
    length = q_ref.shape[1]
    tiles = length // TILE
    keep = causal(1)
    lane = lax.broadcasted_iota(jnp.int32, (length, 128), 1)
    back = do_ref[...].astype(F32)
    product = back * o_ref[...].astype(F32)
    for h in range(2):
        own = (lane < 64) if h == 0 else (lane >= 64)
        centre = jnp.sum(jnp.where(own, product, 0.0), axis=1, keepdims=True)
        moved = back if h == 0 else pltpu.roll(back, 64, 1)
        high, middle, low = split3(-centre)
        extra = jnp.where(
            lane == 64, high, jnp.where(lane == 65, middle, jnp.where(lane == 66, low, 0.0))
        )
        do_aug[h] = jnp.where(lane < 64, moved, extra).astype(BF16)
    k_t[...] = k_ref[0].astype(F32).T[:64, :].astype(BF16)
    low_half = lax.broadcasted_iota(jnp.int32, (TILE, 128), 1) < 64
    for j in range(tiles):
        cols = slice(j * TILE, (j + 1) * TILE)
        k = k_ref[0, cols, :]
        v = v_ref[0, cols, :]
        dk = 0.0
        dv = 0.0
        for i, stop in ((j, j + 1), (j + 1, tiles)):
            if i == tiles:
                continue
            rows = slice(i * TILE, stop * TILE)
            for h in range(2):
                q = q_ref[h, rows, :]
                do = do_aug[h, rows, :]
                probs = jnp.exp(dot(k, q, NT))
                if i == j:
                    probs = jnp.where(keep, probs, 0.0)
                scores = (probs * dot(v, do, NT)).astype(BF16)
                dv = dv + dot(probs.astype(BF16), do)
                dk = dk + dot(scores, q)
                to_q = dot(k_t[:, cols], scores)
                if j == 0:
                    dq_t[h * 64 : (h + 1) * 64, rows] = to_q
                else:
                    dq_t[h * 64 : (h + 1) * 64, rows] += to_q
        dkv_ref[cols, :] = jnp.where(low_half, dk, pltpu.roll(dv, 64, 1))
    dq_ref[...] = dq_t[...].T


def attend_back(q_back, k_aug, v_aug, attended, back_attended, begin, groups):
    _, length, _ = q_back.shape
    by_group = pl.BlockSpec((length, 128), lambda g: (0, g + begin))
    out_group = pl.BlockSpec((length, 128), lambda g: (0, g))
    return pl.pallas_call(
        attend_back_kernel,
        grid=(groups,),
        in_specs=[
            pl.BlockSpec((2, length, 128), lambda g: (g, 0, 0)),
            pl.BlockSpec((1, length, 128), lambda g: (g + begin, 0, 0)),
            pl.BlockSpec((1, length, 128), lambda g: (g + begin, 0, 0)),
            out_group,
            by_group,
        ],
        out_specs=[out_group, out_group],
        out_shape=[jax.ShapeDtypeStruct((length, groups * 128), F32)] * 2,
        scratch_shapes=[
            pltpu.VMEM((2, length, 128), BF16),
            pltpu.VMEM((64, length), BF16),
            pltpu.VMEM((128, length), F32),
        ],
        compiler_params=params(),
        cost_estimate=cost(5 * groups, 3 * groups, groups * 2**20),
        name="attend_back",
    )(q_back, k_aug, v_aug, attended, back_attended)


def output_kernel(layout, me_ref, o0_ref, o1_ref, x_ref, gain_ref, *refs):
    sum_ref, n_ref, nt_ref, w_all = refs[-4:]
    rows = w_all.shape[0] // len(layout)

    @pl.when(pl.program_id(0) == 0)
    def _():
        for k, group in enumerate(grouped(refs, layout)):
            fill(w_all, aligned(me_ref[0] ^ k, rows), group, slice(None))

    total = x_ref[...].astype(F32) + dot(o0_ref[...], w_all[:512, :])
    total = total + dot(o1_ref[...], w_all[512:, :])
    sum_ref[...] = total
    unit, _ = unit_of(total)
    normed = unit * gain_ref[3:4, :]
    n_ref[...] = normed.astype(BF16)
    nt_ref[...] = normed.T.astype(BF16)


def output_rows(pieces, me, attended, x, gain):
    length, width = x.shape
    parts = pieces.count
    rows = width // parts
    return pl.pallas_call(
        lambda *refs: output_kernel(pieces.layout, *refs),
        grid=(length // TILE,),
        in_specs=[SMALL, by_rows(512), by_rows(512), by_rows(width), fixed((16, 1024))]
        + pieces.specs(rows, lambda i: 0),
        out_specs=[by_rows(width), by_rows(width), pl.BlockSpec((width, TILE), lambda i: (0, i))],
        out_shape=[
            jax.ShapeDtypeStruct((length, width), F32),
            jax.ShapeDtypeStruct((length, width), BF16),
            jax.ShapeDtypeStruct((width, length), BF16),
        ],
        scratch_shapes=[pltpu.VMEM((1024, width), BF16)],
        compiler_params=params(),
        cost_estimate=cost(5, 15),
        name="output_rows",
    )(me, *attended, x, gain, *pieces.arrays)


def scatter_rows(me, parts, value, rows, own_ref, sib_ref, at):
    half = me >> 1
    core = me & 1
    for q in range(parts // 2):
        for s, ref in enumerate((own_ref, sib_ref)):
            source = 2 * q + (core ^ s)
            ref[q ^ half, at : at + rows, :] = value[aligned(source, rows), :]


def feed_kernel(layout, paired, me_ref, n_ref, nt_ref, c_ref, *refs):
    parts = len(layout)
    f_ref, b_ref, *grad_refs = refs[sum(layout) : -8]
    w_all, d_all, back, hidden, w_grad, d_grad, f_sum, b_sum = refs[-8:]
    me = me_ref[0]
    rows = w_all.shape[0] // parts
    seg = SLAB // parts
    for k, group in enumerate(grouped(refs, layout)):
        fill(w_all, aligned(me ^ k, rows), group, slice(0, rows))
        fill(d_all, aligned(me ^ k, seg), group, slice(rows, rows + seg))
    step = pl.program_id(0)

    @pl.when(step == 0)
    def _():
        f_sum[...] = jnp.zeros_like(f_sum)
        b_sum[...] = jnp.zeros_like(b_sum)

    both = dot(n_ref[...], w_all[...])
    gate = both[:, :SLAB]
    up = both[:, SLAB:]
    sig = 1.0 / (1.0 + jnp.exp(-gate))
    swish = gate * sig
    hidden[...] = (swish * up).astype(BF16)
    back_hidden = dot(c_ref[...], d_all[...], NT)
    back[:, SLAB:] = (back_hidden * swish).astype(BF16)
    back[:, :SLAB] = (back_hidden * up * sig * (1.0 + gate * (1.0 - sig))).astype(BF16)
    f_sum[...] += dot(hidden[...], d_all[...])
    b_sum[...] += dot(back[...], w_all[...], NT)
    w_grad[...] = dot(nt_ref[...], back[...]).astype(BF16)
    d_grad[...] = dot(hidden[...], c_ref[...], TN).astype(BF16)

    @pl.when(step == pl.num_programs(0) - 1)
    def _():
        f_ref[...] = f_sum[...].astype(BF16)
        b_ref[...] = b_sum[...].astype(BF16)

    if paired:
        own_ref, sib_ref = grad_refs
        scatter_rows(me, parts, w_grad, rows, own_ref, sib_ref, 0)
        scatter_rows(me, parts, d_grad, seg, own_ref, sib_ref, rows)
    else:
        for d in range(parts):
            grad_refs[0][d, :rows, :] = w_grad[d * rows : (d + 1) * rows, :]
            grad_refs[0][d, rows:, :] = d_grad[d * seg : (d + 1) * seg, :]


def feed(pieces, me, begin, slabs, normed, normed_t, cotangent, paired):
    length, width = normed.shape
    parts = pieces.count
    rows = width // parts + SLAB // parts
    depth = parts // 2 if paired else parts
    count = 2 if paired else 1
    grads = pl.BlockSpec((depth, rows, 2 * SLAB), lambda i: (0, i, 0))
    return pl.pallas_call(
        lambda *refs: feed_kernel(pieces.layout, paired, *refs),
        grid=(slabs,),
        in_specs=[SMALL, fixed((length, width)), fixed((width, length)), fixed((length, width))]
        + pieces.specs(rows, lambda i: (begin // 16 + i * (rows // 16)) * 16),
        out_specs=[fixed((length, width)), fixed((length, width))] + [grads] * count,
        out_shape=[
            jax.ShapeDtypeStruct((length, width), BF16),
            jax.ShapeDtypeStruct((length, width), BF16),
        ]
        + [jax.ShapeDtypeStruct((depth, slabs * rows, 2 * SLAB), BF16)] * count,
        scratch_shapes=[
            pltpu.VMEM((width, 2 * SLAB), BF16),
            pltpu.VMEM((SLAB, width), BF16),
            pltpu.VMEM((length, 2 * SLAB), BF16),
            pltpu.VMEM((length, SLAB), BF16),
            pltpu.VMEM((width, 2 * SLAB), BF16),
            pltpu.VMEM((SLAB, width), BF16),
            pltpu.VMEM((length, width), F32),
            pltpu.VMEM((length, width), F32),
        ],
        compiler_params=params(),
        cost_estimate=cost(12.5 * slabs, 20 + 6 * slabs),
        name="feed",
    )(me, normed, normed_t, cotangent, *pieces.arrays)


def middle_kernel(layout, sums, me_ref, s_ref, c_ref, o0_ref, o1_ref, gain_ref, *refs):
    b_refs = refs[:sums]
    f_ref, a_ref, g_ref, w_all, total = refs[-5:]
    rows = w_all.shape[0] // len(layout)
    step = pl.program_id(0)

    @pl.when(step == 0)
    def _():
        for k, group in enumerate(grouped(refs[sums:], layout)):
            fill(w_all, aligned(me_ref[0] ^ k, rows), group, slice(None))

    back = b_refs[0][...].astype(F32)
    for ref in b_refs[1:]:
        back = back + ref[...].astype(F32)
    unit, inverse = unit_of(s_ref[...])
    scaled = back * gain_ref[3:4, :]
    first = c_ref[...].astype(F32) + inverse * (
        scaled - unit * jnp.mean(scaled * unit, axis=-1, keepdims=True)
    )
    f_ref[...] = first
    short = first.astype(BF16)
    a_ref[...] = dot(short, w_all[...], NT).astype(BF16)
    grads = [dot(ref[...], short, TN) for ref in (o0_ref, o1_ref)]

    @pl.when(step == 0)
    def _():
        total[:512, :] = grads[0]
        total[512:, :] = grads[1]

    @pl.when(step > 0)
    def _():
        total[:512, :] += grads[0]
        total[512:, :] += grads[1]

    @pl.when(step == pl.num_programs(0) - 1)
    def _():
        g_ref[...] = total[...].astype(BF16)


def middle(pieces, me, first_sum, cotangent, attended, gain, backs):
    length, width = first_sum.shape
    parts = pieces.count
    rows = width // parts
    return pl.pallas_call(
        lambda *refs: middle_kernel(pieces.layout, len(backs), *refs),
        grid=(length // TILE,),
        in_specs=[SMALL, by_rows(width), by_rows(width), by_rows(512), by_rows(512), fixed((16, 1024))]
        + [by_rows(width)] * len(backs)
        + pieces.specs(rows, lambda i: 0),
        out_specs=[by_rows(width), by_rows(1024), fixed((1024, width))],
        out_shape=[
            jax.ShapeDtypeStruct((length, width), F32),
            jax.ShapeDtypeStruct((length, 1024), BF16),
            jax.ShapeDtypeStruct((1024, width), BF16),
        ],
        scratch_shapes=[pltpu.VMEM((1024, width), BF16), pltpu.VMEM((1024, width), F32)],
        compiler_params=params(),
        cost_estimate=cost(9, 32),
        name="middle",
    )(me, first_sum, cotangent, *attended, gain, *backs, *pieces.arrays)


def raw_back_kernel(
    parts, me_ref, dq0_ref, dq1_ref, dkv0_ref, dkv1_ref, unit_ref, scale_ref, n_ref, cos_ref, sin_ref, gain_ref, wo_ref,
    b_ref, own_ref, sib_ref, total, gains,
):
    step = pl.program_id(0)
    rows = total.shape[0] // parts
    blocks = head_blocks()
    lane = lanes()
    first = (lane % HEAD_SIZE) < HEAD_SIZE // 2
    low = lane < HEAD_SIZE
    cosine, sine = cos_ref[...], sin_ref[...]
    sums = [None, None]
    for p in range(12):
        at = slice(p * 128, (p + 1) * 128)
        if p < 8:
            dq_ref = dq0_ref if p < 4 else dq1_ref
            grads = dq_ref[:, (p % 4) * 128 : (p % 4 + 1) * 128] * HEAD_SIZE**-0.5
        else:
            dkv_ref = dkv0_ref if p < 10 else dkv1_ref
            left = dkv_ref[:, (p % 2) * 256 : (p % 2) * 256 + 128]
            right = dkv_ref[:, (p % 2) * 256 + 128 : (p % 2) * 256 + 256]
            grads = jnp.where(low, left, pltpu.roll(right, 64, 1))
            values = jnp.where(low, pltpu.roll(left, 64, 1), right)
            b_ref[:, 512 + p * 128 : 640 + p * 128] = values.astype(BF16)
        turned = grads * cosine + swap_halves(grads * sine, first)
        unit = unit_ref[:, at].astype(F32)
        inverse = scale_ref[:, at].astype(F32)
        kind = 0 if p < 8 else 1
        part = jnp.sum(turned * unit, axis=0, keepdims=True)
        sums[kind] = part if sums[kind] is None else sums[kind] + part
        scaled = turned * gain_ref[1 + kind : 2 + kind, :128]
        b_ref[:, at] = (inverse * (scaled - unit * head_mean(scaled * unit, blocks))).astype(BF16)
    grad = dot(n_ref[...], b_ref[...], TN)

    @pl.when(step == 0)
    def _():
        total[...] = grad
        gains[...] = jnp.zeros_like(gains)

    @pl.when(step > 0)
    def _():
        total[...] += grad

    gains[0:1, :] += sums[0]
    gains[1:2, :] += sums[1]

    @pl.when(step == pl.num_programs(0) - 1)
    def _():
        me = me_ref[0]
        half = me >> 1
        core = me & 1
        more = gains[...].astype(BF16)
        for q in range(parts // 2):
            for s, ref in enumerate((own_ref, sib_ref)):
                source = aligned(2 * q + (core ^ s), rows)
                block = total[source, :].astype(BF16)
                ref[q ^ half, :rows, :] = block[:, :1024]
                ref[q ^ half, rows : 2 * rows, :] = block[:, 1024:]
                ref[q ^ half, 2 * rows : 3 * rows, :] = wo_ref[source, :]
                ref[q ^ half, 3 * rows :, :] = jnp.zeros((32, 1024), BF16)
                ref[q ^ half, 3 * rows :, :128] = more


def raw_back(parts, me, halves, units, normed, cosine, sine, gains, grad_out):
    length, width = normed.shape
    rows = 3 * (width // parts) + 32
    grads = fixed((parts // 2, rows, 1024))
    return pl.pallas_call(
        lambda *refs: raw_back_kernel(parts, *refs),
        grid=(length // TILE,),
        in_specs=[SMALL] + [by_rows(512)] * 4 + [by_rows(1536)] * 2 + [by_rows(width)]
        + [by_rows(128)] * 2
        + [fixed((16, 1024)), fixed((1024, width))],
        out_specs=[by_rows(2048), grads, grads],
        out_shape=[jax.ShapeDtypeStruct((length, 2048), BF16)]
        + [jax.ShapeDtypeStruct((parts // 2, rows, 1024), BF16)] * 2,
        scratch_shapes=[pltpu.VMEM((width, 2048), F32), pltpu.VMEM((32, 128), F32)],
        compiler_params=params(),
        cost_estimate=cost(10, 30),
        name="raw_back",
    )(me, *halves, *units, normed, cosine, sine, gains, grad_out)


def input_kernel(parts, me_ref, b_ref, x_ref, f_ref, gain_ref, *refs):
    out_ref, w_all = refs[2 * parts :]
    load_pairs(parts, me_ref, refs, w_all)
    unit, inverse = unit_of(x_ref[...].astype(F32))
    scaled = dot(b_ref[...], w_all[...], NT) * gain_ref[0:1, :]
    out_ref[...] = f_ref[...] + inverse * (
        scaled - unit * jnp.mean(scaled * unit, axis=-1, keepdims=True)
    )


def input_back(pieces, me, back_raw, x, back_first, gain):
    length, width = x.shape
    parts = len(pieces)
    arrays, specs = pair_specs(pieces, width // parts)
    return pl.pallas_call(
        lambda *refs: input_kernel(parts, *refs),
        grid=(length // TILE,),
        in_specs=[SMALL, by_rows(2048), by_rows(width), by_rows(width), fixed((16, 1024))] + specs,
        out_specs=by_rows(width),
        out_shape=jax.ShapeDtypeStruct((length, width), F32),
        scratch_shapes=[pltpu.VMEM((width, 2048), BF16)],
        compiler_params=params(),
        cost_estimate=cost(6, 18),
        name="input_back",
    )(me, back_raw, x, back_first, gain, *arrays)


def tables_of(numbers):
    length = numbers.shape[0]
    indices = jnp.arange(length, dtype=jnp.int32)
    starts = jnp.concatenate([jnp.ones((1,), dtype=bool), numbers[1:] != numbers[:-1]])
    begins = lax.cummax(jnp.where(starts, indices, jnp.zeros_like(numbers)), axis=0)
    offsets = (indices - begins).astype(F32).reshape(length, 1)
    frequency = ROPE_BASE ** (-jnp.arange(0, HEAD_SIZE, 2).astype(F32) / HEAD_SIZE)
    angles = offsets * frequency
    cosine = jnp.cos(angles)
    sine = jnp.sin(angles)
    same = (numbers[:, None] == jnp.arange(4)[None]).astype(F32)
    empty = jnp.zeros((length, 64), F32)
    return (
        jnp.concatenate([cosine] * 4, axis=1),
        jnp.concatenate([-sine, sine, -sine, sine], axis=1),
        jnp.concatenate([empty, -FAR * same, empty[:, :60]], axis=1),
        jnp.concatenate([empty, 1 - same, jnp.ones((length, 3)), empty[:, :57]], axis=1),
    )


def pack_kernel(chunks, o_ref, gate_ref, up_ref, down_ref, *out_refs):
    low = lanes(128) < 64
    out_refs[0][:128, :] = o_ref[...]
    places = [(c, i) for c, n in enumerate(chunks) for i in range(n)]
    for t, (c, i) in enumerate(places):
        row = i * 192 + (0 if c else 128)
        for side, ref in enumerate((gate_ref, up_ref)):
            for e in range(4):
                left, right = (18 * e + t) // 2, (18 * e + 9 + t) // 2
                a = ref[:, left * 128 : left * 128 + 128].astype(F32)
                b = ref[:, right * 128 : right * 128 + 128].astype(F32)
                both = pltpu.roll(jnp.where(low, b, a), 64, 1) if t % 2 else jnp.where(low, a, b)
                at = side * SLAB + e * 128
                out_refs[c][row : row + 128, at : at + 128] = both.astype(BF16)
        out_refs[c][row + 128 : row + 192, :] = down_ref[t * 64 : t * 64 + 64, :]


def pack_rows(chunks, w_output, w_gate, w_up, w_down):
    return pl.pallas_call(
        lambda *refs: pack_kernel(chunks, *refs),
        out_shape=[
            jax.ShapeDtypeStruct((n * 192 + (0 if c else 128), 1024), BF16)
            for c, n in enumerate(chunks)
        ],
        compiler_params=params(),
        cost_estimate=cost(0, 7),
        name="pack_rows",
    )(w_output, w_gate, w_up, w_down)


def unpack_kernel(flag_ref, *refs):
    *in_refs, gate_ref, up_ref, down_ref = refs
    low = lanes(128) < 64
    outer = flag_ref[0] > 0

    def rows_of(at, size, columns):
        for inside, outside in zip(in_refs[::2], in_refs[1::2]):
            if at < inside.shape[0]:
                one = inside[at : at + size, columns].astype(F32)
                return jnp.where(outer, outside[at : at + size, columns].astype(F32), one)
            at -= inside.shape[0]

    def segment(side, s, half):
        d = s // 9
        at = side * SLAB + (d // 2) * 128
        tile = rows_of((s % 9) * 192, 128, slice(at, at + 128))
        return tile if d % 2 == half else pltpu.roll(tile, 64, 1)

    for side, out in enumerate((gate_ref, up_ref)):
        for m in range(36):
            out[:, m * 128 : m * 128 + 128] = jnp.where(
                low, segment(side, 2 * m, 0), segment(side, 2 * m + 1, 1)
            )
    for t in range(9):
        down_ref[t * 64 : t * 64 + 64, :] = rows_of(t * 192 + 128, 64, slice(None))


def unpack_rows(flag, *totals):
    whole = pl.BlockSpec(memory_space=pltpu.VMEM)
    return pl.pallas_call(
        unpack_kernel,
        in_specs=[SMALL] + [whole] * len(totals),
        out_shape=[
            jax.ShapeDtypeStruct((128, 4608), F32),
            jax.ShapeDtypeStruct((128, 4608), F32),
            jax.ShapeDtypeStruct((576, 1024), F32),
        ],
        compiler_params=params(),
        cost_estimate=cost(0, 14),
        name="unpack_rows",
    )(flag, *totals)


def tie(*values):
    return lax.optimization_barrier(values)


def after(value, *tokens):
    return tie(value, *tokens)[0]


def hop(array, bit):
    return lax.ppermute(array, "shard", [(i, i ^ bit) for i in range(8)])


def gather_all(pack):
    return lax.all_gather(pack, "shard", axis=0, tiled=False)


def scatter_all(every):
    return lax.psum_scatter(every, "shard", scatter_dimension=0, tiled=True)[0]


def weave(near, far):
    groups = []
    for one, two in zip(near, far):
        groups += [list(one), list(two)]
    return Pieces(groups)


def combine(*outputs):
    terms = [term if isinstance(term, tuple) else (term, None) for out in outputs for term in out]
    rows, width = terms[0][0].shape[-2:]
    step = rows // 2

    def spec(k):
        if k is None:
            return pl.BlockSpec((step, width), lambda i: (i, 0))
        return pl.BlockSpec((pl.Squeezed(), step, width), lambda i: (k, i, 0))

    def kernel(*refs):
        at = 0
        for out, out_ref in zip(outputs, refs[len(terms) :]):
            total = refs[at][...].astype(F32)
            for ref in refs[at + 1 : at + len(out)]:
                total = total + ref[...].astype(F32)
            at += len(out)
            out_ref[...] = total.astype(BF16)

    found = pl.pallas_call(
        kernel,
        grid=(rows // step,),
        in_specs=[spec(k) for _, k in terms],
        out_specs=[pl.BlockSpec((step, width), lambda i: (i, 0))] * len(outputs),
        out_shape=[jax.ShapeDtypeStruct((rows, width), BF16)] * len(outputs),
        compiler_params=params(),
        cost_estimate=cost(0, 4),
        name="combine",
    )(*[array for array, _ in terms])
    return found[0] if len(outputs) == 1 else found


def rep_hop(array, pairs):
    return lax.ppermute(array.astype(BF16), "rep", pairs)


INWARD = [(0, 1), (3, 2)]
ACROSS = [(1, 2), (2, 1)]
OUTWARD = [(1, 0), (2, 3)]


def at_end(inner, outer):
    place = lax.axis_index("rep")
    return jnp.where((place == 0) | (place == 3), outer.astype(F32), inner)


def on_device(sizes, *arrays):
    (
        block_input, document_numbers, attn_gain, w_query, key_weight, value_weight, query_gain,
        key_gain, w_output, ffn_gain, w_gate, w_up, w_down, cotangent,
    ) = arrays
    reps, parts = sizes
    _, length, width = block_input.shape
    ff = w_gate.shape[1]
    paired = parts == 8 and reps == 4
    me = lax.axis_index("shard").astype(jnp.int32)
    place = me.reshape(1) if paired else jnp.zeros((1,), jnp.int32)
    x = block_input.reshape(length, width)
    back_out = cotangent.reshape(length, width)
    numbers = document_numbers.reshape(length)
    rows = width // parts
    seg = SLAB // parts
    slabs = ff // SLAB
    few = query_gain.shape[0]

    lane = jnp.arange(width)

    def spot(gain, times, size):
        share = gain.shape[0]
        wide = jnp.tile(gain, width // share)
        return jnp.where((lane < size * times) & ((lane % size) // share == me), wide, 0)

    empty = jnp.zeros((width,), BF16)
    gain_rows = [
        spot(attn_gain, 1, width),
        spot(query_gain, 2, HEAD_SIZE),
        spot(key_gain, 2, HEAD_SIZE),
        spot(ffn_gain, 1, width),
    ]
    first_pack = jnp.concatenate(
        [
            w_query,
            jnp.concatenate([key_weight, value_weight], axis=1),
            jnp.stack(gain_rows + [empty] * 12),
        ]
    )
    tables = tables_of(numbers)
    run = block_paired if paired else block_simple
    args = (me, place, x, back_out, tables, first_pack, w_output, w_gate, w_up, w_down)
    block_output, input_grad, attn_grad, feed_grads = run(*args)
    grad_gate, grad_up, grad_down = feed_grads
    grad_query = attn_grad[:rows]
    grad_key = attn_grad[rows : 2 * rows, :512]
    grad_value = attn_grad[rows : 2 * rows, 512:]

    def diagonal(*pairs):
        total = 0.0
        for weight, grad in pairs:
            total = total + jnp.sum(weight.astype(F32) * grad, axis=1)
        return total

    grad_gain_attn = diagonal(
        (w_query, grad_query), (key_weight, grad_key), (value_weight, grad_value)
    ) / attn_gain.astype(F32)
    grad_gain_ffn = diagonal((w_gate, grad_gate), (w_up, grad_up)) / ffn_gain.astype(F32)

    def small(row):
        both = attn_grad[3 * rows + row, :64] + attn_grad[3 * rows + row, 64:128]
        return lax.dynamic_slice(both, (me * few,), (few,))

    return (
        block_output[None],
        input_grad[None],
        grad_gain_attn,
        grad_query,
        grad_key,
        grad_value,
        small(0),
        small(1),
        attn_grad[2 * rows : 3 * rows],
        grad_gain_ffn,
        grad_gate,
        grad_up,
        grad_down,
    )


def block_simple(me, place, x, back_out, tables, first_pack, w_output, w_gate, w_up, w_down):
    rows, ff = w_gate.shape
    parts = x.shape[1] // rows
    seg = SLAB // parts
    slabs = ff // SLAB
    tall = rows + seg

    def columns(weight):
        cut = weight.reshape(rows, parts, slabs, seg).transpose(2, 0, 1, 3)
        return cut.reshape(slabs, rows, SLAB)

    pack = jnp.concatenate(
        [
            jnp.concatenate([columns(w_gate), columns(w_up)], axis=2),
            w_down.reshape(slabs, seg, x.shape[1]),
        ],
        axis=1,
    ).reshape(slabs * tall, 2 * SLAB)
    every = gather_all(first_pack)
    pairs = [(every[k], every[k], 1) for k in range(parts)]
    pieces = Pieces(stacked=gather_all(jnp.concatenate([w_output, pack])))
    normed_one, *units, q_aug, k_aug, v_aug, gains = project(pairs, place, x, tables)
    attended_0, q_back_0 = attend(q_aug, k_aug, v_aug, 0, 4)
    attended_1, q_back_1 = attend(q_aug, k_aug, v_aug, 4, 4)
    attended = (attended_0, attended_1)
    first_sum, normed_two, normed_two_t = output_rows(pieces, place, attended, x, gains)
    out, back, grads = feed(
        pieces, place, rows, slabs, normed_two, normed_two_t, back_out, False
    )
    total = lax.psum(scatter_all(grads), "rep").astype(F32).reshape(slabs, tall, 2 * SLAB)
    back_first, back_attended, grad_out = middle(
        pieces, place, first_sum, back_out, attended, gains, [back]
    )
    halves_0 = attend_back(q_back_0, k_aug, v_aug, attended_0, back_attended, 0, 4)
    halves_1 = attend_back(q_back_1, k_aug, v_aug, attended_1, back_attended, 4, 4)
    back_raw, own, sib = raw_back(
        parts, place, (halves_0[0], halves_1[0], halves_0[1], halves_1[1]), units, normed_one,
        tables[0], tables[1], gains, grad_out,
    )
    every = jnp.stack([own, sib], axis=1).reshape((parts,) + own.shape[1:])
    attn_grad = lax.psum(scatter_all(every), "rep").astype(F32)
    input_grad = input_back(pairs, place, back_raw, x, back_first, gains)

    def uncut(block):
        return block.reshape(slabs, rows, parts, seg).transpose(1, 2, 0, 3).reshape(rows, ff)

    feed_grads = (
        uncut(total[:, :rows, :SLAB]),
        uncut(total[:, :rows, SLAB:]),
        total[:, rows:, :].reshape(slabs * seg, x.shape[1]),
    )
    return (first_sum + out).astype(BF16), input_grad, attn_grad, feed_grads


def fence(outputs, *hops):
    found = tie(*outputs, *hops)
    return found[: len(outputs)], list(found[len(outputs) :])


def block_paired(me, place, x, back_out, tables, first_pack, w_output, w_gate, w_up, w_down):
    rows = w_gate.shape[0]
    chunks = (3, 3, 3)

    first = hop(first_pack, 2)
    second = hop(first_pack, 4)
    twin = hop(first_pack, 1)
    made, (first, second, twin) = fence(
        [*pack_rows(chunks, w_output, w_gate, w_up, w_down), *tables], first, second, twin
    )
    packs, tables = list(made[:3]), made[3:]
    corner_a = hop(second[:rows], 2)
    corner_b = hop(first[rows:], 4)
    far = [twin] + [hop(piece, 1) for piece in (first, second, corner_a, corner_b)]
    near = [first_pack, first, second, corner_a, corner_b]
    pairs = []
    for k in range(3):
        pairs += [(near[k], near[k], 1), (far[k], far[k], 1)]
    pairs += [(near[3], near[4], 0), (far[3], far[4], 0)]

    pack = after(packs[0], corner_a, corner_b, far[1], far[2])
    first, second, twin = hop(pack, 2), hop(pack, 4), hop(pack, 1)
    normed_one, *units, q_aug, k_aug, v_aug, gains = project(pairs, place, x, tables)
    (attended_0, q_back_0, k_aug), (first, second, twin) = fence(
        [*attend(q_aug, k_aug, v_aug, 0, 4), k_aug], first, second, twin
    )
    corner_a, corner_b = hop(second[:, :512], 2), hop(first[:, 512:], 4)
    far = [hop(first, 1), hop(second, 1)]
    packs[1] = after(packs[1], first, second)
    waiting = [hop(packs[1], bit) for bit in (1, 2, 4, 6)]
    (attended_1, q_back_1), (corner_a, corner_b, *far) = fence(
        attend(q_aug, k_aug, v_aug, 4, 4), corner_a, corner_b, *far
    )
    attended = (attended_0, attended_1)
    early = weave(
        [[pack], [first], [second], [corner_a, corner_b]],
        [[twin], [far[0]], [far[1]], [hop(corner_a, 1), hop(corner_b, 1)]],
    )
    first_sum, normed_two, normed_two_t = output_rows(early, place, attended, x, gains)

    def finish(pack, twin, first, second, corner):
        near = (first, second, corner)
        far = [hop(piece, 1) for piece in near]
        return weave([[pack]] + [[a] for a in near], [[twin]] + [[a] for a in far])

    def feed_step(pieces, begin, n, paired):
        return feed(pieces, place, begin, n, normed_two, normed_two_t, back_out, paired)

    (out_0, back_0, own_0, sib_0, normed_two), waiting = fence(
        [*feed_step(early, rows, chunks[0], True), normed_two], *waiting
    )
    later = finish(packs[1], *waiting)
    waiting = [hop(packs[2], bit) for bit in (1, 2, 4, 6)]
    other_0 = hop(after(sib_0, *later.arrays), 1)
    (out_1, back_1, own_1, sib_1, normed_two), (other_0, *waiting) = fence(
        [*feed_step(later, 0, chunks[1], True), normed_two], other_0, *waiting
    )
    last = finish(packs[2], *waiting)
    moved_0 = hop(combine([(own_0, 3), (other_0, 3)]), 2)
    other_1 = hop(after(sib_1, *last.arrays), 1)
    (out_2, back_2, own_2, sib_2), (moved_0, other_1) = fence(
        feed_step(last, 0, chunks[2], True), moved_0, other_1
    )
    other_2 = hop(sib_2, 1)
    term, one, two = combine(
        [(own_1, 3), (other_1, 3)],
        [(own_0, 1), (other_0, 1)],
        [(own_0, 2), (other_0, 2), moved_0],
    )
    back_2, term, one, two = tie(back_2, term, one, two)
    moved_1 = hop(term, 4)
    first_0, second_0 = hop(one, 2), hop(two, 4)
    middles = middle(
        early, place, first_sum, back_out, attended, gains, [back_0, back_1, back_2]
    )
    (back_first, back_attended, grad_out), (other_2,) = fence(middles, other_2)
    term = combine([(own_2, 3), (other_2, 3)])
    back_attended, term = tie(back_attended, term)
    moved_2 = hop(term, 2)
    halves = attend_back(q_back_0, k_aug, v_aug, attended_0, back_attended, 0, 4)
    (dq_0, dkv_0, back_attended), (first_0, second_0, moved_1) = fence(
        [*halves, back_attended], first_0, second_0, moved_1
    )
    grads_0, three, four = combine(
        [(own_0, 0), (other_0, 0), first_0, second_0],
        [(own_1, 1), (other_1, 1), moved_1],
        [(own_1, 2), (other_1, 2)],
    )
    back_attended, grads_0, three, four = tie(back_attended, grads_0, three, four)
    first_1, second_1 = hop(three, 2), hop(four, 4)
    inward_0 = rep_hop(grads_0, INWARD)
    halves = attend_back(q_back_1, k_aug, v_aug, attended_1, back_attended, 4, 4)
    (dq_1, dkv_1), (moved_2, inward_0, first_1, second_1) = fence(
        halves, moved_2, inward_0, first_1, second_1
    )
    one, two, grads_1, half_0 = combine(
        [(own_2, 1), (other_2, 1)],
        [(own_2, 2), (other_2, 2), moved_2],
        [(own_1, 0), (other_1, 0), first_1, second_1],
        [grads_0, inward_0],
    )
    dq_1, one, two, grads_1, half_0 = tie(dq_1, one, two, grads_1, half_0)
    first_2, second_2 = hop(one, 2), hop(two, 4)
    inward_1 = rep_hop(grads_1, INWARD)
    across_0 = rep_hop(half_0, ACROSS)
    result = raw_back(
        8, place, (dq_0, dq_1, dkv_0, dkv_1), units, normed_one, tables[0], tables[1], gains,
        grad_out,
    )
    (back_raw, own, sib), (first_2, second_2, inward_1, across_0) = fence(
        result, first_2, second_2, inward_1, across_0
    )
    other = hop(sib, 1)
    half_1, total_0, grads_2 = combine(
        [grads_1, inward_1], [half_0, across_0], [(own_2, 0), (other_2, 0), first_2, second_2]
    )
    back_raw, other, half_1, total_0, grads_2 = tie(back_raw, other, half_1, total_0, grads_2)
    term = combine([(own, 3), (other, 3)])
    back_raw, total_0, half_1, grads_2, term = tie(back_raw, total_0, half_1, grads_2, term)
    moved = hop(term, 4)
    outward_0 = rep_hop(total_0, OUTWARD)
    across_1 = rep_hop(half_1, ACROSS)
    inward_2 = rep_hop(grads_2, INWARD)
    input_grad = input_back(pairs, place, back_raw, x, back_first, gains)
    (input_grad,), (moved,) = fence([input_grad], moved)
    one, two = combine([(own, 1), (other, 1), moved], [(own, 2), (other, 2)])
    one, two, across_1, inward_2, first_sum = tie(one, two, across_1, inward_2, first_sum)
    first, second = hop(one, 2), hop(two, 4)
    total_1, half_2 = combine([half_1, across_1], [grads_2, inward_2])
    first_sum, total_1, half_2, outward_0 = tie(first_sum, total_1, half_2, outward_0)
    outward_1 = rep_hop(total_1, OUTWARD)
    across_2 = rep_hop(half_2, ACROSS)
    outs = out_0.astype(F32) + out_1.astype(F32) + out_2.astype(F32)
    block_output = (first_sum + outs).astype(BF16)
    (block_output,), (first, second) = fence([block_output], first, second)
    grads = combine([(own, 0), (other, 0), first, second])
    inward = rep_hop(grads, INWARD)
    across_2, _ = tie(across_2, grads)
    total_2 = combine([half_2, across_2])
    outward_2 = rep_hop(total_2, OUTWARD)
    inward, outward_1, _ = tie(inward, outward_1, total_2)
    half = combine([grads, inward])
    across = rep_hop(half, ACROSS)
    total = combine([half, across])
    outward = rep_hop(total, OUTWARD)
    total, outward_2 = tie(total, outward_2)
    spot = lax.axis_index("rep")
    flag = ((spot == 0) | (spot == 3)).astype(jnp.int32).reshape(1)
    feed_grads = unpack_rows(flag, total_0, outward_0, total_1, outward_1, total_2, outward_2)
    (*feed_grads,), (outward,) = fence(feed_grads, outward)
    return block_output, input_grad, at_end(total.astype(F32), outward), feed_grads


def solution(mesh):
    sizes = (mesh.shape["rep"], mesh.shape["shard"])
    whole = P(("rep", "shard"), None, None)
    matrix = P("shard", None)
    vector = P("shard")
    in_specs = (
        whole, P(("rep", "shard"), None), vector, matrix, matrix, matrix, vector, vector, matrix,
        vector, matrix, matrix, matrix, whole,
    )
    out_specs = (
        whole, whole, vector, matrix, matrix, matrix, vector, vector, matrix, vector, matrix,
        matrix, matrix,
    )
    return jax.shard_map(
        lambda *arrays: on_device(sizes, *arrays),
        mesh=mesh,
        in_specs=in_specs,
        out_specs=out_specs,
        check_vma=False,
    )
```

```python
import jax
import jax.numpy as jnp
from jax import lax
from jax.experimental import pallas as pl
from jax.experimental.pallas import tpu as pltpu
from jax.sharding import PartitionSpec as P

QUERY_HEADS = 16
KEY_VALUE_HEADS = 8
HEAD_SIZE = 64
EPS = 1e-05
ROPE_BASE = 1000000.0
FAR = 32768.0
TILE = 256
SLAB = 512
VMEM_LIMIT = 60 * 1024 * 1024
NT = ((1,), (1,))
NN = ((1,), (0,))
TN = ((0,), (0,))
BF16 = jnp.bfloat16
F32 = jnp.float32
SMALL = pl.BlockSpec(memory_space=pltpu.SMEM)


def dot(left, right, dims=NN):
    return lax.dot_general(left, right, (dims, ((), ())), preferred_element_type=F32)


def params():
    return pltpu.CompilerParams(vmem_limit_bytes=VMEM_LIMIT)


def cost(giga_flops, mega_bytes, exps=0):
    return pl.CostEstimate(
        flops=int(giga_flops * 10**6),
        bytes_accessed=int(mega_bytes * 10**3),
        transcendentals=exps // 1000,
    )


def fixed(shape, where=None):
    index = (0,) * len(shape) if where is None else where
    return pl.BlockSpec(shape, lambda *_: index, pipeline_mode=pl.Buffered(1))


def by_rows(width, rows=TILE):
    return pl.BlockSpec((rows, width), lambda i: (i, 0))


class Pieces:
    def __init__(self, groups=None, stacked=None):
        self.stacked = stacked
        self.count = len(groups) if stacked is None else stacked.shape[0]
        self.groups = groups if stacked is None else [[stacked]] * self.count
        self.arrays = [array for group in self.groups for array in group]
        self.layout = [len(group) for group in self.groups]

    def specs(self, rows, start):
        once = pl.Buffered(1) if start(0) == start(1) else None
        found = []
        for k, group in enumerate(self.groups):
            for array in group:
                shape = (pl.Element(rows), pl.Element(array.shape[-1]))
                if self.stacked is None:
                    found.append(
                        pl.BlockSpec(shape, lambda i: (start(i), 0), pipeline_mode=once)
                    )
                else:
                    found.append(
                        pl.BlockSpec(
                            (pl.Squeezed(),) + shape,
                            lambda i, k=k: (k, start(i), 0),
                            pipeline_mode=once,
                        )
                    )
        return found


def grouped(refs, layout):
    groups, at = [], 0
    for size in layout:
        groups.append(refs[at : at + size])
        at += size
    return groups


def fill(target, at, group, rows):
    left = 0
    for ref in group:
        right = left + ref.shape[1]
        target[at, left:right] = ref[rows, :]
        left = right


def split3(value):
    high = value.astype(BF16).astype(F32)
    rest = value - high
    middle = rest.astype(BF16).astype(F32)
    return high, middle, rest - middle


def aligned(index, rows):
    return pl.ds(pl.multiple_of(index * rows, rows), rows)


def unit_of(rows):
    inverse = lax.rsqrt(jnp.mean(rows * rows, axis=-1, keepdims=True) + EPS)
    return rows * inverse, inverse


def head_blocks():
    first = lax.broadcasted_iota(jnp.int32, (128, 128), 0) // HEAD_SIZE
    second = lax.broadcasted_iota(jnp.int32, (128, 128), 1) // HEAD_SIZE
    return (first == second).astype(BF16)


def head_mean(rows, blocks):
    return dot(rows.astype(BF16), blocks) * (1.0 / HEAD_SIZE)


def swap_halves(rows, first):
    return jnp.where(first, pltpu.roll(rows, 96, 1), pltpu.roll(rows, 32, 1))


def lanes(rows=TILE):
    return lax.broadcasted_iota(jnp.int32, (rows, 128), 1)


def load_pairs(parts, me_ref, refs, w_all):
    rows = w_all.shape[0] // parts

    @pl.when(pl.program_id(0) == 0)
    def _():
        for k in range(parts):
            at = aligned(me_ref[0] ^ k, rows)
            w_all[at, :1024] = refs[2 * k][...]
            w_all[at, 1024:] = refs[2 * k + 1][...]


def pair_specs(pieces, rows):
    arrays, specs = [], []
    for piece in pieces:
        left, right, at = piece
        arrays += [left, right]
        specs += [fixed((rows, 1024)), fixed((rows, 1024), (at, 0))]
    return arrays, specs


def project_kernel(parts, me_ref, x_ref, cos_ref, sin_ref, qx_ref, kx_ref, *refs):
    gain_refs = refs[2 * parts : 3 * parts]
    n_ref, unit_ref, scale_ref, q_ref, k_ref, v_ref, gain_ref, w_all = refs[3 * parts :]
    load_pairs(parts, me_ref, refs, w_all)

    @pl.when(pl.program_id(0) == 0)
    def _():
        total = gain_refs[0][...].astype(F32)
        for ref in gain_refs[1:]:
            total = total + ref[...].astype(F32)
        gain_ref[...] = total

    unit, _ = unit_of(x_ref[...].astype(F32))
    normed = (unit * gain_ref[0:1, :]).astype(BF16)
    n_ref[...] = normed
    raw = dot(normed, w_all[...])
    blocks = head_blocks()
    lane = lanes()
    first = (lane % HEAD_SIZE) < HEAD_SIZE // 2
    low = lane < HEAD_SIZE
    cosine, sine = cos_ref[...], sin_ref[...]
    for p in range(12):
        at = slice(p * 128, (p + 1) * 128)
        rows_in = raw[:, at]
        inverse = lax.rsqrt(head_mean(rows_in * rows_in, blocks) + EPS)
        unit = rows_in * inverse
        unit_ref[:, at] = unit.astype(BF16)
        scale_ref[:, at] = inverse.astype(BF16)
        scaled = unit * gain_ref[1 + p // 8 : 2 + p // 8, :128]
        turned = scaled * cosine + swap_halves(scaled, first) * sine
        if p < 8:
            turned = turned * HEAD_SIZE**-0.5
            out, more, at = q_ref, qx_ref[...], 2 * p
        else:
            out, more, at = k_ref, kx_ref[...], 2 * (p - 8)
        out[at] = jnp.where(low, turned, more).astype(BF16)
        out[at + 1] = jnp.where(low, pltpu.roll(turned, 64, 1), more).astype(BF16)
    more = ((lane >= 64) & (lane < 67)).astype(F32)
    for p in range(4):
        rows_in = raw[:, 1536 + p * 128 : 1664 + p * 128]
        v_ref[2 * p] = jnp.where(low, rows_in, more).astype(BF16)
        v_ref[2 * p + 1] = jnp.where(low, pltpu.roll(rows_in, 64, 1), more).astype(BF16)


def project(pieces, me, x, tables):
    length, width = x.shape
    parts = len(pieces)
    rows = width // parts
    arrays, specs = pair_specs(pieces, rows)
    gains = [(piece[1], (piece[2] + 1) * rows // 16) for piece in pieces]

    def heads(count):
        return pl.BlockSpec((count, TILE, 128), lambda i: (0, i, 0))

    return pl.pallas_call(
        lambda *refs: project_kernel(parts, *refs),
        grid=(length // TILE,),
        in_specs=[SMALL, by_rows(width)]
        + [by_rows(128)] * 4
        + specs
        + [fixed((16, 1024), (at, 0)) for _, at in gains],
        out_specs=[by_rows(width), by_rows(1536), by_rows(1536), heads(16), heads(8), heads(8)]
        + [fixed((16, 1024))],
        out_shape=[
            jax.ShapeDtypeStruct((length, width), BF16),
            jax.ShapeDtypeStruct((length, 1536), BF16),
            jax.ShapeDtypeStruct((length, 1536), BF16),
            jax.ShapeDtypeStruct((16, length, 128), BF16),
            jax.ShapeDtypeStruct((8, length, 128), BF16),
            jax.ShapeDtypeStruct((8, length, 128), BF16),
            jax.ShapeDtypeStruct((16, 1024), F32),
        ],
        scratch_shapes=[pltpu.VMEM((width, 2048), BF16)],
        compiler_params=params(),
        cost_estimate=cost(8, 25),
        name="project",
    )(me, x, *tables, *arrays, *[array for array, _ in gains])


def causal(query_axis):
    first = lax.broadcasted_iota(jnp.int32, (TILE, TILE), 0)
    second = lax.broadcasted_iota(jnp.int32, (TILE, TILE), 1)
    return (first >= second) if query_axis == 0 else (second >= first)


def attend_kernel(q_ref, k_ref, v_ref, o_ref, qb_ref):
    tiles = q_ref.shape[1] // TILE
    keep = causal(0)
    lane = lax.broadcasted_iota(jnp.int32, (TILE, 128), 1)
    for i in range(tiles):
        rows = slice(i * TILE, (i + 1) * TILE)
        before = slice(0, i * TILE)
        halves = []
        for h in range(2):
            q = q_ref[h, rows, :]
            weights = jnp.where(keep, jnp.exp(dot(q, k_ref[0, rows, :], NT)), 0.0)
            out = dot(weights.astype(BF16), v_ref[0, rows, :])
            if i:
                weights = jnp.exp(dot(q, k_ref[0, before, :], NT)).astype(BF16)
                out = out + dot(weights, v_ref[0, before, :])
            total = out[:, 64:65]
            halves.append(out / total)
            high, middle, low = split3(-jnp.log(total))
            extra = jnp.where(
                lane == 68, high, jnp.where(lane == 69, middle, jnp.where(lane == 70, low, 0.0))
            )
            qb_ref[h, rows, :] = (q.astype(F32) + extra).astype(BF16)
        both = jnp.where(lane < 64, halves[0], pltpu.roll(halves[1], 64, 1))
        o_ref[rows, :] = both.astype(BF16)


def attend(q_aug, k_aug, v_aug, begin, groups):
    _, length, _ = q_aug.shape
    return pl.pallas_call(
        attend_kernel,
        grid=(groups,),
        in_specs=[
            pl.BlockSpec((2, length, 128), lambda g: (g + begin, 0, 0)),
            pl.BlockSpec((1, length, 128), lambda g: (g + begin, 0, 0)),
            pl.BlockSpec((1, length, 128), lambda g: (g + begin, 0, 0)),
        ],
        out_specs=[
            pl.BlockSpec((length, 128), lambda g: (0, g)),
            pl.BlockSpec((2, length, 128), lambda g: (g, 0, 0)),
        ],
        out_shape=[
            jax.ShapeDtypeStruct((length, groups * 128), BF16),
            jax.ShapeDtypeStruct((2 * groups, length, 128), BF16),
        ],
        compiler_params=params(),
        cost_estimate=cost(2.5 * groups, 2 * groups, groups * 2**20),
        name="attend",
    )(q_aug, k_aug, v_aug)


def attend_back_kernel(q_ref, k_ref, v_ref, o_ref, do_ref, dq_ref, dkv_ref, do_aug, k_t, dq_t):
    length = q_ref.shape[1]
    tiles = length // TILE
    keep = causal(1)
    lane = lax.broadcasted_iota(jnp.int32, (length, 128), 1)
    back = do_ref[...].astype(F32)
    product = back * o_ref[...].astype(F32)
    for h in range(2):
        own = (lane < 64) if h == 0 else (lane >= 64)
        centre = jnp.sum(jnp.where(own, product, 0.0), axis=1, keepdims=True)
        moved = back if h == 0 else pltpu.roll(back, 64, 1)
        high, middle, low = split3(-centre)
        extra = jnp.where(
            lane == 64, high, jnp.where(lane == 65, middle, jnp.where(lane == 66, low, 0.0))
        )
        do_aug[h] = jnp.where(lane < 64, moved, extra).astype(BF16)
    k_t[...] = k_ref[0].astype(F32).T[:64, :].astype(BF16)
    low_half = lax.broadcasted_iota(jnp.int32, (TILE, 128), 1) < 64
    for j in range(tiles):
        cols = slice(j * TILE, (j + 1) * TILE)
        k = k_ref[0, cols, :]
        v = v_ref[0, cols, :]
        dk = 0.0
        dv = 0.0
        for i, stop in ((j, j + 1), (j + 1, tiles)):
            if i == tiles:
                continue
            rows = slice(i * TILE, stop * TILE)
            for h in range(2):
                q = q_ref[h, rows, :]
                do = do_aug[h, rows, :]
                probs = jnp.exp(dot(k, q, NT))
                if i == j:
                    probs = jnp.where(keep, probs, 0.0)
                scores = (probs * dot(v, do, NT)).astype(BF16)
                dv = dv + dot(probs.astype(BF16), do)
                dk = dk + dot(scores, q)
                to_q = dot(k_t[:, cols], scores)
                if j == 0:
                    dq_t[h * 64 : (h + 1) * 64, rows] = to_q
                else:
                    dq_t[h * 64 : (h + 1) * 64, rows] += to_q
        dkv_ref[cols, :] = jnp.where(low_half, dk, pltpu.roll(dv, 64, 1))
    dq_ref[...] = dq_t[...].T


def attend_back(q_back, k_aug, v_aug, attended, back_attended, begin, groups):
    _, length, _ = q_back.shape
    by_group = pl.BlockSpec((length, 128), lambda g: (0, g + begin))
    out_group = pl.BlockSpec((length, 128), lambda g: (0, g))
    return pl.pallas_call(
        attend_back_kernel,
        grid=(groups,),
        in_specs=[
            pl.BlockSpec((2, length, 128), lambda g: (g, 0, 0)),
            pl.BlockSpec((1, length, 128), lambda g: (g + begin, 0, 0)),
            pl.BlockSpec((1, length, 128), lambda g: (g + begin, 0, 0)),
            out_group,
            by_group,
        ],
        out_specs=[out_group, out_group],
        out_shape=[jax.ShapeDtypeStruct((length, groups * 128), F32)] * 2,
        scratch_shapes=[
            pltpu.VMEM((2, length, 128), BF16),
            pltpu.VMEM((64, length), BF16),
            pltpu.VMEM((128, length), F32),
        ],
        compiler_params=params(),
        cost_estimate=cost(5 * groups, 3 * groups, groups * 2**20),
        name="attend_back",
    )(q_back, k_aug, v_aug, attended, back_attended)


def output_kernel(layout, me_ref, o0_ref, o1_ref, x_ref, gain_ref, *refs):
    sum_ref, n_ref, nt_ref, w_all = refs[-4:]
    rows = w_all.shape[0] // len(layout)

    @pl.when(pl.program_id(0) == 0)
    def _():
        for k, group in enumerate(grouped(refs, layout)):
            fill(w_all, aligned(me_ref[0] ^ k, rows), group, slice(None))

    total = x_ref[...].astype(F32) + dot(o0_ref[...], w_all[:512, :])
    total = total + dot(o1_ref[...], w_all[512:, :])
    sum_ref[...] = total
    unit, _ = unit_of(total)
    normed = unit * gain_ref[3:4, :]
    n_ref[...] = normed.astype(BF16)
    nt_ref[...] = normed.T.astype(BF16)


def output_rows(pieces, me, attended, x, gain):
    length, width = x.shape
    parts = pieces.count
    rows = width // parts
    return pl.pallas_call(
        lambda *refs: output_kernel(pieces.layout, *refs),
        grid=(length // TILE,),
        in_specs=[SMALL, by_rows(512), by_rows(512), by_rows(width), fixed((16, 1024))]
        + pieces.specs(rows, lambda i: 0),
        out_specs=[by_rows(width), by_rows(width), pl.BlockSpec((width, TILE), lambda i: (0, i))],
        out_shape=[
            jax.ShapeDtypeStruct((length, width), F32),
            jax.ShapeDtypeStruct((length, width), BF16),
            jax.ShapeDtypeStruct((width, length), BF16),
        ],
        scratch_shapes=[pltpu.VMEM((1024, width), BF16)],
        compiler_params=params(),
        cost_estimate=cost(5, 15),
        name="output_rows",
    )(me, *attended, x, gain, *pieces.arrays)


def scatter_rows(me, parts, value, rows, own_ref, sib_ref, at):
    half = me >> 1
    core = me & 1
    for q in range(parts // 2):
        for s, ref in enumerate((own_ref, sib_ref)):
            source = 2 * q + (core ^ s)
            ref[q ^ half, at : at + rows, :] = value[aligned(source, rows), :]


def feed_kernel(layout, paired, me_ref, n_ref, nt_ref, c_ref, *refs):
    parts = len(layout)
    f_ref, b_ref, *grad_refs = refs[sum(layout) : -8]
    w_all, d_all, back, hidden, w_grad, d_grad, f_sum, b_sum = refs[-8:]
    me = me_ref[0]
    rows = w_all.shape[0] // parts
    seg = SLAB // parts
    for k, group in enumerate(grouped(refs, layout)):
        fill(w_all, aligned(me ^ k, rows), group, slice(0, rows))
        fill(d_all, aligned(me ^ k, seg), group, slice(rows, rows + seg))
    step = pl.program_id(0)

    @pl.when(step == 0)
    def _():
        f_sum[...] = jnp.zeros_like(f_sum)
        b_sum[...] = jnp.zeros_like(b_sum)

    both = dot(n_ref[...], w_all[...])
    gate = both[:, :SLAB]
    up = both[:, SLAB:]
    sig = 1.0 / (1.0 + jnp.exp(-gate))
    swish = gate * sig
    hidden[...] = (swish * up).astype(BF16)
    back_hidden = dot(c_ref[...], d_all[...], NT)
    back[:, SLAB:] = (back_hidden * swish).astype(BF16)
    back[:, :SLAB] = (back_hidden * up * sig * (1.0 + gate * (1.0 - sig))).astype(BF16)
    f_sum[...] += dot(hidden[...], d_all[...])
    b_sum[...] += dot(back[...], w_all[...], NT)
    w_grad[...] = dot(nt_ref[...], back[...]).astype(BF16)
    d_grad[...] = dot(hidden[...], c_ref[...], TN).astype(BF16)

    @pl.when(step == pl.num_programs(0) - 1)
    def _():
        f_ref[...] = f_sum[...].astype(BF16)
        b_ref[...] = b_sum[...].astype(BF16)

    if paired:
        own_ref, sib_ref = grad_refs
        scatter_rows(me, parts, w_grad, rows, own_ref, sib_ref, 0)
        scatter_rows(me, parts, d_grad, seg, own_ref, sib_ref, rows)
    else:
        for d in range(parts):
            grad_refs[0][d, :rows, :] = w_grad[d * rows : (d + 1) * rows, :]
            grad_refs[0][d, rows:, :] = d_grad[d * seg : (d + 1) * seg, :]


def feed(pieces, me, begin, slabs, normed, normed_t, cotangent, paired):
    length, width = normed.shape
    parts = pieces.count
    rows = width // parts + SLAB // parts
    depth = parts // 2 if paired else parts
    count = 2 if paired else 1
    grads = pl.BlockSpec((depth, rows, 2 * SLAB), lambda i: (0, i, 0))
    return pl.pallas_call(
        lambda *refs: feed_kernel(pieces.layout, paired, *refs),
        grid=(slabs,),
        in_specs=[SMALL, fixed((length, width)), fixed((width, length)), fixed((length, width))]
        + pieces.specs(rows, lambda i: (begin // 16 + i * (rows // 16)) * 16),
        out_specs=[fixed((length, width)), fixed((length, width))] + [grads] * count,
        out_shape=[
            jax.ShapeDtypeStruct((length, width), BF16),
            jax.ShapeDtypeStruct((length, width), BF16),
        ]
        + [jax.ShapeDtypeStruct((depth, slabs * rows, 2 * SLAB), BF16)] * count,
        scratch_shapes=[
            pltpu.VMEM((width, 2 * SLAB), BF16),
            pltpu.VMEM((SLAB, width), BF16),
            pltpu.VMEM((length, 2 * SLAB), BF16),
            pltpu.VMEM((length, SLAB), BF16),
            pltpu.VMEM((width, 2 * SLAB), BF16),
            pltpu.VMEM((SLAB, width), BF16),
            pltpu.VMEM((length, width), F32),
            pltpu.VMEM((length, width), F32),
        ],
        compiler_params=params(),
        cost_estimate=cost(12.5 * slabs, 20 + 6 * slabs),
        name="feed",
    )(me, normed, normed_t, cotangent, *pieces.arrays)


def middle_kernel(layout, sums, me_ref, s_ref, c_ref, o0_ref, o1_ref, gain_ref, *refs):
    b_refs = refs[:sums]
    f_ref, a_ref, g_ref, w_all, total = refs[-5:]
    rows = w_all.shape[0] // len(layout)
    step = pl.program_id(0)

    @pl.when(step == 0)
    def _():
        for k, group in enumerate(grouped(refs[sums:], layout)):
            fill(w_all, aligned(me_ref[0] ^ k, rows), group, slice(None))

    back = b_refs[0][...].astype(F32)
    for ref in b_refs[1:]:
        back = back + ref[...].astype(F32)
    unit, inverse = unit_of(s_ref[...])
    scaled = back * gain_ref[3:4, :]
    first = c_ref[...].astype(F32) + inverse * (
        scaled - unit * jnp.mean(scaled * unit, axis=-1, keepdims=True)
    )
    f_ref[...] = first
    short = first.astype(BF16)
    a_ref[...] = dot(short, w_all[...], NT).astype(BF16)
    grads = [dot(ref[...], short, TN) for ref in (o0_ref, o1_ref)]

    @pl.when(step == 0)
    def _():
        total[:512, :] = grads[0]
        total[512:, :] = grads[1]

    @pl.when(step > 0)
    def _():
        total[:512, :] += grads[0]
        total[512:, :] += grads[1]

    @pl.when(step == pl.num_programs(0) - 1)
    def _():
        g_ref[...] = total[...].astype(BF16)


def middle(pieces, me, first_sum, cotangent, attended, gain, backs):
    length, width = first_sum.shape
    parts = pieces.count
    rows = width // parts
    return pl.pallas_call(
        lambda *refs: middle_kernel(pieces.layout, len(backs), *refs),
        grid=(length // TILE,),
        in_specs=[SMALL, by_rows(width), by_rows(width), by_rows(512), by_rows(512), fixed((16, 1024))]
        + [by_rows(width)] * len(backs)
        + pieces.specs(rows, lambda i: 0),
        out_specs=[by_rows(width), by_rows(1024), fixed((1024, width))],
        out_shape=[
            jax.ShapeDtypeStruct((length, width), F32),
            jax.ShapeDtypeStruct((length, 1024), BF16),
            jax.ShapeDtypeStruct((1024, width), BF16),
        ],
        scratch_shapes=[pltpu.VMEM((1024, width), BF16), pltpu.VMEM((1024, width), F32)],
        compiler_params=params(),
        cost_estimate=cost(9, 32),
        name="middle",
    )(me, first_sum, cotangent, *attended, gain, *backs, *pieces.arrays)


def raw_back_kernel(
    parts, me_ref, dq0_ref, dq1_ref, dkv0_ref, dkv1_ref, unit_ref, scale_ref, n_ref, cos_ref, sin_ref, gain_ref, wo_ref,
    b_ref, own_ref, sib_ref, total, gains,
):
    step = pl.program_id(0)
    rows = total.shape[0] // parts
    blocks = head_blocks()
    lane = lanes()
    first = (lane % HEAD_SIZE) < HEAD_SIZE // 2
    low = lane < HEAD_SIZE
    cosine, sine = cos_ref[...], sin_ref[...]
    sums = [None, None]
    for p in range(12):
        at = slice(p * 128, (p + 1) * 128)
        if p < 8:
            dq_ref = dq0_ref if p < 4 else dq1_ref
            grads = dq_ref[:, (p % 4) * 128 : (p % 4 + 1) * 128] * HEAD_SIZE**-0.5
        else:
            dkv_ref = dkv0_ref if p < 10 else dkv1_ref
            left = dkv_ref[:, (p % 2) * 256 : (p % 2) * 256 + 128]
            right = dkv_ref[:, (p % 2) * 256 + 128 : (p % 2) * 256 + 256]
            grads = jnp.where(low, left, pltpu.roll(right, 64, 1))
            values = jnp.where(low, pltpu.roll(left, 64, 1), right)
            b_ref[:, 512 + p * 128 : 640 + p * 128] = values.astype(BF16)
        turned = grads * cosine + swap_halves(grads * sine, first)
        unit = unit_ref[:, at].astype(F32)
        inverse = scale_ref[:, at].astype(F32)
        kind = 0 if p < 8 else 1
        part = jnp.sum(turned * unit, axis=0, keepdims=True)
        sums[kind] = part if sums[kind] is None else sums[kind] + part
        scaled = turned * gain_ref[1 + kind : 2 + kind, :128]
        b_ref[:, at] = (inverse * (scaled - unit * head_mean(scaled * unit, blocks))).astype(BF16)
    grad = dot(n_ref[...], b_ref[...], TN)

    @pl.when(step == 0)
    def _():
        total[...] = grad
        gains[...] = jnp.zeros_like(gains)

    @pl.when(step > 0)
    def _():
        total[...] += grad

    gains[0:1, :] += sums[0]
    gains[1:2, :] += sums[1]

    @pl.when(step == pl.num_programs(0) - 1)
    def _():
        me = me_ref[0]
        half = me >> 1
        core = me & 1
        more = gains[...].astype(BF16)
        for q in range(parts // 2):
            for s, ref in enumerate((own_ref, sib_ref)):
                source = aligned(2 * q + (core ^ s), rows)
                block = total[source, :].astype(BF16)
                ref[q ^ half, :rows, :] = block[:, :1024]
                ref[q ^ half, rows : 2 * rows, :] = block[:, 1024:]
                ref[q ^ half, 2 * rows : 3 * rows, :] = wo_ref[source, :]
                ref[q ^ half, 3 * rows :, :] = jnp.zeros((32, 1024), BF16)
                ref[q ^ half, 3 * rows :, :128] = more


def raw_back(parts, me, halves, units, normed, cosine, sine, gains, grad_out):
    length, width = normed.shape
    rows = 3 * (width // parts) + 32
    grads = fixed((parts // 2, rows, 1024))
    return pl.pallas_call(
        lambda *refs: raw_back_kernel(parts, *refs),
        grid=(length // TILE,),
        in_specs=[SMALL] + [by_rows(512)] * 4 + [by_rows(1536)] * 2 + [by_rows(width)]
        + [by_rows(128)] * 2
        + [fixed((16, 1024)), fixed((1024, width))],
        out_specs=[by_rows(2048), grads, grads],
        out_shape=[jax.ShapeDtypeStruct((length, 2048), BF16)]
        + [jax.ShapeDtypeStruct((parts // 2, rows, 1024), BF16)] * 2,
        scratch_shapes=[pltpu.VMEM((width, 2048), F32), pltpu.VMEM((32, 128), F32)],
        compiler_params=params(),
        cost_estimate=cost(10, 30),
        name="raw_back",
    )(me, *halves, *units, normed, cosine, sine, gains, grad_out)


def input_kernel(parts, me_ref, b_ref, x_ref, f_ref, gain_ref, *refs):
    out_ref, w_all = refs[2 * parts :]
    load_pairs(parts, me_ref, refs, w_all)
    unit, inverse = unit_of(x_ref[...].astype(F32))
    scaled = dot(b_ref[...], w_all[...], NT) * gain_ref[0:1, :]
    out_ref[...] = f_ref[...] + inverse * (
        scaled - unit * jnp.mean(scaled * unit, axis=-1, keepdims=True)
    )


def input_back(pieces, me, back_raw, x, back_first, gain):
    length, width = x.shape
    parts = len(pieces)
    arrays, specs = pair_specs(pieces, width // parts)
    return pl.pallas_call(
        lambda *refs: input_kernel(parts, *refs),
        grid=(length // TILE,),
        in_specs=[SMALL, by_rows(2048), by_rows(width), by_rows(width), fixed((16, 1024))] + specs,
        out_specs=by_rows(width),
        out_shape=jax.ShapeDtypeStruct((length, width), F32),
        scratch_shapes=[pltpu.VMEM((width, 2048), BF16)],
        compiler_params=params(),
        cost_estimate=cost(6, 18),
        name="input_back",
    )(me, back_raw, x, back_first, gain, *arrays)


def tables_of(numbers):
    length = numbers.shape[0]
    indices = jnp.arange(length, dtype=jnp.int32)
    starts = jnp.concatenate([jnp.ones((1,), dtype=bool), numbers[1:] != numbers[:-1]])
    begins = lax.cummax(jnp.where(starts, indices, jnp.zeros_like(numbers)), axis=0)
    offsets = (indices - begins).astype(F32).reshape(length, 1)
    frequency = ROPE_BASE ** (-jnp.arange(0, HEAD_SIZE, 2).astype(F32) / HEAD_SIZE)
    angles = offsets * frequency
    cosine = jnp.cos(angles)
    sine = jnp.sin(angles)
    same = (numbers[:, None] == jnp.arange(4)[None]).astype(F32)
    empty = jnp.zeros((length, 64), F32)
    return (
        jnp.concatenate([cosine] * 4, axis=1),
        jnp.concatenate([-sine, sine, -sine, sine], axis=1),
        jnp.concatenate([empty, -FAR * same, empty[:, :60]], axis=1),
        jnp.concatenate([empty, 1 - same, jnp.ones((length, 3)), empty[:, :57]], axis=1),
    )


def pack_kernel(chunks, o_ref, gate_ref, up_ref, down_ref, *out_refs):
    low = lanes(128) < 64
    out_refs[0][:128, :] = o_ref[...]
    places = [(c, i) for c, n in enumerate(chunks) for i in range(n)]
    for t, (c, i) in enumerate(places):
        row = i * 192 + (0 if c else 128)
        for side, ref in enumerate((gate_ref, up_ref)):
            for e in range(4):
                left, right = (18 * e + t) // 2, (18 * e + 9 + t) // 2
                a = ref[:, left * 128 : left * 128 + 128].astype(F32)
                b = ref[:, right * 128 : right * 128 + 128].astype(F32)
                both = pltpu.roll(jnp.where(low, b, a), 64, 1) if t % 2 else jnp.where(low, a, b)
                at = side * SLAB + e * 128
                out_refs[c][row : row + 128, at : at + 128] = both.astype(BF16)
        out_refs[c][row + 128 : row + 192, :] = down_ref[t * 64 : t * 64 + 64, :]


def pack_rows(chunks, w_output, w_gate, w_up, w_down):
    return pl.pallas_call(
        lambda *refs: pack_kernel(chunks, *refs),
        out_shape=[
            jax.ShapeDtypeStruct((n * 192 + (0 if c else 128), 1024), BF16)
            for c, n in enumerate(chunks)
        ],
        compiler_params=params(),
        cost_estimate=cost(0, 7),
        name="pack_rows",
    )(w_output, w_gate, w_up, w_down)


def unpack_kernel(flag_ref, *refs):
    *in_refs, gate_ref, up_ref, down_ref = refs
    low = lanes(128) < 64
    outer = flag_ref[0] > 0

    def rows_of(at, size, columns):
        for inside, outside in zip(in_refs[::2], in_refs[1::2]):
            if at < inside.shape[0]:
                one = inside[at : at + size, columns].astype(F32)
                return jnp.where(outer, outside[at : at + size, columns].astype(F32), one)
            at -= inside.shape[0]

    def segment(side, s, half):
        d = s // 9
        at = side * SLAB + (d // 2) * 128
        tile = rows_of((s % 9) * 192, 128, slice(at, at + 128))
        return tile if d % 2 == half else pltpu.roll(tile, 64, 1)

    for side, out in enumerate((gate_ref, up_ref)):
        for m in range(36):
            out[:, m * 128 : m * 128 + 128] = jnp.where(
                low, segment(side, 2 * m, 0), segment(side, 2 * m + 1, 1)
            )
    for t in range(9):
        down_ref[t * 64 : t * 64 + 64, :] = rows_of(t * 192 + 128, 64, slice(None))


def unpack_rows(flag, *totals):
    whole = pl.BlockSpec(memory_space=pltpu.VMEM)
    return pl.pallas_call(
        unpack_kernel,
        in_specs=[SMALL] + [whole] * len(totals),
        out_shape=[
            jax.ShapeDtypeStruct((128, 4608), F32),
            jax.ShapeDtypeStruct((128, 4608), F32),
            jax.ShapeDtypeStruct((576, 1024), F32),
        ],
        compiler_params=params(),
        cost_estimate=cost(0, 14),
        name="unpack_rows",
    )(flag, *totals)


def tie(*values):
    return lax.optimization_barrier(values)


def after(value, *tokens):
    return tie(value, *tokens)[0]


def hop(array, bit):
    return lax.ppermute(array, "shard", [(i, i ^ bit) for i in range(8)])


def gather_all(pack):
    return lax.all_gather(pack, "shard", axis=0, tiled=False)


def scatter_all(every):
    return lax.psum_scatter(every, "shard", scatter_dimension=0, tiled=True)[0]


def weave(near, far):
    groups = []
    for one, two in zip(near, far):
        groups += [list(one), list(two)]
    return Pieces(groups)


def combine(*outputs):
    terms = [term if isinstance(term, tuple) else (term, None) for out in outputs for term in out]
    rows, width = terms[0][0].shape[-2:]
    step = rows // 2

    def spec(k):
        if k is None:
            return pl.BlockSpec((step, width), lambda i: (i, 0))
        return pl.BlockSpec((pl.Squeezed(), step, width), lambda i: (k, i, 0))

    def kernel(*refs):
        at = 0
        for out, out_ref in zip(outputs, refs[len(terms) :]):
            total = refs[at][...].astype(F32)
            for ref in refs[at + 1 : at + len(out)]:
                total = total + ref[...].astype(F32)
            at += len(out)
            out_ref[...] = total.astype(BF16)

    found = pl.pallas_call(
        kernel,
        grid=(rows // step,),
        in_specs=[spec(k) for _, k in terms],
        out_specs=[pl.BlockSpec((step, width), lambda i: (i, 0))] * len(outputs),
        out_shape=[jax.ShapeDtypeStruct((rows, width), BF16)] * len(outputs),
        compiler_params=params(),
        cost_estimate=cost(0, 4),
        name="combine",
    )(*[array for array, _ in terms])
    return found[0] if len(outputs) == 1 else found


def rep_hop(array, pairs):
    return lax.ppermute(array.astype(BF16), "rep", pairs)


INWARD = [(0, 1), (3, 2)]
ACROSS = [(1, 2), (2, 1)]
OUTWARD = [(1, 0), (2, 3)]


def at_end(inner, outer):
    place = lax.axis_index("rep")
    return jnp.where((place == 0) | (place == 3), outer.astype(F32), inner)


def on_device(sizes, *arrays):
    (
        block_input, document_numbers, attn_gain, w_query, key_weight, value_weight, query_gain,
        key_gain, w_output, ffn_gain, w_gate, w_up, w_down, cotangent,
    ) = arrays
    reps, parts = sizes
    _, length, width = block_input.shape
    ff = w_gate.shape[1]
    paired = parts == 8 and reps == 4
    me = lax.axis_index("shard").astype(jnp.int32)
    place = me.reshape(1) if paired else jnp.zeros((1,), jnp.int32)
    x = block_input.reshape(length, width)
    back_out = cotangent.reshape(length, width)
    numbers = document_numbers.reshape(length)
    rows = width // parts
    seg = SLAB // parts
    slabs = ff // SLAB
    few = query_gain.shape[0]

    lane = jnp.arange(width)

    def spot(gain, times, size):
        share = gain.shape[0]
        wide = jnp.tile(gain, width // share)
        return jnp.where((lane < size * times) & ((lane % size) // share == me), wide, 0)

    empty = jnp.zeros((width,), BF16)
    gain_rows = [
        spot(attn_gain, 1, width),
        spot(query_gain, 2, HEAD_SIZE),
        spot(key_gain, 2, HEAD_SIZE),
        spot(ffn_gain, 1, width),
    ]
    first_pack = jnp.concatenate(
        [
            w_query,
            jnp.concatenate([key_weight, value_weight], axis=1),
            jnp.stack(gain_rows + [empty] * 12),
        ]
    )
    tables = tables_of(numbers)
    run = block_paired if paired else block_simple
    args = (me, place, x, back_out, tables, first_pack, w_output, w_gate, w_up, w_down)
    block_output, input_grad, attn_grad, feed_grads = run(*args)
    grad_gate, grad_up, grad_down = feed_grads
    grad_query = attn_grad[:rows]
    grad_key = attn_grad[rows : 2 * rows, :512]
    grad_value = attn_grad[rows : 2 * rows, 512:]

    def diagonal(*pairs):
        total = 0.0
        for weight, grad in pairs:
            total = total + jnp.sum(weight.astype(F32) * grad, axis=1)
        return total

    grad_gain_attn = diagonal(
        (w_query, grad_query), (key_weight, grad_key), (value_weight, grad_value)
    ) / attn_gain.astype(F32)
    grad_gain_ffn = diagonal((w_gate, grad_gate), (w_up, grad_up)) / ffn_gain.astype(F32)

    def small(row):
        both = attn_grad[3 * rows + row, :64] + attn_grad[3 * rows + row, 64:128]
        return lax.dynamic_slice(both, (me * few,), (few,))

    return (
        block_output[None],
        input_grad[None],
        grad_gain_attn,
        grad_query,
        grad_key,
        grad_value,
        small(0),
        small(1),
        attn_grad[2 * rows : 3 * rows],
        grad_gain_ffn,
        grad_gate,
        grad_up,
        grad_down,
    )


def block_simple(me, place, x, back_out, tables, first_pack, w_output, w_gate, w_up, w_down):
    rows, ff = w_gate.shape
    parts = x.shape[1] // rows
    seg = SLAB // parts
    slabs = ff // SLAB
    tall = rows + seg

    def columns(weight):
        cut = weight.reshape(rows, parts, slabs, seg).transpose(2, 0, 1, 3)
        return cut.reshape(slabs, rows, SLAB)

    pack = jnp.concatenate(
        [
            jnp.concatenate([columns(w_gate), columns(w_up)], axis=2),
            w_down.reshape(slabs, seg, x.shape[1]),
        ],
        axis=1,
    ).reshape(slabs * tall, 2 * SLAB)
    every = gather_all(first_pack)
    pairs = [(every[k], every[k], 1) for k in range(parts)]
    pieces = Pieces(stacked=gather_all(jnp.concatenate([w_output, pack])))
    normed_one, *units, q_aug, k_aug, v_aug, gains = project(pairs, place, x, tables)
    attended_0, q_back_0 = attend(q_aug, k_aug, v_aug, 0, 4)
    attended_1, q_back_1 = attend(q_aug, k_aug, v_aug, 4, 4)
    attended = (attended_0, attended_1)
    first_sum, normed_two, normed_two_t = output_rows(pieces, place, attended, x, gains)
    out, back, grads = feed(
        pieces, place, rows, slabs, normed_two, normed_two_t, back_out, False
    )
    total = lax.psum(scatter_all(grads), "rep").astype(F32).reshape(slabs, tall, 2 * SLAB)
    back_first, back_attended, grad_out = middle(
        pieces, place, first_sum, back_out, attended, gains, [back]
    )
    halves_0 = attend_back(q_back_0, k_aug, v_aug, attended_0, back_attended, 0, 4)
    halves_1 = attend_back(q_back_1, k_aug, v_aug, attended_1, back_attended, 4, 4)
    back_raw, own, sib = raw_back(
        parts, place, (halves_0[0], halves_1[0], halves_0[1], halves_1[1]), units, normed_one,
        tables[0], tables[1], gains, grad_out,
    )
    every = jnp.stack([own, sib], axis=1).reshape((parts,) + own.shape[1:])
    attn_grad = lax.psum(scatter_all(every), "rep").astype(F32)
    input_grad = input_back(pairs, place, back_raw, x, back_first, gains)

    def uncut(block):
        return block.reshape(slabs, rows, parts, seg).transpose(1, 2, 0, 3).reshape(rows, ff)

    feed_grads = (
        uncut(total[:, :rows, :SLAB]),
        uncut(total[:, :rows, SLAB:]),
        total[:, rows:, :].reshape(slabs * seg, x.shape[1]),
    )
    return (first_sum + out).astype(BF16), input_grad, attn_grad, feed_grads


def fence(outputs, *hops):
    found = tie(*outputs, *hops)
    return found[: len(outputs)], list(found[len(outputs) :])


def block_paired(me, place, x, back_out, tables, first_pack, w_output, w_gate, w_up, w_down):
    rows = w_gate.shape[0]
    chunks = (3, 3, 3)

    first = hop(first_pack, 2)
    second = hop(first_pack, 4)
    twin = hop(first_pack, 1)
    made, (first, second, twin) = fence(
        [*pack_rows(chunks, w_output, w_gate, w_up, w_down), *tables], first, second, twin
    )
    packs, tables = list(made[:3]), made[3:]
    corner_a = hop(second[:rows], 2)
    corner_b = hop(first[rows:], 4)
    far = [twin] + [hop(piece, 1) for piece in (first, second, corner_a, corner_b)]
    near = [first_pack, first, second, corner_a, corner_b]
    pairs = []
    for k in range(3):
        pairs += [(near[k], near[k], 1), (far[k], far[k], 1)]
    pairs += [(near[3], near[4], 0), (far[3], far[4], 0)]

    pack = after(packs[0], corner_a, corner_b, far[1], far[2])
    first, second, twin = hop(pack, 2), hop(pack, 4), hop(pack, 1)
    normed_one, *units, q_aug, k_aug, v_aug, gains = project(pairs, place, x, tables)
    (attended_0, q_back_0, k_aug), (first, second, twin) = fence(
        [*attend(q_aug, k_aug, v_aug, 0, 4), k_aug], first, second, twin
    )
    corner_a, corner_b = hop(second[:, :512], 2), hop(first[:, 512:], 4)
    far = [hop(first, 1), hop(second, 1)]
    packs[1] = after(packs[1], first, second)
    waiting = [hop(packs[1], bit) for bit in (1, 2, 4, 6)]
    (attended_1, q_back_1), (corner_a, corner_b, *far) = fence(
        attend(q_aug, k_aug, v_aug, 4, 4), corner_a, corner_b, *far
    )
    attended = (attended_0, attended_1)
    early = weave(
        [[pack], [first], [second], [corner_a, corner_b]],
        [[twin], [far[0]], [far[1]], [hop(corner_a, 1), hop(corner_b, 1)]],
    )
    first_sum, normed_two, normed_two_t = output_rows(early, place, attended, x, gains)

    def finish(pack, twin, first, second, corner):
        near = (first, second, corner)
        far = [hop(piece, 1) for piece in near]
        return weave([[pack]] + [[a] for a in near], [[twin]] + [[a] for a in far])

    def feed_step(pieces, begin, n, paired):
        return feed(pieces, place, begin, n, normed_two, normed_two_t, back_out, paired)

    (out_0, back_0, own_0, sib_0, normed_two), waiting = fence(
        [*feed_step(early, rows, chunks[0], True), normed_two], *waiting
    )
    later = finish(packs[1], *waiting)
    waiting = [hop(packs[2], bit) for bit in (1, 2, 4, 6)]
    other_0 = hop(after(sib_0, *later.arrays), 1)
    (out_1, back_1, own_1, sib_1, normed_two), (other_0, *waiting) = fence(
        [*feed_step(later, 0, chunks[1], True), normed_two], other_0, *waiting
    )
    last = finish(packs[2], *waiting)
    other_1 = hop(sib_1, 1)
    moved_0 = hop(combine([(own_0, 3), (other_0, 3)]), 2)
    normed_two, other_1 = tie(normed_two, other_1)
    term = combine([(own_1, 3), (other_1, 3)])
    normed_two, term = tie(normed_two, term)
    moved_1 = hop(term, 4)
    (out_2, back_2, own_2, sib_2), (moved_0, moved_1) = fence(
        feed_step(last, 0, chunks[2], True), moved_0, moved_1
    )
    other_2 = hop(sib_2, 1)
    one, two, three, four = combine(
        [(own_0, 1), (other_0, 1)],
        [(own_0, 2), (other_0, 2), moved_0],
        [(own_1, 1), (other_1, 1), moved_1],
        [(own_1, 2), (other_1, 2)],
    )
    back_2, one, two, three, four = tie(back_2, one, two, three, four)
    first_0, second_0 = hop(one, 2), hop(two, 4)
    first_1, second_1 = hop(three, 2), hop(four, 4)
    middles = middle(
        early, place, first_sum, back_out, attended, gains, [back_0, back_1, back_2]
    )
    (back_first, back_attended, grad_out), (other_2,) = fence(middles, other_2)
    term = combine([(own_2, 3), (other_2, 3)])
    back_attended, term = tie(back_attended, term)
    moved_2 = hop(term, 2)
    halves = attend_back(q_back_0, k_aug, v_aug, attended_0, back_attended, 0, 4)
    (dq_0, dkv_0, back_attended), (first_0, second_0) = fence(
        [*halves, back_attended], first_0, second_0
    )
    grads_0 = combine([(own_0, 0), (other_0, 0), first_0, second_0])
    back_attended, grads_0 = tie(back_attended, grads_0)
    inward_0 = rep_hop(grads_0, INWARD)
    halves = attend_back(q_back_1, k_aug, v_aug, attended_1, back_attended, 4, 4)
    (dq_1, dkv_1), (moved_2, inward_0, first_1, second_1) = fence(
        halves, moved_2, inward_0, first_1, second_1
    )
    one, two, grads_1, half_0 = combine(
        [(own_2, 1), (other_2, 1)],
        [(own_2, 2), (other_2, 2), moved_2],
        [(own_1, 0), (other_1, 0), first_1, second_1],
        [grads_0, inward_0],
    )
    dq_1, one, two, grads_1, half_0 = tie(dq_1, one, two, grads_1, half_0)
    first_2, second_2 = hop(one, 2), hop(two, 4)
    inward_1 = rep_hop(grads_1, INWARD)
    across_0 = rep_hop(half_0, ACROSS)
    result = raw_back(
        8, place, (dq_0, dq_1, dkv_0, dkv_1), units, normed_one, tables[0], tables[1], gains,
        grad_out,
    )
    (back_raw, own, sib), (first_2, second_2, inward_1, across_0) = fence(
        result, first_2, second_2, inward_1, across_0
    )
    other = hop(sib, 1)
    half_1, total_0, grads_2 = combine(
        [grads_1, inward_1], [half_0, across_0], [(own_2, 0), (other_2, 0), first_2, second_2]
    )
    back_raw, other, half_1, total_0, grads_2 = tie(back_raw, other, half_1, total_0, grads_2)
    term = combine([(own, 3), (other, 3)])
    back_raw, term = tie(back_raw, term)
    moved = hop(term, 4)
    outward_0 = rep_hop(total_0, OUTWARD)
    across_1 = rep_hop(half_1, ACROSS)
    inward_2 = rep_hop(grads_2, INWARD)
    input_grad = input_back(pairs, place, back_raw, x, back_first, gains)
    (input_grad,), (moved,) = fence([input_grad], moved)
    one, two = combine([(own, 1), (other, 1), moved], [(own, 2), (other, 2)])
    one, two, across_1, inward_2, first_sum = tie(one, two, across_1, inward_2, first_sum)
    first, second = hop(one, 2), hop(two, 4)
    total_1, half_2 = combine([half_1, across_1], [grads_2, inward_2])
    first_sum, total_1, half_2, outward_0 = tie(first_sum, total_1, half_2, outward_0)
    outward_1 = rep_hop(total_1, OUTWARD)
    across_2 = rep_hop(half_2, ACROSS)
    outs = out_0.astype(F32) + out_1.astype(F32) + out_2.astype(F32)
    block_output = (first_sum + outs).astype(BF16)
    (block_output,), (first, second) = fence([block_output], first, second)
    grads = combine([(own, 0), (other, 0), first, second])
    inward = rep_hop(grads, INWARD)
    across_2, _ = tie(across_2, grads)
    total_2 = combine([half_2, across_2])
    outward_2 = rep_hop(total_2, OUTWARD)
    inward, outward_1, _ = tie(inward, outward_1, total_2)
    half = combine([grads, inward])
    across = rep_hop(half, ACROSS)
    outward_2, across, _ = tie(outward_2, across, half)
    total = combine([half, across])
    outward = rep_hop(total, OUTWARD)
    total, outward_2 = tie(total, outward_2)
    spot = lax.axis_index("rep")
    flag = ((spot == 0) | (spot == 3)).astype(jnp.int32).reshape(1)
    feed_grads = unpack_rows(flag, total_0, outward_0, total_1, outward_1, total_2, outward_2)
    (*feed_grads,), (outward,) = fence(feed_grads, outward)
    return block_output, input_grad, at_end(total.astype(F32), outward), feed_grads


def solution(mesh):
    sizes = (mesh.shape["rep"], mesh.shape["shard"])
    whole = P(("rep", "shard"), None, None)
    matrix = P("shard", None)
    vector = P("shard")
    in_specs = (
        whole, P(("rep", "shard"), None), vector, matrix, matrix, matrix, vector, vector, matrix,
        vector, matrix, matrix, matrix, whole,
    )
    out_specs = (
        whole, whole, vector, matrix, matrix, matrix, vector, vector, matrix, vector, matrix,
        matrix, matrix,
    )
    return jax.shard_map(
        lambda *arrays: on_device(sizes, *arrays),
        mesh=mesh,
        in_specs=in_specs,
        out_specs=out_specs,
        check_vma=False,
    )
```

```python
import jax
import jax.numpy as jnp
from jax import lax
from jax.experimental import pallas as pl
from jax.experimental.pallas import tpu as pltpu
from jax.sharding import PartitionSpec as P

QUERY_HEADS = 16
KEY_VALUE_HEADS = 8
HEAD_SIZE = 64
EPS = 1e-05
ROPE_BASE = 1000000.0
FAR = 32768.0
TILE = 256
SLAB = 512
VMEM_LIMIT = 60 * 1024 * 1024
NT = ((1,), (1,))
NN = ((1,), (0,))
TN = ((0,), (0,))
BF16 = jnp.bfloat16
F32 = jnp.float32
SMALL = pl.BlockSpec(memory_space=pltpu.SMEM)


def dot(left, right, dims=NN):
    return lax.dot_general(left, right, (dims, ((), ())), preferred_element_type=F32)


def params():
    return pltpu.CompilerParams(vmem_limit_bytes=VMEM_LIMIT)


def cost(giga_flops, mega_bytes, exps=0):
    return pl.CostEstimate(
        flops=int(giga_flops * 10**6),
        bytes_accessed=int(mega_bytes * 10**3),
        transcendentals=exps // 1000,
    )


def fixed(shape, where=None):
    index = (0,) * len(shape) if where is None else where
    return pl.BlockSpec(shape, lambda *_: index, pipeline_mode=pl.Buffered(1))


def by_rows(width, rows=TILE):
    return pl.BlockSpec((rows, width), lambda i: (i, 0))


class Pieces:
    def __init__(self, groups=None, stacked=None):
        self.stacked = stacked
        self.count = len(groups) if stacked is None else stacked.shape[0]
        self.groups = groups if stacked is None else [[stacked]] * self.count
        self.arrays = [array for group in self.groups for array in group]
        self.layout = [len(group) for group in self.groups]

    def specs(self, rows, start):
        once = pl.Buffered(1) if start(0) == start(1) else None
        found = []
        for k, group in enumerate(self.groups):
            for array in group:
                shape = (pl.Element(rows), pl.Element(array.shape[-1]))
                if self.stacked is None:
                    found.append(
                        pl.BlockSpec(shape, lambda i: (start(i), 0), pipeline_mode=once)
                    )
                else:
                    found.append(
                        pl.BlockSpec(
                            (pl.Squeezed(),) + shape,
                            lambda i, k=k: (k, start(i), 0),
                            pipeline_mode=once,
                        )
                    )
        return found


def grouped(refs, layout):
    groups, at = [], 0
    for size in layout:
        groups.append(refs[at : at + size])
        at += size
    return groups


def fill(target, at, group, rows):
    left = 0
    for ref in group:
        right = left + ref.shape[1]
        target[at, left:right] = ref[rows, :]
        left = right


def split3(value):
    high = value.astype(BF16).astype(F32)
    rest = value - high
    middle = rest.astype(BF16).astype(F32)
    return high, middle, rest - middle


def aligned(index, rows):
    return pl.ds(pl.multiple_of(index * rows, rows), rows)


def unit_of(rows):
    inverse = lax.rsqrt(jnp.mean(rows * rows, axis=-1, keepdims=True) + EPS)
    return rows * inverse, inverse


def head_blocks():
    first = lax.broadcasted_iota(jnp.int32, (128, 128), 0) // HEAD_SIZE
    second = lax.broadcasted_iota(jnp.int32, (128, 128), 1) // HEAD_SIZE
    return (first == second).astype(BF16)


def head_mean(rows, blocks):
    return dot(rows.astype(BF16), blocks) * (1.0 / HEAD_SIZE)


def swap_halves(rows, first):
    return jnp.where(first, pltpu.roll(rows, 96, 1), pltpu.roll(rows, 32, 1))


def lanes(rows=TILE):
    return lax.broadcasted_iota(jnp.int32, (rows, 128), 1)


def load_pairs(parts, me_ref, refs, w_all):
    rows = w_all.shape[0] // parts

    @pl.when(pl.program_id(0) == 0)
    def _():
        for k in range(parts):
            at = aligned(me_ref[0] ^ k, rows)
            w_all[at, :1024] = refs[2 * k][...]
            w_all[at, 1024:] = refs[2 * k + 1][...]


def pair_specs(pieces, rows):
    arrays, specs = [], []
    for piece in pieces:
        left, right, at = piece
        arrays += [left, right]
        specs += [fixed((rows, 1024)), fixed((rows, 1024), (at, 0))]
    return arrays, specs


def project_kernel(parts, me_ref, x_ref, cos_ref, sin_ref, qx_ref, kx_ref, *refs):
    gain_refs = refs[2 * parts : 3 * parts]
    n_ref, unit_ref, scale_ref, q_ref, k_ref, v_ref, gain_ref, w_all = refs[3 * parts :]
    load_pairs(parts, me_ref, refs, w_all)

    @pl.when(pl.program_id(0) == 0)
    def _():
        total = gain_refs[0][...].astype(F32)
        for ref in gain_refs[1:]:
            total = total + ref[...].astype(F32)
        gain_ref[...] = total

    unit, _ = unit_of(x_ref[...].astype(F32))
    normed = (unit * gain_ref[0:1, :]).astype(BF16)
    n_ref[...] = normed
    raw = dot(normed, w_all[...])
    blocks = head_blocks()
    lane = lanes()
    first = (lane % HEAD_SIZE) < HEAD_SIZE // 2
    low = lane < HEAD_SIZE
    cosine, sine = cos_ref[...], sin_ref[...]
    for p in range(12):
        at = slice(p * 128, (p + 1) * 128)
        rows_in = raw[:, at]
        inverse = lax.rsqrt(head_mean(rows_in * rows_in, blocks) + EPS)
        unit = rows_in * inverse
        unit_ref[:, at] = unit.astype(BF16)
        scale_ref[:, at] = inverse.astype(BF16)
        scaled = unit * gain_ref[1 + p // 8 : 2 + p // 8, :128]
        turned = scaled * cosine + swap_halves(scaled, first) * sine
        if p < 8:
            turned = turned * HEAD_SIZE**-0.5
            out, more, at = q_ref, qx_ref[...], 2 * p
        else:
            out, more, at = k_ref, kx_ref[...], 2 * (p - 8)
        out[at] = jnp.where(low, turned, more).astype(BF16)
        out[at + 1] = jnp.where(low, pltpu.roll(turned, 64, 1), more).astype(BF16)
    more = ((lane >= 64) & (lane < 67)).astype(F32)
    for p in range(4):
        rows_in = raw[:, 1536 + p * 128 : 1664 + p * 128]
        v_ref[2 * p] = jnp.where(low, rows_in, more).astype(BF16)
        v_ref[2 * p + 1] = jnp.where(low, pltpu.roll(rows_in, 64, 1), more).astype(BF16)


def project(pieces, me, x, tables):
    length, width = x.shape
    parts = len(pieces)
    rows = width // parts
    arrays, specs = pair_specs(pieces, rows)
    gains = [(piece[1], (piece[2] + 1) * rows // 16) for piece in pieces]

    def heads(count):
        return pl.BlockSpec((count, TILE, 128), lambda i: (0, i, 0))

    return pl.pallas_call(
        lambda *refs: project_kernel(parts, *refs),
        grid=(length // TILE,),
        in_specs=[SMALL, by_rows(width)]
        + [by_rows(128)] * 4
        + specs
        + [fixed((16, 1024), (at, 0)) for _, at in gains],
        out_specs=[by_rows(width), by_rows(1536), by_rows(1536), heads(16), heads(8), heads(8)]
        + [fixed((16, 1024))],
        out_shape=[
            jax.ShapeDtypeStruct((length, width), BF16),
            jax.ShapeDtypeStruct((length, 1536), BF16),
            jax.ShapeDtypeStruct((length, 1536), BF16),
            jax.ShapeDtypeStruct((16, length, 128), BF16),
            jax.ShapeDtypeStruct((8, length, 128), BF16),
            jax.ShapeDtypeStruct((8, length, 128), BF16),
            jax.ShapeDtypeStruct((16, 1024), F32),
        ],
        scratch_shapes=[pltpu.VMEM((width, 2048), BF16)],
        compiler_params=params(),
        cost_estimate=cost(8, 25),
        name="project",
    )(me, x, *tables, *arrays, *[array for array, _ in gains])


def causal(query_axis):
    first = lax.broadcasted_iota(jnp.int32, (TILE, TILE), 0)
    second = lax.broadcasted_iota(jnp.int32, (TILE, TILE), 1)
    return (first >= second) if query_axis == 0 else (second >= first)


def attend_kernel(q_ref, k_ref, v_ref, o_ref, qb_ref):
    tiles = q_ref.shape[1] // TILE
    keep = causal(0)
    lane = lax.broadcasted_iota(jnp.int32, (TILE, 128), 1)
    for i in range(tiles):
        rows = slice(i * TILE, (i + 1) * TILE)
        before = slice(0, i * TILE)
        halves = []
        for h in range(2):
            q = q_ref[h, rows, :]
            weights = jnp.where(keep, jnp.exp(dot(q, k_ref[0, rows, :], NT)), 0.0)
            out = dot(weights.astype(BF16), v_ref[0, rows, :])
            if i:
                weights = jnp.exp(dot(q, k_ref[0, before, :], NT)).astype(BF16)
                out = out + dot(weights, v_ref[0, before, :])
            total = out[:, 64:65]
            halves.append(out / total)
            high, middle, low = split3(-jnp.log(total))
            extra = jnp.where(
                lane == 68, high, jnp.where(lane == 69, middle, jnp.where(lane == 70, low, 0.0))
            )
            qb_ref[h, rows, :] = (q.astype(F32) + extra).astype(BF16)
        both = jnp.where(lane < 64, halves[0], pltpu.roll(halves[1], 64, 1))
        o_ref[rows, :] = both.astype(BF16)


def attend(q_aug, k_aug, v_aug, begin, groups):
    _, length, _ = q_aug.shape
    return pl.pallas_call(
        attend_kernel,
        grid=(groups,),
        in_specs=[
            pl.BlockSpec((2, length, 128), lambda g: (g + begin, 0, 0)),
            pl.BlockSpec((1, length, 128), lambda g: (g + begin, 0, 0)),
            pl.BlockSpec((1, length, 128), lambda g: (g + begin, 0, 0)),
        ],
        out_specs=[
            pl.BlockSpec((length, 128), lambda g: (0, g)),
            pl.BlockSpec((2, length, 128), lambda g: (g, 0, 0)),
        ],
        out_shape=[
            jax.ShapeDtypeStruct((length, groups * 128), BF16),
            jax.ShapeDtypeStruct((2 * groups, length, 128), BF16),
        ],
        compiler_params=params(),
        cost_estimate=cost(2.5 * groups, 2 * groups, groups * 2**20),
        name="attend",
    )(q_aug, k_aug, v_aug)


def attend_back_kernel(q_ref, k_ref, v_ref, o_ref, do_ref, dq_ref, dkv_ref, do_aug, k_t, dq_t):
    length = q_ref.shape[1]
    tiles = length // TILE
    keep = causal(1)
    lane = lax.broadcasted_iota(jnp.int32, (length, 128), 1)
    back = do_ref[...].astype(F32)
    product = back * o_ref[...].astype(F32)
    for h in range(2):
        own = (lane < 64) if h == 0 else (lane >= 64)
        centre = jnp.sum(jnp.where(own, product, 0.0), axis=1, keepdims=True)
        moved = back if h == 0 else pltpu.roll(back, 64, 1)
        high, middle, low = split3(-centre)
        extra = jnp.where(
            lane == 64, high, jnp.where(lane == 65, middle, jnp.where(lane == 66, low, 0.0))
        )
        do_aug[h] = jnp.where(lane < 64, moved, extra).astype(BF16)
    k_t[...] = k_ref[0].astype(F32).T[:64, :].astype(BF16)
    low_half = lax.broadcasted_iota(jnp.int32, (TILE, 128), 1) < 64
    for j in range(tiles):
        cols = slice(j * TILE, (j + 1) * TILE)
        k = k_ref[0, cols, :]
        v = v_ref[0, cols, :]
        dk = 0.0
        dv = 0.0
        for i, stop in ((j, j + 1), (j + 1, tiles)):
            if i == tiles:
                continue
            rows = slice(i * TILE, stop * TILE)
            for h in range(2):
                q = q_ref[h, rows, :]
                do = do_aug[h, rows, :]
                probs = jnp.exp(dot(k, q, NT))
                if i == j:
                    probs = jnp.where(keep, probs, 0.0)
                scores = (probs * dot(v, do, NT)).astype(BF16)
                dv = dv + dot(probs.astype(BF16), do)
                dk = dk + dot(scores, q)
                to_q = dot(k_t[:, cols], scores)
                if j == 0:
                    dq_t[h * 64 : (h + 1) * 64, rows] = to_q
                else:
                    dq_t[h * 64 : (h + 1) * 64, rows] += to_q
        dkv_ref[cols, :] = jnp.where(low_half, dk, pltpu.roll(dv, 64, 1))
    dq_ref[...] = dq_t[...].T


def attend_back(q_back, k_aug, v_aug, attended, back_attended, begin, groups):
    _, length, _ = q_back.shape
    by_group = pl.BlockSpec((length, 128), lambda g: (0, g + begin))
    out_group = pl.BlockSpec((length, 128), lambda g: (0, g))
    return pl.pallas_call(
        attend_back_kernel,
        grid=(groups,),
        in_specs=[
            pl.BlockSpec((2, length, 128), lambda g: (g, 0, 0)),
            pl.BlockSpec((1, length, 128), lambda g: (g + begin, 0, 0)),
            pl.BlockSpec((1, length, 128), lambda g: (g + begin, 0, 0)),
            out_group,
            by_group,
        ],
        out_specs=[out_group, out_group],
        out_shape=[jax.ShapeDtypeStruct((length, groups * 128), F32)] * 2,
        scratch_shapes=[
            pltpu.VMEM((2, length, 128), BF16),
            pltpu.VMEM((64, length), BF16),
            pltpu.VMEM((128, length), F32),
        ],
        compiler_params=params(),
        cost_estimate=cost(5 * groups, 3 * groups, groups * 2**20),
        name="attend_back",
    )(q_back, k_aug, v_aug, attended, back_attended)


def output_kernel(layout, me_ref, o0_ref, o1_ref, x_ref, gain_ref, *refs):
    sum_ref, n_ref, nt_ref, w_all = refs[-4:]
    rows = w_all.shape[0] // len(layout)

    @pl.when(pl.program_id(0) == 0)
    def _():
        for k, group in enumerate(grouped(refs, layout)):
            fill(w_all, aligned(me_ref[0] ^ k, rows), group, slice(None))

    total = x_ref[...].astype(F32) + dot(o0_ref[...], w_all[:512, :])
    total = total + dot(o1_ref[...], w_all[512:, :])
    sum_ref[...] = total
    unit, _ = unit_of(total)
    normed = unit * gain_ref[3:4, :]
    n_ref[...] = normed.astype(BF16)
    nt_ref[...] = normed.T.astype(BF16)


def output_rows(pieces, me, attended, x, gain):
    length, width = x.shape
    parts = pieces.count
    rows = width // parts
    return pl.pallas_call(
        lambda *refs: output_kernel(pieces.layout, *refs),
        grid=(length // TILE,),
        in_specs=[SMALL, by_rows(512), by_rows(512), by_rows(width), fixed((16, 1024))]
        + pieces.specs(rows, lambda i: 0),
        out_specs=[by_rows(width), by_rows(width), pl.BlockSpec((width, TILE), lambda i: (0, i))],
        out_shape=[
            jax.ShapeDtypeStruct((length, width), F32),
            jax.ShapeDtypeStruct((length, width), BF16),
            jax.ShapeDtypeStruct((width, length), BF16),
        ],
        scratch_shapes=[pltpu.VMEM((1024, width), BF16)],
        compiler_params=params(),
        cost_estimate=cost(5, 15),
        name="output_rows",
    )(me, *attended, x, gain, *pieces.arrays)


def scatter_rows(me, parts, value, rows, own_ref, sib_ref, at):
    half = me >> 1
    core = me & 1
    for q in range(parts // 2):
        for s, ref in enumerate((own_ref, sib_ref)):
            source = 2 * q + (core ^ s)
            ref[q ^ half, at : at + rows, :] = value[aligned(source, rows), :]


def feed_kernel(layout, paired, me_ref, n_ref, nt_ref, c_ref, *refs):
    parts = len(layout)
    f_ref, b_ref, *grad_refs = refs[sum(layout) : -8]
    w_all, d_all, back, hidden, w_grad, d_grad, f_sum, b_sum = refs[-8:]
    me = me_ref[0]
    rows = w_all.shape[0] // parts
    seg = SLAB // parts
    for k, group in enumerate(grouped(refs, layout)):
        fill(w_all, aligned(me ^ k, rows), group, slice(0, rows))
        fill(d_all, aligned(me ^ k, seg), group, slice(rows, rows + seg))
    step = pl.program_id(0)

    @pl.when(step == 0)
    def _():
        f_sum[...] = jnp.zeros_like(f_sum)
        b_sum[...] = jnp.zeros_like(b_sum)

    both = dot(n_ref[...], w_all[...])
    gate = both[:, :SLAB]
    up = both[:, SLAB:]
    sig = 1.0 / (1.0 + jnp.exp(-gate))
    swish = gate * sig
    hidden[...] = (swish * up).astype(BF16)
    back_hidden = dot(c_ref[...], d_all[...], NT)
    back[:, SLAB:] = (back_hidden * swish).astype(BF16)
    back[:, :SLAB] = (back_hidden * up * sig * (1.0 + gate * (1.0 - sig))).astype(BF16)
    f_sum[...] += dot(hidden[...], d_all[...])
    b_sum[...] += dot(back[...], w_all[...], NT)
    w_grad[...] = dot(nt_ref[...], back[...]).astype(BF16)
    d_grad[...] = dot(hidden[...], c_ref[...], TN).astype(BF16)

    @pl.when(step == pl.num_programs(0) - 1)
    def _():
        f_ref[...] = f_sum[...].astype(BF16)
        b_ref[...] = b_sum[...].astype(BF16)

    if paired:
        own_ref, sib_ref = grad_refs
        scatter_rows(me, parts, w_grad, rows, own_ref, sib_ref, 0)
        scatter_rows(me, parts, d_grad, seg, own_ref, sib_ref, rows)
    else:
        for d in range(parts):
            grad_refs[0][d, :rows, :] = w_grad[d * rows : (d + 1) * rows, :]
            grad_refs[0][d, rows:, :] = d_grad[d * seg : (d + 1) * seg, :]


def feed(pieces, me, begin, slabs, normed, normed_t, cotangent, paired):
    length, width = normed.shape
    parts = pieces.count
    rows = width // parts + SLAB // parts
    depth = parts // 2 if paired else parts
    count = 2 if paired else 1
    grads = pl.BlockSpec((depth, rows, 2 * SLAB), lambda i: (0, i, 0))
    return pl.pallas_call(
        lambda *refs: feed_kernel(pieces.layout, paired, *refs),
        grid=(slabs,),
        in_specs=[SMALL, fixed((length, width)), fixed((width, length)), fixed((length, width))]
        + pieces.specs(rows, lambda i: (begin // 16 + i * (rows // 16)) * 16),
        out_specs=[fixed((length, width)), fixed((length, width))] + [grads] * count,
        out_shape=[
            jax.ShapeDtypeStruct((length, width), BF16),
            jax.ShapeDtypeStruct((length, width), BF16),
        ]
        + [jax.ShapeDtypeStruct((depth, slabs * rows, 2 * SLAB), BF16)] * count,
        scratch_shapes=[
            pltpu.VMEM((width, 2 * SLAB), BF16),
            pltpu.VMEM((SLAB, width), BF16),
            pltpu.VMEM((length, 2 * SLAB), BF16),
            pltpu.VMEM((length, SLAB), BF16),
            pltpu.VMEM((width, 2 * SLAB), BF16),
            pltpu.VMEM((SLAB, width), BF16),
            pltpu.VMEM((length, width), F32),
            pltpu.VMEM((length, width), F32),
        ],
        compiler_params=params(),
        cost_estimate=cost(12.5 * slabs, 20 + 6 * slabs),
        name="feed",
    )(me, normed, normed_t, cotangent, *pieces.arrays)


def middle_kernel(layout, sums, me_ref, s_ref, c_ref, o0_ref, o1_ref, gain_ref, *refs):
    b_refs = refs[:sums]
    f_ref, a_ref, g_ref, w_all, total = refs[-5:]
    rows = w_all.shape[0] // len(layout)
    step = pl.program_id(0)

    @pl.when(step == 0)
    def _():
        for k, group in enumerate(grouped(refs[sums:], layout)):
            fill(w_all, aligned(me_ref[0] ^ k, rows), group, slice(None))

    back = b_refs[0][...].astype(F32)
    for ref in b_refs[1:]:
        back = back + ref[...].astype(F32)
    unit, inverse = unit_of(s_ref[...])
    scaled = back * gain_ref[3:4, :]
    first = c_ref[...].astype(F32) + inverse * (
        scaled - unit * jnp.mean(scaled * unit, axis=-1, keepdims=True)
    )
    f_ref[...] = first
    short = first.astype(BF16)
    a_ref[...] = dot(short, w_all[...], NT).astype(BF16)
    grads = [dot(ref[...], short, TN) for ref in (o0_ref, o1_ref)]

    @pl.when(step == 0)
    def _():
        total[:512, :] = grads[0]
        total[512:, :] = grads[1]

    @pl.when(step > 0)
    def _():
        total[:512, :] += grads[0]
        total[512:, :] += grads[1]

    @pl.when(step == pl.num_programs(0) - 1)
    def _():
        g_ref[...] = total[...].astype(BF16)


def middle(pieces, me, first_sum, cotangent, attended, gain, backs):
    length, width = first_sum.shape
    parts = pieces.count
    rows = width // parts
    return pl.pallas_call(
        lambda *refs: middle_kernel(pieces.layout, len(backs), *refs),
        grid=(length // TILE,),
        in_specs=[SMALL, by_rows(width), by_rows(width), by_rows(512), by_rows(512), fixed((16, 1024))]
        + [by_rows(width)] * len(backs)
        + pieces.specs(rows, lambda i: 0),
        out_specs=[by_rows(width), by_rows(1024), fixed((1024, width))],
        out_shape=[
            jax.ShapeDtypeStruct((length, width), F32),
            jax.ShapeDtypeStruct((length, 1024), BF16),
            jax.ShapeDtypeStruct((1024, width), BF16),
        ],
        scratch_shapes=[pltpu.VMEM((1024, width), BF16), pltpu.VMEM((1024, width), F32)],
        compiler_params=params(),
        cost_estimate=cost(9, 32),
        name="middle",
    )(me, first_sum, cotangent, *attended, gain, *backs, *pieces.arrays)


def raw_back_kernel(
    parts, me_ref, dq0_ref, dq1_ref, dkv0_ref, dkv1_ref, unit_ref, scale_ref, n_ref, cos_ref, sin_ref, gain_ref, wo_ref,
    b_ref, own_ref, sib_ref, total, gains,
):
    step = pl.program_id(0)
    rows = total.shape[0] // parts
    blocks = head_blocks()
    lane = lanes()
    first = (lane % HEAD_SIZE) < HEAD_SIZE // 2
    low = lane < HEAD_SIZE
    cosine, sine = cos_ref[...], sin_ref[...]
    sums = [None, None]
    for p in range(12):
        at = slice(p * 128, (p + 1) * 128)
        if p < 8:
            dq_ref = dq0_ref if p < 4 else dq1_ref
            grads = dq_ref[:, (p % 4) * 128 : (p % 4 + 1) * 128] * HEAD_SIZE**-0.5
        else:
            dkv_ref = dkv0_ref if p < 10 else dkv1_ref
            left = dkv_ref[:, (p % 2) * 256 : (p % 2) * 256 + 128]
            right = dkv_ref[:, (p % 2) * 256 + 128 : (p % 2) * 256 + 256]
            grads = jnp.where(low, left, pltpu.roll(right, 64, 1))
            values = jnp.where(low, pltpu.roll(left, 64, 1), right)
            b_ref[:, 512 + p * 128 : 640 + p * 128] = values.astype(BF16)
        turned = grads * cosine + swap_halves(grads * sine, first)
        unit = unit_ref[:, at].astype(F32)
        inverse = scale_ref[:, at].astype(F32)
        kind = 0 if p < 8 else 1
        part = jnp.sum(turned * unit, axis=0, keepdims=True)
        sums[kind] = part if sums[kind] is None else sums[kind] + part
        scaled = turned * gain_ref[1 + kind : 2 + kind, :128]
        b_ref[:, at] = (inverse * (scaled - unit * head_mean(scaled * unit, blocks))).astype(BF16)
    grad = dot(n_ref[...], b_ref[...], TN)

    @pl.when(step == 0)
    def _():
        total[...] = grad
        gains[...] = jnp.zeros_like(gains)

    @pl.when(step > 0)
    def _():
        total[...] += grad

    gains[0:1, :] += sums[0]
    gains[1:2, :] += sums[1]

    @pl.when(step == pl.num_programs(0) - 1)
    def _():
        me = me_ref[0]
        half = me >> 1
        core = me & 1
        more = gains[...].astype(BF16)
        for q in range(parts // 2):
            for s, ref in enumerate((own_ref, sib_ref)):
                source = aligned(2 * q + (core ^ s), rows)
                block = total[source, :].astype(BF16)
                ref[q ^ half, :rows, :] = block[:, :1024]
                ref[q ^ half, rows : 2 * rows, :] = block[:, 1024:]
                ref[q ^ half, 2 * rows : 3 * rows, :] = wo_ref[source, :]
                ref[q ^ half, 3 * rows :, :] = jnp.zeros((32, 1024), BF16)
                ref[q ^ half, 3 * rows :, :128] = more


def raw_back(parts, me, halves, units, normed, cosine, sine, gains, grad_out):
    length, width = normed.shape
    rows = 3 * (width // parts) + 32
    grads = fixed((parts // 2, rows, 1024))
    return pl.pallas_call(
        lambda *refs: raw_back_kernel(parts, *refs),
        grid=(length // TILE,),
        in_specs=[SMALL] + [by_rows(512)] * 4 + [by_rows(1536)] * 2 + [by_rows(width)]
        + [by_rows(128)] * 2
        + [fixed((16, 1024)), fixed((1024, width))],
        out_specs=[by_rows(2048), grads, grads],
        out_shape=[jax.ShapeDtypeStruct((length, 2048), BF16)]
        + [jax.ShapeDtypeStruct((parts // 2, rows, 1024), BF16)] * 2,
        scratch_shapes=[pltpu.VMEM((width, 2048), F32), pltpu.VMEM((32, 128), F32)],
        compiler_params=params(),
        cost_estimate=cost(10, 30),
        name="raw_back",
    )(me, *halves, *units, normed, cosine, sine, gains, grad_out)


def input_kernel(parts, me_ref, b_ref, x_ref, f_ref, gain_ref, *refs):
    out_ref, w_all = refs[2 * parts :]
    load_pairs(parts, me_ref, refs, w_all)
    unit, inverse = unit_of(x_ref[...].astype(F32))
    scaled = dot(b_ref[...], w_all[...], NT) * gain_ref[0:1, :]
    out_ref[...] = f_ref[...] + inverse * (
        scaled - unit * jnp.mean(scaled * unit, axis=-1, keepdims=True)
    )


def input_back(pieces, me, back_raw, x, back_first, gain):
    length, width = x.shape
    parts = len(pieces)
    arrays, specs = pair_specs(pieces, width // parts)
    return pl.pallas_call(
        lambda *refs: input_kernel(parts, *refs),
        grid=(length // TILE,),
        in_specs=[SMALL, by_rows(2048), by_rows(width), by_rows(width), fixed((16, 1024))] + specs,
        out_specs=by_rows(width),
        out_shape=jax.ShapeDtypeStruct((length, width), F32),
        scratch_shapes=[pltpu.VMEM((width, 2048), BF16)],
        compiler_params=params(),
        cost_estimate=cost(6, 18),
        name="input_back",
    )(me, back_raw, x, back_first, gain, *arrays)


def tables_of(numbers):
    length = numbers.shape[0]
    indices = jnp.arange(length, dtype=jnp.int32)
    starts = jnp.concatenate([jnp.ones((1,), dtype=bool), numbers[1:] != numbers[:-1]])
    begins = lax.cummax(jnp.where(starts, indices, jnp.zeros_like(numbers)), axis=0)
    offsets = (indices - begins).astype(F32).reshape(length, 1)
    frequency = ROPE_BASE ** (-jnp.arange(0, HEAD_SIZE, 2).astype(F32) / HEAD_SIZE)
    angles = offsets * frequency
    cosine = jnp.cos(angles)
    sine = jnp.sin(angles)
    same = (numbers[:, None] == jnp.arange(4)[None]).astype(F32)
    empty = jnp.zeros((length, 64), F32)
    return (
        jnp.concatenate([cosine] * 4, axis=1),
        jnp.concatenate([-sine, sine, -sine, sine], axis=1),
        jnp.concatenate([empty, -FAR * same, empty[:, :60]], axis=1),
        jnp.concatenate([empty, 1 - same, jnp.ones((length, 3)), empty[:, :57]], axis=1),
    )


def pack_kernel(chunks, o_ref, gate_ref, up_ref, down_ref, *out_refs):
    low = lanes(128) < 64
    out_refs[0][:128, :] = o_ref[...]
    places = [(c, i) for c, n in enumerate(chunks) for i in range(n)]
    for t, (c, i) in enumerate(places):
        row = i * 192 + (0 if c else 128)
        for side, ref in enumerate((gate_ref, up_ref)):
            for e in range(4):
                left, right = (18 * e + t) // 2, (18 * e + 9 + t) // 2
                a = ref[:, left * 128 : left * 128 + 128].astype(F32)
                b = ref[:, right * 128 : right * 128 + 128].astype(F32)
                both = pltpu.roll(jnp.where(low, b, a), 64, 1) if t % 2 else jnp.where(low, a, b)
                at = side * SLAB + e * 128
                out_refs[c][row : row + 128, at : at + 128] = both.astype(BF16)
        out_refs[c][row + 128 : row + 192, :] = down_ref[t * 64 : t * 64 + 64, :]


def pack_rows(chunks, w_output, w_gate, w_up, w_down):
    return pl.pallas_call(
        lambda *refs: pack_kernel(chunks, *refs),
        out_shape=[
            jax.ShapeDtypeStruct((n * 192 + (0 if c else 128), 1024), BF16)
            for c, n in enumerate(chunks)
        ],
        compiler_params=params(),
        cost_estimate=cost(0, 7),
        name="pack_rows",
    )(w_output, w_gate, w_up, w_down)


def unpack_kernel(flag_ref, *refs):
    *in_refs, gate_ref, up_ref, down_ref = refs
    low = lanes(128) < 64
    outer = flag_ref[0] > 0

    def rows_of(at, size, columns):
        for inside, outside in zip(in_refs[::2], in_refs[1::2]):
            if at < inside.shape[0]:
                one = inside[at : at + size, columns].astype(F32)
                return jnp.where(outer, outside[at : at + size, columns].astype(F32), one)
            at -= inside.shape[0]

    def segment(side, s, half):
        d = s // 9
        at = side * SLAB + (d // 2) * 128
        tile = rows_of((s % 9) * 192, 128, slice(at, at + 128))
        return tile if d % 2 == half else pltpu.roll(tile, 64, 1)

    for side, out in enumerate((gate_ref, up_ref)):
        for m in range(36):
            out[:, m * 128 : m * 128 + 128] = jnp.where(
                low, segment(side, 2 * m, 0), segment(side, 2 * m + 1, 1)
            )
    for t in range(9):
        down_ref[t * 64 : t * 64 + 64, :] = rows_of(t * 192 + 128, 64, slice(None))


def unpack_rows(flag, *totals):
    whole = pl.BlockSpec(memory_space=pltpu.VMEM)
    return pl.pallas_call(
        unpack_kernel,
        in_specs=[SMALL] + [whole] * len(totals),
        out_shape=[
            jax.ShapeDtypeStruct((128, 4608), F32),
            jax.ShapeDtypeStruct((128, 4608), F32),
            jax.ShapeDtypeStruct((576, 1024), F32),
        ],
        compiler_params=params(),
        cost_estimate=cost(0, 14),
        name="unpack_rows",
    )(flag, *totals)


def tie(*values):
    return lax.optimization_barrier(values)


def after(value, *tokens):
    return tie(value, *tokens)[0]


def hop(array, bit):
    return lax.ppermute(array, "shard", [(i, i ^ bit) for i in range(8)])


def gather_all(pack):
    return lax.all_gather(pack, "shard", axis=0, tiled=False)


def scatter_all(every):
    return lax.psum_scatter(every, "shard", scatter_dimension=0, tiled=True)[0]


def weave(near, far):
    groups = []
    for one, two in zip(near, far):
        groups += [list(one), list(two)]
    return Pieces(groups)


def combine(*outputs):
    terms = [term if isinstance(term, tuple) else (term, None) for out in outputs for term in out]
    rows, width = terms[0][0].shape[-2:]
    step = rows // 2

    def spec(k):
        if k is None:
            return pl.BlockSpec((step, width), lambda i: (i, 0))
        return pl.BlockSpec((pl.Squeezed(), step, width), lambda i: (k, i, 0))

    def kernel(*refs):
        at = 0
        for out, out_ref in zip(outputs, refs[len(terms) :]):
            total = refs[at][...].astype(F32)
            for ref in refs[at + 1 : at + len(out)]:
                total = total + ref[...].astype(F32)
            at += len(out)
            out_ref[...] = total.astype(BF16)

    found = pl.pallas_call(
        kernel,
        grid=(rows // step,),
        in_specs=[spec(k) for _, k in terms],
        out_specs=[pl.BlockSpec((step, width), lambda i: (i, 0))] * len(outputs),
        out_shape=[jax.ShapeDtypeStruct((rows, width), BF16)] * len(outputs),
        compiler_params=params(),
        cost_estimate=cost(0, 4),
        name="combine",
    )(*[array for array, _ in terms])
    return found[0] if len(outputs) == 1 else found


def rep_hop(array, pairs):
    return lax.ppermute(array.astype(BF16), "rep", pairs)


INWARD = [(0, 1), (3, 2)]
ACROSS = [(1, 2), (2, 1)]
OUTWARD = [(1, 0), (2, 3)]


def at_end(inner, outer):
    place = lax.axis_index("rep")
    return jnp.where((place == 0) | (place == 3), outer.astype(F32), inner)


def on_device(sizes, *arrays):
    (
        block_input, document_numbers, attn_gain, w_query, key_weight, value_weight, query_gain,
        key_gain, w_output, ffn_gain, w_gate, w_up, w_down, cotangent,
    ) = arrays
    reps, parts = sizes
    _, length, width = block_input.shape
    ff = w_gate.shape[1]
    paired = parts == 8 and reps == 4
    me = lax.axis_index("shard").astype(jnp.int32)
    place = me.reshape(1) if paired else jnp.zeros((1,), jnp.int32)
    x = block_input.reshape(length, width)
    back_out = cotangent.reshape(length, width)
    numbers = document_numbers.reshape(length)
    rows = width // parts
    seg = SLAB // parts
    slabs = ff // SLAB
    few = query_gain.shape[0]

    lane = jnp.arange(width)

    def spot(gain, times, size):
        share = gain.shape[0]
        wide = jnp.tile(gain, width // share)
        return jnp.where((lane < size * times) & ((lane % size) // share == me), wide, 0)

    empty = jnp.zeros((width,), BF16)
    gain_rows = [
        spot(attn_gain, 1, width),
        spot(query_gain, 2, HEAD_SIZE),
        spot(key_gain, 2, HEAD_SIZE),
        spot(ffn_gain, 1, width),
    ]
    first_pack = jnp.concatenate(
        [
            w_query,
            jnp.concatenate([key_weight, value_weight], axis=1),
            jnp.stack(gain_rows + [empty] * 12),
        ]
    )
    tables = tables_of(numbers)
    run = block_paired if paired else block_simple
    args = (me, place, x, back_out, tables, first_pack, w_output, w_gate, w_up, w_down)
    block_output, input_grad, attn_grad, feed_grads = run(*args)
    grad_gate, grad_up, grad_down = feed_grads
    grad_query = attn_grad[:rows]
    grad_key = attn_grad[rows : 2 * rows, :512]
    grad_value = attn_grad[rows : 2 * rows, 512:]

    def diagonal(*pairs):
        total = 0.0
        for weight, grad in pairs:
            total = total + jnp.sum(weight.astype(F32) * grad, axis=1)
        return total

    grad_gain_attn = diagonal(
        (w_query, grad_query), (key_weight, grad_key), (value_weight, grad_value)
    ) / attn_gain.astype(F32)
    grad_gain_ffn = diagonal((w_gate, grad_gate), (w_up, grad_up)) / ffn_gain.astype(F32)

    def small(row):
        both = attn_grad[3 * rows + row, :64] + attn_grad[3 * rows + row, 64:128]
        return lax.dynamic_slice(both, (me * few,), (few,))

    return (
        block_output[None],
        input_grad[None],
        grad_gain_attn,
        grad_query,
        grad_key,
        grad_value,
        small(0),
        small(1),
        attn_grad[2 * rows : 3 * rows],
        grad_gain_ffn,
        grad_gate,
        grad_up,
        grad_down,
    )


def block_simple(me, place, x, back_out, tables, first_pack, w_output, w_gate, w_up, w_down):
    rows, ff = w_gate.shape
    parts = x.shape[1] // rows
    seg = SLAB // parts
    slabs = ff // SLAB
    tall = rows + seg

    def columns(weight):
        cut = weight.reshape(rows, parts, slabs, seg).transpose(2, 0, 1, 3)
        return cut.reshape(slabs, rows, SLAB)

    pack = jnp.concatenate(
        [
            jnp.concatenate([columns(w_gate), columns(w_up)], axis=2),
            w_down.reshape(slabs, seg, x.shape[1]),
        ],
        axis=1,
    ).reshape(slabs * tall, 2 * SLAB)
    every = gather_all(first_pack)
    pairs = [(every[k], every[k], 1) for k in range(parts)]
    pieces = Pieces(stacked=gather_all(jnp.concatenate([w_output, pack])))
    normed_one, *units, q_aug, k_aug, v_aug, gains = project(pairs, place, x, tables)
    attended_0, q_back_0 = attend(q_aug, k_aug, v_aug, 0, 4)
    attended_1, q_back_1 = attend(q_aug, k_aug, v_aug, 4, 4)
    attended = (attended_0, attended_1)
    first_sum, normed_two, normed_two_t = output_rows(pieces, place, attended, x, gains)
    out, back, grads = feed(
        pieces, place, rows, slabs, normed_two, normed_two_t, back_out, False
    )
    total = lax.psum(scatter_all(grads), "rep").astype(F32).reshape(slabs, tall, 2 * SLAB)
    back_first, back_attended, grad_out = middle(
        pieces, place, first_sum, back_out, attended, gains, [back]
    )
    halves_0 = attend_back(q_back_0, k_aug, v_aug, attended_0, back_attended, 0, 4)
    halves_1 = attend_back(q_back_1, k_aug, v_aug, attended_1, back_attended, 4, 4)
    back_raw, own, sib = raw_back(
        parts, place, (halves_0[0], halves_1[0], halves_0[1], halves_1[1]), units, normed_one,
        tables[0], tables[1], gains, grad_out,
    )
    every = jnp.stack([own, sib], axis=1).reshape((parts,) + own.shape[1:])
    attn_grad = lax.psum(scatter_all(every), "rep").astype(F32)
    input_grad = input_back(pairs, place, back_raw, x, back_first, gains)

    def uncut(block):
        return block.reshape(slabs, rows, parts, seg).transpose(1, 2, 0, 3).reshape(rows, ff)

    feed_grads = (
        uncut(total[:, :rows, :SLAB]),
        uncut(total[:, :rows, SLAB:]),
        total[:, rows:, :].reshape(slabs * seg, x.shape[1]),
    )
    return (first_sum + out).astype(BF16), input_grad, attn_grad, feed_grads


def fence(outputs, *hops):
    found = tie(*outputs, *hops)
    return found[: len(outputs)], list(found[len(outputs) :])


def block_paired(me, place, x, back_out, tables, first_pack, w_output, w_gate, w_up, w_down):
    rows = w_gate.shape[0]
    chunks = (3, 3, 3)

    first = hop(first_pack, 2)
    second = hop(first_pack, 4)
    twin = hop(first_pack, 1)
    made, (first, second, twin) = fence(
        [*pack_rows(chunks, w_output, w_gate, w_up, w_down), *tables], first, second, twin
    )
    packs, tables = list(made[:3]), made[3:]
    corner_a = hop(second[:rows], 2)
    corner_b = hop(first[rows:], 4)
    far = [twin] + [hop(piece, 1) for piece in (first, second, corner_a, corner_b)]
    near = [first_pack, first, second, corner_a, corner_b]
    pairs = []
    for k in range(3):
        pairs += [(near[k], near[k], 1), (far[k], far[k], 1)]
    pairs += [(near[3], near[4], 0), (far[3], far[4], 0)]

    pack = after(packs[0], corner_a, corner_b, far[1], far[2])
    first, second, twin = hop(pack, 2), hop(pack, 4), hop(pack, 1)
    normed_one, *units, q_aug, k_aug, v_aug, gains = project(pairs, place, x, tables)
    (attended_0, q_back_0, k_aug), (first, second, twin) = fence(
        [*attend(q_aug, k_aug, v_aug, 0, 4), k_aug], first, second, twin
    )
    corner_a, corner_b = hop(second[:, :512], 2), hop(first[:, 512:], 4)
    far = [hop(first, 1), hop(second, 1)]
    packs[1] = after(packs[1], first, second)
    waiting = [hop(packs[1], bit) for bit in (1, 2, 4, 6)]
    (attended_1, q_back_1), (corner_a, corner_b, *far) = fence(
        attend(q_aug, k_aug, v_aug, 4, 4), corner_a, corner_b, *far
    )
    attended = (attended_0, attended_1)
    early = weave(
        [[pack], [first], [second], [corner_a, corner_b]],
        [[twin], [far[0]], [far[1]], [hop(corner_a, 1), hop(corner_b, 1)]],
    )
    first_sum, normed_two, normed_two_t = output_rows(early, place, attended, x, gains)

    def finish(pack, twin, first, second, corner):
        near = (first, second, corner)
        far = [hop(piece, 1) for piece in near]
        return weave([[pack]] + [[a] for a in near], [[twin]] + [[a] for a in far])

    def feed_step(pieces, begin, n, paired):
        return feed(pieces, place, begin, n, normed_two, normed_two_t, back_out, paired)

    (out_0, back_0, own_0, sib_0, normed_two), waiting = fence(
        [*feed_step(early, rows, chunks[0], True), normed_two], *waiting
    )
    later = finish(packs[1], *waiting)
    waiting = [hop(packs[2], bit) for bit in (1, 2, 4, 6)]
    other_0 = hop(after(sib_0, *later.arrays), 1)
    (out_1, back_1, own_1, sib_1, normed_two), (other_0, *waiting) = fence(
        [*feed_step(later, 0, chunks[1], True), normed_two], other_0, *waiting
    )
    last = finish(packs[2], *waiting)
    terms = combine(*[[(own_0, k), (other_0, k)] for k in (1, 2, 3)])
    other_1 = hop(after(sib_1, *last.arrays), 1)
    normed_two, *terms = tie(normed_two, *terms)
    steps = [hop(term, 2 * k) for k, term in zip((1, 2, 3), terms)]
    (out_2, back_2, own_2, sib_2), (other_1, *steps) = fence(
        feed(last, place, 0, chunks[2], normed_two, normed_two_t, back_out, True), other_1, *steps
    )
    other_2 = hop(sib_2, 1)
    grads_0, term = combine(
        [(own_0, 0), (other_0, 0), *steps], [(own_1, 3), (other_1, 3)]
    )
    back_2, grads_0, term = tie(back_2, grads_0, term)
    moved_1 = hop(term, 4)
    inward_0 = rep_hop(grads_0, INWARD)
    middles = middle(
        early, place, first_sum, back_out, attended, gains, [back_0, back_1, back_2]
    )
    (back_first, back_attended, grad_out), (other_2,) = fence(middles, other_2)
    term = combine([(own_2, 3), (other_2, 3)])
    back_attended, term = tie(back_attended, term)
    moved_2 = hop(term, 2)
    halves = attend_back(q_back_0, k_aug, v_aug, attended_0, back_attended, 0, 4)
    (dq_0, dkv_0, back_attended), (moved_1, moved_2, inward_0) = fence(
        [*halves, back_attended], moved_1, moved_2, inward_0
    )
    one, two, three, four, half_0 = combine(
        [(own_1, 1), (other_1, 1), moved_1],
        [(own_1, 2), (other_1, 2)],
        [(own_2, 1), (other_2, 1)],
        [(own_2, 2), (other_2, 2), moved_2],
        [grads_0, inward_0],
    )
    back_attended, one, two, three, four, half_0 = tie(
        back_attended, one, two, three, four, half_0
    )
    first_1, second_1 = hop(one, 2), hop(two, 4)
    first_2, second_2 = hop(three, 2), hop(four, 4)
    across_0 = rep_hop(half_0, ACROSS)
    halves = attend_back(q_back_1, k_aug, v_aug, attended_1, back_attended, 4, 4)
    (dq_1, dkv_1), (first_1, second_1, across_0) = fence(halves, first_1, second_1, across_0)
    grads_1, total_0 = combine(
        [(own_1, 0), (other_1, 0), first_1, second_1], [half_0, across_0]
    )
    dq_1, grads_1, total_0 = tie(dq_1, grads_1, total_0)
    inward_1 = rep_hop(grads_1, INWARD)
    outward_0 = rep_hop(total_0, OUTWARD)
    result = raw_back(
        8, place, (dq_0, dq_1, dkv_0, dkv_1), units, normed_one, tables[0], tables[1], gains,
        grad_out,
    )
    (back_raw, own, sib), (first_2, second_2, inward_1, outward_0) = fence(
        result, first_2, second_2, inward_1, outward_0
    )
    other = hop(sib, 1)
    half_1, grads_2 = combine(
        [grads_1, inward_1], [(own_2, 0), (other_2, 0), first_2, second_2]
    )
    back_raw, other, half_1, grads_2 = tie(back_raw, other, half_1, grads_2)
    term = combine([(own, 3), (other, 3)])
    back_raw, term = tie(back_raw, term)
    moved = hop(term, 4)
    across_1 = rep_hop(half_1, ACROSS)
    inward_2 = rep_hop(grads_2, INWARD)
    input_grad = input_back(pairs, place, back_raw, x, back_first, gains)
    (input_grad,), (moved,) = fence([input_grad], moved)
    one, two = combine([(own, 1), (other, 1), moved], [(own, 2), (other, 2)])
    one, two, across_1, inward_2, first_sum = tie(one, two, across_1, inward_2, first_sum)
    first, second = hop(one, 2), hop(two, 4)
    total_1, half_2 = combine([half_1, across_1], [grads_2, inward_2])
    first_sum, total_1, half_2 = tie(first_sum, total_1, half_2)
    outward_1 = rep_hop(total_1, OUTWARD)
    across_2 = rep_hop(half_2, ACROSS)
    outs = out_0.astype(F32) + out_1.astype(F32) + out_2.astype(F32)
    block_output = (first_sum + outs).astype(BF16)
    (block_output,), (first, second) = fence([block_output], first, second)
    grads = combine([(own, 0), (other, 0), first, second])
    inward = rep_hop(grads, INWARD)
    across_2, _ = tie(across_2, grads)
    total_2 = combine([half_2, across_2])
    outward_2 = rep_hop(total_2, OUTWARD)
    inward, outward_1, _ = tie(inward, outward_1, total_2)
    half = combine([grads, inward])
    across = rep_hop(half, ACROSS)
    outward_2, across, _ = tie(outward_2, across, half)
    total = combine([half, across])
    outward = rep_hop(total, OUTWARD)
    total, outward_2 = tie(total, outward_2)
    spot = lax.axis_index("rep")
    flag = ((spot == 0) | (spot == 3)).astype(jnp.int32).reshape(1)
    feed_grads = unpack_rows(flag, total_0, outward_0, total_1, outward_1, total_2, outward_2)
    (*feed_grads,), (outward,) = fence(feed_grads, outward)
    return block_output, input_grad, at_end(total.astype(F32), outward), feed_grads


def solution(mesh):
    sizes = (mesh.shape["rep"], mesh.shape["shard"])
    whole = P(("rep", "shard"), None, None)
    matrix = P("shard", None)
    vector = P("shard")
    in_specs = (
        whole, P(("rep", "shard"), None), vector, matrix, matrix, matrix, vector, vector, matrix,
        vector, matrix, matrix, matrix, whole,
    )
    out_specs = (
        whole, whole, vector, matrix, matrix, matrix, vector, vector, matrix, vector, matrix,
        matrix, matrix,
    )
    return jax.shard_map(
        lambda *arrays: on_device(sizes, *arrays),
        mesh=mesh,
        in_specs=in_specs,
        out_specs=out_specs,
        check_vma=False,
    )
```

```python
import jax
import jax.numpy as jnp
from jax import lax
from jax.experimental import pallas as pl
from jax.experimental.pallas import tpu as pltpu
from jax.sharding import PartitionSpec as P

QUERY_HEADS = 16
KEY_VALUE_HEADS = 8
HEAD_SIZE = 64
EPS = 1e-05
ROPE_BASE = 1000000.0
FAR = 32768.0
TILE = 256
SLAB = 512
VMEM_LIMIT = 60 * 1024 * 1024
NT = ((1,), (1,))
NN = ((1,), (0,))
TN = ((0,), (0,))
BF16 = jnp.bfloat16
F32 = jnp.float32
SMALL = pl.BlockSpec(memory_space=pltpu.SMEM)


def dot(left, right, dims=NN):
    return lax.dot_general(left, right, (dims, ((), ())), preferred_element_type=F32)


def params():
    return pltpu.CompilerParams(vmem_limit_bytes=VMEM_LIMIT)


def cost(giga_flops, mega_bytes, exps=0):
    return pl.CostEstimate(
        flops=int(giga_flops * 10**6),
        bytes_accessed=int(mega_bytes * 10**3),
        transcendentals=exps // 1000,
    )


def fixed(shape, where=None):
    index = (0,) * len(shape) if where is None else where
    return pl.BlockSpec(shape, lambda *_: index, pipeline_mode=pl.Buffered(1))


def by_rows(width, rows=TILE):
    return pl.BlockSpec((rows, width), lambda i: (i, 0))


class Pieces:
    def __init__(self, groups=None, stacked=None):
        self.stacked = stacked
        self.count = len(groups) if stacked is None else stacked.shape[0]
        self.groups = groups if stacked is None else [[stacked]] * self.count
        self.arrays = [array for group in self.groups for array in group]
        self.layout = [len(group) for group in self.groups]

    def specs(self, rows, start):
        once = pl.Buffered(1) if start(0) == start(1) else None
        found = []
        for k, group in enumerate(self.groups):
            for array in group:
                shape = (pl.Element(rows), pl.Element(array.shape[-1]))
                if self.stacked is None:
                    found.append(
                        pl.BlockSpec(shape, lambda i: (start(i), 0), pipeline_mode=once)
                    )
                else:
                    found.append(
                        pl.BlockSpec(
                            (pl.Squeezed(),) + shape,
                            lambda i, k=k: (k, start(i), 0),
                            pipeline_mode=once,
                        )
                    )
        return found


def grouped(refs, layout):
    groups, at = [], 0
    for size in layout:
        groups.append(refs[at : at + size])
        at += size
    return groups


def fill(target, at, group, rows):
    left = 0
    for ref in group:
        right = left + ref.shape[1]
        target[at, left:right] = ref[rows, :]
        left = right


def split3(value):
    high = value.astype(BF16).astype(F32)
    rest = value - high
    middle = rest.astype(BF16).astype(F32)
    return high, middle, rest - middle


def aligned(index, rows):
    return pl.ds(pl.multiple_of(index * rows, rows), rows)


def unit_of(rows):
    inverse = lax.rsqrt(jnp.mean(rows * rows, axis=-1, keepdims=True) + EPS)
    return rows * inverse, inverse


def head_blocks():
    first = lax.broadcasted_iota(jnp.int32, (128, 128), 0) // HEAD_SIZE
    second = lax.broadcasted_iota(jnp.int32, (128, 128), 1) // HEAD_SIZE
    return (first == second).astype(BF16)


def head_mean(rows, blocks):
    return dot(rows.astype(BF16), blocks) * (1.0 / HEAD_SIZE)


def swap_halves(rows, first):
    return jnp.where(first, pltpu.roll(rows, 96, 1), pltpu.roll(rows, 32, 1))


def lanes(rows=TILE):
    return lax.broadcasted_iota(jnp.int32, (rows, 128), 1)


def load_pairs(parts, me_ref, refs, w_all):
    rows = w_all.shape[0] // parts

    @pl.when(pl.program_id(0) == 0)
    def _():
        for k in range(parts):
            at = aligned(me_ref[0] ^ k, rows)
            w_all[at, :1024] = refs[2 * k][...]
            w_all[at, 1024:] = refs[2 * k + 1][...]


def pair_specs(pieces, rows):
    arrays, specs = [], []
    for piece in pieces:
        left, right, at = piece
        arrays += [left, right]
        specs += [fixed((rows, 1024)), fixed((rows, 1024), (at, 0))]
    return arrays, specs


def project_kernel(parts, me_ref, x_ref, cos_ref, sin_ref, qx_ref, kx_ref, *refs):
    gain_refs = refs[2 * parts : 3 * parts]
    n_ref, unit_ref, scale_ref, q_ref, k_ref, v_ref, gain_ref, w_all = refs[3 * parts :]
    load_pairs(parts, me_ref, refs, w_all)

    @pl.when(pl.program_id(0) == 0)
    def _():
        total = gain_refs[0][...].astype(F32)
        for ref in gain_refs[1:]:
            total = total + ref[...].astype(F32)
        gain_ref[...] = total

    unit, _ = unit_of(x_ref[...].astype(F32))
    normed = (unit * gain_ref[0:1, :]).astype(BF16)
    n_ref[...] = normed
    raw = dot(normed, w_all[...])
    blocks = head_blocks()
    lane = lanes()
    first = (lane % HEAD_SIZE) < HEAD_SIZE // 2
    low = lane < HEAD_SIZE
    cosine, sine = cos_ref[...], sin_ref[...]
    for p in range(12):
        at = slice(p * 128, (p + 1) * 128)
        rows_in = raw[:, at]
        inverse = lax.rsqrt(head_mean(rows_in * rows_in, blocks) + EPS)
        unit = rows_in * inverse
        unit_ref[:, at] = unit.astype(BF16)
        scale_ref[:, at] = inverse.astype(BF16)
        scaled = unit * gain_ref[1 + p // 8 : 2 + p // 8, :128]
        turned = scaled * cosine + swap_halves(scaled, first) * sine
        if p < 8:
            turned = turned * HEAD_SIZE**-0.5
            out, more, at = q_ref, qx_ref[...], 2 * p
        else:
            out, more, at = k_ref, kx_ref[...], 2 * (p - 8)
        out[at] = jnp.where(low, turned, more).astype(BF16)
        out[at + 1] = jnp.where(low, pltpu.roll(turned, 64, 1), more).astype(BF16)
    more = ((lane >= 64) & (lane < 67)).astype(F32)
    for p in range(4):
        rows_in = raw[:, 1536 + p * 128 : 1664 + p * 128]
        v_ref[2 * p] = jnp.where(low, rows_in, more).astype(BF16)
        v_ref[2 * p + 1] = jnp.where(low, pltpu.roll(rows_in, 64, 1), more).astype(BF16)


def project(pieces, me, x, tables):
    length, width = x.shape
    parts = len(pieces)
    rows = width // parts
    arrays, specs = pair_specs(pieces, rows)
    gains = [(piece[1], (piece[2] + 1) * rows // 16) for piece in pieces]

    def heads(count):
        return pl.BlockSpec((count, TILE, 128), lambda i: (0, i, 0))

    return pl.pallas_call(
        lambda *refs: project_kernel(parts, *refs),
        grid=(length // TILE,),
        in_specs=[SMALL, by_rows(width)]
        + [by_rows(128)] * 4
        + specs
        + [fixed((16, 1024), (at, 0)) for _, at in gains],
        out_specs=[by_rows(width), by_rows(1536), by_rows(1536), heads(16), heads(8), heads(8)]
        + [fixed((16, 1024))],
        out_shape=[
            jax.ShapeDtypeStruct((length, width), BF16),
            jax.ShapeDtypeStruct((length, 1536), BF16),
            jax.ShapeDtypeStruct((length, 1536), BF16),
            jax.ShapeDtypeStruct((16, length, 128), BF16),
            jax.ShapeDtypeStruct((8, length, 128), BF16),
            jax.ShapeDtypeStruct((8, length, 128), BF16),
            jax.ShapeDtypeStruct((16, 1024), F32),
        ],
        scratch_shapes=[pltpu.VMEM((width, 2048), BF16)],
        compiler_params=params(),
        cost_estimate=cost(8, 25),
        name="project",
    )(me, x, *tables, *arrays, *[array for array, _ in gains])


def causal(query_axis):
    first = lax.broadcasted_iota(jnp.int32, (TILE, TILE), 0)
    second = lax.broadcasted_iota(jnp.int32, (TILE, TILE), 1)
    return (first >= second) if query_axis == 0 else (second >= first)


def attend_kernel(q_ref, k_ref, v_ref, o_ref, qb_ref):
    tiles = q_ref.shape[1] // TILE
    keep = causal(0)
    lane = lax.broadcasted_iota(jnp.int32, (TILE, 128), 1)
    for i in range(tiles):
        rows = slice(i * TILE, (i + 1) * TILE)
        before = slice(0, i * TILE)
        halves = []
        for h in range(2):
            q = q_ref[h, rows, :]
            weights = jnp.where(keep, jnp.exp(dot(q, k_ref[0, rows, :], NT)), 0.0)
            out = dot(weights.astype(BF16), v_ref[0, rows, :])
            if i:
                weights = jnp.exp(dot(q, k_ref[0, before, :], NT)).astype(BF16)
                out = out + dot(weights, v_ref[0, before, :])
            total = out[:, 64:65]
            halves.append(out / total)
            high, middle, low = split3(-jnp.log(total))
            extra = jnp.where(
                lane == 68, high, jnp.where(lane == 69, middle, jnp.where(lane == 70, low, 0.0))
            )
            qb_ref[h, rows, :] = (q.astype(F32) + extra).astype(BF16)
        both = jnp.where(lane < 64, halves[0], pltpu.roll(halves[1], 64, 1))
        o_ref[rows, :] = both.astype(BF16)


def attend(q_aug, k_aug, v_aug, begin, groups):
    _, length, _ = q_aug.shape
    return pl.pallas_call(
        attend_kernel,
        grid=(groups,),
        in_specs=[
            pl.BlockSpec((2, length, 128), lambda g: (g + begin, 0, 0)),
            pl.BlockSpec((1, length, 128), lambda g: (g + begin, 0, 0)),
            pl.BlockSpec((1, length, 128), lambda g: (g + begin, 0, 0)),
        ],
        out_specs=[
            pl.BlockSpec((length, 128), lambda g: (0, g)),
            pl.BlockSpec((2, length, 128), lambda g: (g, 0, 0)),
        ],
        out_shape=[
            jax.ShapeDtypeStruct((length, groups * 128), BF16),
            jax.ShapeDtypeStruct((2 * groups, length, 128), BF16),
        ],
        compiler_params=params(),
        cost_estimate=cost(2.5 * groups, 2 * groups, groups * 2**20),
        name="attend",
    )(q_aug, k_aug, v_aug)


def attend_back_kernel(q_ref, k_ref, v_ref, o_ref, do_ref, dq_ref, dkv_ref, do_aug, k_t, dq_t):
    length = q_ref.shape[1]
    tiles = length // TILE
    keep = causal(1)
    lane = lax.broadcasted_iota(jnp.int32, (length, 128), 1)
    back = do_ref[...].astype(F32)
    product = back * o_ref[...].astype(F32)
    for h in range(2):
        own = (lane < 64) if h == 0 else (lane >= 64)
        centre = jnp.sum(jnp.where(own, product, 0.0), axis=1, keepdims=True)
        moved = back if h == 0 else pltpu.roll(back, 64, 1)
        high, middle, low = split3(-centre)
        extra = jnp.where(
            lane == 64, high, jnp.where(lane == 65, middle, jnp.where(lane == 66, low, 0.0))
        )
        do_aug[h] = jnp.where(lane < 64, moved, extra).astype(BF16)
    k_t[...] = k_ref[0].astype(F32).T[:64, :].astype(BF16)
    low_half = lax.broadcasted_iota(jnp.int32, (TILE, 128), 1) < 64
    for j in range(tiles):
        cols = slice(j * TILE, (j + 1) * TILE)
        k = k_ref[0, cols, :]
        v = v_ref[0, cols, :]
        dk = 0.0
        dv = 0.0
        for i, stop in ((j, j + 1), (j + 1, tiles)):
            if i == tiles:
                continue
            rows = slice(i * TILE, stop * TILE)
            for h in range(2):
                q = q_ref[h, rows, :]
                do = do_aug[h, rows, :]
                probs = jnp.exp(dot(k, q, NT))
                if i == j:
                    probs = jnp.where(keep, probs, 0.0)
                scores = (probs * dot(v, do, NT)).astype(BF16)
                dv = dv + dot(probs.astype(BF16), do)
                dk = dk + dot(scores, q)
                to_q = dot(k_t[:, cols], scores)
                if j == 0:
                    dq_t[h * 64 : (h + 1) * 64, rows] = to_q
                else:
                    dq_t[h * 64 : (h + 1) * 64, rows] += to_q
        dkv_ref[cols, :] = jnp.where(low_half, dk, pltpu.roll(dv, 64, 1))
    dq_ref[...] = dq_t[...].T


def attend_back(q_back, k_aug, v_aug, attended, back_attended, begin, groups):
    _, length, _ = q_back.shape
    by_group = pl.BlockSpec((length, 128), lambda g: (0, g + begin))
    out_group = pl.BlockSpec((length, 128), lambda g: (0, g))
    return pl.pallas_call(
        attend_back_kernel,
        grid=(groups,),
        in_specs=[
            pl.BlockSpec((2, length, 128), lambda g: (g, 0, 0)),
            pl.BlockSpec((1, length, 128), lambda g: (g + begin, 0, 0)),
            pl.BlockSpec((1, length, 128), lambda g: (g + begin, 0, 0)),
            out_group,
            by_group,
        ],
        out_specs=[out_group, out_group],
        out_shape=[jax.ShapeDtypeStruct((length, groups * 128), F32)] * 2,
        scratch_shapes=[
            pltpu.VMEM((2, length, 128), BF16),
            pltpu.VMEM((64, length), BF16),
            pltpu.VMEM((128, length), F32),
        ],
        compiler_params=params(),
        cost_estimate=cost(5 * groups, 3 * groups, groups * 2**20),
        name="attend_back",
    )(q_back, k_aug, v_aug, attended, back_attended)


def output_kernel(layout, me_ref, o0_ref, o1_ref, x_ref, gain_ref, *refs):
    sum_ref, n_ref, nt_ref, w_all = refs[-4:]
    rows = w_all.shape[0] // len(layout)

    @pl.when(pl.program_id(0) == 0)
    def _():
        for k, group in enumerate(grouped(refs, layout)):
            fill(w_all, aligned(me_ref[0] ^ k, rows), group, slice(None))

    total = x_ref[...].astype(F32) + dot(o0_ref[...], w_all[:512, :])
    total = total + dot(o1_ref[...], w_all[512:, :])
    sum_ref[...] = total
    unit, _ = unit_of(total)
    normed = unit * gain_ref[3:4, :]
    n_ref[...] = normed.astype(BF16)
    nt_ref[...] = normed.T.astype(BF16)


def output_rows(pieces, me, attended, x, gain):
    length, width = x.shape
    parts = pieces.count
    rows = width // parts
    return pl.pallas_call(
        lambda *refs: output_kernel(pieces.layout, *refs),
        grid=(length // TILE,),
        in_specs=[SMALL, by_rows(512), by_rows(512), by_rows(width), fixed((16, 1024))]
        + pieces.specs(rows, lambda i: 0),
        out_specs=[by_rows(width), by_rows(width), pl.BlockSpec((width, TILE), lambda i: (0, i))],
        out_shape=[
            jax.ShapeDtypeStruct((length, width), F32),
            jax.ShapeDtypeStruct((length, width), BF16),
            jax.ShapeDtypeStruct((width, length), BF16),
        ],
        scratch_shapes=[pltpu.VMEM((1024, width), BF16)],
        compiler_params=params(),
        cost_estimate=cost(5, 15),
        name="output_rows",
    )(me, *attended, x, gain, *pieces.arrays)


def scatter_rows(me, parts, value, rows, own_ref, sib_ref, at):
    half = me >> 1
    core = me & 1
    for q in range(parts // 2):
        for s, ref in enumerate((own_ref, sib_ref)):
            source = 2 * q + (core ^ s)
            ref[q ^ half, at : at + rows, :] = value[aligned(source, rows), :]


def feed_kernel(layout, paired, me_ref, n_ref, nt_ref, c_ref, *refs):
    parts = len(layout)
    f_ref, b_ref, *grad_refs = refs[sum(layout) : -8]
    w_all, d_all, back, hidden, w_grad, d_grad, f_sum, b_sum = refs[-8:]
    me = me_ref[0]
    rows = w_all.shape[0] // parts
    seg = SLAB // parts
    for k, group in enumerate(grouped(refs, layout)):
        fill(w_all, aligned(me ^ k, rows), group, slice(0, rows))
        fill(d_all, aligned(me ^ k, seg), group, slice(rows, rows + seg))
    step = pl.program_id(0)

    @pl.when(step == 0)
    def _():
        f_sum[...] = jnp.zeros_like(f_sum)
        b_sum[...] = jnp.zeros_like(b_sum)

    both = dot(n_ref[...], w_all[...])
    gate = both[:, :SLAB]
    up = both[:, SLAB:]
    sig = 1.0 / (1.0 + jnp.exp(-gate))
    swish = gate * sig
    hidden[...] = (swish * up).astype(BF16)
    back_hidden = dot(c_ref[...], d_all[...], NT)
    back[:, SLAB:] = (back_hidden * swish).astype(BF16)
    back[:, :SLAB] = (back_hidden * up * sig * (1.0 + gate * (1.0 - sig))).astype(BF16)
    f_sum[...] += dot(hidden[...], d_all[...])
    b_sum[...] += dot(back[...], w_all[...], NT)
    w_grad[...] = dot(nt_ref[...], back[...]).astype(BF16)
    d_grad[...] = dot(hidden[...], c_ref[...], TN).astype(BF16)

    @pl.when(step == pl.num_programs(0) - 1)
    def _():
        f_ref[...] = f_sum[...].astype(BF16)
        b_ref[...] = b_sum[...].astype(BF16)

    if paired:
        own_ref, sib_ref = grad_refs
        scatter_rows(me, parts, w_grad, rows, own_ref, sib_ref, 0)
        scatter_rows(me, parts, d_grad, seg, own_ref, sib_ref, rows)
    else:
        for d in range(parts):
            grad_refs[0][d, :rows, :] = w_grad[d * rows : (d + 1) * rows, :]
            grad_refs[0][d, rows:, :] = d_grad[d * seg : (d + 1) * seg, :]


def feed(pieces, me, begin, slabs, normed, normed_t, cotangent, paired):
    length, width = normed.shape
    parts = pieces.count
    rows = width // parts + SLAB // parts
    depth = parts // 2 if paired else parts
    count = 2 if paired else 1
    grads = pl.BlockSpec((depth, rows, 2 * SLAB), lambda i: (0, i, 0))
    return pl.pallas_call(
        lambda *refs: feed_kernel(pieces.layout, paired, *refs),
        grid=(slabs,),
        in_specs=[SMALL, fixed((length, width)), fixed((width, length)), fixed((length, width))]
        + pieces.specs(rows, lambda i: (begin // 16 + i * (rows // 16)) * 16),
        out_specs=[fixed((length, width)), fixed((length, width))] + [grads] * count,
        out_shape=[
            jax.ShapeDtypeStruct((length, width), BF16),
            jax.ShapeDtypeStruct((length, width), BF16),
        ]
        + [jax.ShapeDtypeStruct((depth, slabs * rows, 2 * SLAB), BF16)] * count,
        scratch_shapes=[
            pltpu.VMEM((width, 2 * SLAB), BF16),
            pltpu.VMEM((SLAB, width), BF16),
            pltpu.VMEM((length, 2 * SLAB), BF16),
            pltpu.VMEM((length, SLAB), BF16),
            pltpu.VMEM((width, 2 * SLAB), BF16),
            pltpu.VMEM((SLAB, width), BF16),
            pltpu.VMEM((length, width), F32),
            pltpu.VMEM((length, width), F32),
        ],
        compiler_params=params(),
        cost_estimate=cost(12.5 * slabs, 20 + 6 * slabs),
        name="feed",
    )(me, normed, normed_t, cotangent, *pieces.arrays)


def middle_kernel(layout, sums, me_ref, s_ref, c_ref, o0_ref, o1_ref, gain_ref, *refs):
    b_refs = refs[:sums]
    f_ref, a_ref, g_ref, w_all, total = refs[-5:]
    rows = w_all.shape[0] // len(layout)
    step = pl.program_id(0)

    @pl.when(step == 0)
    def _():
        for k, group in enumerate(grouped(refs[sums:], layout)):
            fill(w_all, aligned(me_ref[0] ^ k, rows), group, slice(None))

    back = b_refs[0][...].astype(F32)
    for ref in b_refs[1:]:
        back = back + ref[...].astype(F32)
    unit, inverse = unit_of(s_ref[...])
    scaled = back * gain_ref[3:4, :]
    first = c_ref[...].astype(F32) + inverse * (
        scaled - unit * jnp.mean(scaled * unit, axis=-1, keepdims=True)
    )
    f_ref[...] = first
    short = first.astype(BF16)
    a_ref[...] = dot(short, w_all[...], NT).astype(BF16)
    grads = [dot(ref[...], short, TN) for ref in (o0_ref, o1_ref)]

    @pl.when(step == 0)
    def _():
        total[:512, :] = grads[0]
        total[512:, :] = grads[1]

    @pl.when(step > 0)
    def _():
        total[:512, :] += grads[0]
        total[512:, :] += grads[1]

    @pl.when(step == pl.num_programs(0) - 1)
    def _():
        g_ref[...] = total[...].astype(BF16)


def middle(pieces, me, first_sum, cotangent, attended, gain, backs):
    length, width = first_sum.shape
    parts = pieces.count
    rows = width // parts
    return pl.pallas_call(
        lambda *refs: middle_kernel(pieces.layout, len(backs), *refs),
        grid=(length // TILE,),
        in_specs=[SMALL, by_rows(width), by_rows(width), by_rows(512), by_rows(512), fixed((16, 1024))]
        + [by_rows(width)] * len(backs)
        + pieces.specs(rows, lambda i: 0),
        out_specs=[by_rows(width), by_rows(1024), fixed((1024, width))],
        out_shape=[
            jax.ShapeDtypeStruct((length, width), F32),
            jax.ShapeDtypeStruct((length, 1024), BF16),
            jax.ShapeDtypeStruct((1024, width), BF16),
        ],
        scratch_shapes=[pltpu.VMEM((1024, width), BF16), pltpu.VMEM((1024, width), F32)],
        compiler_params=params(),
        cost_estimate=cost(9, 32),
        name="middle",
    )(me, first_sum, cotangent, *attended, gain, *backs, *pieces.arrays)


def raw_back_kernel(
    parts, me_ref, dq0_ref, dq1_ref, dkv0_ref, dkv1_ref, unit_ref, scale_ref, n_ref, cos_ref, sin_ref, gain_ref, wo_ref,
    b_ref, own_ref, sib_ref, total, gains,
):
    step = pl.program_id(0)
    rows = total.shape[0] // parts
    blocks = head_blocks()
    lane = lanes()
    first = (lane % HEAD_SIZE) < HEAD_SIZE // 2
    low = lane < HEAD_SIZE
    cosine, sine = cos_ref[...], sin_ref[...]
    sums = [None, None]
    for p in range(12):
        at = slice(p * 128, (p + 1) * 128)
        if p < 8:
            dq_ref = dq0_ref if p < 4 else dq1_ref
            grads = dq_ref[:, (p % 4) * 128 : (p % 4 + 1) * 128] * HEAD_SIZE**-0.5
        else:
            dkv_ref = dkv0_ref if p < 10 else dkv1_ref
            left = dkv_ref[:, (p % 2) * 256 : (p % 2) * 256 + 128]
            right = dkv_ref[:, (p % 2) * 256 + 128 : (p % 2) * 256 + 256]
            grads = jnp.where(low, left, pltpu.roll(right, 64, 1))
            values = jnp.where(low, pltpu.roll(left, 64, 1), right)
            b_ref[:, 512 + p * 128 : 640 + p * 128] = values.astype(BF16)
        turned = grads * cosine + swap_halves(grads * sine, first)
        unit = unit_ref[:, at].astype(F32)
        inverse = scale_ref[:, at].astype(F32)
        kind = 0 if p < 8 else 1
        part = jnp.sum(turned * unit, axis=0, keepdims=True)
        sums[kind] = part if sums[kind] is None else sums[kind] + part
        scaled = turned * gain_ref[1 + kind : 2 + kind, :128]
        b_ref[:, at] = (inverse * (scaled - unit * head_mean(scaled * unit, blocks))).astype(BF16)
    grad = dot(n_ref[...], b_ref[...], TN)

    @pl.when(step == 0)
    def _():
        total[...] = grad
        gains[...] = jnp.zeros_like(gains)

    @pl.when(step > 0)
    def _():
        total[...] += grad

    gains[0:1, :] += sums[0]
    gains[1:2, :] += sums[1]

    @pl.when(step == pl.num_programs(0) - 1)
    def _():
        me = me_ref[0]
        half = me >> 1
        core = me & 1
        more = gains[...].astype(BF16)
        for q in range(parts // 2):
            for s, ref in enumerate((own_ref, sib_ref)):
                source = aligned(2 * q + (core ^ s), rows)
                block = total[source, :].astype(BF16)
                ref[q ^ half, :rows, :] = block[:, :1024]
                ref[q ^ half, rows : 2 * rows, :] = block[:, 1024:]
                ref[q ^ half, 2 * rows : 3 * rows, :] = wo_ref[source, :]
                ref[q ^ half, 3 * rows :, :] = jnp.zeros((32, 1024), BF16)
                ref[q ^ half, 3 * rows :, :128] = more


def raw_back(parts, me, halves, units, normed, cosine, sine, gains, grad_out):
    length, width = normed.shape
    rows = 3 * (width // parts) + 32
    grads = fixed((parts // 2, rows, 1024))
    return pl.pallas_call(
        lambda *refs: raw_back_kernel(parts, *refs),
        grid=(length // TILE,),
        in_specs=[SMALL] + [by_rows(512)] * 4 + [by_rows(1536)] * 2 + [by_rows(width)]
        + [by_rows(128)] * 2
        + [fixed((16, 1024)), fixed((1024, width))],
        out_specs=[by_rows(2048), grads, grads],
        out_shape=[jax.ShapeDtypeStruct((length, 2048), BF16)]
        + [jax.ShapeDtypeStruct((parts // 2, rows, 1024), BF16)] * 2,
        scratch_shapes=[pltpu.VMEM((width, 2048), F32), pltpu.VMEM((32, 128), F32)],
        compiler_params=params(),
        cost_estimate=cost(10, 30),
        name="raw_back",
    )(me, *halves, *units, normed, cosine, sine, gains, grad_out)


def input_kernel(parts, me_ref, b_ref, x_ref, f_ref, gain_ref, *refs):
    out_ref, w_all = refs[2 * parts :]
    load_pairs(parts, me_ref, refs, w_all)
    unit, inverse = unit_of(x_ref[...].astype(F32))
    scaled = dot(b_ref[...], w_all[...], NT) * gain_ref[0:1, :]
    out_ref[...] = f_ref[...] + inverse * (
        scaled - unit * jnp.mean(scaled * unit, axis=-1, keepdims=True)
    )


def input_back(pieces, me, back_raw, x, back_first, gain):
    length, width = x.shape
    parts = len(pieces)
    arrays, specs = pair_specs(pieces, width // parts)
    return pl.pallas_call(
        lambda *refs: input_kernel(parts, *refs),
        grid=(length // TILE,),
        in_specs=[SMALL, by_rows(2048), by_rows(width), by_rows(width), fixed((16, 1024))] + specs,
        out_specs=by_rows(width),
        out_shape=jax.ShapeDtypeStruct((length, width), F32),
        scratch_shapes=[pltpu.VMEM((width, 2048), BF16)],
        compiler_params=params(),
        cost_estimate=cost(6, 18),
        name="input_back",
    )(me, back_raw, x, back_first, gain, *arrays)


def tables_of(numbers):
    length = numbers.shape[0]
    indices = jnp.arange(length, dtype=jnp.int32)
    starts = jnp.concatenate([jnp.ones((1,), dtype=bool), numbers[1:] != numbers[:-1]])
    begins = lax.cummax(jnp.where(starts, indices, jnp.zeros_like(numbers)), axis=0)
    offsets = (indices - begins).astype(F32).reshape(length, 1)
    frequency = ROPE_BASE ** (-jnp.arange(0, HEAD_SIZE, 2).astype(F32) / HEAD_SIZE)
    angles = offsets * frequency
    cosine = jnp.cos(angles)
    sine = jnp.sin(angles)
    same = (numbers[:, None] == jnp.arange(4)[None]).astype(F32)
    empty = jnp.zeros((length, 64), F32)
    return (
        jnp.concatenate([cosine] * 4, axis=1),
        jnp.concatenate([-sine, sine, -sine, sine], axis=1),
        jnp.concatenate([empty, -FAR * same, empty[:, :60]], axis=1),
        jnp.concatenate([empty, 1 - same, jnp.ones((length, 3)), empty[:, :57]], axis=1),
    )


def pack_kernel(chunks, o_ref, gate_ref, up_ref, down_ref, *out_refs):
    low = lanes(128) < 64
    out_refs[0][:128, :] = o_ref[...]
    places = [(c, i) for c, n in enumerate(chunks) for i in range(n)]
    for t, (c, i) in enumerate(places):
        row = i * 192 + (0 if c else 128)
        for side, ref in enumerate((gate_ref, up_ref)):
            for e in range(4):
                left, right = (18 * e + t) // 2, (18 * e + 9 + t) // 2
                a = ref[:, left * 128 : left * 128 + 128].astype(F32)
                b = ref[:, right * 128 : right * 128 + 128].astype(F32)
                both = pltpu.roll(jnp.where(low, b, a), 64, 1) if t % 2 else jnp.where(low, a, b)
                at = side * SLAB + e * 128
                out_refs[c][row : row + 128, at : at + 128] = both.astype(BF16)
        out_refs[c][row + 128 : row + 192, :] = down_ref[t * 64 : t * 64 + 64, :]


def pack_rows(chunks, w_output, w_gate, w_up, w_down):
    return pl.pallas_call(
        lambda *refs: pack_kernel(chunks, *refs),
        out_shape=[
            jax.ShapeDtypeStruct((n * 192 + (0 if c else 128), 1024), BF16)
            for c, n in enumerate(chunks)
        ],
        compiler_params=params(),
        cost_estimate=cost(0, 7),
        name="pack_rows",
    )(w_output, w_gate, w_up, w_down)


def unpack_kernel(flag_ref, *refs):
    *in_refs, gate_ref, up_ref, down_ref = refs
    low = lanes(128) < 64
    outer = flag_ref[0] > 0

    def rows_of(at, size, columns):
        for inside, outside in zip(in_refs[::2], in_refs[1::2]):
            if at < inside.shape[0]:
                one = inside[at : at + size, columns].astype(F32)
                return jnp.where(outer, outside[at : at + size, columns].astype(F32), one)
            at -= inside.shape[0]

    def segment(side, s, half):
        d = s // 9
        at = side * SLAB + (d // 2) * 128
        tile = rows_of((s % 9) * 192, 128, slice(at, at + 128))
        return tile if d % 2 == half else pltpu.roll(tile, 64, 1)

    for side, out in enumerate((gate_ref, up_ref)):
        for m in range(36):
            out[:, m * 128 : m * 128 + 128] = jnp.where(
                low, segment(side, 2 * m, 0), segment(side, 2 * m + 1, 1)
            )
    for t in range(9):
        down_ref[t * 64 : t * 64 + 64, :] = rows_of(t * 192 + 128, 64, slice(None))


def unpack_rows(flag, *totals):
    whole = pl.BlockSpec(memory_space=pltpu.VMEM)
    return pl.pallas_call(
        unpack_kernel,
        in_specs=[SMALL] + [whole] * len(totals),
        out_shape=[
            jax.ShapeDtypeStruct((128, 4608), F32),
            jax.ShapeDtypeStruct((128, 4608), F32),
            jax.ShapeDtypeStruct((576, 1024), F32),
        ],
        compiler_params=params(),
        cost_estimate=cost(0, 14),
        name="unpack_rows",
    )(flag, *totals)


def tie(*values):
    return lax.optimization_barrier(values)


def after(value, *tokens):
    return tie(value, *tokens)[0]


def hop(array, bit):
    return lax.ppermute(array, "shard", [(i, i ^ bit) for i in range(8)])


def gather_all(pack):
    return lax.all_gather(pack, "shard", axis=0, tiled=False)


def scatter_all(every):
    return lax.psum_scatter(every, "shard", scatter_dimension=0, tiled=True)[0]


def weave(near, far):
    groups = []
    for one, two in zip(near, far):
        groups += [list(one), list(two)]
    return Pieces(groups)


def combine(*outputs):
    terms = [term if isinstance(term, tuple) else (term, None) for out in outputs for term in out]
    rows, width = terms[0][0].shape[-2:]
    step = rows // 2

    def spec(k):
        if k is None:
            return pl.BlockSpec((step, width), lambda i: (i, 0))
        return pl.BlockSpec((pl.Squeezed(), step, width), lambda i: (k, i, 0))

    def kernel(*refs):
        at = 0
        for out, out_ref in zip(outputs, refs[len(terms) :]):
            total = refs[at][...].astype(F32)
            for ref in refs[at + 1 : at + len(out)]:
                total = total + ref[...].astype(F32)
            at += len(out)
            out_ref[...] = total.astype(BF16)

    found = pl.pallas_call(
        kernel,
        grid=(rows // step,),
        in_specs=[spec(k) for _, k in terms],
        out_specs=[pl.BlockSpec((step, width), lambda i: (i, 0))] * len(outputs),
        out_shape=[jax.ShapeDtypeStruct((rows, width), BF16)] * len(outputs),
        compiler_params=params(),
        cost_estimate=cost(0, 4),
        name="combine",
    )(*[array for array, _ in terms])
    return found[0] if len(outputs) == 1 else found


def rep_hop(array, pairs):
    return lax.ppermute(array.astype(BF16), "rep", pairs)


INWARD = [(0, 1), (3, 2)]
ACROSS = [(1, 2), (2, 1)]
OUTWARD = [(1, 0), (2, 3)]


def at_end(inner, outer):
    place = lax.axis_index("rep")
    return jnp.where((place == 0) | (place == 3), outer.astype(F32), inner)


def on_device(sizes, *arrays):
    (
        block_input, document_numbers, attn_gain, w_query, key_weight, value_weight, query_gain,
        key_gain, w_output, ffn_gain, w_gate, w_up, w_down, cotangent,
    ) = arrays
    reps, parts = sizes
    _, length, width = block_input.shape
    ff = w_gate.shape[1]
    paired = parts == 8 and reps == 4
    me = lax.axis_index("shard").astype(jnp.int32)
    place = me.reshape(1) if paired else jnp.zeros((1,), jnp.int32)
    x = block_input.reshape(length, width)
    back_out = cotangent.reshape(length, width)
    numbers = document_numbers.reshape(length)
    rows = width // parts
    seg = SLAB // parts
    slabs = ff // SLAB
    few = query_gain.shape[0]

    lane = jnp.arange(width)

    def spot(gain, times, size):
        share = gain.shape[0]
        wide = jnp.tile(gain, width // share)
        return jnp.where((lane < size * times) & ((lane % size) // share == me), wide, 0)

    empty = jnp.zeros((width,), BF16)
    gain_rows = [
        spot(attn_gain, 1, width),
        spot(query_gain, 2, HEAD_SIZE),
        spot(key_gain, 2, HEAD_SIZE),
        spot(ffn_gain, 1, width),
    ]
    first_pack = jnp.concatenate(
        [
            w_query,
            jnp.concatenate([key_weight, value_weight], axis=1),
            jnp.stack(gain_rows + [empty] * 12),
        ]
    )
    tables = tables_of(numbers)
    run = block_paired if paired else block_simple
    args = (me, place, x, back_out, tables, first_pack, w_output, w_gate, w_up, w_down)
    block_output, input_grad, attn_grad, feed_grads = run(*args)
    grad_gate, grad_up, grad_down = feed_grads
    grad_query = attn_grad[:rows]
    grad_key = attn_grad[rows : 2 * rows, :512]
    grad_value = attn_grad[rows : 2 * rows, 512:]

    def diagonal(*pairs):
        total = 0.0
        for weight, grad in pairs:
            total = total + jnp.sum(weight.astype(F32) * grad, axis=1)
        return total

    grad_gain_attn = diagonal(
        (w_query, grad_query), (key_weight, grad_key), (value_weight, grad_value)
    ) / attn_gain.astype(F32)
    grad_gain_ffn = diagonal((w_gate, grad_gate), (w_up, grad_up)) / ffn_gain.astype(F32)

    def small(row):
        both = attn_grad[3 * rows + row, :64] + attn_grad[3 * rows + row, 64:128]
        return lax.dynamic_slice(both, (me * few,), (few,))

    return (
        block_output[None],
        input_grad[None],
        grad_gain_attn,
        grad_query,
        grad_key,
        grad_value,
        small(0),
        small(1),
        attn_grad[2 * rows : 3 * rows],
        grad_gain_ffn,
        grad_gate,
        grad_up,
        grad_down,
    )


def block_simple(me, place, x, back_out, tables, first_pack, w_output, w_gate, w_up, w_down):
    rows, ff = w_gate.shape
    parts = x.shape[1] // rows
    seg = SLAB // parts
    slabs = ff // SLAB
    tall = rows + seg

    def columns(weight):
        cut = weight.reshape(rows, parts, slabs, seg).transpose(2, 0, 1, 3)
        return cut.reshape(slabs, rows, SLAB)

    pack = jnp.concatenate(
        [
            jnp.concatenate([columns(w_gate), columns(w_up)], axis=2),
            w_down.reshape(slabs, seg, x.shape[1]),
        ],
        axis=1,
    ).reshape(slabs * tall, 2 * SLAB)
    every = gather_all(first_pack)
    pairs = [(every[k], every[k], 1) for k in range(parts)]
    pieces = Pieces(stacked=gather_all(jnp.concatenate([w_output, pack])))
    normed_one, *units, q_aug, k_aug, v_aug, gains = project(pairs, place, x, tables)
    attended_0, q_back_0 = attend(q_aug, k_aug, v_aug, 0, 4)
    attended_1, q_back_1 = attend(q_aug, k_aug, v_aug, 4, 4)
    attended = (attended_0, attended_1)
    first_sum, normed_two, normed_two_t = output_rows(pieces, place, attended, x, gains)
    out, back, grads = feed(
        pieces, place, rows, slabs, normed_two, normed_two_t, back_out, False
    )
    total = lax.psum(scatter_all(grads), "rep").astype(F32).reshape(slabs, tall, 2 * SLAB)
    back_first, back_attended, grad_out = middle(
        pieces, place, first_sum, back_out, attended, gains, [back]
    )
    halves_0 = attend_back(q_back_0, k_aug, v_aug, attended_0, back_attended, 0, 4)
    halves_1 = attend_back(q_back_1, k_aug, v_aug, attended_1, back_attended, 4, 4)
    back_raw, own, sib = raw_back(
        parts, place, (halves_0[0], halves_1[0], halves_0[1], halves_1[1]), units, normed_one,
        tables[0], tables[1], gains, grad_out,
    )
    every = jnp.stack([own, sib], axis=1).reshape((parts,) + own.shape[1:])
    attn_grad = lax.psum(scatter_all(every), "rep").astype(F32)
    input_grad = input_back(pairs, place, back_raw, x, back_first, gains)

    def uncut(block):
        return block.reshape(slabs, rows, parts, seg).transpose(1, 2, 0, 3).reshape(rows, ff)

    feed_grads = (
        uncut(total[:, :rows, :SLAB]),
        uncut(total[:, :rows, SLAB:]),
        total[:, rows:, :].reshape(slabs * seg, x.shape[1]),
    )
    return (first_sum + out).astype(BF16), input_grad, attn_grad, feed_grads


def fence(outputs, *hops):
    found = tie(*outputs, *hops)
    return found[: len(outputs)], list(found[len(outputs) :])


def block_paired(me, place, x, back_out, tables, first_pack, w_output, w_gate, w_up, w_down):
    rows = w_gate.shape[0]
    chunks = (3, 3, 3)

    first = hop(first_pack, 2)
    second = hop(first_pack, 4)
    twin = hop(first_pack, 1)
    made, (first, second, twin) = fence(
        [*pack_rows(chunks, w_output, w_gate, w_up, w_down), *tables], first, second, twin
    )
    packs, tables = list(made[:3]), made[3:]
    corner_a = hop(second[:rows], 2)
    corner_b = hop(first[rows:], 4)
    far = [twin] + [hop(piece, 1) for piece in (first, second, corner_a, corner_b)]
    near = [first_pack, first, second, corner_a, corner_b]
    pairs = []
    for k in range(3):
        pairs += [(near[k], near[k], 1), (far[k], far[k], 1)]
    pairs += [(near[3], near[4], 0), (far[3], far[4], 0)]

    pack = after(packs[0], corner_a, corner_b, far[1], far[2])
    first, second, twin = hop(pack, 2), hop(pack, 4), hop(pack, 1)
    normed_one, *units, q_aug, k_aug, v_aug, gains = project(pairs, place, x, tables)
    (attended_0, q_back_0, k_aug), (first, second, twin) = fence(
        [*attend(q_aug, k_aug, v_aug, 0, 4), k_aug], first, second, twin
    )
    corner_a, corner_b = hop(second[:, :512], 2), hop(first[:, 512:], 4)
    far = [hop(first, 1), hop(second, 1)]
    packs[1] = after(packs[1], first, second)
    waiting = [hop(packs[1], bit) for bit in (1, 2, 4, 6)]
    (attended_1, q_back_1), (corner_a, corner_b, *far) = fence(
        attend(q_aug, k_aug, v_aug, 4, 4), corner_a, corner_b, *far
    )
    attended = (attended_0, attended_1)
    early = weave(
        [[pack], [first], [second], [corner_a, corner_b]],
        [[twin], [far[0]], [far[1]], [hop(corner_a, 1), hop(corner_b, 1)]],
    )
    first_sum, normed_two, normed_two_t = output_rows(early, place, attended, x, gains)

    def finish(pack, twin, first, second, corner):
        near = (first, second, corner)
        far = [hop(piece, 1) for piece in near]
        return weave([[pack]] + [[a] for a in near], [[twin]] + [[a] for a in far])

    def feed_step(pieces, begin, n, paired):
        return feed(pieces, place, begin, n, normed_two, normed_two_t, back_out, paired)

    (out_0, back_0, own_0, sib_0, normed_two), waiting = fence(
        [*feed_step(early, rows, chunks[0], True), normed_two], *waiting
    )
    later = finish(packs[1], *waiting)
    waiting = [hop(packs[2], bit) for bit in (1, 2, 4, 6)]
    other_0 = hop(after(sib_0, *later.arrays), 1)
    *early_rows, corner = waiting
    (out_1, back_1, own_1, sib_1, normed_two), (other_0, *early_rows) = fence(
        [*feed_step(later, 0, chunks[1], True), normed_two], other_0, *early_rows
    )
    terms = combine(*[[(own_0, k), (other_0, k)] for k in (1, 2, 3)])
    corner, *terms = tie(corner, *terms)
    last = finish(packs[2], *early_rows, corner)
    other_1 = hop(after(sib_1, *last.arrays), 1)
    steps = [hop(term, 2 * k) for k, term in zip((1, 2, 3), terms)]
    (out_2, back_2, own_2, sib_2), (other_1, *steps) = fence(
        feed(last, place, 0, chunks[2], normed_two, normed_two_t, back_out, True), other_1, *steps
    )
    other_2 = hop(sib_2, 1)
    grads_0, term = combine(
        [(own_0, 0), (other_0, 0), *steps], [(own_1, 3), (other_1, 3)]
    )
    back_2, grads_0, term = tie(back_2, grads_0, term)
    moved_1 = hop(term, 4)
    inward_0 = rep_hop(grads_0, INWARD)
    middles = middle(
        early, place, first_sum, back_out, attended, gains, [back_0, back_1, back_2]
    )
    (back_first, back_attended, grad_out), (other_2,) = fence(middles, other_2)
    term = combine([(own_2, 3), (other_2, 3)])
    back_attended, term = tie(back_attended, term)
    moved_2 = hop(term, 2)
    halves = attend_back(q_back_0, k_aug, v_aug, attended_0, back_attended, 0, 4)
    (dq_0, dkv_0, back_attended), (moved_1, moved_2, inward_0) = fence(
        [*halves, back_attended], moved_1, moved_2, inward_0
    )
    one, two, three, four, half_0 = combine(
        [(own_1, 1), (other_1, 1), moved_1],
        [(own_1, 2), (other_1, 2)],
        [(own_2, 1), (other_2, 1)],
        [(own_2, 2), (other_2, 2), moved_2],
        [grads_0, inward_0],
    )
    back_attended, one, two, three, four, half_0 = tie(
        back_attended, one, two, three, four, half_0
    )
    first_1, second_1 = hop(one, 2), hop(two, 4)
    first_2, second_2 = hop(three, 2), hop(four, 4)
    across_0 = rep_hop(half_0, ACROSS)
    halves = attend_back(q_back_1, k_aug, v_aug, attended_1, back_attended, 4, 4)
    (dq_1, dkv_1), (first_1, second_1, across_0) = fence(halves, first_1, second_1, across_0)
    grads_1, total_0 = combine(
        [(own_1, 0), (other_1, 0), first_1, second_1], [half_0, across_0]
    )
    dq_1, grads_1, total_0 = tie(dq_1, grads_1, total_0)
    inward_1 = rep_hop(grads_1, INWARD)
    outward_0 = rep_hop(total_0, OUTWARD)
    result = raw_back(
        8, place, (dq_0, dq_1, dkv_0, dkv_1), units, normed_one, tables[0], tables[1], gains,
        grad_out,
    )
    (back_raw, own, sib), (first_2, second_2, inward_1, outward_0) = fence(
        result, first_2, second_2, inward_1, outward_0
    )
    other = hop(sib, 1)
    half_1, grads_2 = combine(
        [grads_1, inward_1], [(own_2, 0), (other_2, 0), first_2, second_2]
    )
    back_raw, other, half_1, grads_2 = tie(back_raw, other, half_1, grads_2)
    terms = combine(*[[(own, k), (other, k)] for k in (1, 2, 3)])
    back_raw, *terms = tie(back_raw, *terms)
    steps = [hop(term, 2 * k) for k, term in zip((1, 2, 3), terms)]
    across_1 = rep_hop(half_1, ACROSS)
    inward_2 = rep_hop(grads_2, INWARD)
    input_grad = input_back(pairs, place, back_raw, x, back_first, gains)
    (input_grad,), (across_1, inward_2) = fence([input_grad], across_1, inward_2)
    total_1, half_2 = combine([half_1, across_1], [grads_2, inward_2])
    first_sum, total_1, half_2 = tie(first_sum, total_1, half_2)
    outward_1 = rep_hop(total_1, OUTWARD)
    across_2 = rep_hop(half_2, ACROSS)
    outs = out_0.astype(F32) + out_1.astype(F32) + out_2.astype(F32)
    block_output = (first_sum + outs).astype(BF16)
    (block_output,), steps = fence([block_output], *steps)
    grads = combine([(own, 0), (other, 0), *steps])
    inward = rep_hop(grads, INWARD)
    across_2, _ = tie(across_2, grads)
    total_2 = combine([half_2, across_2])
    outward_2 = rep_hop(total_2, OUTWARD)
    inward, outward_1, _ = tie(inward, outward_1, total_2)
    half = combine([grads, inward])
    across = rep_hop(half, ACROSS)
    outward_2, across, _ = tie(outward_2, across, half)
    total = combine([half, across])
    outward = rep_hop(total, OUTWARD)
    total, outward_2 = tie(total, outward_2)
    spot = lax.axis_index("rep")
    flag = ((spot == 0) | (spot == 3)).astype(jnp.int32).reshape(1)
    feed_grads = unpack_rows(flag, total_0, outward_0, total_1, outward_1, total_2, outward_2)
    (*feed_grads,), (outward,) = fence(feed_grads, outward)
    return block_output, input_grad, at_end(total.astype(F32), outward), feed_grads


def solution(mesh):
    sizes = (mesh.shape["rep"], mesh.shape["shard"])
    whole = P(("rep", "shard"), None, None)
    matrix = P("shard", None)
    vector = P("shard")
    in_specs = (
        whole, P(("rep", "shard"), None), vector, matrix, matrix, matrix, vector, vector, matrix,
        vector, matrix, matrix, matrix, whole,
    )
    out_specs = (
        whole, whole, vector, matrix, matrix, matrix, vector, vector, matrix, vector, matrix,
        matrix, matrix,
    )
    return jax.shard_map(
        lambda *arrays: on_device(sizes, *arrays),
        mesh=mesh,
        in_specs=in_specs,
        out_specs=out_specs,
        check_vma=False,
    )
```

```python
import jax
import jax.numpy as jnp
from jax import lax
from jax.experimental import pallas as pl
from jax.experimental.pallas import tpu as pltpu
from jax.sharding import PartitionSpec as P

QUERY_HEADS = 16
KEY_VALUE_HEADS = 8
HEAD_SIZE = 64
EPS = 1e-05
ROPE_BASE = 1000000.0
FAR = 32768.0
TILE = 256
SLAB = 512
NT = ((1,), (1,))
NN = ((1,), (0,))
TN = ((0,), (0,))
BF16 = jnp.bfloat16
F32 = jnp.float32
SMALL = pl.BlockSpec(memory_space=pltpu.SMEM)


def dot(left, right, dims=NN):
    return lax.dot_general(left, right, (dims, ((), ())), preferred_element_type=F32)


def params(mega_bytes=60):
    return pltpu.CompilerParams(vmem_limit_bytes=mega_bytes * 1024 * 1024)


def cost(giga_flops, mega_bytes, exps=0):
    return pl.CostEstimate(
        flops=int(giga_flops * 10**6),
        bytes_accessed=int(mega_bytes * 10**3),
        transcendentals=exps // 1000,
    )


def fixed(shape, where=None):
    index = (0,) * len(shape) if where is None else where
    return pl.BlockSpec(shape, lambda *_: index, pipeline_mode=pl.Buffered(1))


def by_rows(width, rows=TILE):
    return pl.BlockSpec((rows, width), lambda i: (i, 0))


class Pieces:
    def __init__(self, groups=None, stacked=None):
        self.stacked = stacked
        self.count = len(groups) if stacked is None else stacked.shape[0]
        self.groups = groups if stacked is None else [[stacked]] * self.count
        self.arrays = [array for group in self.groups for array in group]
        self.layout = [len(group) for group in self.groups]

    def specs(self, rows, start):
        once = pl.Buffered(1) if start(0) == start(1) else None
        found = []
        for k, group in enumerate(self.groups):
            for array in group:
                shape = (pl.Element(rows), pl.Element(array.shape[-1]))
                if self.stacked is None:
                    found.append(
                        pl.BlockSpec(shape, lambda i: (start(i), 0), pipeline_mode=once)
                    )
                else:
                    found.append(
                        pl.BlockSpec(
                            (pl.Squeezed(),) + shape,
                            lambda i, k=k: (k, start(i), 0),
                            pipeline_mode=once,
                        )
                    )
        return found


def grouped(refs, layout):
    groups, at = [], 0
    for size in layout:
        groups.append(refs[at : at + size])
        at += size
    return groups


def fill(target, at, group, rows):
    left = 0
    for ref in group:
        right = left + ref.shape[1]
        target[at, left:right] = ref[rows, :]
        left = right


def split3(value):
    high = value.astype(BF16).astype(F32)
    rest = value - high
    middle = rest.astype(BF16).astype(F32)
    return high, middle, rest - middle


def aligned(index, rows):
    return pl.ds(pl.multiple_of(index * rows, rows), rows)


def unit_of(rows):
    inverse = lax.rsqrt(jnp.mean(rows * rows, axis=-1, keepdims=True) + EPS)
    return rows * inverse, inverse


def head_blocks():
    first = lax.broadcasted_iota(jnp.int32, (128, 128), 0) // HEAD_SIZE
    second = lax.broadcasted_iota(jnp.int32, (128, 128), 1) // HEAD_SIZE
    return (first == second).astype(BF16)


def head_mean(rows, blocks):
    return dot(rows.astype(BF16), blocks) * (1.0 / HEAD_SIZE)


def swap_halves(rows, first):
    return jnp.where(first, pltpu.roll(rows, 96, 1), pltpu.roll(rows, 32, 1))


def lanes(rows=TILE):
    return lax.broadcasted_iota(jnp.int32, (rows, 128), 1)


def load_pairs(parts, me_ref, refs, w_all):
    rows = w_all.shape[0] // parts

    @pl.when(pl.program_id(0) == 0)
    def _():
        for k in range(parts):
            at = aligned(me_ref[0] ^ k, rows)
            w_all[at, :1024] = refs[2 * k][...]
            w_all[at, 1024:] = refs[2 * k + 1][...]


def pair_specs(pieces, rows):
    arrays, specs = [], []
    for piece in pieces:
        left, right, at = piece
        arrays += [left, right]
        specs += [fixed((rows, 1024)), fixed((rows, 1024), (at, 0))]
    return arrays, specs


def project_kernel(parts, me_ref, x_ref, cos_ref, sin_ref, qx_ref, kx_ref, *refs):
    gain_refs = refs[2 * parts : 3 * parts]
    n_ref, unit_ref, scale_ref, q_ref, k_ref, v_ref, gain_ref, w_all = refs[3 * parts :]
    load_pairs(parts, me_ref, refs, w_all)

    @pl.when(pl.program_id(0) == 0)
    def _():
        total = gain_refs[0][...].astype(F32)
        for ref in gain_refs[1:]:
            total = total + ref[...].astype(F32)
        gain_ref[...] = total

    unit, _ = unit_of(x_ref[...].astype(F32))
    normed = (unit * gain_ref[0:1, :]).astype(BF16)
    n_ref[...] = normed
    raw = dot(normed, w_all[...])
    blocks = head_blocks()
    lane = lanes()
    first = (lane % HEAD_SIZE) < HEAD_SIZE // 2
    low = lane < HEAD_SIZE
    cosine, sine = cos_ref[...], sin_ref[...]
    for p in range(12):
        at = slice(p * 128, (p + 1) * 128)
        rows_in = raw[:, at]
        inverse = lax.rsqrt(head_mean(rows_in * rows_in, blocks) + EPS)
        unit = rows_in * inverse
        unit_ref[:, at] = unit.astype(BF16)
        scale_ref[:, at] = inverse.astype(BF16)
        scaled = unit * gain_ref[1 + p // 8 : 2 + p // 8, :128]
        turned = scaled * cosine + swap_halves(scaled, first) * sine
        if p < 8:
            turned = turned * HEAD_SIZE**-0.5
            out, more, at = q_ref, qx_ref[...], 2 * p
        else:
            out, more, at = k_ref, kx_ref[...], 2 * (p - 8)
        out[at] = jnp.where(low, turned, more).astype(BF16)
        out[at + 1] = jnp.where(low, pltpu.roll(turned, 64, 1), more).astype(BF16)
    more = ((lane >= 64) & (lane < 67)).astype(F32)
    for p in range(4):
        rows_in = raw[:, 1536 + p * 128 : 1664 + p * 128]
        v_ref[2 * p] = jnp.where(low, rows_in, more).astype(BF16)
        v_ref[2 * p + 1] = jnp.where(low, pltpu.roll(rows_in, 64, 1), more).astype(BF16)


def project(pieces, me, x, tables):
    length, width = x.shape
    parts = len(pieces)
    rows = width // parts
    arrays, specs = pair_specs(pieces, rows)
    gains = [(piece[1], (piece[2] + 1) * rows // 16) for piece in pieces]

    def heads(count):
        return pl.BlockSpec((count, TILE, 128), lambda i: (0, i, 0))

    return pl.pallas_call(
        lambda *refs: project_kernel(parts, *refs),
        grid=(length // TILE,),
        in_specs=[SMALL, by_rows(width)]
        + [by_rows(128)] * 4
        + specs
        + [fixed((16, 1024), (at, 0)) for _, at in gains],
        out_specs=[by_rows(width), by_rows(1536), by_rows(1536), heads(16), heads(8), heads(8)]
        + [fixed((16, 1024))],
        out_shape=[
            jax.ShapeDtypeStruct((length, width), BF16),
            jax.ShapeDtypeStruct((length, 1536), BF16),
            jax.ShapeDtypeStruct((length, 1536), BF16),
            jax.ShapeDtypeStruct((16, length, 128), BF16),
            jax.ShapeDtypeStruct((8, length, 128), BF16),
            jax.ShapeDtypeStruct((8, length, 128), BF16),
            jax.ShapeDtypeStruct((16, 1024), F32),
        ],
        scratch_shapes=[pltpu.VMEM((width, 2048), BF16)],
        compiler_params=params(32),
        cost_estimate=cost(8, 25),
        name="project",
    )(me, x, *tables, *arrays, *[array for array, _ in gains])


def causal(query_axis):
    first = lax.broadcasted_iota(jnp.int32, (TILE, TILE), 0)
    second = lax.broadcasted_iota(jnp.int32, (TILE, TILE), 1)
    return (first >= second) if query_axis == 0 else (second >= first)


def attend_kernel(q_ref, k_ref, v_ref, o_ref, qb_ref):
    tiles = q_ref.shape[1] // TILE
    keep = causal(0)
    lane = lax.broadcasted_iota(jnp.int32, (TILE, 128), 1)
    for i in range(tiles):
        rows = slice(i * TILE, (i + 1) * TILE)
        before = slice(0, i * TILE)
        halves = []
        for h in range(2):
            q = q_ref[h, rows, :]
            weights = jnp.where(keep, jnp.exp(dot(q, k_ref[0, rows, :], NT)), 0.0)
            out = dot(weights.astype(BF16), v_ref[0, rows, :])
            if i:
                weights = jnp.exp(dot(q, k_ref[0, before, :], NT)).astype(BF16)
                out = out + dot(weights, v_ref[0, before, :])
            total = out[:, 64:65]
            halves.append(out / total)
            high, middle, low = split3(-jnp.log(total))
            extra = jnp.where(
                lane == 68, high, jnp.where(lane == 69, middle, jnp.where(lane == 70, low, 0.0))
            )
            qb_ref[h, rows, :] = (q.astype(F32) + extra).astype(BF16)
        both = jnp.where(lane < 64, halves[0], pltpu.roll(halves[1], 64, 1))
        o_ref[rows, :] = both.astype(BF16)


def attend(q_aug, k_aug, v_aug, begin, groups):
    _, length, _ = q_aug.shape
    return pl.pallas_call(
        attend_kernel,
        grid=(groups,),
        in_specs=[
            pl.BlockSpec((2, length, 128), lambda g: (g + begin, 0, 0)),
            pl.BlockSpec((1, length, 128), lambda g: (g + begin, 0, 0)),
            pl.BlockSpec((1, length, 128), lambda g: (g + begin, 0, 0)),
        ],
        out_specs=[
            pl.BlockSpec((length, 128), lambda g: (0, g)),
            pl.BlockSpec((2, length, 128), lambda g: (g, 0, 0)),
        ],
        out_shape=[
            jax.ShapeDtypeStruct((length, groups * 128), BF16),
            jax.ShapeDtypeStruct((2 * groups, length, 128), BF16),
        ],
        compiler_params=params(32),
        cost_estimate=cost(2.5 * groups, 2 * groups, groups * 2**20),
        name="attend",
    )(q_aug, k_aug, v_aug)


def attend_back_kernel(q_ref, k_ref, v_ref, o_ref, do_ref, dq_ref, dkv_ref, do_aug, k_t, dq_t):
    length = q_ref.shape[1]
    tiles = length // TILE
    keep = causal(1)
    lane = lax.broadcasted_iota(jnp.int32, (length, 128), 1)
    back = do_ref[...].astype(F32)
    product = back * o_ref[...].astype(F32)
    for h in range(2):
        own = (lane < 64) if h == 0 else (lane >= 64)
        centre = jnp.sum(jnp.where(own, product, 0.0), axis=1, keepdims=True)
        moved = back if h == 0 else pltpu.roll(back, 64, 1)
        high, middle, low = split3(-centre)
        extra = jnp.where(
            lane == 64, high, jnp.where(lane == 65, middle, jnp.where(lane == 66, low, 0.0))
        )
        do_aug[h] = jnp.where(lane < 64, moved, extra).astype(BF16)
    k_t[...] = k_ref[0].astype(F32).T[:64, :].astype(BF16)
    low_half = lax.broadcasted_iota(jnp.int32, (TILE, 128), 1) < 64
    for j in range(tiles):
        cols = slice(j * TILE, (j + 1) * TILE)
        k = k_ref[0, cols, :]
        v = v_ref[0, cols, :]
        dk = 0.0
        dv = 0.0
        for i, stop in ((j, j + 1), (j + 1, tiles)):
            if i == tiles:
                continue
            rows = slice(i * TILE, stop * TILE)
            for h in range(2):
                q = q_ref[h, rows, :]
                do = do_aug[h, rows, :]
                probs = jnp.exp(dot(k, q, NT))
                if i == j:
                    probs = jnp.where(keep, probs, 0.0)
                scores = (probs * dot(v, do, NT)).astype(BF16)
                dv = dv + dot(probs.astype(BF16), do)
                dk = dk + dot(scores, q)
                to_q = dot(k_t[:, cols], scores)
                if j == 0:
                    dq_t[h * 64 : (h + 1) * 64, rows] = to_q
                else:
                    dq_t[h * 64 : (h + 1) * 64, rows] += to_q
        dkv_ref[cols, :] = jnp.where(low_half, dk, pltpu.roll(dv, 64, 1))
    dq_ref[...] = dq_t[...].T


def attend_back(q_back, k_aug, v_aug, attended, back_attended, begin, groups):
    _, length, _ = q_back.shape
    by_group = pl.BlockSpec((length, 128), lambda g: (0, g + begin))
    out_group = pl.BlockSpec((length, 128), lambda g: (0, g))
    return pl.pallas_call(
        attend_back_kernel,
        grid=(groups,),
        in_specs=[
            pl.BlockSpec((2, length, 128), lambda g: (g, 0, 0)),
            pl.BlockSpec((1, length, 128), lambda g: (g + begin, 0, 0)),
            pl.BlockSpec((1, length, 128), lambda g: (g + begin, 0, 0)),
            out_group,
            by_group,
        ],
        out_specs=[out_group, out_group],
        out_shape=[jax.ShapeDtypeStruct((length, groups * 128), F32)] * 2,
        scratch_shapes=[
            pltpu.VMEM((2, length, 128), BF16),
            pltpu.VMEM((64, length), BF16),
            pltpu.VMEM((128, length), F32),
        ],
        compiler_params=params(36),
        cost_estimate=cost(5 * groups, 3 * groups, groups * 2**20),
        name="attend_back",
    )(q_back, k_aug, v_aug, attended, back_attended)


def output_kernel(layout, me_ref, o0_ref, o1_ref, x_ref, gain_ref, *refs):
    sum_ref, n_ref, nt_ref, w_all = refs[-4:]
    rows = w_all.shape[0] // len(layout)

    @pl.when(pl.program_id(0) == 0)
    def _():
        for k, group in enumerate(grouped(refs, layout)):
            fill(w_all, aligned(me_ref[0] ^ k, rows), group, slice(None))

    total = x_ref[...].astype(F32) + dot(o0_ref[...], w_all[:512, :])
    total = total + dot(o1_ref[...], w_all[512:, :])
    sum_ref[...] = total
    unit, _ = unit_of(total)
    normed = unit * gain_ref[3:4, :]
    n_ref[...] = normed.astype(BF16)
    nt_ref[...] = normed.T.astype(BF16)


def output_rows(pieces, me, attended, x, gain):
    length, width = x.shape
    parts = pieces.count
    rows = width // parts
    return pl.pallas_call(
        lambda *refs: output_kernel(pieces.layout, *refs),
        grid=(length // TILE,),
        in_specs=[SMALL, by_rows(512), by_rows(512), by_rows(width), fixed((16, 1024))]
        + pieces.specs(rows, lambda i: 0),
        out_specs=[by_rows(width), by_rows(width), pl.BlockSpec((width, TILE), lambda i: (0, i))],
        out_shape=[
            jax.ShapeDtypeStruct((length, width), F32),
            jax.ShapeDtypeStruct((length, width), BF16),
            jax.ShapeDtypeStruct((width, length), BF16),
        ],
        scratch_shapes=[pltpu.VMEM((1024, width), BF16)],
        compiler_params=params(32),
        cost_estimate=cost(5, 15),
        name="output_rows",
    )(me, *attended, x, gain, *pieces.arrays)


def scatter_rows(me, parts, value, rows, own_ref, sib_ref, at):
    half = me >> 1
    core = me & 1
    for q in range(parts // 2):
        for s, ref in enumerate((own_ref, sib_ref)):
            source = 2 * q + (core ^ s)
            ref[q ^ half, at : at + rows, :] = value[aligned(source, rows), :]


def feed_kernel(layout, paired, me_ref, n_ref, nt_ref, c_ref, *refs):
    parts = len(layout)
    f_ref, b_ref, *grad_refs = refs[sum(layout) : -8]
    w_all, d_all, back, hidden, w_grad, d_grad, f_sum, b_sum = refs[-8:]
    me = me_ref[0]
    rows = w_all.shape[0] // parts
    seg = SLAB // parts
    for k, group in enumerate(grouped(refs, layout)):
        fill(w_all, aligned(me ^ k, rows), group, slice(0, rows))
        fill(d_all, aligned(me ^ k, seg), group, slice(rows, rows + seg))
    step = pl.program_id(0)

    @pl.when(step == 0)
    def _():
        f_sum[...] = jnp.zeros_like(f_sum)
        b_sum[...] = jnp.zeros_like(b_sum)

    both = dot(n_ref[...], w_all[...])
    gate = both[:, :SLAB]
    up = both[:, SLAB:]
    sig = 1.0 / (1.0 + jnp.exp(-gate))
    swish = gate * sig
    hidden[...] = (swish * up).astype(BF16)
    back_hidden = dot(c_ref[...], d_all[...], NT)
    back[:, SLAB:] = (back_hidden * swish).astype(BF16)
    back[:, :SLAB] = (back_hidden * up * sig * (1.0 + gate * (1.0 - sig))).astype(BF16)
    f_sum[...] += dot(hidden[...], d_all[...])
    b_sum[...] += dot(back[...], w_all[...], NT)
    w_grad[...] = dot(nt_ref[...], back[...]).astype(BF16)
    d_grad[...] = dot(hidden[...], c_ref[...], TN).astype(BF16)

    @pl.when(step == pl.num_programs(0) - 1)
    def _():
        f_ref[...] = f_sum[...].astype(BF16)
        b_ref[...] = b_sum[...].astype(BF16)

    if paired:
        own_ref, sib_ref = grad_refs
        scatter_rows(me, parts, w_grad, rows, own_ref, sib_ref, 0)
        scatter_rows(me, parts, d_grad, seg, own_ref, sib_ref, rows)
    else:
        for d in range(parts):
            grad_refs[0][d, :rows, :] = w_grad[d * rows : (d + 1) * rows, :]
            grad_refs[0][d, rows:, :] = d_grad[d * seg : (d + 1) * seg, :]


def feed(pieces, me, begin, slabs, normed, normed_t, cotangent, paired):
    length, width = normed.shape
    parts = pieces.count
    rows = width // parts + SLAB // parts
    depth = parts // 2 if paired else parts
    count = 2 if paired else 1
    grads = pl.BlockSpec((depth, rows, 2 * SLAB), lambda i: (0, i, 0))
    return pl.pallas_call(
        lambda *refs: feed_kernel(pieces.layout, paired, *refs),
        grid=(slabs,),
        in_specs=[SMALL, fixed((length, width)), fixed((width, length)), fixed((length, width))]
        + pieces.specs(rows, lambda i: (begin // 16 + i * (rows // 16)) * 16),
        out_specs=[fixed((length, width)), fixed((length, width))] + [grads] * count,
        out_shape=[
            jax.ShapeDtypeStruct((length, width), BF16),
            jax.ShapeDtypeStruct((length, width), BF16),
        ]
        + [jax.ShapeDtypeStruct((depth, slabs * rows, 2 * SLAB), BF16)] * count,
        scratch_shapes=[
            pltpu.VMEM((width, 2 * SLAB), BF16),
            pltpu.VMEM((SLAB, width), BF16),
            pltpu.VMEM((length, 2 * SLAB), BF16),
            pltpu.VMEM((length, SLAB), BF16),
            pltpu.VMEM((width, 2 * SLAB), BF16),
            pltpu.VMEM((SLAB, width), BF16),
            pltpu.VMEM((length, width), F32),
            pltpu.VMEM((length, width), F32),
        ],
        compiler_params=params(),
        cost_estimate=cost(12.5 * slabs, 20 + 6 * slabs),
        name="feed",
    )(me, normed, normed_t, cotangent, *pieces.arrays)


def middle_kernel(layout, sums, me_ref, s_ref, c_ref, o0_ref, o1_ref, gain_ref, *refs):
    b_refs = refs[:sums]
    f_ref, a_ref, g_ref, w_all, total = refs[-5:]
    rows = w_all.shape[0] // len(layout)
    step = pl.program_id(0)

    @pl.when(step == 0)
    def _():
        for k, group in enumerate(grouped(refs[sums:], layout)):
            fill(w_all, aligned(me_ref[0] ^ k, rows), group, slice(None))

    back = b_refs[0][...].astype(F32)
    for ref in b_refs[1:]:
        back = back + ref[...].astype(F32)
    unit, inverse = unit_of(s_ref[...])
    scaled = back * gain_ref[3:4, :]
    first = c_ref[...].astype(F32) + inverse * (
        scaled - unit * jnp.mean(scaled * unit, axis=-1, keepdims=True)
    )
    f_ref[...] = first
    short = first.astype(BF16)
    a_ref[...] = dot(short, w_all[...], NT).astype(BF16)
    grads = [dot(ref[...], short, TN) for ref in (o0_ref, o1_ref)]

    @pl.when(step == 0)
    def _():
        total[:512, :] = grads[0]
        total[512:, :] = grads[1]

    @pl.when(step > 0)
    def _():
        total[:512, :] += grads[0]
        total[512:, :] += grads[1]

    @pl.when(step == pl.num_programs(0) - 1)
    def _():
        g_ref[...] = total[...].astype(BF16)


def middle(pieces, me, first_sum, cotangent, attended, gain, backs):
    length, width = first_sum.shape
    parts = pieces.count
    rows = width // parts
    return pl.pallas_call(
        lambda *refs: middle_kernel(pieces.layout, len(backs), *refs),
        grid=(length // TILE,),
        in_specs=[SMALL, by_rows(width), by_rows(width), by_rows(512), by_rows(512), fixed((16, 1024))]
        + [by_rows(width)] * len(backs)
        + pieces.specs(rows, lambda i: 0),
        out_specs=[by_rows(width), by_rows(1024), fixed((1024, width))],
        out_shape=[
            jax.ShapeDtypeStruct((length, width), F32),
            jax.ShapeDtypeStruct((length, 1024), BF16),
            jax.ShapeDtypeStruct((1024, width), BF16),
        ],
        scratch_shapes=[pltpu.VMEM((1024, width), BF16), pltpu.VMEM((1024, width), F32)],
        compiler_params=params(32),
        cost_estimate=cost(9, 32),
        name="middle",
    )(me, first_sum, cotangent, *attended, gain, *backs, *pieces.arrays)


def raw_back_kernel(
    parts, me_ref, dq0_ref, dq1_ref, dkv0_ref, dkv1_ref, unit_ref, scale_ref, n_ref, cos_ref, sin_ref, gain_ref, wo_ref,
    b_ref, own_ref, sib_ref, total, gains,
):
    step = pl.program_id(0)
    rows = total.shape[0] // parts
    blocks = head_blocks()
    lane = lanes()
    first = (lane % HEAD_SIZE) < HEAD_SIZE // 2
    low = lane < HEAD_SIZE
    cosine, sine = cos_ref[...], sin_ref[...]
    sums = [None, None]
    for p in range(12):
        at = slice(p * 128, (p + 1) * 128)
        if p < 8:
            dq_ref = dq0_ref if p < 4 else dq1_ref
            grads = dq_ref[:, (p % 4) * 128 : (p % 4 + 1) * 128] * HEAD_SIZE**-0.5
        else:
            dkv_ref = dkv0_ref if p < 10 else dkv1_ref
            left = dkv_ref[:, (p % 2) * 256 : (p % 2) * 256 + 128]
            right = dkv_ref[:, (p % 2) * 256 + 128 : (p % 2) * 256 + 256]
            grads = jnp.where(low, left, pltpu.roll(right, 64, 1))
            values = jnp.where(low, pltpu.roll(left, 64, 1), right)
            b_ref[:, 512 + p * 128 : 640 + p * 128] = values.astype(BF16)
        turned = grads * cosine + swap_halves(grads * sine, first)
        unit = unit_ref[:, at].astype(F32)
        inverse = scale_ref[:, at].astype(F32)
        kind = 0 if p < 8 else 1
        part = jnp.sum(turned * unit, axis=0, keepdims=True)
        sums[kind] = part if sums[kind] is None else sums[kind] + part
        scaled = turned * gain_ref[1 + kind : 2 + kind, :128]
        b_ref[:, at] = (inverse * (scaled - unit * head_mean(scaled * unit, blocks))).astype(BF16)
    grad = dot(n_ref[...], b_ref[...], TN)

    @pl.when(step == 0)
    def _():
        total[...] = grad
        gains[...] = jnp.zeros_like(gains)

    @pl.when(step > 0)
    def _():
        total[...] += grad

    gains[0:1, :] += sums[0]
    gains[1:2, :] += sums[1]

    @pl.when(step == pl.num_programs(0) - 1)
    def _():
        me = me_ref[0]
        half = me >> 1
        core = me & 1
        more = gains[...].astype(BF16)
        for q in range(parts // 2):
            for s, ref in enumerate((own_ref, sib_ref)):
                source = aligned(2 * q + (core ^ s), rows)
                block = total[source, :].astype(BF16)
                ref[q ^ half, :rows, :] = block[:, :1024]
                ref[q ^ half, rows : 2 * rows, :] = block[:, 1024:]
                ref[q ^ half, 2 * rows : 3 * rows, :] = wo_ref[source, :]
                ref[q ^ half, 3 * rows :, :] = jnp.zeros((32, 1024), BF16)
                ref[q ^ half, 3 * rows :, :128] = more


def raw_back(parts, me, halves, units, normed, cosine, sine, gains, grad_out):
    length, width = normed.shape
    rows = 3 * (width // parts) + 32
    grads = fixed((parts // 2, rows, 1024))
    return pl.pallas_call(
        lambda *refs: raw_back_kernel(parts, *refs),
        grid=(length // TILE,),
        in_specs=[SMALL] + [by_rows(512)] * 4 + [by_rows(1536)] * 2 + [by_rows(width)]
        + [by_rows(128)] * 2
        + [fixed((16, 1024)), fixed((1024, width))],
        out_specs=[by_rows(2048), grads, grads],
        out_shape=[jax.ShapeDtypeStruct((length, 2048), BF16)]
        + [jax.ShapeDtypeStruct((parts // 2, rows, 1024), BF16)] * 2,
        scratch_shapes=[pltpu.VMEM((width, 2048), F32), pltpu.VMEM((32, 128), F32)],
        compiler_params=params(44),
        cost_estimate=cost(10, 30),
        name="raw_back",
    )(me, *halves, *units, normed, cosine, sine, gains, grad_out)


def input_kernel(parts, me_ref, b_ref, x_ref, f_ref, gain_ref, *refs):
    out_ref, w_all = refs[2 * parts :]
    load_pairs(parts, me_ref, refs, w_all)
    unit, inverse = unit_of(x_ref[...].astype(F32))
    scaled = dot(b_ref[...], w_all[...], NT) * gain_ref[0:1, :]
    out_ref[...] = f_ref[...] + inverse * (
        scaled - unit * jnp.mean(scaled * unit, axis=-1, keepdims=True)
    )


def input_back(pieces, me, back_raw, x, back_first, gain):
    length, width = x.shape
    parts = len(pieces)
    arrays, specs = pair_specs(pieces, width // parts)
    return pl.pallas_call(
        lambda *refs: input_kernel(parts, *refs),
        grid=(length // TILE,),
        in_specs=[SMALL, by_rows(2048), by_rows(width), by_rows(width), fixed((16, 1024))] + specs,
        out_specs=by_rows(width),
        out_shape=jax.ShapeDtypeStruct((length, width), F32),
        scratch_shapes=[pltpu.VMEM((width, 2048), BF16)],
        compiler_params=params(32),
        cost_estimate=cost(6, 18),
        name="input_back",
    )(me, back_raw, x, back_first, gain, *arrays)


def tables_of(numbers):
    length = numbers.shape[0]
    indices = jnp.arange(length, dtype=jnp.int32)
    starts = jnp.concatenate([jnp.ones((1,), dtype=bool), numbers[1:] != numbers[:-1]])
    begins = lax.cummax(jnp.where(starts, indices, jnp.zeros_like(numbers)), axis=0)
    offsets = (indices - begins).astype(F32).reshape(length, 1)
    frequency = ROPE_BASE ** (-jnp.arange(0, HEAD_SIZE, 2).astype(F32) / HEAD_SIZE)
    angles = offsets * frequency
    cosine = jnp.cos(angles)
    sine = jnp.sin(angles)
    same = (numbers[:, None] == jnp.arange(4)[None]).astype(F32)
    empty = jnp.zeros((length, 64), F32)
    return (
        jnp.concatenate([cosine] * 4, axis=1),
        jnp.concatenate([-sine, sine, -sine, sine], axis=1),
        jnp.concatenate([empty, -FAR * same, empty[:, :60]], axis=1),
        jnp.concatenate([empty, 1 - same, jnp.ones((length, 3)), empty[:, :57]], axis=1),
    )


def pack_kernel(chunks, o_ref, gate_ref, up_ref, down_ref, *out_refs):
    low = lanes(128) < 64
    out_refs[0][:128, :] = o_ref[...]
    places = [(c, i) for c, n in enumerate(chunks) for i in range(n)]
    for t, (c, i) in enumerate(places):
        row = i * 192 + (0 if c else 128)
        for side, ref in enumerate((gate_ref, up_ref)):
            for e in range(4):
                left, right = (18 * e + t) // 2, (18 * e + 9 + t) // 2
                a = ref[:, left * 128 : left * 128 + 128].astype(F32)
                b = ref[:, right * 128 : right * 128 + 128].astype(F32)
                both = pltpu.roll(jnp.where(low, b, a), 64, 1) if t % 2 else jnp.where(low, a, b)
                at = side * SLAB + e * 128
                out_refs[c][row : row + 128, at : at + 128] = both.astype(BF16)
        out_refs[c][row + 128 : row + 192, :] = down_ref[t * 64 : t * 64 + 64, :]


def pack_rows(chunks, w_output, w_gate, w_up, w_down):
    return pl.pallas_call(
        lambda *refs: pack_kernel(chunks, *refs),
        out_shape=[
            jax.ShapeDtypeStruct((n * 192 + (0 if c else 128), 1024), BF16)
            for c, n in enumerate(chunks)
        ],
        compiler_params=params(32),
        cost_estimate=cost(0, 7),
        name="pack_rows",
    )(w_output, w_gate, w_up, w_down)


def unpack_kernel(flag_ref, *refs):
    *in_refs, gate_ref, up_ref, down_ref = refs
    low = lanes(128) < 64
    outer = flag_ref[0] > 0

    def rows_of(at, size, columns):
        for inside, outside in zip(in_refs[::2], in_refs[1::2]):
            if at < inside.shape[0]:
                one = inside[at : at + size, columns].astype(F32)
                return jnp.where(outer, outside[at : at + size, columns].astype(F32), one)
            at -= inside.shape[0]

    def segment(side, s, half):
        d = s // 9
        at = side * SLAB + (d // 2) * 128
        tile = rows_of((s % 9) * 192, 128, slice(at, at + 128))
        return tile if d % 2 == half else pltpu.roll(tile, 64, 1)

    for side, out in enumerate((gate_ref, up_ref)):
        for m in range(36):
            out[:, m * 128 : m * 128 + 128] = jnp.where(
                low, segment(side, 2 * m, 0), segment(side, 2 * m + 1, 1)
            )
    for t in range(9):
        down_ref[t * 64 : t * 64 + 64, :] = rows_of(t * 192 + 128, 64, slice(None))


def unpack_rows(flag, *totals):
    whole = pl.BlockSpec(memory_space=pltpu.VMEM)
    return pl.pallas_call(
        unpack_kernel,
        in_specs=[SMALL] + [whole] * len(totals),
        out_shape=[
            jax.ShapeDtypeStruct((128, 4608), F32),
            jax.ShapeDtypeStruct((128, 4608), F32),
            jax.ShapeDtypeStruct((576, 1024), F32),
        ],
        compiler_params=params(44),
        cost_estimate=cost(0, 14),
        name="unpack_rows",
    )(flag, *totals)


def tie(*values):
    return lax.optimization_barrier(values)


def after(value, *tokens):
    return tie(value, *tokens)[0]


def hop(array, bit):
    return lax.ppermute(array, "shard", [(i, i ^ bit) for i in range(8)])


def gather_all(pack):
    return lax.all_gather(pack, "shard", axis=0, tiled=False)


def scatter_all(every):
    return lax.psum_scatter(every, "shard", scatter_dimension=0, tiled=True)[0]


def weave(near, far):
    groups = []
    for one, two in zip(near, far):
        groups += [list(one), list(two)]
    return Pieces(groups)


def combine(*outputs):
    terms = [term if isinstance(term, tuple) else (term, None) for out in outputs for term in out]
    rows, width = terms[0][0].shape[-2:]
    step = rows // 2

    def spec(k):
        if k is None:
            return pl.BlockSpec((step, width), lambda i: (i, 0))
        return pl.BlockSpec((pl.Squeezed(), step, width), lambda i: (k, i, 0))

    def kernel(*refs):
        at = 0
        for out, out_ref in zip(outputs, refs[len(terms) :]):
            total = refs[at][...].astype(F32)
            for ref in refs[at + 1 : at + len(out)]:
                total = total + ref[...].astype(F32)
            at += len(out)
            out_ref[...] = total.astype(BF16)

    found = pl.pallas_call(
        kernel,
        grid=(rows // step,),
        in_specs=[spec(k) for _, k in terms],
        out_specs=[pl.BlockSpec((step, width), lambda i: (i, 0))] * len(outputs),
        out_shape=[jax.ShapeDtypeStruct((rows, width), BF16)] * len(outputs),
        compiler_params=params(30),
        cost_estimate=cost(0, 4),
        name="combine",
    )(*[array for array, _ in terms])
    return found[0] if len(outputs) == 1 else found


def rep_hop(array, pairs):
    return lax.ppermute(array.astype(BF16), "rep", pairs)


INWARD = [(0, 1), (3, 2)]
ACROSS = [(1, 2), (2, 1)]
OUTWARD = [(1, 0), (2, 3)]


def at_end(inner, outer):
    place = lax.axis_index("rep")
    return jnp.where((place == 0) | (place == 3), outer.astype(F32), inner)


def on_device(sizes, *arrays):
    (
        block_input, document_numbers, attn_gain, w_query, key_weight, value_weight, query_gain,
        key_gain, w_output, ffn_gain, w_gate, w_up, w_down, cotangent,
    ) = arrays
    reps, parts = sizes
    _, length, width = block_input.shape
    ff = w_gate.shape[1]
    paired = parts == 8 and reps == 4
    me = lax.axis_index("shard").astype(jnp.int32)
    place = me.reshape(1) if paired else jnp.zeros((1,), jnp.int32)
    x = block_input.reshape(length, width)
    back_out = cotangent.reshape(length, width)
    numbers = document_numbers.reshape(length)
    rows = width // parts
    seg = SLAB // parts
    slabs = ff // SLAB
    few = query_gain.shape[0]

    lane = jnp.arange(width)

    def spot(gain, times, size):
        share = gain.shape[0]
        wide = jnp.tile(gain, width // share)
        return jnp.where((lane < size * times) & ((lane % size) // share == me), wide, 0)

    empty = jnp.zeros((width,), BF16)
    gain_rows = [
        spot(attn_gain, 1, width),
        spot(query_gain, 2, HEAD_SIZE),
        spot(key_gain, 2, HEAD_SIZE),
        spot(ffn_gain, 1, width),
    ]
    first_pack = jnp.concatenate(
        [
            w_query,
            jnp.concatenate([key_weight, value_weight], axis=1),
            jnp.stack(gain_rows + [empty] * 12),
        ]
    )
    tables = tables_of(numbers)
    run = block_paired if paired else block_simple
    args = (me, place, x, back_out, tables, first_pack, w_output, w_gate, w_up, w_down)
    block_output, input_grad, attn_grad, feed_grads = run(*args)
    grad_gate, grad_up, grad_down = feed_grads
    grad_query = attn_grad[:rows]
    grad_key = attn_grad[rows : 2 * rows, :512]
    grad_value = attn_grad[rows : 2 * rows, 512:]

    def diagonal(*pairs):
        total = 0.0
        for weight, grad in pairs:
            total = total + jnp.sum(weight.astype(F32) * grad, axis=1)
        return total

    grad_gain_attn = diagonal(
        (w_query, grad_query), (key_weight, grad_key), (value_weight, grad_value)
    ) / attn_gain.astype(F32)
    grad_gain_ffn = diagonal((w_gate, grad_gate), (w_up, grad_up)) / ffn_gain.astype(F32)

    def small(row):
        both = attn_grad[3 * rows + row, :64] + attn_grad[3 * rows + row, 64:128]
        return lax.dynamic_slice(both, (me * few,), (few,))

    return (
        block_output[None],
        input_grad[None],
        grad_gain_attn,
        grad_query,
        grad_key,
        grad_value,
        small(0),
        small(1),
        attn_grad[2 * rows : 3 * rows],
        grad_gain_ffn,
        grad_gate,
        grad_up,
        grad_down,
    )


def block_simple(me, place, x, back_out, tables, first_pack, w_output, w_gate, w_up, w_down):
    rows, ff = w_gate.shape
    parts = x.shape[1] // rows
    seg = SLAB // parts
    slabs = ff // SLAB
    tall = rows + seg

    def columns(weight):
        cut = weight.reshape(rows, parts, slabs, seg).transpose(2, 0, 1, 3)
        return cut.reshape(slabs, rows, SLAB)

    pack = jnp.concatenate(
        [
            jnp.concatenate([columns(w_gate), columns(w_up)], axis=2),
            w_down.reshape(slabs, seg, x.shape[1]),
        ],
        axis=1,
    ).reshape(slabs * tall, 2 * SLAB)
    every = gather_all(first_pack)
    pairs = [(every[k], every[k], 1) for k in range(parts)]
    pieces = Pieces(stacked=gather_all(jnp.concatenate([w_output, pack])))
    normed_one, *units, q_aug, k_aug, v_aug, gains = project(pairs, place, x, tables)
    attended_0, q_back_0 = attend(q_aug, k_aug, v_aug, 0, 4)
    attended_1, q_back_1 = attend(q_aug, k_aug, v_aug, 4, 4)
    attended = (attended_0, attended_1)
    first_sum, normed_two, normed_two_t = output_rows(pieces, place, attended, x, gains)
    out, back, grads = feed(
        pieces, place, rows, slabs, normed_two, normed_two_t, back_out, False
    )
    total = lax.psum(scatter_all(grads), "rep").astype(F32).reshape(slabs, tall, 2 * SLAB)
    back_first, back_attended, grad_out = middle(
        pieces, place, first_sum, back_out, attended, gains, [back]
    )
    halves_0 = attend_back(q_back_0, k_aug, v_aug, attended_0, back_attended, 0, 4)
    halves_1 = attend_back(q_back_1, k_aug, v_aug, attended_1, back_attended, 4, 4)
    back_raw, own, sib = raw_back(
        parts, place, (halves_0[0], halves_1[0], halves_0[1], halves_1[1]), units, normed_one,
        tables[0], tables[1], gains, grad_out,
    )
    every = jnp.stack([own, sib], axis=1).reshape((parts,) + own.shape[1:])
    attn_grad = lax.psum(scatter_all(every), "rep").astype(F32)
    input_grad = input_back(pairs, place, back_raw, x, back_first, gains)

    def uncut(block):
        return block.reshape(slabs, rows, parts, seg).transpose(1, 2, 0, 3).reshape(rows, ff)

    feed_grads = (
        uncut(total[:, :rows, :SLAB]),
        uncut(total[:, :rows, SLAB:]),
        total[:, rows:, :].reshape(slabs * seg, x.shape[1]),
    )
    return (first_sum + out).astype(BF16), input_grad, attn_grad, feed_grads


def fence(outputs, *hops):
    found = tie(*outputs, *hops)
    return found[: len(outputs)], list(found[len(outputs) :])


def block_paired(me, place, x, back_out, tables, first_pack, w_output, w_gate, w_up, w_down):
    rows = w_gate.shape[0]
    chunks = (3, 3, 3)

    first = hop(first_pack, 2)
    second = hop(first_pack, 4)
    twin = hop(first_pack, 1)
    made, (first, second, twin) = fence(
        [*pack_rows(chunks, w_output, w_gate, w_up, w_down), *tables], first, second, twin
    )
    packs, tables = list(made[:3]), made[3:]
    corner_a = hop(second[:rows], 2)
    corner_b = hop(first[rows:], 4)
    far = [twin] + [hop(piece, 1) for piece in (first, second, corner_a, corner_b)]
    near = [first_pack, first, second, corner_a, corner_b]
    pairs = []
    for k in range(3):
        pairs += [(near[k], near[k], 1), (far[k], far[k], 1)]
    pairs += [(near[3], near[4], 0), (far[3], far[4], 0)]

    pack = after(packs[0], corner_a, corner_b, far[1], far[2])
    first, second, twin = hop(pack, 2), hop(pack, 4), hop(pack, 1)
    normed_one, *units, q_aug, k_aug, v_aug, gains = project(pairs, place, x, tables)
    (attended_0, q_back_0, k_aug), (first, second, twin) = fence(
        [*attend(q_aug, k_aug, v_aug, 0, 4), k_aug], first, second, twin
    )
    corner_a, corner_b = hop(second[:, :512], 2), hop(first[:, 512:], 4)
    far = [hop(first, 1), hop(second, 1)]
    packs[1] = after(packs[1], first, second)
    waiting = [hop(packs[1], bit) for bit in (1, 2, 4, 6)]
    (attended_1, q_back_1), (corner_a, corner_b, *far) = fence(
        attend(q_aug, k_aug, v_aug, 4, 4), corner_a, corner_b, *far
    )
    attended = (attended_0, attended_1)
    early = weave(
        [[pack], [first], [second], [corner_a, corner_b]],
        [[twin], [far[0]], [far[1]], [hop(corner_a, 1), hop(corner_b, 1)]],
    )
    first_sum, normed_two, normed_two_t = output_rows(early, place, attended, x, gains)

    def finish(pack, twin, first, second, corner):
        near = (first, second, corner)
        far = [hop(piece, 1) for piece in near]
        return weave([[pack]] + [[a] for a in near], [[twin]] + [[a] for a in far])

    def feed_step(pieces, begin, n, paired):
        return feed(pieces, place, begin, n, normed_two, normed_two_t, back_out, paired)

    (out_0, back_0, own_0, sib_0, normed_two), waiting = fence(
        [*feed_step(early, rows, chunks[0], True), normed_two], *waiting
    )
    later = finish(packs[1], *waiting)
    waiting = [hop(packs[2], bit) for bit in (1, 2, 4, 6)]
    other_0 = hop(after(sib_0, *later.arrays), 1)
    *early_rows, corner = waiting
    (out_1, back_1, own_1, sib_1, normed_two), (other_0, *early_rows) = fence(
        [*feed_step(later, 0, chunks[1], True), normed_two], other_0, *early_rows
    )
    terms = combine(*[[(own_0, k), (other_0, k)] for k in (1, 2, 3)])
    corner, *terms = tie(corner, *terms)
    last = finish(packs[2], *early_rows, corner)
    other_1 = hop(after(sib_1, *last.arrays), 1)
    steps = [hop(term, 2 * k) for k, term in zip((1, 2, 3), terms)]
    (out_2, back_2, own_2, sib_2), (other_1, *steps) = fence(
        feed(last, place, 0, chunks[2], normed_two, normed_two_t, back_out, True), other_1, *steps
    )
    other_2 = hop(sib_2, 1)
    grads_0, term = combine(
        [(own_0, 0), (other_0, 0), *steps], [(own_1, 3), (other_1, 3)]
    )
    back_2, grads_0, term = tie(back_2, grads_0, term)
    moved_1 = hop(term, 4)
    inward_0 = rep_hop(grads_0, INWARD)
    middles = middle(
        early, place, first_sum, back_out, attended, gains, [back_0, back_1, back_2]
    )
    (back_first, back_attended, grad_out), (other_2,) = fence(middles, other_2)
    term = combine([(own_2, 3), (other_2, 3)])
    back_attended, term = tie(back_attended, term)
    moved_2 = hop(term, 2)
    halves = attend_back(q_back_0, k_aug, v_aug, attended_0, back_attended, 0, 4)
    (dq_0, dkv_0, back_attended), (moved_1, moved_2, inward_0) = fence(
        [*halves, back_attended], moved_1, moved_2, inward_0
    )
    one, two, three, four, half_0 = combine(
        [(own_1, 1), (other_1, 1), moved_1],
        [(own_1, 2), (other_1, 2)],
        [(own_2, 1), (other_2, 1)],
        [(own_2, 2), (other_2, 2), moved_2],
        [grads_0, inward_0],
    )
    back_attended, one, two, three, four, half_0 = tie(
        back_attended, one, two, three, four, half_0
    )
    first_1, second_1 = hop(one, 2), hop(two, 4)
    first_2, second_2 = hop(three, 2), hop(four, 4)
    across_0 = rep_hop(half_0, ACROSS)
    halves = attend_back(q_back_1, k_aug, v_aug, attended_1, back_attended, 4, 4)
    (dq_1, dkv_1), (first_1, second_1, across_0) = fence(halves, first_1, second_1, across_0)
    grads_1, total_0 = combine(
        [(own_1, 0), (other_1, 0), first_1, second_1], [half_0, across_0]
    )
    dq_1, grads_1, total_0 = tie(dq_1, grads_1, total_0)
    inward_1 = rep_hop(grads_1, INWARD)
    outward_0 = rep_hop(total_0, OUTWARD)
    result = raw_back(
        8, place, (dq_0, dq_1, dkv_0, dkv_1), units, normed_one, tables[0], tables[1], gains,
        grad_out,
    )
    (back_raw, own, sib), (first_2, second_2, inward_1, outward_0) = fence(
        result, first_2, second_2, inward_1, outward_0
    )
    other = hop(sib, 1)
    half_1, grads_2 = combine(
        [grads_1, inward_1], [(own_2, 0), (other_2, 0), first_2, second_2]
    )
    back_raw, other, half_1, grads_2 = tie(back_raw, other, half_1, grads_2)
    terms = combine(*[[(own, k), (other, k)] for k in (1, 2, 3)])
    back_raw, *terms = tie(back_raw, *terms)
    steps = [hop(term, 2 * k) for k, term in zip((1, 2, 3), terms)]
    across_1 = rep_hop(half_1, ACROSS)
    inward_2 = rep_hop(grads_2, INWARD)
    input_grad = input_back(pairs, place, back_raw, x, back_first, gains)
    (input_grad,), (across_1, inward_2) = fence([input_grad], across_1, inward_2)
    total_1, half_2 = combine([half_1, across_1], [grads_2, inward_2])
    first_sum, total_1, half_2 = tie(first_sum, total_1, half_2)
    outward_1 = rep_hop(total_1, OUTWARD)
    across_2 = rep_hop(half_2, ACROSS)
    outs = out_0.astype(F32) + out_1.astype(F32) + out_2.astype(F32)
    block_output = (first_sum + outs).astype(BF16)
    (block_output,), steps = fence([block_output], *steps)
    grads = combine([(own, 0), (other, 0), *steps])
    inward = rep_hop(grads, INWARD)
    across_2, _ = tie(across_2, grads)
    total_2 = combine([half_2, across_2])
    outward_2 = rep_hop(total_2, OUTWARD)
    inward, outward_1, _ = tie(inward, outward_1, total_2)
    half = combine([grads, inward])
    across = rep_hop(half, ACROSS)
    outward_2, across, _ = tie(outward_2, across, half)
    total = combine([half, across])
    outward = rep_hop(total, OUTWARD)
    total, outward_2 = tie(total, outward_2)
    spot = lax.axis_index("rep")
    flag = ((spot == 0) | (spot == 3)).astype(jnp.int32).reshape(1)
    feed_grads = unpack_rows(flag, total_0, outward_0, total_1, outward_1, total_2, outward_2)
    (*feed_grads,), (outward,) = fence(feed_grads, outward)
    return block_output, input_grad, at_end(total.astype(F32), outward), feed_grads


def solution(mesh):
    sizes = (mesh.shape["rep"], mesh.shape["shard"])
    whole = P(("rep", "shard"), None, None)
    matrix = P("shard", None)
    vector = P("shard")
    in_specs = (
        whole, P(("rep", "shard"), None), vector, matrix, matrix, matrix, vector, vector, matrix,
        vector, matrix, matrix, matrix, whole,
    )
    out_specs = (
        whole, whole, vector, matrix, matrix, matrix, vector, vector, matrix, vector, matrix,
        matrix, matrix,
    )
    return jax.shard_map(
        lambda *arrays: on_device(sizes, *arrays),
        mesh=mesh,
        in_specs=in_specs,
        out_specs=out_specs,
        check_vma=False,
    )
```
